32 devices in a mesh: ctx: 4 (over z), fsdp: 8 (over y, x, core).
Axes of the slice: x: 2, y: 2, z: 4, core: 2. Of those that a mesh axis runs over, the one named last changes fastest.
Arguments:
- hidden: bfloat16 [8, 1536, 2048], P('fsdp', 'ctx'), may hold values from -6 to 6
- token_order: int32 [8, 1536], P('fsdp'), may hold values from 0 to 1535, each once within a row
- lengths: int32 [8, 3], P('fsdp'), may hold values from 1 to 1024, 1536 in all within a row
- routes: int32 [8, 1536, 8], P('fsdp', 'ctx'), may hold values from 0 to 31, all different within a row; in each aligned block of 384 rows (0 to 383, 384 to 767, ..., all dimensions but the last counted through in order) at most 120 rows name the same one
- grad_output: bfloat16 [8, 1536, 2048], P('fsdp', 'ctx'), may hold values from -6 to 6
- w_query: bfloat16 [2048, 2048], P(('ctx', 'fsdp')), may hold values from -0.125 to 0.125
- w_key: bfloat16 [2048, 2048], P(('ctx', 'fsdp')), may hold values from -0.125 to 0.125
- w_value: bfloat16 [2048, 2048], P(('ctx', 'fsdp')), may hold values from -0.125 to 0.125
- w_out: bfloat16 [2048, 2048], P(('ctx', 'fsdp')), may hold values from -1 to 1
- w_router: bfloat16 [2048, 32], P(('ctx', 'fsdp')), may hold values from -0.1875 to 0.1875
- attn_gain: bfloat16 [2048], P(('ctx', 'fsdp')), may hold values from 0.099609375 to 1.8984375
- ffn_gain: bfloat16 [2048], P(('ctx', 'fsdp')), may hold values from 0.099609375 to 1.8984375
- query_gain: bfloat16 [2048], P(('ctx', 'fsdp')), may hold values from 0.099609375 to 1.8984375
- key_gain: bfloat16 [2048], P(('ctx', 'fsdp')), may hold values from 0.099609375 to 1.8984375
- w_gate: bfloat16 [32, 2048, 1024], P('fsdp', 'ctx'), may hold values from -0.125 to 0.125
- w_up: bfloat16 [32, 2048, 1024], P('fsdp', 'ctx'), may hold values from -0.125 to 0.125
- w_down: bfloat16 [32, 1024, 2048], P('fsdp', 'ctx'), may hold values from -0.1875 to 0.1875
Outputs:
- output: bfloat16 [8, 1536, 2048], P('fsdp', 'ctx')
- grad_hidden: float32 [8, 1536, 2048], P('fsdp', 'ctx')
- grad_w_query: float32 [2048, 2048], P(('ctx', 'fsdp'))
- grad_w_key: float32 [2048, 2048], P(('ctx', 'fsdp'))
- grad_w_value: float32 [2048, 2048], P(('ctx', 'fsdp'))
- grad_w_out: float32 [2048, 2048], P(('ctx', 'fsdp'))
- grad_w_router: float32 [2048, 32], P(('ctx', 'fsdp'))
- grad_attn_gain: float32 [2048], P(('ctx', 'fsdp'))
- grad_ffn_gain: float32 [2048], P(('ctx', 'fsdp'))
- grad_query_gain: float32 [2048], P(('ctx', 'fsdp'))
- grad_key_gain: float32 [2048], P(('ctx', 'fsdp'))
- grad_w_gate: float32 [32, 2048, 1024], P('fsdp', 'ctx')
- grad_w_up: float32 [32, 2048, 1024], P('fsdp', 'ctx')
- grad_w_down: float32 [32, 1024, 2048], P('fsdp', 'ctx')
The draws below stay inside these ranges and needn't reach their ends.
Inputs may be any that keep to these rules, and one draw needn't show every extreme that they name: `token_order`: each row of a group is a permutation of the 1536 packed positions. The 3 lengths of a group add up to 1536; the longest is exactly 1024. `routes`: A token names 8 different experts. Among the rows of one device no expert is named by more than 120 rows, a bound that some block reaches.
All inputs are finite; a program needn't handle non-finite values.
Results may differ from the reference program's by a relative error of at most 0.018.
Values may be sent and summed in bfloat16 or wider, within the bound.
A program may use at most 448 MiB of HBM per device.

```python
import math
import jax
import jax.numpy as jnp
import numpy as np
from jax import lax

D = 2048
HEAD_DIM = 128
FF = 1024
TOP = 8
NSEQ = 3
TOK_DEV = 384
EXPERTS = 32
GROUPS = 8
GROUP_TOK = 1536
SEQ_MOST = 1024
CAP = 120
N_CTX = 4


def steps_of(own_key, shape, shards, smallest, largest):
    level, own = 1.0, jax.random.fold_in(own_key, 6)
    for position, blocks in shards:
        steps = jnp.exp(jax.random.uniform(jax.random.fold_in(own, position), (blocks,), jnp.float32, smallest / len(shards), largest / len(shards)))
        level = level * jnp.repeat(steps, shape[position] // blocks).reshape([-1 if axis == position else 1 for axis in range(len(shape))])
    return level


def split_up(number_of, total, reach, slope):
    weights = [(1 << 20) // math.isqrt(standing ** slope) + 1 for standing in range(2, number_of + 1)]
    rest, given = total - reach - (number_of - 1), [1] * (number_of - 1)
    while rest > 0:
        candidates = [i for i in range(number_of - 1) if given[i] < reach]
        mass, budget = sum([weights[i] for i in candidates]), rest
        for i in candidates:
            more = min(reach - given[i], max(1, budget * weights[i] // mass), rest)
            given[i] = given[i] + more
            rest = rest - more
    return np.array([reach] + given)


def uneven_parts(key, number_of, total, bound, skew):
    if number_of == 2:
        one = jax.random.randint(key, (), max(1, total - bound), min(bound, total - 1) + 1)
        return jnp.stack([one, total - one])
    tallies = jnp.asarray(split_up(number_of, total, bound, skew), jnp.int32)
    pairs = (number_of - 1) // 2
    giver, sink = tallies[1:1 + 2 * pairs:2], tallies[2:2 + 2 * pairs:2]
    slack = jnp.minimum(giver - 1, bound - sink)
    moved = jax.random.randint(jax.random.fold_in(key, 1), (pairs,), 0, 1 << 20) % (slack + 1)
    tallies = tallies.at[1:1 + 2 * pairs:2].set(giver - moved).at[2:2 + 2 * pairs:2].set(sink + moved)
    return tallies[jax.random.permutation(jax.random.fold_in(key, 2), number_of)]


def deal_out(rng, own, number, rows, number_of, top, bound, slope):
    ranking = jax.random.permutation(rng, number_of)
    packed, ordinary = portions_of(number_of, rows * top, bound, slope, True), portions_of(number_of, rows * top, bound, slope, False)
    places = jnp.arange(number_of)

    def named(sizes, rotation):
        used = int((sizes > 0).sum())
        fixed = max(1, used // 4)
        shifted = fixed + (places - fixed + rotation * (used - fixed)) % max(1, number_of - fixed)
        return jnp.zeros((number_of,), jnp.int32).at[ranking[jnp.where(places < fixed, places, shifted)]].set(jnp.asarray(sizes, jnp.int32))

    sizes = jnp.where(number % 4 == 0, named(packed, number // 4), named(ordinary, number - number // 4 - 1))
    mixed = jax.random.permutation(jax.random.fold_in(own, 3), number_of)
    donor, sink = mixed[0:number_of // 2 * 2:2], mixed[1:number_of // 2 * 2:2]
    margin = jnp.minimum(sizes[donor] - 1, bound - sizes[sink]) // 2
    margin = jnp.where((donor == ranking[0]) | (sink == ranking[0]) | (sizes[sink] == 0), 0, jnp.maximum(margin, 0))
    shifted = jax.random.randint(jax.random.fold_in(own, 4), (number_of // 2,), 0, 1 << 20) % (margin + 1)
    sizes = sizes.at[donor].add(-shifted).at[sink].add(shifted)
    labels = jnp.searchsorted(jnp.cumsum(sizes), jnp.arange(rows * top), side="right").astype(jnp.int32)
    listing = labels.reshape(top, rows).T
    listing = listing[jax.random.permutation(jax.random.fold_in(own, 1), rows)]
    rotation = jax.random.randint(jax.random.fold_in(own, 2), (rows, 1), 0, top)
    return jnp.take_along_axis(listing, (jnp.arange(top)[None, :] + rotation) % top, axis=1)


def portions_of(count, total, most, slope, full):
    loads = [(1 << 20) // math.isqrt(grade ** slope) + 1 for grade in range(1, count + 1)]
    largest = most if full else min(most, max(-(-total // count), total * loads[0] // sum(loads)))
    least = 1 if total - largest >= count - 1 else 0
    holding, surplus = [largest] + [least] * (count - 1), total - largest - least * (count - 1)
    while surplus > 0:
        free = [i for i in range(1, count) if holding[i] < largest] or [i for i in range(1, count) if holding[i] < most]
        pool, remaining = sum([loads[i] for i in free]), surplus
        for i in free:
            extra = min(most - holding[i], max(1, remaining * loads[i] // pool), surplus)
            holding[i] = holding[i] + extra
            surplus = surplus - extra
    return np.array(holding)


def centred(rng, dims, width, most, shards=(), kind=jnp.bfloat16):
    loudness = steps_of(rng, dims, shards, -0.22, 0.18) if shards else 1.0
    drawn = jax.random.normal(rng, dims, jnp.float32) * width * loudness
    return jnp.minimum(jnp.maximum(drawn, -most), most).astype(kind)


def setup_inputs(seed: int = 0) -> dict:
    key_of = jax.random.split(jax.random.key(seed), 18)
    hidden = centred(key_of[0], (GROUPS, GROUP_TOK, D), 1.0, 6.0, ((0, 8), (1, 4)))
    token_order = jax.vmap(lambda own: jax.random.permutation(own, GROUP_TOK))(jax.random.split(key_of[1], GROUPS)).reshape((GROUPS, GROUP_TOK)).astype(jnp.int32)
    lengths = jax.vmap(lambda own: uneven_parts(own, NSEQ, GROUP_TOK, SEQ_MOST, 2))(jax.random.split(key_of[2], GROUPS)).reshape((GROUPS, NSEQ)).astype(jnp.int32)
    routes_keys = jax.random.split(jax.random.fold_in(key_of[3], 1), GROUPS * GROUP_TOK // TOK_DEV)
    routes_turns = jax.random.permutation(jax.random.fold_in(key_of[3], 3), GROUPS * GROUP_TOK // TOK_DEV)
    routes = jax.vmap(lambda own, number: deal_out(jax.random.fold_in(key_of[3], 2), own, number, TOK_DEV, EXPERTS, TOP, CAP, 1))(routes_keys, routes_turns).reshape((GROUPS, GROUP_TOK, TOP))
    grad_output = centred(key_of[4], (GROUPS, GROUP_TOK, D), 1.0, 6.0, ((0, 8), (1, 4)))
    w_query = centred(key_of[5], (D, D), D ** -0.5, 0.125, ((0, 32),))
    w_key = centred(key_of[6], (D, D), D ** -0.5, 0.125, ((0, 32),))
    w_value = centred(key_of[7], (D, D), D ** -0.5, 0.125, ((0, 32),))
    w_out = centred(key_of[8], (D, D), (D // 64) ** -0.5, 1.0, ((0, 32),))
    w_router = centred(key_of[9], (D, EXPERTS), (D // 2) ** -0.5, 0.1875, ((0, 32),))
    attn_gain = jnp.clip(1.0 + 0.18 * jax.random.normal(key_of[10], (D,), jnp.float32), 0.099609375, 1.8984375).astype(jnp.bfloat16)
    ffn_gain = jnp.clip(1.0 + 0.18 * jax.random.normal(key_of[11], (D,), jnp.float32), 0.099609375, 1.8984375).astype(jnp.bfloat16)
    query_gain = jnp.clip(1.0 + 0.18 * jax.random.normal(key_of[12], (D,), jnp.float32), 0.099609375, 1.8984375).astype(jnp.bfloat16)
    key_gain = jnp.clip(1.0 + 0.18 * jax.random.normal(key_of[13], (D,), jnp.float32), 0.099609375, 1.8984375).astype(jnp.bfloat16)
    w_gate = centred(key_of[14], (EXPERTS, D, FF), D ** -0.5, 0.125, ((0, 8), (1, 4)))
    w_up = centred(key_of[15], (EXPERTS, D, FF), D ** -0.5, 0.125, ((0, 8), (1, 4)))
    w_down = centred(key_of[16], (EXPERTS, FF, D), FF ** -0.5, 0.1875, ((0, 8), (1, 4)))
    return {"hidden": hidden, "token_order": token_order, "lengths": lengths, "routes": routes, "grad_output": grad_output, "w_query": w_query, "w_key": w_key, "w_value": w_value, "w_out": w_out, "w_router": w_router, "attn_gain": attn_gain, "ffn_gain": ffn_gain, "query_gain": query_gain, "key_gain": key_gain, "w_gate": w_gate, "w_up": w_up, "w_down": w_down}


epsilon = 1e-06
rope_base = 10000.0
masked_value = -1e+30
highest = lax.Precision.HIGHEST

@jax.custom_vjp
def low(v):
    return lax.optimization_barrier(v.astype(jnp.bfloat16)).astype(jnp.float32)

@jax.custom_vjp
def low_back(v):
    return v

def low_keep(v):
    return (low(v), None)

def low_pass(kept, grad):
    return (grad,)

def back_keep(v):
    return (v, None)

def back_low(kept, grad):
    return (low(grad),)
low.defvjp(low_keep, low_pass)
low_back.defvjp(back_keep, back_low)

def matmul(left, right):
    return jnp.dot(left, right, precision=highest, preferred_element_type=jnp.float32)

def rms_scaled(values, gain):
    return values * lax.rsqrt(lax.optimization_barrier(jnp.mean(values * values, axis=-1, keepdims=True)) + epsilon) * gain

def rotate(values, places):
    row_count = values.shape[0]
    head_count = values.shape[1] // HEAD_DIM
    half_width = HEAD_DIM // 2
    frequency = rope_base ** (-2.0 * jnp.arange(half_width).astype(values.dtype) / HEAD_DIM)
    angles = places.astype(values.dtype)[:, None] * frequency[None, :]
    cosine = jnp.cos(angles)[:, None, :]
    sine_part = jnp.sin(angles)[:, None, :]
    split_heads = values.reshape(row_count, head_count, HEAD_DIM)
    first_half = split_heads[:, :, :half_width]
    second_half = split_heads[:, :, half_width:]
    turned = jnp.concatenate([first_half * cosine - second_half * sine_part, second_half * cosine + first_half * sine_part], axis=-1)
    return turned.reshape(row_count, head_count * HEAD_DIM)

def seq_layout(order_row, seq_lengths):
    seq_ends = jnp.cumsum(seq_lengths).astype(jnp.int32)
    seq_ids = lax.optimization_barrier(jnp.sum((order_row[:, None] >= seq_ends[None, :]).astype(jnp.int32), axis=1)).astype(jnp.int32)
    starts = (seq_ends - seq_lengths).astype(jnp.int32)
    chosen = seq_ids[:, None] == jnp.arange(seq_lengths.shape[0]).astype(jnp.int32)[None, :]
    seq_start = lax.optimization_barrier(jnp.sum(jnp.where(chosen, starts[None, :], 0), axis=1)).astype(jnp.int32)
    return (seq_ids, (order_row - seq_start).astype(jnp.int32))

def group_forward(weights, rows_in, order_row, seq_lengths, route_rows):
    w_query, w_key, w_value, w_out, w_router, attn_gain, ffn_gain, query_gain, key_gain, w_gate, w_up, w_down = weights
    row_count = rows_in.shape[0]
    model_width = rows_in.shape[1]
    head_count = model_width // HEAD_DIM
    expert_count = w_router.shape[1]
    top_k = route_rows.shape[1]
    score_scale = 1.0 / HEAD_DIM ** 0.5
    seq_ids, places = seq_layout(order_row, seq_lengths)
    same_seq = seq_ids[:, None] == seq_ids[None, :]
    h_one = low(rms_scaled(rows_in, attn_gain))
    queries = low(rotate(rms_scaled(low_back(matmul(h_one, w_query)), query_gain), places))
    keys_rot = low(rotate(rms_scaled(low_back(matmul(h_one, w_key)), key_gain), places))
    values_low = low(low_back(matmul(h_one, w_value)))
    query_heads = queries.reshape(row_count, head_count, HEAD_DIM)
    key_heads = keys_rot.reshape(row_count, head_count, HEAD_DIM)
    value_heads = values_low.reshape(row_count, head_count, HEAD_DIM)
    raw_scores = jnp.einsum('thd,khd->htk', query_heads, key_heads, precision=highest, preferred_element_type=jnp.float32)
    scores = low_back(raw_scores * score_scale)
    scores = jnp.where(same_seq[None, :, :], scores, masked_value)
    attn_probs = low(jax.nn.softmax(scores, axis=-1))
    attended = jnp.einsum('htk,khd->thd', attn_probs, value_heads, precision=highest, preferred_element_type=jnp.float32)
    attended = low(low_back(attended.reshape(row_count, model_width)))
    middle = rows_in + low_back(matmul(attended, w_out))
    h_two = low(rms_scaled(middle, ffn_gain))
    router_probs = jax.nn.softmax(low_back(matmul(h_two, w_router)), axis=-1)
    chosen = route_rows[:, :, None] == jnp.arange(expert_count).astype(jnp.int32)[None, None, :]
    picked = lax.optimization_barrier(jnp.sum(jnp.where(chosen, router_probs[:, None, :], 0.0), axis=-1))
    pair_count = row_count * top_k
    pair_expert = route_rows.reshape(pair_count).astype(jnp.int32)
    one_hot = (pair_expert[:, None] == jnp.arange(expert_count).astype(jnp.int32)[None, :]).astype(jnp.int32)
    slot_rank = lax.optimization_barrier(jnp.sum(one_hot * (jnp.cumsum(one_hot, axis=0) - 1), axis=1)).astype(jnp.int32)
    bucket = N_CTX * CAP
    slot_ids = (pair_expert * bucket + slot_rank).astype(jnp.int32)
    source = jnp.full((expert_count * bucket,), pair_count, jnp.int32).at[slot_ids].set(jnp.arange(pair_count).astype(jnp.int32))
    filled = source < pair_count
    source_token = (jnp.minimum(source, pair_count - 1) // top_k).astype(jnp.int32)
    arrived = jnp.where(filled[:, None], h_two[source_token], 0.0)
    arrived = low_back(arrived).reshape(expert_count, bucket, model_width)
    gate_pre = low_back(jnp.einsum('ecd,edf->ecf', arrived, w_gate, precision=highest, preferred_element_type=jnp.float32))
    up_pre = low_back(jnp.einsum('ecd,edf->ecf', arrived, w_up, precision=highest, preferred_element_type=jnp.float32))
    act = low(jax.nn.silu(gate_pre) * up_pre)
    expert_out = jnp.einsum('ecf,efd->ecd', act, w_down, precision=highest, preferred_element_type=jnp.float32)
    expert_out = low(low_back(expert_out)).reshape(expert_count * bucket, model_width)
    pair_out = expert_out[slot_ids].reshape(row_count, top_k, model_width)
    return middle + lax.optimization_barrier(jnp.sum(picked[:, :, None] * pair_out, axis=1))

def reference(hidden, token_order, lengths, routes, grad_output, w_query, w_key, w_value, w_out, w_router, attn_gain, ffn_gain, query_gain, key_gain, w_gate, w_up, w_down):
    weights = tuple((array.astype(jnp.float32) for array in (w_query, w_key, w_value, w_out, w_router, attn_gain, ffn_gain, query_gain, key_gain, w_gate, w_up, w_down)))

    def forward(rows_all, params):

        def group_step(state_dummy, inputs):
            rows_in, order_row, seq_lengths, route_rows = inputs
            return (state_dummy, group_forward(params, rows_in, order_row, seq_lengths, route_rows))
        state_end, outputs = lax.scan(jax.checkpoint(group_step), jnp.zeros((), jnp.float32), (rows_all, token_order, lengths, routes))
        return outputs
    output, pullback = jax.vjp(forward, hidden.astype(jnp.float32), weights)
    grad_input, grads = pullback(grad_output.astype(jnp.float32))
    return (output.astype(jnp.bfloat16), grad_input, grads[0], grads[1], grads[2], grads[3], grads[4], grads[5], grads[6], grads[7], grads[8], grads[9], grads[10], grads[11])
```

```python
from functools import partial
import math

import jax
import jax.numpy as jnp
from jax import lax
from jax.experimental import pallas as pl
from jax.experimental.pallas import tpu as pltpu
from jax.sharding import PartitionSpec as P

HEAD_DIM = 128


epsilon = 1e-06
rope_base = 10000.0
masked_value = -1e30


def rms_scaled(values, gain):
    return values * lax.rsqrt(jnp.mean(values * values, axis=-1, keepdims=True) + epsilon) * gain


def rotate(values, places):
    row_count = values.shape[0]
    head_count = values.shape[1] // HEAD_DIM
    half_width = HEAD_DIM // 2
    frequency = rope_base ** (-2.0 * jnp.arange(half_width).astype(jnp.float32) / HEAD_DIM)
    angles = places.astype(jnp.float32)[:, None] * frequency[None, :]
    cosine = jnp.cos(angles)[:, None, :]
    sine_part = jnp.sin(angles)[:, None, :]
    split_heads = values.reshape(row_count, head_count, HEAD_DIM)
    first_half = split_heads[:, :, :half_width]
    second_half = split_heads[:, :, half_width:]
    turned = jnp.concatenate(
        [
            first_half * cosine - second_half * sine_part,
            second_half * cosine + first_half * sine_part,
        ],
        axis=-1,
    )
    return turned.reshape(row_count, head_count * HEAD_DIM)


def qk_post(values, gain, places):
    return rotate(rms_scaled(values, gain), places)


def route_weights(logits, chosen):
    router_probs = jax.nn.softmax(logits, axis=-1)
    return jnp.sum(jnp.where(chosen, router_probs[:, None, :], 0.0), axis=-1)


def seq_layout(order_row, seq_lengths):
    seq_ends = jnp.cumsum(seq_lengths)
    seq_ids = jnp.sum((order_row[:, None] >= seq_ends[None, :]).astype(jnp.int32), axis=1)
    starts = seq_ends - seq_lengths
    chosen = seq_ids[:, None] == jnp.arange(seq_lengths.shape[0], dtype=jnp.int32)[None, :]
    seq_start = jnp.sum(jnp.where(chosen, starts[None, :], 0), axis=1)
    return (seq_ids, order_row - seq_start)


def general_shards(
    hidden,
    token_order,
    lengths,
    routes,
    grad_output,
    w_query,
    w_key,
    w_value,
    w_out,
    w_router,
    attn_gain,
    ffn_gain,
    query_gain,
    key_gain,
    w_gate,
    w_up,
    w_down,
):
    hidden_in = hidden[0].astype(jnp.float32)
    row_count = hidden_in.shape[0]
    model_width = hidden_in.shape[1]
    head_count = model_width // HEAD_DIM
    score_scale = 1.0 / math.sqrt(HEAD_DIM)
    seq_all, place_all = seq_layout(token_order[0], lengths[0])
    first_row = lax.axis_index("ctx") * row_count
    seq_mine = lax.dynamic_slice_in_dim(seq_all, first_row, row_count)
    place_mine = lax.dynamic_slice_in_dim(place_all, first_row, row_count)
    same_seq = seq_mine[:, None] == seq_all[None, :]
    gathered = (
        lax.all_gather(w_query, ("ctx", "fsdp"), axis=0, tiled=True),
        lax.all_gather(w_key, ("ctx", "fsdp"), axis=0, tiled=True),
        lax.all_gather(w_value, ("ctx", "fsdp"), axis=0, tiled=True),
        lax.all_gather(w_out, ("ctx", "fsdp"), axis=0, tiled=True),
        lax.all_gather(w_router, ("ctx", "fsdp"), axis=0, tiled=True),
        lax.all_gather(attn_gain, ("ctx", "fsdp"), axis=0, tiled=True),
        lax.all_gather(ffn_gain, ("ctx", "fsdp"), axis=0, tiled=True),
        lax.all_gather(query_gain, ("ctx", "fsdp"), axis=0, tiled=True),
        lax.all_gather(key_gain, ("ctx", "fsdp"), axis=0, tiled=True),
    )
    (
        full_query,
        full_key,
        full_value,
        full_out,
        full_router,
        gain_attn,
        gain_ffn,
        gain_query,
        gain_key,
    ) = gathered
    gain_attn = gain_attn.astype(jnp.float32)
    gain_ffn = gain_ffn.astype(jnp.float32)
    gain_query = gain_query.astype(jnp.float32)
    gain_key = gain_key.astype(jnp.float32)
    h_one, norm_one_back = jax.vjp(rms_scaled, hidden_in, gain_attn)
    h_one_low = h_one.astype(jnp.bfloat16)
    query_raw = jnp.dot(h_one_low, full_query, preferred_element_type=jnp.float32)
    key_raw = jnp.dot(h_one_low, full_key, preferred_element_type=jnp.float32)
    values_low = jnp.dot(h_one_low, full_value, preferred_element_type=jnp.float32).astype(
        jnp.bfloat16
    )
    query_rot, query_back = jax.vjp(partial(qk_post, places=place_mine), query_raw, gain_query)
    key_rot, key_back = jax.vjp(partial(qk_post, places=place_mine), key_raw, gain_key)
    query_low = query_rot.astype(jnp.bfloat16)
    key_low = key_rot.astype(jnp.bfloat16)
    key_all, value_all = (
        lax.all_gather(key_low, "ctx", axis=0, tiled=True),
        lax.all_gather(values_low, "ctx", axis=0, tiled=True),
    )
    query_heads = query_low.reshape(row_count, head_count, HEAD_DIM)
    key_heads = key_all.reshape(-1, head_count, HEAD_DIM)
    value_heads = value_all.reshape(-1, head_count, HEAD_DIM)

    def scores_of():
        raw_scores = (
            jnp.einsum("thd,khd->htk", query_heads, key_heads, preferred_element_type=jnp.float32)
            * score_scale
        )
        return jnp.where(same_seq[None, :, :], raw_scores, masked_value)

    scores = scores_of()
    row_top = jnp.max(scores, axis=-1, keepdims=True)
    log_total = row_top + jnp.log(jnp.sum(jnp.exp(scores - row_top), axis=-1, keepdims=True))
    probs_low = jnp.exp(scores - log_total).astype(jnp.bfloat16)
    attended = jnp.einsum(
        "htk,khd->thd", probs_low, value_heads, preferred_element_type=jnp.float32
    )
    attended_low = attended.reshape(row_count, model_width).astype(jnp.bfloat16)
    middle = hidden_in + jnp.dot(attended_low, full_out, preferred_element_type=jnp.float32)
    h_two, norm_two_back = jax.vjp(rms_scaled, middle, gain_ffn)
    h_two_low = h_two.astype(jnp.bfloat16)
    logits = jnp.dot(h_two_low, full_router, preferred_element_type=jnp.float32)
    expert_count = full_router.shape[1]
    route_rows = routes[0]
    top_k = route_rows.shape[1]
    chosen = route_rows[:, :, None] == jnp.arange(expert_count, dtype=jnp.int32)[None, None, :]
    picked, route_back = jax.vjp(partial(route_weights, chosen=chosen), logits)
    pair_count = row_count * top_k
    capacity = 5 * row_count * top_k // (4 * expert_count)
    slot_count = expert_count * capacity
    group_size = lax.axis_size("fsdp")
    local_experts = w_gate.shape[0]
    pair_expert = route_rows.reshape(pair_count)
    one_hot = (pair_expert[:, None] == jnp.arange(expert_count, dtype=jnp.int32)[None, :]).astype(
        jnp.int32
    )
    slot_rank = jnp.sum(one_hot * (jnp.cumsum(one_hot, axis=0) - 1), axis=1)
    slot_ids = pair_expert * capacity + slot_rank
    source = (
        jnp.full((slot_count,), pair_count, jnp.int32)
        .at[slot_ids]
        .set(jnp.arange(pair_count, dtype=jnp.int32))
    )
    filled = source < pair_count
    source_pair = jnp.minimum(source, pair_count - 1)
    send_rows = jnp.where(
        filled[:, None], h_two_low[source_pair // top_k], jnp.zeros((), jnp.bfloat16)
    )
    send_rows = send_rows.reshape(group_size, local_experts, capacity, model_width)
    gate_full, up_full, down_full = (
        lax.all_gather(w_gate, "ctx", axis=1, tiled=True),
        lax.all_gather(w_up, "ctx", axis=1, tiled=True),
        lax.all_gather(w_down, "ctx", axis=1, tiled=True),
    )
    arrived_rows = lax.all_to_all(send_rows, "fsdp", split_axis=0, concat_axis=0, tiled=True)
    gate_part = jnp.einsum(
        "secd,edf->secf", arrived_rows, gate_full, preferred_element_type=jnp.float32
    )
    up_part = jnp.einsum(
        "secd,edf->secf", arrived_rows, up_full, preferred_element_type=jnp.float32
    )
    act_part = (jax.nn.silu(gate_part) * up_part).astype(jnp.bfloat16)
    result = jnp.einsum(
        "secf,efd->secd", act_part, down_full, preferred_element_type=jnp.float32
    ).astype(jnp.bfloat16)
    returned = lax.all_to_all(result, "fsdp", split_axis=0, concat_axis=0, tiled=True).reshape(
        slot_count, model_width
    )
    pair_out = returned[slot_ids].reshape(row_count, top_k, model_width)
    output = (middle + jnp.sum(picked[:, :, None] * pair_out, axis=1)).astype(jnp.bfloat16)
    grad_top = grad_output[0].astype(jnp.float32)
    grad_picked = jnp.sum(grad_top[:, None, :] * pair_out, axis=-1)
    grad_pair = (
        (picked[:, :, None] * grad_top[:, None, :])
        .astype(jnp.bfloat16)
        .reshape(pair_count, model_width)
    )
    grad_send = jnp.where(filled[:, None], grad_pair[source_pair], jnp.zeros((), jnp.bfloat16))
    grad_send = grad_send.reshape(group_size, local_experts, capacity, model_width)
    grad_arrived = lax.all_to_all(grad_send, "fsdp", split_axis=0, concat_axis=0, tiled=True)
    sigma = jax.nn.sigmoid(gate_part)
    act_low = (gate_part * sigma * up_part).astype(jnp.bfloat16)
    grad_act = jnp.einsum(
        "secd,efd->secf", grad_arrived, down_full, preferred_element_type=jnp.float32
    )
    grad_gate = (grad_act * up_part * sigma * (1.0 + gate_part * (1.0 - sigma))).astype(
        jnp.bfloat16
    )
    grad_up = (grad_act * gate_part * sigma).astype(jnp.bfloat16)
    grad_back = jnp.einsum(
        "secf,edf->secd", grad_gate, gate_full, preferred_element_type=jnp.float32
    )
    grad_back = (
        grad_back
        + jnp.einsum("secf,edf->secd", grad_up, up_full, preferred_element_type=jnp.float32)
    ).astype(jnp.bfloat16)
    grad_return = lax.all_to_all(
        grad_back, "fsdp", split_axis=0, concat_axis=0, tiled=True
    ).reshape(slot_count, model_width)
    grad_h_two = jnp.sum(
        grad_return[slot_ids].reshape(row_count, top_k, model_width).astype(jnp.float32), axis=1
    )
    (grad_logits,) = route_back(grad_picked)
    grad_logits_low = grad_logits.astype(jnp.bfloat16)
    grad_h_two = grad_h_two + jnp.einsum(
        "te,de->td", grad_logits_low, full_router, preferred_element_type=jnp.float32
    )
    grad_router = jnp.einsum(
        "td,te->de", h_two_low, grad_logits_low, preferred_element_type=jnp.float32
    )
    grad_middle, grad_ffn_gain = norm_two_back(grad_h_two)
    grad_middle = grad_middle + grad_top
    grad_branch = grad_middle.astype(jnp.bfloat16)
    grad_out_w = jnp.einsum(
        "td,te->de", attended_low, grad_branch, preferred_element_type=jnp.float32
    )
    grad_att = jnp.einsum(
        "te,de->td", grad_branch, full_out, preferred_element_type=jnp.float32
    ).astype(jnp.bfloat16)
    grad_att = grad_att.reshape(row_count, head_count, HEAD_DIM)
    scores = scores_of()
    probs_full = jnp.exp(scores - log_total)
    probs_again = probs_full.astype(jnp.bfloat16)
    grad_probs = jnp.einsum(
        "thd,khd->htk", grad_att, value_heads, preferred_element_type=jnp.float32
    )
    spread = jnp.sum(probs_full * grad_probs, axis=-1, keepdims=True)
    grad_scores = (probs_full * (grad_probs - spread)).astype(jnp.bfloat16)
    grad_query = (
        jnp.einsum(
            "htk,khd->thd", grad_scores, key_heads, preferred_element_type=jnp.float32
        ).reshape(row_count, model_width)
        * score_scale
    )
    grad_key_part = (
        jnp.einsum(
            "htk,thd->khd", grad_scores, query_heads, preferred_element_type=jnp.float32
        ).reshape(-1, model_width)
        * score_scale
    )
    grad_value_part = jnp.einsum(
        "htk,thd->khd", probs_again, grad_att, preferred_element_type=jnp.float32
    ).reshape(-1, model_width)
    grad_key, grad_value = (
        lax.psum_scatter(
            grad_key_part.astype(jnp.bfloat16), "ctx", scatter_dimension=0, tiled=True
        ).astype(jnp.float32),
        lax.psum_scatter(
            grad_value_part.astype(jnp.bfloat16), "ctx", scatter_dimension=0, tiled=True
        ).astype(jnp.float32),
    )
    grad_q_raw, grad_q_gain = query_back(grad_query)
    grad_k_raw, grad_k_gain = key_back(grad_key)
    grad_q_low = grad_q_raw.astype(jnp.bfloat16)
    grad_k_low = grad_k_raw.astype(jnp.bfloat16)
    grad_v_low = grad_value.astype(jnp.bfloat16)
    grad_query_w = jnp.einsum(
        "td,te->de", h_one_low, grad_q_low, preferred_element_type=jnp.float32
    )
    grad_key_w = jnp.einsum("td,te->de", h_one_low, grad_k_low, preferred_element_type=jnp.float32)
    grad_value_w = jnp.einsum(
        "td,te->de", h_one_low, grad_v_low, preferred_element_type=jnp.float32
    )
    grad_h_one = jnp.einsum("te,de->td", grad_q_low, full_query, preferred_element_type=jnp.float32)
    grad_h_one = grad_h_one + jnp.einsum(
        "te,de->td", grad_k_low, full_key, preferred_element_type=jnp.float32
    )
    grad_h_one = grad_h_one + jnp.einsum(
        "te,de->td", grad_v_low, full_value, preferred_element_type=jnp.float32
    )
    grad_input_norm, grad_attn_gain = norm_one_back(grad_h_one)
    grad_input = grad_middle + grad_input_norm
    totals = (
        lax.psum_scatter(grad_query_w, ("ctx", "fsdp"), scatter_dimension=0, tiled=True),
        lax.psum_scatter(grad_key_w, ("ctx", "fsdp"), scatter_dimension=0, tiled=True),
        lax.psum_scatter(grad_value_w, ("ctx", "fsdp"), scatter_dimension=0, tiled=True),
        lax.psum_scatter(grad_out_w, ("ctx", "fsdp"), scatter_dimension=0, tiled=True),
        lax.psum_scatter(grad_router, ("ctx", "fsdp"), scatter_dimension=0, tiled=True),
        lax.psum_scatter(grad_attn_gain, ("ctx", "fsdp"), scatter_dimension=0, tiled=True),
        lax.psum_scatter(grad_ffn_gain, ("ctx", "fsdp"), scatter_dimension=0, tiled=True),
        lax.psum_scatter(grad_q_gain, ("ctx", "fsdp"), scatter_dimension=0, tiled=True),
        lax.psum_scatter(grad_k_gain, ("ctx", "fsdp"), scatter_dimension=0, tiled=True),
    )
    grad_down_w = jnp.einsum(
        "secf,secd->efd", act_low, grad_arrived, preferred_element_type=jnp.float32
    )
    grad_gate_w = jnp.einsum(
        "secd,secf->edf", arrived_rows, grad_gate, preferred_element_type=jnp.float32
    )
    grad_up_w = jnp.einsum(
        "secd,secf->edf", arrived_rows, grad_up, preferred_element_type=jnp.float32
    )
    gate_grad, up_grad, down_grad = (
        lax.psum_scatter(
            grad_gate_w.astype(jnp.bfloat16), "ctx", scatter_dimension=1, tiled=True
        ).astype(jnp.float32),
        lax.psum_scatter(
            grad_up_w.astype(jnp.bfloat16), "ctx", scatter_dimension=1, tiled=True
        ).astype(jnp.float32),
        lax.psum_scatter(
            grad_down_w.astype(jnp.bfloat16), "ctx", scatter_dimension=1, tiled=True
        ).astype(jnp.float32),
    )
    return (
        output[None],
        grad_input[None],
        totals[0],
        totals[1],
        totals[2],
        totals[3],
        totals[4],
        totals[5],
        totals[6],
        totals[7],
        totals[8],
        gate_grad,
        up_grad,
        down_grad,
    )


def masked_probs(query, key, seq_rows, seq_cols, scale):
    scores = (
        lax.dot_general(query, key, (((1,), (1,)), ((), ())), preferred_element_type=jnp.float32)
        * scale
    )
    scores = jnp.where(seq_rows == seq_cols, scores, masked_value)
    top = jnp.max(scores, axis=-1, keepdims=True)
    weights = jnp.exp(scores - top)
    return weights / jnp.sum(weights, axis=-1, keepdims=True)


def attend_kernel(scale, seq_rows, seq_cols, query, key, value, out):
    probs = masked_probs(query[...], key[...], seq_rows[...], seq_cols[...], scale)
    out[...] = jnp.dot(
        probs.astype(jnp.bfloat16), value[...], preferred_element_type=jnp.float32
    ).astype(out.dtype)


def attend_back_kernel(
    scale, seq_rows, seq_cols, query, key, value, grad, grad_query, grad_key, grad_value
):
    @pl.when(pl.program_id(1) == 0)
    def _():
        grad_key[...] = jnp.zeros_like(grad_key)
        grad_value[...] = jnp.zeros_like(grad_value)

    probs = masked_probs(query[...], key[...], seq_rows[...], seq_cols[...], scale)
    grad_probs = lax.dot_general(
        grad[...], value[...], (((1,), (1,)), ((), ())), preferred_element_type=jnp.float32
    )
    spread = jnp.sum(probs * grad_probs, axis=-1, keepdims=True)
    grad_scores = (probs * (grad_probs - spread)).astype(jnp.bfloat16)
    grad_query[...] = (
        jnp.dot(grad_scores, key[...], preferred_element_type=jnp.float32) * scale
    )
    grad_key[...] += (
        lax.dot_general(
            grad_scores,
            query[...],
            (((0,), (0,)), ((), ())),
            preferred_element_type=jnp.float32,
        )
        * scale
    )
    grad_value[...] += lax.dot_general(
        probs.astype(jnp.bfloat16),
        grad[...],
        (((0,), (0,)), ((), ())),
        preferred_element_type=jnp.float32,
    )


def attention_specs(rows, block):
    per_block = pl.BlockSpec((block, HEAD_DIM), lambda h, i: (i, h))
    per_head = pl.BlockSpec((rows, HEAD_DIM), lambda h, i: (0, h))
    seqs = [
        pl.BlockSpec((block, 1), lambda h, i: (i, 0)),
        pl.BlockSpec((1, rows), lambda h, i: (0, 0)),
    ]
    return per_block, per_head, seqs


def attend(seq_ids, query, key, value):
    rows, width = query.shape
    block = math.gcd(rows, 256)
    per_block, per_head, seqs = attention_specs(rows, block)
    pairs = rows * rows * width
    return pl.pallas_call(
        partial(attend_kernel, 1.0 / math.sqrt(HEAD_DIM)),
        grid=(width // HEAD_DIM, rows // block),
        in_specs=seqs + [per_block, per_head, per_head],
        out_specs=per_block,
        out_shape=jax.ShapeDtypeStruct((rows, width), jnp.bfloat16),
        cost_estimate=pl.CostEstimate(
            flops=4 * pairs, bytes_accessed=8 * rows * width, transcendentals=pairs // HEAD_DIM
        ),
        compiler_params=pltpu.CompilerParams(vmem_limit_bytes=48 << 20),
        name="attend",
    )(seq_ids[:, None], seq_ids[None, :], query, key, value)


def attend_back(seq_ids, query, key, value, grad):
    rows, width = query.shape
    block = math.gcd(rows, 256)
    per_block, per_head, seqs = attention_specs(rows, block)
    pairs = rows * rows * width
    return pl.pallas_call(
        partial(attend_back_kernel, 1.0 / math.sqrt(HEAD_DIM)),
        grid=(width // HEAD_DIM, rows // block),
        in_specs=seqs + [per_block, per_head, per_head, per_block],
        out_specs=(per_block, per_head, per_head),
        out_shape=(jax.ShapeDtypeStruct((rows, width), jnp.float32),) * 3,
        cost_estimate=pl.CostEstimate(
            flops=10 * pairs, bytes_accessed=20 * rows * width, transcendentals=pairs // HEAD_DIM
        ),
        compiler_params=pltpu.CompilerParams(vmem_limit_bytes=48 << 20),
        name="attend_back",
    )(seq_ids[:, None], seq_ids[None, :], query, key, value, grad)


def turn(values, cosine, sine, inverse=False):
    rows, width = values.shape
    split = values.reshape(rows, width // HEAD_DIM, 2, HEAD_DIM // 2)
    first, second = split[:, :, 0], split[:, :, 1]
    cosine = cosine[:, None, :]
    sine = sine[:, None, :]
    if inverse:
        sine = -sine
    return jnp.stack(
        [first * cosine - second * sine, second * cosine + first * sine], axis=2
    ).reshape(rows, width)


def tie(array, *others):
    anywhere = pl.BlockSpec(memory_space=pl.ANY)
    return pl.pallas_call(
        lambda *refs: None,
        in_specs=[anywhere] * (1 + len(others)),
        out_specs=anywhere,
        out_shape=jax.ShapeDtypeStruct(array.shape, array.dtype),
        input_output_aliases={0: 0},
        name="tie",
    )(array, *others)


def mm(left, right):
    return jnp.dot(left, right, preferred_element_type=jnp.float32)


def mm_t(left, right):
    return lax.dot_general(
        left, right, (((1,), (1,)), ((), ())), preferred_element_type=jnp.float32
    )


def t_mm(left, right):
    return lax.dot_general(
        left, right, (((0,), (0,)), ((), ())), preferred_element_type=jnp.float32
    )


def plane_shards(
    hidden,
    token_order,
    lengths,
    routes,
    grad_output,
    w_query,
    w_key,
    w_value,
    w_out,
    w_router,
    attn_gain,
    ffn_gain,
    query_gain,
    key_gain,
    w_gate,
    w_up,
    w_down,
):
    f32, bf16 = jnp.float32, jnp.bfloat16
    both = ("ctx", "fsdp")
    planes = lax.axis_size("ctx")
    columns = lax.axis_size("fsdp")
    plane = lax.axis_index("ctx")
    row_count, width = hidden.shape[1:]
    group_rows = row_count * planes
    share = width // planes
    strip = w_query.shape[0]
    first_row = plane * row_count

    hidden_all = lax.all_gather(hidden[0], "ctx", axis=0, tiled=True)
    experts = w_router.shape[1]
    qkv = jnp.stack([w_query, w_key, w_value], axis=1).reshape(strip, 3, planes, share)
    qkv = qkv.transpose(2, 0, 1, 3).reshape(planes, strip, 3 * share)
    small = jnp.concatenate(
        [w_router] + [g[:, None] for g in (attn_gain, ffn_gain, query_gain, key_gain)], axis=1
    )
    small_rows = -(-small.size // (3 * share))
    route_size = routes.size // (3 * share)
    small_flat = jnp.pad(small.reshape(-1), (0, small_rows * 3 * share - small.size))
    tail = jnp.concatenate(
        [small_flat.reshape(small_rows, -1), routes.astype(bf16).reshape(route_size, -1)]
    )
    tail = jnp.broadcast_to(tail[None], (planes,) + tail.shape)
    packed = lax.all_to_all(jnp.concatenate([qkv, tail], axis=1), "ctx", 0, 0, tiled=True)
    routes_all = packed[:, strip + small_rows :].astype(jnp.int32).reshape(group_rows, -1)
    packed = lax.all_gather(packed[:, : strip + small_rows], "fsdp", axis=1, tiled=True)
    packed = packed.reshape(planes, columns, strip + small_rows, 3 * share)
    qkv = packed[:, :, :strip].reshape(width, 3 * share)
    small = packed[:, :, strip:].reshape(planes * columns, -1)[:, : small.size]
    small = small.reshape(width, experts + 4)
    full_router = small[:, :experts]
    gain_attn, gain_ffn, gain_query, gain_key = [
        small[:, experts + i].astype(f32) for i in range(4)
    ]
    out_rows = lax.all_gather(w_out, "fsdp", axis=0, tiled=True)
    def exchange(parts):
        came = [parts[plane]]
        for step in range(1, 4):
            pairs = [(i, i ^ step) for i in range(4)]
            came.append(lax.ppermute(parts[plane ^ step], "ctx", pairs))
        came = jnp.stack(came)
        return [came[plane ^ i] for i in range(4)]

    gate = jnp.concatenate(exchange(w_gate))
    up = jnp.concatenate(exchange(w_up))
    down = jnp.concatenate(exchange(w_down))
    grad_all = lax.all_gather(grad_output[0], "ctx", axis=0, tiled=True)

    seq_ids, places = seq_layout(token_order[0], lengths[0])
    experts_here = w_gate.shape[0]
    column_expert = experts_here * jnp.arange(columns, dtype=jnp.int32) + plane
    named = jnp.any(routes_all[:, :, None] == column_expert[None, None, :], axis=1)
    named = named.reshape(planes, row_count, columns)
    capacity = 5 * row_count * routes.shape[2] // (4 * experts)
    rank = jnp.cumsum(named.astype(jnp.int32), axis=1) - 1
    position = jnp.where(named, rank, -1).transpose(2, 0, 1)
    slots = jnp.arange(capacity, dtype=jnp.int32)
    holds = position[:, :, None, :] == slots[None, None, :, None]
    select = holds.astype(bf16)

    def dispatch(rows):
        rows = rows.reshape(planes, row_count, width)
        picked_rows = jnp.einsum("fbsr,brd->fbsd", select, rows, preferred_element_type=f32)
        return picked_rows.astype(bf16)

    def combine(rows):
        rows = rows.reshape(columns, planes, capacity, width)
        sums = jnp.einsum("fbsr,fbsd->brd", select, rows, preferred_element_type=f32)
        return sums.reshape(group_rows, width).astype(bf16)

    grad_send = dispatch(grad_all)
    grad_in = lax.all_to_all(grad_send, "fsdp", 0, 0, tiled=True).reshape(-1, width)

    frequency = rope_base ** (
        -2.0 * jnp.arange(HEAD_DIM // 2).astype(f32) / HEAD_DIM
    )
    angles = places.astype(f32)[:, None] * frequency[None, :]
    cosine, sine = lax.optimization_barrier((jnp.cos(angles), jnp.sin(angles)))
    hidden_wide = hidden_all.astype(f32)
    scale_one = lax.rsqrt(jnp.mean(hidden_wide * hidden_wide, axis=-1, keepdims=True) + epsilon)
    h_one = (hidden_wide * scale_one * gain_attn).astype(bf16)
    raw = mm(h_one, qkv)
    query_raw, key_raw = raw[:, :share], raw[:, share : 2 * share]
    values = raw[:, 2 * share :].astype(bf16)
    squares = jnp.stack([jnp.sum(query_raw**2, axis=1), jnp.sum(key_raw**2, axis=1)])
    squares = lax.psum(squares, "ctx")
    scales = lax.rsqrt(squares / width + epsilon)[:, :, None]
    query_hat, key_hat = query_raw * scales[0], key_raw * scales[1]
    my_query_gain = lax.dynamic_slice_in_dim(gain_query, plane * share, share)
    my_key_gain = lax.dynamic_slice_in_dim(gain_key, plane * share, share)
    query = turn(query_hat * my_query_gain, cosine, sine).astype(bf16)
    key = turn(key_hat * my_key_gain, cosine, sine).astype(bf16)
    attended = attend(seq_ids, query, key, values)
    attended = tie(attended, gate, grad_send)
    branch = lax.psum_scatter(
        mm(attended, out_rows).astype(bf16), "ctx", scatter_dimension=0, tiled=True
    )
    middle = hidden[0].astype(f32) + branch.astype(f32)
    scale_two = lax.rsqrt(jnp.mean(middle * middle, axis=-1, keepdims=True) + epsilon)
    middle_hat = middle * scale_two
    h_two = (middle_hat * gain_ffn).astype(bf16)

    h_all = tie(lax.all_gather(h_two, "ctx", axis=0, tiled=True), grad_in)
    probs_all = jax.nn.softmax(mm(h_all, full_router), axis=-1)
    probs = jax.nn.softmax(mm(h_two, full_router), axis=-1)
    probs_plane = lax.dynamic_index_in_dim(
        probs_all.reshape(group_rows, columns, experts_here), plane, 2, keepdims=False
    )
    rows_in = lax.all_to_all(dispatch(h_all), "fsdp", 0, 0, tiled=True).reshape(-1, width)
    probs_plane = probs_plane.reshape(planes, row_count, columns).transpose(2, 0, 1)
    slot_probs = jnp.sum(jnp.where(holds, probs_plane[:, :, None, :], 0.0), axis=3)
    picked = lax.all_to_all(slot_probs, "fsdp", 0, 0, tiled=True).reshape(-1, 1)
    gate_pre = mm(rows_in, gate)
    up_pre = mm(rows_in, up)
    sigma = jax.nn.sigmoid(gate_pre)
    silu = gate_pre * sigma
    act = (silu * up_pre).astype(bf16)
    grad_raw = mm_t(grad_in, down)
    grad_act = grad_raw * picked
    grad_gate = (grad_act * up_pre * sigma * (1.0 + gate_pre * (1.0 - sigma))).astype(bf16)
    grad_up = (grad_act * silu).astype(bf16)
    grad_picked = jnp.sum(grad_raw * act.astype(f32), axis=1)
    grad_rows = (mm_t(grad_gate, gate) + mm_t(grad_up, up)).astype(bf16)
    grad_rows = lax.all_to_all(
        grad_rows.reshape(columns, planes * capacity, width), "fsdp", 0, 0, tiled=True
    )
    grad_picked = lax.all_to_all(
        grad_picked.reshape(columns, planes, capacity), "fsdp", 0, 0, tiled=True
    )
    act_picked = (act.astype(f32) * picked).astype(bf16)
    grad_gate_w = t_mm(rows_in, grad_gate).astype(bf16)
    grad_up_w = t_mm(rows_in, grad_up).astype(bf16)

    def spread_out(whole):
        parts = whole.reshape(planes, whole.shape[0] // planes, whole.shape[1])
        return jnp.stack(exchange(parts)).astype(f32)

    gate_grad, up_grad = spread_out(grad_gate_w), spread_out(grad_up_w)
    grad_rows = tie(grad_rows, gate_grad, up_grad)
    grad_h_two = lax.psum_scatter(
        combine(grad_rows), "ctx", scatter_dimension=0, tiled=True
    ).astype(f32)
    expert_out = (mm(act, down) * picked).astype(bf16)
    expert_out = lax.all_to_all(
        expert_out.reshape(columns, planes * capacity, width), "fsdp", 0, 0, tiled=True
    )
    mixed_part = combine(expert_out)
    mixed = lax.psum_scatter(mixed_part, "ctx", scatter_dimension=0, tiled=True)
    output = (middle + mixed.astype(f32)).astype(bf16)
    down_grad = spread_out(t_mm(act_picked, grad_in).astype(bf16))

    u_plane = jnp.sum(jnp.where(holds, grad_picked[..., None], 0.0), axis=2)
    u_mine = lax.all_to_all(
        u_plane, "ctx", 1, 1, tiled=True
    )
    u_mine = u_mine.reshape(experts, row_count).T
    grad_logits = probs * (u_mine - jnp.sum(probs * u_mine, axis=-1, keepdims=True))
    grad_logits = grad_logits.astype(bf16)
    grad_h_two = grad_h_two + mm_t(grad_logits, full_router)
    grad_router = t_mm(h_two, grad_logits)

    grad_top = grad_output[0].astype(f32)
    grad_ffn_gain = jnp.sum(grad_h_two * middle_hat, axis=0)
    grad_hat = grad_h_two * gain_ffn
    grad_middle = grad_top + scale_two * (
        grad_hat - middle_hat * jnp.mean(grad_hat * middle_hat, axis=-1, keepdims=True)
    )
    grad_branch = lax.all_gather(grad_middle.astype(bf16), "ctx", axis=0, tiled=True)
    grad_att = tie(mm_t(grad_branch, out_rows).astype(bf16), mixed_part)
    grad_query, grad_key, grad_value = attend_back(seq_ids, query, key, values, grad_att)
    grad_out_w = lax.psum_scatter(
        t_mm(attended, grad_branch).astype(bf16), "fsdp", scatter_dimension=0, tiled=True
    ).astype(f32)
    grad_query = turn(grad_query, cosine, sine, inverse=True)
    grad_key = turn(grad_key, cosine, sine, inverse=True)
    grad_q_gain = jnp.sum(grad_query * query_hat, axis=0)
    grad_k_gain = jnp.sum(grad_key * key_hat, axis=0)
    grad_query = grad_query * my_query_gain
    grad_key = grad_key * my_key_gain
    dots = jnp.stack(
        [jnp.sum(grad_query * query_hat, axis=1), jnp.sum(grad_key * key_hat, axis=1)]
    )
    dots = (lax.psum(dots, "ctx") / width)[:, :, None]
    grad_qkv = jnp.concatenate(
        [
            scales[0] * (grad_query - query_hat * dots[0]),
            scales[1] * (grad_key - key_hat * dots[1]),
            grad_value,
        ],
        axis=1,
    ).astype(bf16)
    grad_qkv = tie(grad_qkv, down_grad, mixed)
    grad_part = mm_t(grad_qkv, qkv)
    grad_h_one = lax.psum_scatter(
        grad_part.astype(bf16), "ctx", scatter_dimension=0, tiled=True
    ).astype(f32)
    grad_attn_gain = jnp.sum(grad_part * (hidden_wide * scale_one), axis=0)
    grad_qkv_w = t_mm(h_one, grad_qkv).reshape(planes, columns, strip, 3 * share)
    grad_qkv_w = lax.all_to_all(
        grad_qkv_w.transpose(1, 0, 2, 3).astype(bf16), "fsdp", 0, 0, tiled=True
    )
    grad_qkv_w = jnp.sum(grad_qkv_w.astype(f32), axis=0).astype(bf16)
    grad_qkv_w = lax.all_to_all(grad_qkv_w, "ctx", 0, 0, tiled=True)
    grad_qkv_w = grad_qkv_w.reshape(planes, strip, 3, share).transpose(2, 1, 0, 3)
    grad_qkv_w = grad_qkv_w.reshape(3, strip, width).astype(f32)

    x_hat = hidden[0].astype(f32)
    scale_mine = lax.rsqrt(jnp.mean(x_hat * x_hat, axis=-1, keepdims=True) + epsilon)
    x_hat = x_hat * scale_mine
    grad_hat = grad_h_one * gain_attn
    grad_input = grad_middle + scale_mine * (
        grad_hat - x_hat * jnp.mean(grad_hat * x_hat, axis=-1, keepdims=True)
    )

    def summed(arrays):
        parts = jnp.concatenate(
            [x.reshape(planes * columns, -1) for x in arrays], axis=1
        )
        return jnp.sum(lax.all_to_all(parts, both, 0, 0, tiled=True), axis=0)

    totals = summed([grad_router, grad_ffn_gain])
    own = jnp.arange(planes)[:, None] == plane
    gains = [jnp.where(own, g[None], 0.0) for g in (grad_q_gain, grad_k_gain)]
    gains = summed([grad_attn_gain] + gains)
    return (
        output[None],
        grad_input[None],
        grad_qkv_w[0],
        grad_qkv_w[1],
        grad_qkv_w[2],
        grad_out_w,
        totals[: strip * experts].reshape(strip, experts),
        gains[:strip],
        totals[strip * experts :],
        gains[strip : 2 * strip],
        gains[2 * strip :],
        gate_grad,
        up_grad,
        down_grad,
    )


def solution(mesh):
    placed = (
        P("fsdp", "ctx", None),
        P("fsdp", None),
        P("fsdp", None),
        P("fsdp", "ctx", None),
        P("fsdp", "ctx", None),
        P(("ctx", "fsdp"), None),
        P(("ctx", "fsdp"), None),
        P(("ctx", "fsdp"), None),
        P(("ctx", "fsdp"), None),
        P(("ctx", "fsdp"), None),
        P(("ctx", "fsdp")),
        P(("ctx", "fsdp")),
        P(("ctx", "fsdp")),
        P(("ctx", "fsdp")),
        P("fsdp", "ctx", None),
        P("fsdp", "ctx", None),
        P("fsdp", "ctx", None),
    )

    def shards(*operands):
        experts_here = operands[14].shape[0]
        heads = operands[0].shape[2] // HEAD_DIM
        planes = mesh.shape["ctx"]
        whole_experts = experts_here == planes and heads % planes == 0
        return (plane_shards if whole_experts else general_shards)(*operands)

    return jax.shard_map(
        shards,
        mesh=mesh,
        in_specs=placed,
        out_specs=(
            P("fsdp", "ctx", None),
            P("fsdp", "ctx", None),
            P(("ctx", "fsdp"), None),
            P(("ctx", "fsdp"), None),
            P(("ctx", "fsdp"), None),
            P(("ctx", "fsdp"), None),
            P(("ctx", "fsdp"), None),
            P(("ctx", "fsdp")),
            P(("ctx", "fsdp")),
            P(("ctx", "fsdp")),
            P(("ctx", "fsdp")),
            P("fsdp", "ctx", None),
            P("fsdp", "ctx", None),
            P("fsdp", "ctx", None),
        ),
        check_vma=False,
    )
```

```python
from functools import partial
import math

import jax
import jax.numpy as jnp
from jax import lax
from jax.experimental import pallas as pl
from jax.experimental.pallas import tpu as pltpu
from jax.sharding import PartitionSpec as P

HEAD_DIM = 128


epsilon = 1e-06
rope_base = 10000.0
masked_value = -1e30


def rms_scaled(values, gain):
    return values * lax.rsqrt(jnp.mean(values * values, axis=-1, keepdims=True) + epsilon) * gain


def rotate(values, places):
    row_count = values.shape[0]
    head_count = values.shape[1] // HEAD_DIM
    half_width = HEAD_DIM // 2
    frequency = rope_base ** (-2.0 * jnp.arange(half_width).astype(jnp.float32) / HEAD_DIM)
    angles = places.astype(jnp.float32)[:, None] * frequency[None, :]
    cosine = jnp.cos(angles)[:, None, :]
    sine_part = jnp.sin(angles)[:, None, :]
    split_heads = values.reshape(row_count, head_count, HEAD_DIM)
    first_half = split_heads[:, :, :half_width]
    second_half = split_heads[:, :, half_width:]
    turned = jnp.concatenate(
        [
            first_half * cosine - second_half * sine_part,
            second_half * cosine + first_half * sine_part,
        ],
        axis=-1,
    )
    return turned.reshape(row_count, head_count * HEAD_DIM)


def qk_post(values, gain, places):
    return rotate(rms_scaled(values, gain), places)


def route_weights(logits, chosen):
    router_probs = jax.nn.softmax(logits, axis=-1)
    return jnp.sum(jnp.where(chosen, router_probs[:, None, :], 0.0), axis=-1)


def seq_layout(order_row, seq_lengths):
    seq_ends = jnp.cumsum(seq_lengths)
    seq_ids = jnp.sum((order_row[:, None] >= seq_ends[None, :]).astype(jnp.int32), axis=1)
    starts = seq_ends - seq_lengths
    chosen = seq_ids[:, None] == jnp.arange(seq_lengths.shape[0], dtype=jnp.int32)[None, :]
    seq_start = jnp.sum(jnp.where(chosen, starts[None, :], 0), axis=1)
    return (seq_ids, order_row - seq_start)


def general_shards(
    hidden,
    token_order,
    lengths,
    routes,
    grad_output,
    w_query,
    w_key,
    w_value,
    w_out,
    w_router,
    attn_gain,
    ffn_gain,
    query_gain,
    key_gain,
    w_gate,
    w_up,
    w_down,
):
    hidden_in = hidden[0].astype(jnp.float32)
    row_count = hidden_in.shape[0]
    model_width = hidden_in.shape[1]
    head_count = model_width // HEAD_DIM
    score_scale = 1.0 / math.sqrt(HEAD_DIM)
    seq_all, place_all = seq_layout(token_order[0], lengths[0])
    first_row = lax.axis_index("ctx") * row_count
    seq_mine = lax.dynamic_slice_in_dim(seq_all, first_row, row_count)
    place_mine = lax.dynamic_slice_in_dim(place_all, first_row, row_count)
    same_seq = seq_mine[:, None] == seq_all[None, :]
    gathered = (
        lax.all_gather(w_query, ("ctx", "fsdp"), axis=0, tiled=True),
        lax.all_gather(w_key, ("ctx", "fsdp"), axis=0, tiled=True),
        lax.all_gather(w_value, ("ctx", "fsdp"), axis=0, tiled=True),
        lax.all_gather(w_out, ("ctx", "fsdp"), axis=0, tiled=True),
        lax.all_gather(w_router, ("ctx", "fsdp"), axis=0, tiled=True),
        lax.all_gather(attn_gain, ("ctx", "fsdp"), axis=0, tiled=True),
        lax.all_gather(ffn_gain, ("ctx", "fsdp"), axis=0, tiled=True),
        lax.all_gather(query_gain, ("ctx", "fsdp"), axis=0, tiled=True),
        lax.all_gather(key_gain, ("ctx", "fsdp"), axis=0, tiled=True),
    )
    (
        full_query,
        full_key,
        full_value,
        full_out,
        full_router,
        gain_attn,
        gain_ffn,
        gain_query,
        gain_key,
    ) = gathered
    gain_attn = gain_attn.astype(jnp.float32)
    gain_ffn = gain_ffn.astype(jnp.float32)
    gain_query = gain_query.astype(jnp.float32)
    gain_key = gain_key.astype(jnp.float32)
    h_one, norm_one_back = jax.vjp(rms_scaled, hidden_in, gain_attn)
    h_one_low = h_one.astype(jnp.bfloat16)
    query_raw = jnp.dot(h_one_low, full_query, preferred_element_type=jnp.float32)
    key_raw = jnp.dot(h_one_low, full_key, preferred_element_type=jnp.float32)
    values_low = jnp.dot(h_one_low, full_value, preferred_element_type=jnp.float32).astype(
        jnp.bfloat16
    )
    query_rot, query_back = jax.vjp(partial(qk_post, places=place_mine), query_raw, gain_query)
    key_rot, key_back = jax.vjp(partial(qk_post, places=place_mine), key_raw, gain_key)
    query_low = query_rot.astype(jnp.bfloat16)
    key_low = key_rot.astype(jnp.bfloat16)
    key_all, value_all = (
        lax.all_gather(key_low, "ctx", axis=0, tiled=True),
        lax.all_gather(values_low, "ctx", axis=0, tiled=True),
    )
    query_heads = query_low.reshape(row_count, head_count, HEAD_DIM)
    key_heads = key_all.reshape(-1, head_count, HEAD_DIM)
    value_heads = value_all.reshape(-1, head_count, HEAD_DIM)

    def scores_of():
        raw_scores = (
            jnp.einsum("thd,khd->htk", query_heads, key_heads, preferred_element_type=jnp.float32)
            * score_scale
        )
        return jnp.where(same_seq[None, :, :], raw_scores, masked_value)

    scores = scores_of()
    row_top = jnp.max(scores, axis=-1, keepdims=True)
    log_total = row_top + jnp.log(jnp.sum(jnp.exp(scores - row_top), axis=-1, keepdims=True))
    probs_low = jnp.exp(scores - log_total).astype(jnp.bfloat16)
    attended = jnp.einsum(
        "htk,khd->thd", probs_low, value_heads, preferred_element_type=jnp.float32
    )
    attended_low = attended.reshape(row_count, model_width).astype(jnp.bfloat16)
    middle = hidden_in + jnp.dot(attended_low, full_out, preferred_element_type=jnp.float32)
    h_two, norm_two_back = jax.vjp(rms_scaled, middle, gain_ffn)
    h_two_low = h_two.astype(jnp.bfloat16)
    logits = jnp.dot(h_two_low, full_router, preferred_element_type=jnp.float32)
    expert_count = full_router.shape[1]
    route_rows = routes[0]
    top_k = route_rows.shape[1]
    chosen = route_rows[:, :, None] == jnp.arange(expert_count, dtype=jnp.int32)[None, None, :]
    picked, route_back = jax.vjp(partial(route_weights, chosen=chosen), logits)
    pair_count = row_count * top_k
    capacity = 5 * row_count * top_k // (4 * expert_count)
    slot_count = expert_count * capacity
    group_size = lax.axis_size("fsdp")
    local_experts = w_gate.shape[0]
    pair_expert = route_rows.reshape(pair_count)
    one_hot = (pair_expert[:, None] == jnp.arange(expert_count, dtype=jnp.int32)[None, :]).astype(
        jnp.int32
    )
    slot_rank = jnp.sum(one_hot * (jnp.cumsum(one_hot, axis=0) - 1), axis=1)
    slot_ids = pair_expert * capacity + slot_rank
    source = (
        jnp.full((slot_count,), pair_count, jnp.int32)
        .at[slot_ids]
        .set(jnp.arange(pair_count, dtype=jnp.int32))
    )
    filled = source < pair_count
    source_pair = jnp.minimum(source, pair_count - 1)
    send_rows = jnp.where(
        filled[:, None], h_two_low[source_pair // top_k], jnp.zeros((), jnp.bfloat16)
    )
    send_rows = send_rows.reshape(group_size, local_experts, capacity, model_width)
    gate_full, up_full, down_full = (
        lax.all_gather(w_gate, "ctx", axis=1, tiled=True),
        lax.all_gather(w_up, "ctx", axis=1, tiled=True),
        lax.all_gather(w_down, "ctx", axis=1, tiled=True),
    )
    arrived_rows = lax.all_to_all(send_rows, "fsdp", split_axis=0, concat_axis=0, tiled=True)
    gate_part = jnp.einsum(
        "secd,edf->secf", arrived_rows, gate_full, preferred_element_type=jnp.float32
    )
    up_part = jnp.einsum(
        "secd,edf->secf", arrived_rows, up_full, preferred_element_type=jnp.float32
    )
    act_part = (jax.nn.silu(gate_part) * up_part).astype(jnp.bfloat16)
    result = jnp.einsum(
        "secf,efd->secd", act_part, down_full, preferred_element_type=jnp.float32
    ).astype(jnp.bfloat16)
    returned = lax.all_to_all(result, "fsdp", split_axis=0, concat_axis=0, tiled=True).reshape(
        slot_count, model_width
    )
    pair_out = returned[slot_ids].reshape(row_count, top_k, model_width)
    output = (middle + jnp.sum(picked[:, :, None] * pair_out, axis=1)).astype(jnp.bfloat16)
    grad_top = grad_output[0].astype(jnp.float32)
    grad_picked = jnp.sum(grad_top[:, None, :] * pair_out, axis=-1)
    grad_pair = (
        (picked[:, :, None] * grad_top[:, None, :])
        .astype(jnp.bfloat16)
        .reshape(pair_count, model_width)
    )
    grad_send = jnp.where(filled[:, None], grad_pair[source_pair], jnp.zeros((), jnp.bfloat16))
    grad_send = grad_send.reshape(group_size, local_experts, capacity, model_width)
    grad_arrived = lax.all_to_all(grad_send, "fsdp", split_axis=0, concat_axis=0, tiled=True)
    sigma = jax.nn.sigmoid(gate_part)
    act_low = (gate_part * sigma * up_part).astype(jnp.bfloat16)
    grad_act = jnp.einsum(
        "secd,efd->secf", grad_arrived, down_full, preferred_element_type=jnp.float32
    )
    grad_gate = (grad_act * up_part * sigma * (1.0 + gate_part * (1.0 - sigma))).astype(
        jnp.bfloat16
    )
    grad_up = (grad_act * gate_part * sigma).astype(jnp.bfloat16)
    grad_back = jnp.einsum(
        "secf,edf->secd", grad_gate, gate_full, preferred_element_type=jnp.float32
    )
    grad_back = (
        grad_back
        + jnp.einsum("secf,edf->secd", grad_up, up_full, preferred_element_type=jnp.float32)
    ).astype(jnp.bfloat16)
    grad_return = lax.all_to_all(
        grad_back, "fsdp", split_axis=0, concat_axis=0, tiled=True
    ).reshape(slot_count, model_width)
    grad_h_two = jnp.sum(
        grad_return[slot_ids].reshape(row_count, top_k, model_width).astype(jnp.float32), axis=1
    )
    (grad_logits,) = route_back(grad_picked)
    grad_logits_low = grad_logits.astype(jnp.bfloat16)
    grad_h_two = grad_h_two + jnp.einsum(
        "te,de->td", grad_logits_low, full_router, preferred_element_type=jnp.float32
    )
    grad_router = jnp.einsum(
        "td,te->de", h_two_low, grad_logits_low, preferred_element_type=jnp.float32
    )
    grad_middle, grad_ffn_gain = norm_two_back(grad_h_two)
    grad_middle = grad_middle + grad_top
    grad_branch = grad_middle.astype(jnp.bfloat16)
    grad_out_w = jnp.einsum(
        "td,te->de", attended_low, grad_branch, preferred_element_type=jnp.float32
    )
    grad_att = jnp.einsum(
        "te,de->td", grad_branch, full_out, preferred_element_type=jnp.float32
    ).astype(jnp.bfloat16)
    grad_att = grad_att.reshape(row_count, head_count, HEAD_DIM)
    scores = scores_of()
    probs_full = jnp.exp(scores - log_total)
    probs_again = probs_full.astype(jnp.bfloat16)
    grad_probs = jnp.einsum(
        "thd,khd->htk", grad_att, value_heads, preferred_element_type=jnp.float32
    )
    spread = jnp.sum(probs_full * grad_probs, axis=-1, keepdims=True)
    grad_scores = (probs_full * (grad_probs - spread)).astype(jnp.bfloat16)
    grad_query = (
        jnp.einsum(
            "htk,khd->thd", grad_scores, key_heads, preferred_element_type=jnp.float32
        ).reshape(row_count, model_width)
        * score_scale
    )
    grad_key_part = (
        jnp.einsum(
            "htk,thd->khd", grad_scores, query_heads, preferred_element_type=jnp.float32
        ).reshape(-1, model_width)
        * score_scale
    )
    grad_value_part = jnp.einsum(
        "htk,thd->khd", probs_again, grad_att, preferred_element_type=jnp.float32
    ).reshape(-1, model_width)
    grad_key, grad_value = (
        lax.psum_scatter(
            grad_key_part.astype(jnp.bfloat16), "ctx", scatter_dimension=0, tiled=True
        ).astype(jnp.float32),
        lax.psum_scatter(
            grad_value_part.astype(jnp.bfloat16), "ctx", scatter_dimension=0, tiled=True
        ).astype(jnp.float32),
    )
    grad_q_raw, grad_q_gain = query_back(grad_query)
    grad_k_raw, grad_k_gain = key_back(grad_key)
    grad_q_low = grad_q_raw.astype(jnp.bfloat16)
    grad_k_low = grad_k_raw.astype(jnp.bfloat16)
    grad_v_low = grad_value.astype(jnp.bfloat16)
    grad_query_w = jnp.einsum(
        "td,te->de", h_one_low, grad_q_low, preferred_element_type=jnp.float32
    )
    grad_key_w = jnp.einsum("td,te->de", h_one_low, grad_k_low, preferred_element_type=jnp.float32)
    grad_value_w = jnp.einsum(
        "td,te->de", h_one_low, grad_v_low, preferred_element_type=jnp.float32
    )
    grad_h_one = jnp.einsum("te,de->td", grad_q_low, full_query, preferred_element_type=jnp.float32)
    grad_h_one = grad_h_one + jnp.einsum(
        "te,de->td", grad_k_low, full_key, preferred_element_type=jnp.float32
    )
    grad_h_one = grad_h_one + jnp.einsum(
        "te,de->td", grad_v_low, full_value, preferred_element_type=jnp.float32
    )
    grad_input_norm, grad_attn_gain = norm_one_back(grad_h_one)
    grad_input = grad_middle + grad_input_norm
    totals = (
        lax.psum_scatter(grad_query_w, ("ctx", "fsdp"), scatter_dimension=0, tiled=True),
        lax.psum_scatter(grad_key_w, ("ctx", "fsdp"), scatter_dimension=0, tiled=True),
        lax.psum_scatter(grad_value_w, ("ctx", "fsdp"), scatter_dimension=0, tiled=True),
        lax.psum_scatter(grad_out_w, ("ctx", "fsdp"), scatter_dimension=0, tiled=True),
        lax.psum_scatter(grad_router, ("ctx", "fsdp"), scatter_dimension=0, tiled=True),
        lax.psum_scatter(grad_attn_gain, ("ctx", "fsdp"), scatter_dimension=0, tiled=True),
        lax.psum_scatter(grad_ffn_gain, ("ctx", "fsdp"), scatter_dimension=0, tiled=True),
        lax.psum_scatter(grad_q_gain, ("ctx", "fsdp"), scatter_dimension=0, tiled=True),
        lax.psum_scatter(grad_k_gain, ("ctx", "fsdp"), scatter_dimension=0, tiled=True),
    )
    grad_down_w = jnp.einsum(
        "secf,secd->efd", act_low, grad_arrived, preferred_element_type=jnp.float32
    )
    grad_gate_w = jnp.einsum(
        "secd,secf->edf", arrived_rows, grad_gate, preferred_element_type=jnp.float32
    )
    grad_up_w = jnp.einsum(
        "secd,secf->edf", arrived_rows, grad_up, preferred_element_type=jnp.float32
    )
    gate_grad, up_grad, down_grad = (
        lax.psum_scatter(
            grad_gate_w.astype(jnp.bfloat16), "ctx", scatter_dimension=1, tiled=True
        ).astype(jnp.float32),
        lax.psum_scatter(
            grad_up_w.astype(jnp.bfloat16), "ctx", scatter_dimension=1, tiled=True
        ).astype(jnp.float32),
        lax.psum_scatter(
            grad_down_w.astype(jnp.bfloat16), "ctx", scatter_dimension=1, tiled=True
        ).astype(jnp.float32),
    )
    return (
        output[None],
        grad_input[None],
        totals[0],
        totals[1],
        totals[2],
        totals[3],
        totals[4],
        totals[5],
        totals[6],
        totals[7],
        totals[8],
        gate_grad,
        up_grad,
        down_grad,
    )


def masked_probs(query, key, seq_rows, seq_cols, scale):
    scores = (
        lax.dot_general(query, key, (((1,), (1,)), ((), ())), preferred_element_type=jnp.float32)
        * scale
    )
    scores = jnp.where(seq_rows == seq_cols, scores, masked_value)
    top = jnp.max(scores, axis=-1, keepdims=True)
    weights = jnp.exp(scores - top)
    return weights / jnp.sum(weights, axis=-1, keepdims=True)


def attend_kernel(scale, seq_rows, seq_cols, query, key, value, out):
    probs = masked_probs(query[...], key[...], seq_rows[...], seq_cols[...], scale)
    out[...] = jnp.dot(
        probs.astype(jnp.bfloat16), value[...], preferred_element_type=jnp.float32
    ).astype(out.dtype)


def attend_back_kernel(
    scale, seq_rows, seq_cols, query, key, value, grad, grad_query, grad_key, grad_value
):
    @pl.when(pl.program_id(1) == 0)
    def _():
        grad_key[...] = jnp.zeros_like(grad_key)
        grad_value[...] = jnp.zeros_like(grad_value)

    probs = masked_probs(query[...], key[...], seq_rows[...], seq_cols[...], scale)
    grad_probs = lax.dot_general(
        grad[...], value[...], (((1,), (1,)), ((), ())), preferred_element_type=jnp.float32
    )
    spread = jnp.sum(probs * grad_probs, axis=-1, keepdims=True)
    grad_scores = (probs * (grad_probs - spread)).astype(jnp.bfloat16)
    grad_query[...] = (
        jnp.dot(grad_scores, key[...], preferred_element_type=jnp.float32) * scale
    )
    grad_key[...] += (
        lax.dot_general(
            grad_scores,
            query[...],
            (((0,), (0,)), ((), ())),
            preferred_element_type=jnp.float32,
        )
        * scale
    )
    grad_value[...] += lax.dot_general(
        probs.astype(jnp.bfloat16),
        grad[...],
        (((0,), (0,)), ((), ())),
        preferred_element_type=jnp.float32,
    )


def attention_specs(rows, block):
    per_block = pl.BlockSpec((block, HEAD_DIM), lambda h, i: (i, h))
    per_head = pl.BlockSpec((rows, HEAD_DIM), lambda h, i: (0, h))
    seqs = [
        pl.BlockSpec((block, 1), lambda h, i: (i, 0)),
        pl.BlockSpec((1, rows), lambda h, i: (0, 0)),
    ]
    return per_block, per_head, seqs


def attend(seq_ids, query, key, value):
    rows, width = query.shape
    block = math.gcd(rows, 256)
    per_block, per_head, seqs = attention_specs(rows, block)
    pairs = rows * rows * width
    return pl.pallas_call(
        partial(attend_kernel, 1.0 / math.sqrt(HEAD_DIM)),
        grid=(width // HEAD_DIM, rows // block),
        in_specs=seqs + [per_block, per_head, per_head],
        out_specs=per_block,
        out_shape=jax.ShapeDtypeStruct((rows, width), jnp.bfloat16),
        cost_estimate=pl.CostEstimate(
            flops=4 * pairs, bytes_accessed=8 * rows * width, transcendentals=pairs // HEAD_DIM
        ),
        compiler_params=pltpu.CompilerParams(vmem_limit_bytes=48 << 20),
        name="attend",
    )(seq_ids[:, None], seq_ids[None, :], query, key, value)


def attend_back(seq_ids, query, key, value, grad):
    rows, width = query.shape
    block = math.gcd(rows, 256)
    per_block, per_head, seqs = attention_specs(rows, block)
    pairs = rows * rows * width
    return pl.pallas_call(
        partial(attend_back_kernel, 1.0 / math.sqrt(HEAD_DIM)),
        grid=(width // HEAD_DIM, rows // block),
        in_specs=seqs + [per_block, per_head, per_head, per_block],
        out_specs=(per_block, per_head, per_head),
        out_shape=(jax.ShapeDtypeStruct((rows, width), jnp.float32),) * 3,
        cost_estimate=pl.CostEstimate(
            flops=10 * pairs, bytes_accessed=20 * rows * width, transcendentals=pairs // HEAD_DIM
        ),
        compiler_params=pltpu.CompilerParams(vmem_limit_bytes=48 << 20),
        name="attend_back",
    )(seq_ids[:, None], seq_ids[None, :], query, key, value, grad)


def dispatch_kernel(position, rows, out):
    columns, _, capacity, width = out.shape
    count = rows.shape[1]
    slots = lax.broadcasted_iota(jnp.int32, (columns, capacity, count), 1)
    select = jnp.where(slots == position[:, 0], 1.0, 0.0)
    select = select.reshape(columns * capacity, count).astype(jnp.bfloat16)
    step = math.gcd(width, 512)
    for at in range(0, width, step):
        part = jnp.dot(select, rows[0, :, at : at + step], preferred_element_type=jnp.float32)
        part = part.reshape(columns, capacity, step).astype(out.dtype)
        out[:, 0, :, at : at + step] = part


def dispatch(position, capacity, rows):
    columns, planes, count = position.shape
    width = rows.shape[1]
    return pl.pallas_call(
        dispatch_kernel,
        grid=(planes,),
        in_specs=[
            pl.BlockSpec((columns, 1, 1, count), lambda b: (0, b, 0, 0)),
            pl.BlockSpec((1, count, width), lambda b: (b, 0, 0)),
        ],
        out_specs=pl.BlockSpec((columns, 1, capacity, width), lambda b: (0, b, 0, 0)),
        out_shape=jax.ShapeDtypeStruct((columns, planes, capacity, width), jnp.bfloat16),
        cost_estimate=pl.CostEstimate(
            flops=2 * position.size * capacity * width,
            bytes_accessed=2 * columns * planes * capacity * width,
            transcendentals=0,
        ),
        compiler_params=pltpu.CompilerParams(vmem_limit_bytes=40 << 20),
        name="dispatch",
    )(position[:, :, None], rows.reshape(planes, count, width))


def heads_of(width):
    return [slice(at, at + HEAD_DIM) for at in range(0, width, HEAD_DIM)]


def turn_kernel(raw, scales, gains, cosine, sine, query, key, value):
    width = query.shape[1]
    for which, out in ((0, query), (1, key)):
        scale = scales[:, which : which + 1]
        for head in heads_of(width):
            part = raw[:, which * width + head.start : which * width + head.stop]
            part = part * scale * gains[which : which + 1, head]
            swapped = pltpu.roll(part, HEAD_DIM // 2, 1)
            out[:, head] = (part * cosine[...] + swapped * sine[...]).astype(out.dtype)
    value[...] = raw[:, 2 * width : 3 * width].astype(value.dtype)


def turn_back_kernel(
    raw, scales, gains, cosine, sine, grad_query, grad_key, out_query, out_key, dots, grad_gains
):
    @pl.when(pl.program_id(0) == 0)
    def _():
        grad_gains[...] = jnp.zeros_like(grad_gains)

    width = grad_query.shape[1]
    for which, grad, out in ((0, grad_query, out_query), (1, grad_key, out_key)):
        scale = scales[:, which : which + 1]
        total = jnp.zeros_like(scale)
        for head in heads_of(width):
            part = grad[:, head]
            part = part * cosine[...] - pltpu.roll(part, HEAD_DIM // 2, 1) * sine[...]
            hat = raw[:, which * width + head.start : which * width + head.stop] * scale
            grad_gains[which : which + 1, head] += jnp.sum(part * hat, axis=0, keepdims=True)
            part = part * gains[which : which + 1, head]
            total += jnp.sum(part * hat, axis=1, keepdims=True)
            out[:, head] = part
        dots[:, which : which + 1] = total


def turn_specs(raw, gains):
    block = math.gcd(raw.shape[0], 256)
    return block, [
        pl.BlockSpec((block, raw.shape[1]), lambda i: (i, 0)),
        pl.BlockSpec((block, 2), lambda i: (i, 0)),
        pl.BlockSpec(gains.shape, lambda i: (0, 0)),
        pl.BlockSpec((block, HEAD_DIM), lambda i: (i, 0)),
        pl.BlockSpec((block, HEAD_DIM), lambda i: (i, 0)),
    ]


def turn(raw, scales, gains, cosine, sine):
    rows, width = raw.shape[0], gains.shape[1]
    block, specs = turn_specs(raw, gains)
    return pl.pallas_call(
        turn_kernel,
        grid=(rows // block,),
        in_specs=specs,
        out_specs=(pl.BlockSpec((block, width), lambda i: (i, 0)),) * 3,
        out_shape=(jax.ShapeDtypeStruct((rows, width), jnp.bfloat16),) * 3,
        cost_estimate=pl.CostEstimate(
            flops=16 * rows * width, bytes_accessed=18 * rows * width, transcendentals=0
        ),
        compiler_params=pltpu.CompilerParams(vmem_limit_bytes=40 << 20),
        name="turn",
    )(raw, scales, gains, cosine, sine)


def turn_back(raw, scales, gains, cosine, sine, grad_query, grad_key):
    rows, width = grad_query.shape
    block, specs = turn_specs(raw, gains)
    wide = pl.BlockSpec((block, width), lambda i: (i, 0))
    f32 = jnp.float32
    return pl.pallas_call(
        turn_back_kernel,
        grid=(rows // block,),
        in_specs=specs + [wide, wide],
        out_specs=(
            wide,
            wide,
            pl.BlockSpec((block, 2), lambda i: (i, 0)),
            pl.BlockSpec((2, width), lambda i: (0, 0)),
        ),
        out_shape=(
            jax.ShapeDtypeStruct((rows, width), f32),
            jax.ShapeDtypeStruct((rows, width), f32),
            jax.ShapeDtypeStruct((rows, 2), f32),
            jax.ShapeDtypeStruct((2, width), f32),
        ),
        cost_estimate=pl.CostEstimate(
            flops=24 * rows * width, bytes_accessed=28 * rows * width, transcendentals=0
        ),
        compiler_params=pltpu.CompilerParams(vmem_limit_bytes=40 << 20),
        name="turn_back",
    )(raw, scales, gains, cosine, sine, grad_query, grad_key)


def expert_kernel(
    rows, grad, picked, gate, up, down, act_out, grad_gate, grad_up, grad_picked
):
    gate_pre = jnp.dot(rows[...], gate[...], preferred_element_type=jnp.float32)
    up_pre = jnp.dot(rows[...], up[...], preferred_element_type=jnp.float32)
    grad_raw = lax.dot_general(
        grad[...], down[...], (((1,), (1,)), ((), ())), preferred_element_type=jnp.float32
    )
    sigma = jax.nn.sigmoid(gate_pre)
    silu = gate_pre * sigma
    act = (silu * up_pre).astype(jnp.bfloat16).astype(jnp.float32)
    act_out[...] = (act * picked[...]).astype(jnp.bfloat16)
    grad_picked[...] = jnp.sum(grad_raw * act, axis=1, keepdims=True)
    grad_act = grad_raw * picked[...]
    grad_gate[...] = (
        grad_act * up_pre * (sigma + silu * (1.0 - sigma))
    ).astype(jnp.bfloat16)
    grad_up[...] = (grad_act * silu).astype(jnp.bfloat16)


def expert(rows, grad, picked, gate, up, down, block):
    count, width = rows.shape
    hidden = gate.shape[1]
    once = pl.Buffered(1)
    wide = pl.BlockSpec((block, width), lambda i: (i, 0))
    narrow = pl.BlockSpec((block, hidden), lambda i: (i, 0))
    one = pl.BlockSpec((block, 1), lambda i: (i, 0))
    into = pl.BlockSpec((width, hidden), lambda i: (0, 0), pipeline_mode=once)
    outof = pl.BlockSpec((hidden, width), lambda i: (0, 0), pipeline_mode=once)
    low = jax.ShapeDtypeStruct((count, hidden), jnp.bfloat16)
    return pl.pallas_call(
        expert_kernel,
        grid=(count // block,),
        in_specs=[wide, wide, one, into, into, outof],
        out_specs=(narrow, narrow, narrow, one),
        out_shape=(low, low, low, jax.ShapeDtypeStruct((count, 1), jnp.float32)),
        cost_estimate=pl.CostEstimate(
            flops=6 * count * width * hidden,
            bytes_accessed=4 * count * width + 6 * (count + width) * hidden,
            transcendentals=count * hidden,
        ),
        compiler_params=pltpu.CompilerParams(vmem_limit_bytes=56 << 20),
        name="expert",
    )(rows, grad, picked, gate, up, down)


def tie(array, *others):
    anywhere = pl.BlockSpec(memory_space=pl.ANY)
    return pl.pallas_call(
        lambda *refs: None,
        in_specs=[anywhere] * (1 + len(others)),
        out_specs=anywhere,
        out_shape=jax.ShapeDtypeStruct(array.shape, array.dtype),
        input_output_aliases={0: 0},
        name="tie",
    )(array, *others)


def mm(left, right):
    return jnp.dot(left, right, preferred_element_type=jnp.float32)


def mm_t(left, right):
    return lax.dot_general(
        left, right, (((1,), (1,)), ((), ())), preferred_element_type=jnp.float32
    )


def t_mm(left, right):
    return lax.dot_general(
        left, right, (((0,), (0,)), ((), ())), preferred_element_type=jnp.float32
    )


def plane_shards(
    hidden,
    token_order,
    lengths,
    routes,
    grad_output,
    w_query,
    w_key,
    w_value,
    w_out,
    w_router,
    attn_gain,
    ffn_gain,
    query_gain,
    key_gain,
    w_gate,
    w_up,
    w_down,
):
    f32, bf16 = jnp.float32, jnp.bfloat16
    both = ("ctx", "fsdp")
    planes = lax.axis_size("ctx")
    columns = lax.axis_size("fsdp")
    plane = lax.axis_index("ctx")
    row_count, width = hidden.shape[1:]
    group_rows = row_count * planes
    share = width // planes
    strip = w_query.shape[0]
    first_row = plane * row_count

    hidden_all = lax.all_gather(hidden[0], "ctx", axis=0, tiled=True)
    experts = w_router.shape[1]
    qkv = jnp.stack([w_query, w_key, w_value], axis=1).reshape(strip, 3, planes, share)
    qkv = qkv.transpose(2, 0, 1, 3).reshape(planes, strip, 3 * share)
    small = [w_router] + [g[:, None] for g in (attn_gain, ffn_gain, query_gain, key_gain)]
    small = jnp.concatenate(small + [routes.astype(bf16).reshape(strip, -1)], axis=1)
    spare = -small.shape[1] % 128
    small = jnp.pad(small, ((0, 0), (0, spare)))
    small = jnp.broadcast_to(small[None], (planes,) + small.shape)
    own_out = jnp.broadcast_to(w_out[None], (planes,) + w_out.shape)
    packed = jnp.concatenate([qkv, small, own_out], axis=2)
    packed = lax.all_to_all(packed, "ctx", 0, 0, tiled=True)
    packed, out_rows = packed[:, :, :-width], packed[:, :, -width:]
    routes_at = 3 * share + experts + 4
    routes_all = packed[:, :, routes_at : packed.shape[2] - spare].astype(jnp.int32)
    routes_all = routes_all.reshape(group_rows, -1)
    packed = jnp.broadcast_to(packed[None], (columns,) + packed.shape)
    packed = lax.all_to_all(packed, "fsdp", 0, 0, tiled=True)
    packed = packed.transpose(1, 0, 2, 3).reshape(width, -1)
    full_router = packed[:, 3 * share : 3 * share + experts]
    gain_attn, gain_ffn, gain_query, gain_key = [
        packed[:, 3 * share + experts + i].astype(f32) for i in range(4)
    ]
    def swap(part, step):
        return lax.ppermute(part, "ctx", [(i, i ^ step) for i in range(planes)])

    def by_plane(came):
        came = jnp.stack(came)
        return [came[plane ^ i] for i in range(planes)]

    def exchange(parts, first=None, last=None):
        came = [parts[plane]]
        for step in range(1, planes):
            part = parts[plane ^ step]
            part = swap(part if first is None else tie(part, first), step)
            came.append(part if last is None else tie(part, last))
        return by_plane(came)

    def exchange_after(parts, earlier):
        came = [
            swap(part if before is None else tie(part, before), step)
            for step, before in enumerate(earlier, 1)
            for part in [parts[plane ^ step]]
        ]
        return came, jnp.stack(by_plane([parts[plane]] + came)).astype(f32)

    def plane_sum(part):
        return part + sum(swap(part, step) for step in range(1, planes))

    grad_all = lax.all_gather(tie(grad_output[0], hidden_all), "ctx", axis=0, tiled=True)
    full_out = jnp.broadcast_to(tie(out_rows, packed)[None], (columns,) + out_rows.shape)
    full_out = lax.all_to_all(full_out, "fsdp", 0, 0, tiled=True)
    full_out = full_out.transpose(1, 0, 2, 3).reshape(width, width)

    seq_ids, places = seq_layout(token_order[0], lengths[0])
    experts_here = w_gate.shape[0]
    column_expert = experts_here * jnp.arange(columns, dtype=jnp.int32) + plane
    named = jnp.any(routes_all[:, :, None] == column_expert[None, None, :], axis=1)
    named = named.reshape(planes, row_count, columns)
    capacity = 5 * row_count * routes.shape[2] // (4 * experts)
    rank = jnp.cumsum(named.astype(jnp.int32), axis=1) - 1
    position = jnp.where(named, rank, -1).transpose(2, 0, 1)
    slots = jnp.arange(capacity, dtype=jnp.int32)
    holds = position[:, :, None, :] == slots[None, None, :, None]
    select = holds.astype(bf16)

    def combine(rows):
        rows = rows.reshape(columns, planes, capacity, width)
        sums = jnp.einsum("fbsr,fbsd->brd", select, rows, preferred_element_type=f32)
        return sums.reshape(group_rows, width).astype(bf16)


    frequency = rope_base ** (
        -2.0 * jnp.arange(HEAD_DIM // 2).astype(f32) / HEAD_DIM
    )
    angles = places.astype(f32)[:, None] * frequency[None, :]
    cosine, sine = jnp.cos(angles), jnp.sin(angles)
    cosine = jnp.concatenate([cosine, cosine], axis=1)
    sine = jnp.concatenate([-sine, sine], axis=1)
    hidden_wide = hidden_all.astype(f32)
    scale_one = lax.rsqrt(jnp.mean(hidden_wide * hidden_wide, axis=-1, keepdims=True) + epsilon)
    h_one = (hidden_wide * scale_one * gain_attn).astype(bf16)
    raw = mm(h_one, packed)
    squares = jnp.stack(
        [jnp.sum(raw[:, :share] ** 2, axis=1), jnp.sum(raw[:, share : 2 * share] ** 2, axis=1)]
    )
    squares = plane_sum(squares)
    scales = lax.rsqrt(squares / width + epsilon).T
    gains = lax.dynamic_slice_in_dim(
        jnp.stack([gain_query, gain_key]), plane * share, share, axis=1
    )
    query, key, values = turn(raw, scales, gains, cosine, sine)
    attended = attend(seq_ids, query, key, values)
    grad_send = dispatch(position, capacity, tie(grad_all, attended, full_out))
    grad_in = lax.all_to_all(grad_send, "fsdp", 0, 0, tiled=True).reshape(-1, width)
    attended = tie(attended, grad_send).reshape(planes, row_count, share)
    attended = jnp.concatenate(exchange(attended), axis=1)
    middle = hidden[0].astype(f32) + mm(attended, full_out)
    scale_two = lax.rsqrt(jnp.mean(middle * middle, axis=-1, keepdims=True) + epsilon)
    middle_hat = middle * scale_two
    h_two = (middle_hat * gain_ffn).astype(bf16)

    h_two_all = lax.all_gather(h_two, "ctx", axis=0, tiled=True)
    h_all = tie(h_two_all, grad_in)
    gate = jnp.concatenate(exchange(w_gate, h_two_all))
    up = jnp.concatenate(exchange(w_up, h_all))
    down = jnp.concatenate(exchange(w_down, h_all))
    probs_all = jax.nn.softmax(mm(h_all, full_router), axis=-1)
    probs = jax.nn.softmax(mm(h_two, full_router), axis=-1)
    probs_plane = lax.dynamic_index_in_dim(
        probs_all.reshape(group_rows, columns, experts_here), plane, 2, keepdims=False
    )
    rows_in = lax.all_to_all(dispatch(position, capacity, h_all), "fsdp", 0, 0, tiled=True).reshape(-1, width)
    probs_plane = probs_plane.reshape(planes, row_count, columns).transpose(2, 0, 1)
    slot_probs = jnp.sum(jnp.where(holds, probs_plane[:, :, None, :], 0.0), axis=3)
    picked = lax.all_to_all(slot_probs, "fsdp", 0, 0, tiled=True).reshape(-1, 1)
    act_picked, grad_gate, grad_up, grad_picked = expert(
        rows_in, grad_in, picked, gate, up, down, planes * capacity
    )
    grad_picked = lax.all_to_all(
        grad_picked.reshape(columns, planes, capacity), "fsdp", 0, 0, tiled=True
    )
    grad_down_w = t_mm(act_picked, grad_in).astype(bf16)
    grad_gate = tie(grad_gate, grad_down_w, grad_picked)

    def blocks(whole):
        return whole.reshape(planes, whole.shape[0] // planes, whole.shape[1])

    came, down_grad = exchange_after(blocks(grad_down_w), [None] * (planes - 1))
    grad_rows = (mm_t(grad_gate, gate) + mm_t(grad_up, up)).astype(bf16)
    grad_rows = tie(grad_rows, *came[:-1])
    grad_rows = lax.all_to_all(
        grad_rows.reshape(columns, planes * capacity, width), "fsdp", 0, 0, tiled=True
    )
    grad_gate_w = t_mm(rows_in, grad_gate).astype(bf16)
    grad_up_w = t_mm(rows_in, grad_up).astype(bf16)
    came, up_grad = exchange_after(blocks(grad_up_w), came)
    came, gate_grad = exchange_after(blocks(grad_gate_w), came)
    expert_out = mm(act_picked, down).astype(bf16)
    grad_rows = tie(grad_rows, *came, expert_out)
    expert_out = lax.all_to_all(
        expert_out.reshape(columns, planes * capacity, width), "fsdp", 0, 0, tiled=True
    )
    grad_h_two = lax.psum_scatter(
        combine(grad_rows), "ctx", scatter_dimension=0, tiled=True
    ).astype(f32)

    u_plane = jnp.sum(jnp.where(holds, grad_picked[..., None], 0.0), axis=2)
    u_mine = exchange(u_plane.transpose(1, 0, 2))
    u_mine = jnp.stack(u_mine, axis=1).reshape(experts, row_count).T
    grad_logits = probs * (u_mine - jnp.sum(probs * u_mine, axis=-1, keepdims=True))
    grad_logits = grad_logits.astype(bf16)
    grad_h_two = grad_h_two + mm_t(grad_logits, full_router)
    grad_router = t_mm(h_two, grad_logits)

    grad_top = grad_output[0].astype(f32)
    grad_ffn_gain = jnp.sum(grad_h_two * middle_hat, axis=0)
    grad_hat = grad_h_two * gain_ffn
    grad_middle = grad_top + scale_two * (
        grad_hat - middle_hat * jnp.mean(grad_hat * middle_hat, axis=-1, keepdims=True)
    )
    grad_branch = grad_middle.astype(bf16)
    grad_att = mm_t(grad_branch, full_out).astype(bf16)
    grad_att = grad_att.reshape(row_count, planes, share).transpose(1, 0, 2)
    grad_att = jnp.concatenate(exchange(grad_att))
    mixed_part = combine(tie(expert_out, grad_att))
    mixed = lax.psum_scatter(mixed_part, "ctx", scatter_dimension=0, tiled=True)
    output = (middle + mixed.astype(f32)).astype(bf16)
    grad_out_w = t_mm(attended, grad_branch).astype(bf16)
    grad_out_w = grad_out_w.reshape(planes, columns, strip, width).transpose(1, 0, 2, 3)
    grad_out_w = lax.all_to_all(
        tie(grad_out_w, mixed_part), "fsdp", 0, 0, tiled=True
    )
    grad_att = tie(grad_att, mixed_part)
    grad_query, grad_key, grad_value = attend_back(seq_ids, query, key, values, grad_att)
    grad_query, grad_key, dots, grad_gains = turn_back(
        raw, scales, gains, cosine, sine, grad_query, grad_key
    )
    dots = plane_sum(dots.T).T * (scales * scales) / width
    grad_qkv = jnp.concatenate(
        [
            scales[:, :1] * grad_query - raw[:, :share] * (scales[:, :1] * dots[:, :1]),
            scales[:, 1:] * grad_key - raw[:, share : 2 * share] * (scales[:, 1:] * dots[:, 1:]),
            grad_value,
        ],
        axis=1,
    ).astype(bf16)
    grad_qkv = tie(grad_qkv, mixed, grad_out_w)
    grad_out_w = jnp.sum(grad_out_w.astype(f32), axis=0).astype(bf16)
    grad_part = mm_t(grad_qkv, packed[:, : 3 * share])
    grad_h_one = lax.psum_scatter(
        grad_part.astype(bf16), "ctx", scatter_dimension=0, tiled=True
    ).astype(f32)
    grad_attn_gain = jnp.sum(grad_part * (hidden_wide * scale_one), axis=0)
    grad_qkv_w = t_mm(h_one, grad_qkv).reshape(planes, columns, strip, 3 * share)
    grad_qkv_w = lax.all_to_all(
        grad_qkv_w.transpose(1, 0, 2, 3).astype(bf16), "fsdp", 0, 0, tiled=True
    )
    grad_qkv_w = jnp.sum(grad_qkv_w.astype(f32), axis=0).astype(bf16)
    grad_qkv_w = jnp.concatenate([grad_qkv_w, grad_out_w], axis=2)
    grad_qkv_w = lax.all_to_all(grad_qkv_w, "ctx", 0, 0, tiled=True)
    grad_out_w = jnp.sum(grad_qkv_w[:, :, 3 * share :].astype(f32), axis=0)
    grad_qkv_w = grad_qkv_w[:, :, : 3 * share].reshape(planes, strip, 3, share).transpose(2, 1, 0, 3)
    grad_qkv_w = grad_qkv_w.reshape(3, strip, width).astype(f32)

    x_hat = hidden[0].astype(f32)
    scale_mine = lax.rsqrt(jnp.mean(x_hat * x_hat, axis=-1, keepdims=True) + epsilon)
    x_hat = x_hat * scale_mine
    grad_hat = grad_h_one * gain_attn
    grad_input = grad_middle + scale_mine * (
        grad_hat - x_hat * jnp.mean(grad_hat * x_hat, axis=-1, keepdims=True)
    )

    def summed(arrays):
        parts = jnp.concatenate(
            [x.reshape(planes * columns, -1) for x in arrays], axis=1
        )
        parts = tie(parts, grad_qkv_w)
        return jnp.sum(lax.all_to_all(parts, both, 0, 0, tiled=True), axis=0)

    own = jnp.arange(planes)[:, None] == plane
    gains = [jnp.where(own, g[None], 0.0) for g in grad_gains]
    totals = summed([grad_router, grad_attn_gain, grad_ffn_gain] + gains)
    gains = totals[strip * experts :].reshape(4, strip)
    return (
        output[None],
        grad_input[None],
        grad_qkv_w[0],
        grad_qkv_w[1],
        grad_qkv_w[2],
        grad_out_w,
        totals[: strip * experts].reshape(strip, experts),
        gains[0],
        gains[1],
        gains[2],
        gains[3],
        gate_grad,
        up_grad,
        down_grad,
    )


def solution(mesh):
    placed = (
        P("fsdp", "ctx", None),
        P("fsdp", None),
        P("fsdp", None),
        P("fsdp", "ctx", None),
        P("fsdp", "ctx", None),
        P(("ctx", "fsdp"), None),
        P(("ctx", "fsdp"), None),
        P(("ctx", "fsdp"), None),
        P(("ctx", "fsdp"), None),
        P(("ctx", "fsdp"), None),
        P(("ctx", "fsdp")),
        P(("ctx", "fsdp")),
        P(("ctx", "fsdp")),
        P(("ctx", "fsdp")),
        P("fsdp", "ctx", None),
        P("fsdp", "ctx", None),
        P("fsdp", "ctx", None),
    )

    def shards(*operands):
        experts_here = operands[14].shape[0]
        heads = operands[0].shape[2] // HEAD_DIM
        planes = mesh.shape["ctx"]
        whole_experts = experts_here == planes and heads % planes == 0 and planes in (2, 4)
        return (plane_shards if whole_experts else general_shards)(*operands)

    return jax.shard_map(
        shards,
        mesh=mesh,
        in_specs=placed,
        out_specs=(
            P("fsdp", "ctx", None),
            P("fsdp", "ctx", None),
            P(("ctx", "fsdp"), None),
            P(("ctx", "fsdp"), None),
            P(("ctx", "fsdp"), None),
            P(("ctx", "fsdp"), None),
            P(("ctx", "fsdp"), None),
            P(("ctx", "fsdp")),
            P(("ctx", "fsdp")),
            P(("ctx", "fsdp")),
            P(("ctx", "fsdp")),
            P("fsdp", "ctx", None),
            P("fsdp", "ctx", None),
            P("fsdp", "ctx", None),
        ),
        check_vma=False,
    )
```

```python
from functools import partial
import math

import jax
import jax.numpy as jnp
from jax import lax
from jax.experimental import pallas as pl
from jax.experimental.pallas import tpu as pltpu
from jax.sharding import PartitionSpec as P

HEAD_DIM = 128


epsilon = 1e-06
rope_base = 10000.0
masked_value = -1e30


def rms_scaled(values, gain):
    return values * lax.rsqrt(jnp.mean(values * values, axis=-1, keepdims=True) + epsilon) * gain


def rotate(values, places):
    row_count = values.shape[0]
    head_count = values.shape[1] // HEAD_DIM
    half_width = HEAD_DIM // 2
    frequency = rope_base ** (-2.0 * jnp.arange(half_width).astype(jnp.float32) / HEAD_DIM)
    angles = places.astype(jnp.float32)[:, None] * frequency[None, :]
    cosine = jnp.cos(angles)[:, None, :]
    sine_part = jnp.sin(angles)[:, None, :]
    split_heads = values.reshape(row_count, head_count, HEAD_DIM)
    first_half = split_heads[:, :, :half_width]
    second_half = split_heads[:, :, half_width:]
    turned = jnp.concatenate(
        [
            first_half * cosine - second_half * sine_part,
            second_half * cosine + first_half * sine_part,
        ],
        axis=-1,
    )
    return turned.reshape(row_count, head_count * HEAD_DIM)


def qk_post(values, gain, places):
    return rotate(rms_scaled(values, gain), places)


def route_weights(logits, chosen):
    router_probs = jax.nn.softmax(logits, axis=-1)
    return jnp.sum(jnp.where(chosen, router_probs[:, None, :], 0.0), axis=-1)


def seq_layout(order_row, seq_lengths):
    seq_ends = jnp.cumsum(seq_lengths)
    seq_ids = jnp.sum((order_row[:, None] >= seq_ends[None, :]).astype(jnp.int32), axis=1)
    starts = seq_ends - seq_lengths
    chosen = seq_ids[:, None] == jnp.arange(seq_lengths.shape[0], dtype=jnp.int32)[None, :]
    seq_start = jnp.sum(jnp.where(chosen, starts[None, :], 0), axis=1)
    return (seq_ids, order_row - seq_start)


def general_shards(
    hidden,
    token_order,
    lengths,
    routes,
    grad_output,
    w_query,
    w_key,
    w_value,
    w_out,
    w_router,
    attn_gain,
    ffn_gain,
    query_gain,
    key_gain,
    w_gate,
    w_up,
    w_down,
):
    hidden_in = hidden[0].astype(jnp.float32)
    row_count = hidden_in.shape[0]
    model_width = hidden_in.shape[1]
    head_count = model_width // HEAD_DIM
    score_scale = 1.0 / math.sqrt(HEAD_DIM)
    seq_all, place_all = seq_layout(token_order[0], lengths[0])
    first_row = lax.axis_index("ctx") * row_count
    seq_mine = lax.dynamic_slice_in_dim(seq_all, first_row, row_count)
    place_mine = lax.dynamic_slice_in_dim(place_all, first_row, row_count)
    same_seq = seq_mine[:, None] == seq_all[None, :]
    gathered = (
        lax.all_gather(w_query, ("ctx", "fsdp"), axis=0, tiled=True),
        lax.all_gather(w_key, ("ctx", "fsdp"), axis=0, tiled=True),
        lax.all_gather(w_value, ("ctx", "fsdp"), axis=0, tiled=True),
        lax.all_gather(w_out, ("ctx", "fsdp"), axis=0, tiled=True),
        lax.all_gather(w_router, ("ctx", "fsdp"), axis=0, tiled=True),
        lax.all_gather(attn_gain, ("ctx", "fsdp"), axis=0, tiled=True),
        lax.all_gather(ffn_gain, ("ctx", "fsdp"), axis=0, tiled=True),
        lax.all_gather(query_gain, ("ctx", "fsdp"), axis=0, tiled=True),
        lax.all_gather(key_gain, ("ctx", "fsdp"), axis=0, tiled=True),
    )
    (
        full_query,
        full_key,
        full_value,
        full_out,
        full_router,
        gain_attn,
        gain_ffn,
        gain_query,
        gain_key,
    ) = gathered
    gain_attn = gain_attn.astype(jnp.float32)
    gain_ffn = gain_ffn.astype(jnp.float32)
    gain_query = gain_query.astype(jnp.float32)
    gain_key = gain_key.astype(jnp.float32)
    h_one, norm_one_back = jax.vjp(rms_scaled, hidden_in, gain_attn)
    h_one_low = h_one.astype(jnp.bfloat16)
    query_raw = jnp.dot(h_one_low, full_query, preferred_element_type=jnp.float32)
    key_raw = jnp.dot(h_one_low, full_key, preferred_element_type=jnp.float32)
    values_low = jnp.dot(h_one_low, full_value, preferred_element_type=jnp.float32).astype(
        jnp.bfloat16
    )
    query_rot, query_back = jax.vjp(partial(qk_post, places=place_mine), query_raw, gain_query)
    key_rot, key_back = jax.vjp(partial(qk_post, places=place_mine), key_raw, gain_key)
    query_low = query_rot.astype(jnp.bfloat16)
    key_low = key_rot.astype(jnp.bfloat16)
    key_all, value_all = (
        lax.all_gather(key_low, "ctx", axis=0, tiled=True),
        lax.all_gather(values_low, "ctx", axis=0, tiled=True),
    )
    query_heads = query_low.reshape(row_count, head_count, HEAD_DIM)
    key_heads = key_all.reshape(-1, head_count, HEAD_DIM)
    value_heads = value_all.reshape(-1, head_count, HEAD_DIM)

    def scores_of():
        raw_scores = (
            jnp.einsum("thd,khd->htk", query_heads, key_heads, preferred_element_type=jnp.float32)
            * score_scale
        )
        return jnp.where(same_seq[None, :, :], raw_scores, masked_value)

    scores = scores_of()
    row_top = jnp.max(scores, axis=-1, keepdims=True)
    log_total = row_top + jnp.log(jnp.sum(jnp.exp(scores - row_top), axis=-1, keepdims=True))
    probs_low = jnp.exp(scores - log_total).astype(jnp.bfloat16)
    attended = jnp.einsum(
        "htk,khd->thd", probs_low, value_heads, preferred_element_type=jnp.float32
    )
    attended_low = attended.reshape(row_count, model_width).astype(jnp.bfloat16)
    middle = hidden_in + jnp.dot(attended_low, full_out, preferred_element_type=jnp.float32)
    h_two, norm_two_back = jax.vjp(rms_scaled, middle, gain_ffn)
    h_two_low = h_two.astype(jnp.bfloat16)
    logits = jnp.dot(h_two_low, full_router, preferred_element_type=jnp.float32)
    expert_count = full_router.shape[1]
    route_rows = routes[0]
    top_k = route_rows.shape[1]
    chosen = route_rows[:, :, None] == jnp.arange(expert_count, dtype=jnp.int32)[None, None, :]
    picked, route_back = jax.vjp(partial(route_weights, chosen=chosen), logits)
    pair_count = row_count * top_k
    capacity = 5 * row_count * top_k // (4 * expert_count)
    slot_count = expert_count * capacity
    group_size = lax.axis_size("fsdp")
    local_experts = w_gate.shape[0]
    pair_expert = route_rows.reshape(pair_count)
    one_hot = (pair_expert[:, None] == jnp.arange(expert_count, dtype=jnp.int32)[None, :]).astype(
        jnp.int32
    )
    slot_rank = jnp.sum(one_hot * (jnp.cumsum(one_hot, axis=0) - 1), axis=1)
    slot_ids = pair_expert * capacity + slot_rank
    source = (
        jnp.full((slot_count,), pair_count, jnp.int32)
        .at[slot_ids]
        .set(jnp.arange(pair_count, dtype=jnp.int32))
    )
    filled = source < pair_count
    source_pair = jnp.minimum(source, pair_count - 1)
    send_rows = jnp.where(
        filled[:, None], h_two_low[source_pair // top_k], jnp.zeros((), jnp.bfloat16)
    )
    send_rows = send_rows.reshape(group_size, local_experts, capacity, model_width)
    gate_full, up_full, down_full = (
        lax.all_gather(w_gate, "ctx", axis=1, tiled=True),
        lax.all_gather(w_up, "ctx", axis=1, tiled=True),
        lax.all_gather(w_down, "ctx", axis=1, tiled=True),
    )
    arrived_rows = lax.all_to_all(send_rows, "fsdp", split_axis=0, concat_axis=0, tiled=True)
    gate_part = jnp.einsum(
        "secd,edf->secf", arrived_rows, gate_full, preferred_element_type=jnp.float32
    )
    up_part = jnp.einsum(
        "secd,edf->secf", arrived_rows, up_full, preferred_element_type=jnp.float32
    )
    act_part = (jax.nn.silu(gate_part) * up_part).astype(jnp.bfloat16)
    result = jnp.einsum(
        "secf,efd->secd", act_part, down_full, preferred_element_type=jnp.float32
    ).astype(jnp.bfloat16)
    returned = lax.all_to_all(result, "fsdp", split_axis=0, concat_axis=0, tiled=True).reshape(
        slot_count, model_width
    )
    pair_out = returned[slot_ids].reshape(row_count, top_k, model_width)
    output = (middle + jnp.sum(picked[:, :, None] * pair_out, axis=1)).astype(jnp.bfloat16)
    grad_top = grad_output[0].astype(jnp.float32)
    grad_picked = jnp.sum(grad_top[:, None, :] * pair_out, axis=-1)
    grad_pair = (
        (picked[:, :, None] * grad_top[:, None, :])
        .astype(jnp.bfloat16)
        .reshape(pair_count, model_width)
    )
    grad_send = jnp.where(filled[:, None], grad_pair[source_pair], jnp.zeros((), jnp.bfloat16))
    grad_send = grad_send.reshape(group_size, local_experts, capacity, model_width)
    grad_arrived = lax.all_to_all(grad_send, "fsdp", split_axis=0, concat_axis=0, tiled=True)
    sigma = jax.nn.sigmoid(gate_part)
    act_low = (gate_part * sigma * up_part).astype(jnp.bfloat16)
    grad_act = jnp.einsum(
        "secd,efd->secf", grad_arrived, down_full, preferred_element_type=jnp.float32
    )
    grad_gate = (grad_act * up_part * sigma * (1.0 + gate_part * (1.0 - sigma))).astype(
        jnp.bfloat16
    )
    grad_up = (grad_act * gate_part * sigma).astype(jnp.bfloat16)
    grad_back = jnp.einsum(
        "secf,edf->secd", grad_gate, gate_full, preferred_element_type=jnp.float32
    )
    grad_back = (
        grad_back
        + jnp.einsum("secf,edf->secd", grad_up, up_full, preferred_element_type=jnp.float32)
    ).astype(jnp.bfloat16)
    grad_return = lax.all_to_all(
        grad_back, "fsdp", split_axis=0, concat_axis=0, tiled=True
    ).reshape(slot_count, model_width)
    grad_h_two = jnp.sum(
        grad_return[slot_ids].reshape(row_count, top_k, model_width).astype(jnp.float32), axis=1
    )
    (grad_logits,) = route_back(grad_picked)
    grad_logits_low = grad_logits.astype(jnp.bfloat16)
    grad_h_two = grad_h_two + jnp.einsum(
        "te,de->td", grad_logits_low, full_router, preferred_element_type=jnp.float32
    )
    grad_router = jnp.einsum(
        "td,te->de", h_two_low, grad_logits_low, preferred_element_type=jnp.float32
    )
    grad_middle, grad_ffn_gain = norm_two_back(grad_h_two)
    grad_middle = grad_middle + grad_top
    grad_branch = grad_middle.astype(jnp.bfloat16)
    grad_out_w = jnp.einsum(
        "td,te->de", attended_low, grad_branch, preferred_element_type=jnp.float32
    )
    grad_att = jnp.einsum(
        "te,de->td", grad_branch, full_out, preferred_element_type=jnp.float32
    ).astype(jnp.bfloat16)
    grad_att = grad_att.reshape(row_count, head_count, HEAD_DIM)
    scores = scores_of()
    probs_full = jnp.exp(scores - log_total)
    probs_again = probs_full.astype(jnp.bfloat16)
    grad_probs = jnp.einsum(
        "thd,khd->htk", grad_att, value_heads, preferred_element_type=jnp.float32
    )
    spread = jnp.sum(probs_full * grad_probs, axis=-1, keepdims=True)
    grad_scores = (probs_full * (grad_probs - spread)).astype(jnp.bfloat16)
    grad_query = (
        jnp.einsum(
            "htk,khd->thd", grad_scores, key_heads, preferred_element_type=jnp.float32
        ).reshape(row_count, model_width)
        * score_scale
    )
    grad_key_part = (
        jnp.einsum(
            "htk,thd->khd", grad_scores, query_heads, preferred_element_type=jnp.float32
        ).reshape(-1, model_width)
        * score_scale
    )
    grad_value_part = jnp.einsum(
        "htk,thd->khd", probs_again, grad_att, preferred_element_type=jnp.float32
    ).reshape(-1, model_width)
    grad_key, grad_value = (
        lax.psum_scatter(
            grad_key_part.astype(jnp.bfloat16), "ctx", scatter_dimension=0, tiled=True
        ).astype(jnp.float32),
        lax.psum_scatter(
            grad_value_part.astype(jnp.bfloat16), "ctx", scatter_dimension=0, tiled=True
        ).astype(jnp.float32),
    )
    grad_q_raw, grad_q_gain = query_back(grad_query)
    grad_k_raw, grad_k_gain = key_back(grad_key)
    grad_q_low = grad_q_raw.astype(jnp.bfloat16)
    grad_k_low = grad_k_raw.astype(jnp.bfloat16)
    grad_v_low = grad_value.astype(jnp.bfloat16)
    grad_query_w = jnp.einsum(
        "td,te->de", h_one_low, grad_q_low, preferred_element_type=jnp.float32
    )
    grad_key_w = jnp.einsum("td,te->de", h_one_low, grad_k_low, preferred_element_type=jnp.float32)
    grad_value_w = jnp.einsum(
        "td,te->de", h_one_low, grad_v_low, preferred_element_type=jnp.float32
    )
    grad_h_one = jnp.einsum("te,de->td", grad_q_low, full_query, preferred_element_type=jnp.float32)
    grad_h_one = grad_h_one + jnp.einsum(
        "te,de->td", grad_k_low, full_key, preferred_element_type=jnp.float32
    )
    grad_h_one = grad_h_one + jnp.einsum(
        "te,de->td", grad_v_low, full_value, preferred_element_type=jnp.float32
    )
    grad_input_norm, grad_attn_gain = norm_one_back(grad_h_one)
    grad_input = grad_middle + grad_input_norm
    totals = (
        lax.psum_scatter(grad_query_w, ("ctx", "fsdp"), scatter_dimension=0, tiled=True),
        lax.psum_scatter(grad_key_w, ("ctx", "fsdp"), scatter_dimension=0, tiled=True),
        lax.psum_scatter(grad_value_w, ("ctx", "fsdp"), scatter_dimension=0, tiled=True),
        lax.psum_scatter(grad_out_w, ("ctx", "fsdp"), scatter_dimension=0, tiled=True),
        lax.psum_scatter(grad_router, ("ctx", "fsdp"), scatter_dimension=0, tiled=True),
        lax.psum_scatter(grad_attn_gain, ("ctx", "fsdp"), scatter_dimension=0, tiled=True),
        lax.psum_scatter(grad_ffn_gain, ("ctx", "fsdp"), scatter_dimension=0, tiled=True),
        lax.psum_scatter(grad_q_gain, ("ctx", "fsdp"), scatter_dimension=0, tiled=True),
        lax.psum_scatter(grad_k_gain, ("ctx", "fsdp"), scatter_dimension=0, tiled=True),
    )
    grad_down_w = jnp.einsum(
        "secf,secd->efd", act_low, grad_arrived, preferred_element_type=jnp.float32
    )
    grad_gate_w = jnp.einsum(
        "secd,secf->edf", arrived_rows, grad_gate, preferred_element_type=jnp.float32
    )
    grad_up_w = jnp.einsum(
        "secd,secf->edf", arrived_rows, grad_up, preferred_element_type=jnp.float32
    )
    gate_grad, up_grad, down_grad = (
        lax.psum_scatter(
            grad_gate_w.astype(jnp.bfloat16), "ctx", scatter_dimension=1, tiled=True
        ).astype(jnp.float32),
        lax.psum_scatter(
            grad_up_w.astype(jnp.bfloat16), "ctx", scatter_dimension=1, tiled=True
        ).astype(jnp.float32),
        lax.psum_scatter(
            grad_down_w.astype(jnp.bfloat16), "ctx", scatter_dimension=1, tiled=True
        ).astype(jnp.float32),
    )
    return (
        output[None],
        grad_input[None],
        totals[0],
        totals[1],
        totals[2],
        totals[3],
        totals[4],
        totals[5],
        totals[6],
        totals[7],
        totals[8],
        gate_grad,
        up_grad,
        down_grad,
    )


def masked_probs(query, key, seq_rows, seq_cols, scale):
    scores = (
        lax.dot_general(query, key, (((1,), (1,)), ((), ())), preferred_element_type=jnp.float32)
        * scale
    )
    scores = jnp.where(seq_rows == seq_cols, scores, masked_value)
    top = jnp.max(scores, axis=-1, keepdims=True)
    weights = jnp.exp(scores - top)
    return weights / jnp.sum(weights, axis=-1, keepdims=True)


def attend_kernel(scale, seq_rows, seq_cols, query, key, value, out):
    probs = masked_probs(query[...], key[...], seq_rows[...], seq_cols[...], scale)
    out[...] = jnp.dot(
        probs.astype(jnp.bfloat16), value[...], preferred_element_type=jnp.float32
    ).astype(out.dtype)


def attend_back_kernel(
    scale, seq_rows, seq_cols, query, key, value, grad, grad_query, grad_key, grad_value
):
    @pl.when(pl.program_id(1) == 0)
    def _():
        grad_key[...] = jnp.zeros_like(grad_key)
        grad_value[...] = jnp.zeros_like(grad_value)

    probs = masked_probs(query[...], key[...], seq_rows[...], seq_cols[...], scale)
    grad_probs = lax.dot_general(
        grad[...], value[...], (((1,), (1,)), ((), ())), preferred_element_type=jnp.float32
    )
    spread = jnp.sum(probs * grad_probs, axis=-1, keepdims=True)
    grad_scores = (probs * (grad_probs - spread)).astype(jnp.bfloat16)
    grad_query[...] = (
        jnp.dot(grad_scores, key[...], preferred_element_type=jnp.float32) * scale
    )
    grad_key[...] += (
        lax.dot_general(
            grad_scores,
            query[...],
            (((0,), (0,)), ((), ())),
            preferred_element_type=jnp.float32,
        )
        * scale
    )
    grad_value[...] += lax.dot_general(
        probs.astype(jnp.bfloat16),
        grad[...],
        (((0,), (0,)), ((), ())),
        preferred_element_type=jnp.float32,
    )


def attention_specs(rows, block):
    per_block = pl.BlockSpec((block, HEAD_DIM), lambda h, i: (i, h))
    per_head = pl.BlockSpec((rows, HEAD_DIM), lambda h, i: (0, h))
    seqs = [
        pl.BlockSpec((block, 1), lambda h, i: (i, 0)),
        pl.BlockSpec((1, rows), lambda h, i: (0, 0)),
    ]
    return per_block, per_head, seqs


def attend(seq_ids, query, key, value):
    rows, width = query.shape
    block = math.gcd(rows, 256)
    per_block, per_head, seqs = attention_specs(rows, block)
    pairs = rows * rows * width
    return pl.pallas_call(
        partial(attend_kernel, 1.0 / math.sqrt(HEAD_DIM)),
        grid=(width // HEAD_DIM, rows // block),
        in_specs=seqs + [per_block, per_head, per_head],
        out_specs=per_block,
        out_shape=jax.ShapeDtypeStruct((rows, width), jnp.bfloat16),
        cost_estimate=pl.CostEstimate(
            flops=4 * pairs, bytes_accessed=8 * rows * width, transcendentals=pairs // HEAD_DIM
        ),
        compiler_params=pltpu.CompilerParams(vmem_limit_bytes=48 << 20),
        name="attend",
    )(seq_ids[:, None], seq_ids[None, :], query, key, value)


def attend_back(seq_ids, query, key, value, grad):
    rows, width = query.shape
    block = math.gcd(rows, 256)
    per_block, per_head, seqs = attention_specs(rows, block)
    pairs = rows * rows * width
    return pl.pallas_call(
        partial(attend_back_kernel, 1.0 / math.sqrt(HEAD_DIM)),
        grid=(width // HEAD_DIM, rows // block),
        in_specs=seqs + [per_block, per_head, per_head, per_block],
        out_specs=(per_block, per_head, per_head),
        out_shape=(jax.ShapeDtypeStruct((rows, width), jnp.float32),) * 3,
        cost_estimate=pl.CostEstimate(
            flops=10 * pairs, bytes_accessed=20 * rows * width, transcendentals=pairs // HEAD_DIM
        ),
        compiler_params=pltpu.CompilerParams(vmem_limit_bytes=48 << 20),
        name="attend_back",
    )(seq_ids[:, None], seq_ids[None, :], query, key, value, grad)


def dispatch_kernel(position, rows, out):
    columns, _, capacity, width = out.shape
    count = rows.shape[1]
    slots = lax.broadcasted_iota(jnp.int32, (columns, capacity, count), 1)
    select = jnp.where(slots == position[:, 0], 1.0, 0.0)
    select = select.reshape(columns * capacity, count).astype(jnp.bfloat16)
    step = math.gcd(width, 512)
    for at in range(0, width, step):
        part = jnp.dot(select, rows[0, :, at : at + step], preferred_element_type=jnp.float32)
        part = part.reshape(columns, capacity, step).astype(out.dtype)
        out[:, 0, :, at : at + step] = part


def dispatch(position, capacity, rows):
    columns, planes, count = position.shape
    width = rows.shape[1]
    return pl.pallas_call(
        dispatch_kernel,
        grid=(planes,),
        in_specs=[
            pl.BlockSpec((columns, 1, 1, count), lambda b: (0, b, 0, 0)),
            pl.BlockSpec((1, count, width), lambda b: (b, 0, 0)),
        ],
        out_specs=pl.BlockSpec((columns, 1, capacity, width), lambda b: (0, b, 0, 0)),
        out_shape=jax.ShapeDtypeStruct((columns, planes, capacity, width), jnp.bfloat16),
        cost_estimate=pl.CostEstimate(
            flops=2 * position.size * capacity * width,
            bytes_accessed=2 * columns * planes * capacity * width,
            transcendentals=0,
        ),
        compiler_params=pltpu.CompilerParams(vmem_limit_bytes=40 << 20),
        name="dispatch",
    )(position[:, :, None], rows.reshape(planes, count, width))


def heads_of(width):
    return [slice(at, at + HEAD_DIM) for at in range(0, width, HEAD_DIM)]


def turn_kernel(raw, scales, gains, cosine, sine, query, key, value):
    width = query.shape[1]
    for which, out in ((0, query), (1, key)):
        scale = scales[:, which : which + 1]
        for head in heads_of(width):
            part = raw[:, which * width + head.start : which * width + head.stop]
            part = part * scale * gains[which : which + 1, head]
            swapped = pltpu.roll(part, HEAD_DIM // 2, 1)
            out[:, head] = (part * cosine[...] + swapped * sine[...]).astype(out.dtype)
    value[...] = raw[:, 2 * width : 3 * width].astype(value.dtype)


def turn_back_kernel(
    raw, scales, gains, cosine, sine, grad_query, grad_key, out_query, out_key, dots, grad_gains
):
    @pl.when(pl.program_id(0) == 0)
    def _():
        grad_gains[...] = jnp.zeros_like(grad_gains)

    width = grad_query.shape[1]
    for which, grad, out in ((0, grad_query, out_query), (1, grad_key, out_key)):
        scale = scales[:, which : which + 1]
        total = jnp.zeros_like(scale)
        for head in heads_of(width):
            part = grad[:, head]
            part = part * cosine[...] - pltpu.roll(part, HEAD_DIM // 2, 1) * sine[...]
            hat = raw[:, which * width + head.start : which * width + head.stop] * scale
            grad_gains[which : which + 1, head] += jnp.sum(part * hat, axis=0, keepdims=True)
            part = part * gains[which : which + 1, head]
            total += jnp.sum(part * hat, axis=1, keepdims=True)
            out[:, head] = part
        dots[:, which : which + 1] = total


def turn_specs(raw, gains):
    block = math.gcd(raw.shape[0], 256)
    return block, [
        pl.BlockSpec((block, raw.shape[1]), lambda i: (i, 0)),
        pl.BlockSpec((block, 2), lambda i: (i, 0)),
        pl.BlockSpec(gains.shape, lambda i: (0, 0)),
        pl.BlockSpec((block, HEAD_DIM), lambda i: (i, 0)),
        pl.BlockSpec((block, HEAD_DIM), lambda i: (i, 0)),
    ]


def turn(raw, scales, gains, cosine, sine):
    rows, width = raw.shape[0], gains.shape[1]
    block, specs = turn_specs(raw, gains)
    return pl.pallas_call(
        turn_kernel,
        grid=(rows // block,),
        in_specs=specs,
        out_specs=(pl.BlockSpec((block, width), lambda i: (i, 0)),) * 3,
        out_shape=(jax.ShapeDtypeStruct((rows, width), jnp.bfloat16),) * 3,
        cost_estimate=pl.CostEstimate(
            flops=16 * rows * width, bytes_accessed=18 * rows * width, transcendentals=0
        ),
        compiler_params=pltpu.CompilerParams(vmem_limit_bytes=40 << 20),
        name="turn",
    )(raw, scales, gains, cosine, sine)


def turn_back(raw, scales, gains, cosine, sine, grad_query, grad_key):
    rows, width = grad_query.shape
    block, specs = turn_specs(raw, gains)
    wide = pl.BlockSpec((block, width), lambda i: (i, 0))
    f32 = jnp.float32
    return pl.pallas_call(
        turn_back_kernel,
        grid=(rows // block,),
        in_specs=specs + [wide, wide],
        out_specs=(
            wide,
            wide,
            pl.BlockSpec((block, 2), lambda i: (i, 0)),
            pl.BlockSpec((2, width), lambda i: (0, 0)),
        ),
        out_shape=(
            jax.ShapeDtypeStruct((rows, width), f32),
            jax.ShapeDtypeStruct((rows, width), f32),
            jax.ShapeDtypeStruct((rows, 2), f32),
            jax.ShapeDtypeStruct((2, width), f32),
        ),
        cost_estimate=pl.CostEstimate(
            flops=24 * rows * width, bytes_accessed=28 * rows * width, transcendentals=0
        ),
        compiler_params=pltpu.CompilerParams(vmem_limit_bytes=40 << 20),
        name="turn_back",
    )(raw, scales, gains, cosine, sine, grad_query, grad_key)


def expert_in_kernel(
    rows, gate, up, router, own, gate_out, up_out, act_out, picked_out
):
    logits = jnp.dot(rows[...], router[...], preferred_element_type=jnp.float32)
    weights = jnp.exp(logits - jnp.max(logits, axis=1, keepdims=True))
    picked = jnp.sum(weights * own[...], axis=1, keepdims=True)
    picked = picked / jnp.sum(weights, axis=1, keepdims=True)
    gate_pre = jnp.dot(rows[...], gate[...], preferred_element_type=jnp.float32)
    up_pre = jnp.dot(rows[...], up[...], preferred_element_type=jnp.float32)
    act = (gate_pre * jax.nn.sigmoid(gate_pre) * up_pre).astype(jnp.bfloat16)
    gate_out[...] = gate_pre
    up_out[...] = up_pre
    act_out[...] = (act.astype(jnp.float32) * picked).astype(jnp.bfloat16)
    picked_out[...] = picked


def expert_back_kernel(
    grad, gate_in, up_in, picked, gate, up, down, grad_gate, grad_up, grad_picked, grad_rows
):
    grad_raw = lax.dot_general(
        grad[...], down[...], (((1,), (1,)), ((), ())), preferred_element_type=jnp.float32
    )
    gate_pre, up_pre = gate_in[...], up_in[...]
    sigma = jax.nn.sigmoid(gate_pre)
    silu = gate_pre * sigma
    act = (silu * up_pre).astype(jnp.bfloat16).astype(jnp.float32)
    grad_picked[...] = jnp.sum(grad_raw * act, axis=1, keepdims=True)
    grad_act = grad_raw * picked[...]
    low_gate = (grad_act * up_pre * (sigma + silu * (1.0 - sigma))).astype(jnp.bfloat16)
    low_up = (grad_act * silu).astype(jnp.bfloat16)
    grad_gate[...] = low_gate
    grad_up[...] = low_up
    back = lax.dot_general(
        low_gate, gate[...], (((1,), (1,)), ((), ())), preferred_element_type=jnp.float32
    )
    back = back + lax.dot_general(
        low_up, up[...], (((1,), (1,)), ((), ())), preferred_element_type=jnp.float32
    )
    grad_rows[...] = back.astype(jnp.bfloat16)


def whole(shape):
    return pl.BlockSpec(shape, lambda i: (0, 0), pipeline_mode=pl.Buffered(1))


def row_blocks(block, width):
    return pl.BlockSpec((block, width), lambda i: (i, 0))


def expert_in(rows, gate, up, router, own, block):
    count, width = rows.shape
    hidden = gate.shape[1]
    narrow = row_blocks(block, hidden)
    f32 = jnp.float32
    return pl.pallas_call(
        expert_in_kernel,
        grid=(count // block,),
        in_specs=[
            row_blocks(block, width),
            whole(gate.shape),
            whole(up.shape),
            whole(router.shape),
            whole(own.shape),
        ],
        out_specs=(narrow, narrow, narrow, row_blocks(block, 1)),
        out_shape=(
            jax.ShapeDtypeStruct((count, hidden), f32),
            jax.ShapeDtypeStruct((count, hidden), f32),
            jax.ShapeDtypeStruct((count, hidden), jnp.bfloat16),
            jax.ShapeDtypeStruct((count, 1), f32),
        ),
        cost_estimate=pl.CostEstimate(
            flops=4 * count * width * hidden,
            bytes_accessed=2 * count * width + (10 * count + 4 * width) * hidden,
            transcendentals=count * hidden,
        ),
        compiler_params=pltpu.CompilerParams(vmem_limit_bytes=56 << 20),
        name="expert_in",
    )(rows, gate, up, router, own)


def expert_back(grad, gate_pre, up_pre, picked, gate, up, down, block):
    count, width = grad.shape
    hidden = down.shape[0]
    wide, narrow, one = [row_blocks(block, size) for size in (width, hidden, 1)]
    low = jax.ShapeDtypeStruct((count, hidden), jnp.bfloat16)
    return pl.pallas_call(
        expert_back_kernel,
        grid=(count // block,),
        in_specs=[wide, narrow, narrow, one, whole(gate.shape), whole(up.shape), whole(down.shape)],
        out_specs=(narrow, narrow, one, wide),
        out_shape=(
            low,
            low,
            jax.ShapeDtypeStruct((count, 1), jnp.float32),
            jax.ShapeDtypeStruct((count, width), jnp.bfloat16),
        ),
        cost_estimate=pl.CostEstimate(
            flops=6 * count * width * hidden,
            bytes_accessed=4 * count * width + (12 * count + 6 * width) * hidden,
            transcendentals=count * hidden,
        ),
        compiler_params=pltpu.CompilerParams(vmem_limit_bytes=58 << 20),
        name="expert_back",
    )(grad, gate_pre, up_pre, picked, gate, up, down)


def tie(array, *others):
    anywhere = pl.BlockSpec(memory_space=pl.ANY)
    return pl.pallas_call(
        lambda *refs: None,
        in_specs=[anywhere] * (1 + len(others)),
        out_specs=anywhere,
        out_shape=jax.ShapeDtypeStruct(array.shape, array.dtype),
        input_output_aliases={0: 0},
        name="tie",
    )(array, *others)


def mm(left, right):
    return jnp.dot(left, right, preferred_element_type=jnp.float32)


def mm_t(left, right):
    return lax.dot_general(
        left, right, (((1,), (1,)), ((), ())), preferred_element_type=jnp.float32
    )


def t_mm(left, right):
    return lax.dot_general(
        left, right, (((0,), (0,)), ((), ())), preferred_element_type=jnp.float32
    )


def plane_shards(
    hidden,
    token_order,
    lengths,
    routes,
    grad_output,
    w_query,
    w_key,
    w_value,
    w_out,
    w_router,
    attn_gain,
    ffn_gain,
    query_gain,
    key_gain,
    w_gate,
    w_up,
    w_down,
):
    f32, bf16 = jnp.float32, jnp.bfloat16
    both = ("ctx", "fsdp")
    planes = lax.axis_size("ctx")
    columns = lax.axis_size("fsdp")
    plane = lax.axis_index("ctx")
    row_count, width = hidden.shape[1:]
    group_rows = row_count * planes
    share = width // planes
    strip = w_query.shape[0]
    first_row = plane * row_count

    experts = w_router.shape[1]
    qkv = jnp.stack([w_query, w_key, w_value], axis=1).reshape(strip, 3, planes, share)
    qkv = qkv.transpose(2, 0, 1, 3).reshape(planes, strip, 3 * share)
    small = [w_router] + [g[:, None] for g in (attn_gain, ffn_gain, query_gain, key_gain)]
    small = jnp.concatenate(small + [routes.astype(bf16).reshape(strip, -1)], axis=1)
    spare = -small.shape[1] % 128
    small = jnp.pad(small, ((0, 0), (0, spare)))
    small = jnp.broadcast_to(small[None], (planes,) + small.shape)
    own_out = jnp.broadcast_to(w_out[None], (planes,) + w_out.shape)
    packed = jnp.concatenate([qkv, small, own_out], axis=2)
    packed = lax.all_to_all(packed, "ctx", 0, 0, tiled=True)
    hidden_all = lax.all_gather(tie(hidden[0], packed), "ctx", axis=0, tiled=True)
    packed, out_rows = packed[:, :, :-width], packed[:, :, -width:]
    routes_at = 3 * share + experts + 4
    routes_all = packed[:, :, routes_at : packed.shape[2] - spare].astype(jnp.int32)
    routes_all = routes_all.reshape(group_rows, -1)
    packed = jnp.broadcast_to(packed[None], (columns,) + packed.shape)
    packed = lax.all_to_all(packed, "fsdp", 0, 0, tiled=True)
    packed = packed.transpose(1, 0, 2, 3).reshape(width, -1)
    full_router = packed[:, 3 * share : 3 * share + experts]
    gain_attn, gain_ffn, gain_query, gain_key = [
        packed[:, 3 * share + experts + i].astype(f32) for i in range(4)
    ]
    def swap(part, step):
        return lax.ppermute(part, "ctx", [(i, i ^ step) for i in range(planes)])

    def by_plane(came):
        came = jnp.stack(came)
        return [came[plane ^ i] for i in range(planes)]

    def exchange(parts, first=None, last=None):
        came = [parts[plane]]
        for step in range(1, planes):
            part = parts[plane ^ step]
            part = swap(part if first is None else tie(part, first), step)
            came.append(part if last is None else tie(part, last))
        return by_plane(came)

    def exchange_after(parts, earlier):
        came = [
            swap(part if before is None else tie(part, before), step)
            for step, before in enumerate(earlier, 1)
            for part in [parts[plane ^ step]]
        ]
        return came, jnp.stack(by_plane([parts[plane]] + came)).astype(f32)

    def plane_sum(part):
        return part + sum(swap(part, step) for step in range(1, planes))

    out_rows = jnp.broadcast_to(out_rows[None], (columns,) + out_rows.shape)
    grad_all = lax.all_gather(
        tie(grad_output[0], hidden_all, packed, out_rows), "ctx", axis=0, tiled=True
    )
    full_out = lax.all_to_all(out_rows, "fsdp", 0, 0, tiled=True)
    full_out = full_out.transpose(1, 0, 2, 3).reshape(width, width)

    seq_ids, places = seq_layout(token_order[0], lengths[0])
    experts_here = w_gate.shape[0]
    column_expert = experts_here * jnp.arange(columns, dtype=jnp.int32) + plane
    named = jnp.any(routes_all[:, :, None] == column_expert[None, None, :], axis=1)
    named = named.reshape(planes, row_count, columns)
    capacity = 5 * row_count * routes.shape[2] // (4 * experts)
    rank = jnp.cumsum(named.astype(jnp.int32), axis=1) - 1
    position = jnp.where(named, rank, -1).transpose(2, 0, 1)
    slots = jnp.arange(capacity, dtype=jnp.int32)
    holds = position[:, :, None, :] == slots[None, None, :, None]
    select = holds.astype(bf16)

    def combine(rows):
        rows = rows.reshape(columns, planes, capacity, width)
        sums = jnp.einsum("fbsr,fbsd->brd", select, rows, preferred_element_type=f32)
        return sums.reshape(group_rows, width).astype(bf16)


    frequency = rope_base ** (
        -2.0 * jnp.arange(HEAD_DIM // 2).astype(f32) / HEAD_DIM
    )
    angles = places.astype(f32)[:, None] * frequency[None, :]
    cosine, sine = jnp.cos(angles), jnp.sin(angles)
    cosine = jnp.concatenate([cosine, cosine], axis=1)
    sine = jnp.concatenate([-sine, sine], axis=1)
    hidden_wide = hidden_all.astype(f32)
    scale_one = lax.rsqrt(jnp.mean(hidden_wide * hidden_wide, axis=-1, keepdims=True) + epsilon)
    h_one = (hidden_wide * scale_one * gain_attn).astype(bf16)
    raw = mm(h_one, packed)
    squares = jnp.stack(
        [jnp.sum(raw[:, :share] ** 2, axis=1), jnp.sum(raw[:, share : 2 * share] ** 2, axis=1)]
    )
    squares = plane_sum(squares)
    scales = lax.rsqrt(squares / width + epsilon).T
    gains = lax.dynamic_slice_in_dim(
        jnp.stack([gain_query, gain_key]), plane * share, share, axis=1
    )
    query, key, values = turn(raw, scales, gains, cosine, sine)
    attended = attend(seq_ids, query, key, values)
    attended = attended.reshape(planes, row_count, share)
    attended = jnp.concatenate(exchange(attended), axis=1)
    grad_send = dispatch(position, capacity, tie(grad_all, attended))
    grad_in = lax.all_to_all(grad_send, "fsdp", 0, 0, tiled=True).reshape(-1, width)
    middle = hidden[0].astype(f32) + mm(attended, full_out)
    scale_two = lax.rsqrt(jnp.mean(middle * middle, axis=-1, keepdims=True) + epsilon)
    middle_hat = middle * scale_two
    h_two = (middle_hat * gain_ffn).astype(bf16)

    h_two_all = lax.all_gather(tie(h_two, grad_send), "ctx", axis=0, tiled=True)
    came = [swap(tie(w_gate[plane ^ step], h_two_all), step) for step in range(1, planes)]
    gate = jnp.concatenate(by_plane([w_gate[plane]] + came))
    h_all = tie(h_two_all, grad_in, *came[:-1])
    up = jnp.concatenate(exchange(w_up, h_two_all))
    probs = jax.nn.softmax(mm(h_two, full_router), axis=-1)
    rows_in = lax.all_to_all(dispatch(position, capacity, h_all), "fsdp", 0, 0, tiled=True)
    rows_in = rows_in.reshape(-1, width)
    own = experts_here * lax.axis_index("fsdp") + plane
    own = (jnp.arange(experts)[None, :] == own).astype(f32)
    slot_block = planes * capacity
    gate_pre, up_pre, act_picked, picked = expert_in(
        rows_in, gate, up, full_router, own, slot_block
    )
    down = jnp.concatenate(exchange(w_down, h_two_all, act_picked))
    grad_down_w = t_mm(act_picked, grad_in).astype(bf16)
    grad_gate, grad_up, grad_picked, grad_rows = expert_back(
        grad_in, tie(gate_pre, grad_down_w), up_pre, picked, gate, up, down, slot_block
    )

    def blocks(matrix):
        return matrix.reshape(planes, matrix.shape[0] // planes, matrix.shape[1])

    came, down_grad = exchange_after(blocks(grad_down_w), [None] * (planes - 1))
    grad_rows = tie(grad_rows, *came)
    grad_rows = lax.all_to_all(
        grad_rows.reshape(columns, planes * capacity, width), "fsdp", 0, 0, tiled=True
    )
    grad_gate_w = t_mm(rows_in, grad_gate).astype(bf16)
    grad_up_w = t_mm(rows_in, grad_up).astype(bf16)
    came, up_grad = exchange_after(blocks(grad_up_w), came)
    came, gate_grad = exchange_after(blocks(grad_gate_w), came)
    expert_out = mm(act_picked, down).astype(bf16)
    grad_picked = lax.all_to_all(
        tie(grad_picked, grad_rows).reshape(columns, planes, capacity), "fsdp", 0, 0, tiled=True
    )
    grad_rows = tie(grad_rows, *came, expert_out, grad_picked)
    expert_out = lax.all_to_all(
        expert_out.reshape(columns, planes * capacity, width), "fsdp", 0, 0, tiled=True
    )
    grad_h_two = lax.psum_scatter(
        combine(grad_rows), "ctx", scatter_dimension=0, tiled=True
    ).astype(f32)

    u_plane = jnp.sum(jnp.where(holds, grad_picked[..., None], 0.0), axis=2)
    u_mine = exchange(u_plane.transpose(1, 0, 2))
    u_mine = jnp.stack(u_mine, axis=1).reshape(experts, row_count).T
    grad_logits = probs * (u_mine - jnp.sum(probs * u_mine, axis=-1, keepdims=True))
    grad_logits = grad_logits.astype(bf16)
    grad_h_two = grad_h_two + mm_t(grad_logits, full_router)
    grad_router = t_mm(h_two, grad_logits)

    grad_top = grad_output[0].astype(f32)
    grad_ffn_gain = jnp.sum(grad_h_two * middle_hat, axis=0)
    grad_hat = grad_h_two * gain_ffn
    grad_middle = grad_top + scale_two * (
        grad_hat - middle_hat * jnp.mean(grad_hat * middle_hat, axis=-1, keepdims=True)
    )
    grad_branch = grad_middle.astype(bf16)
    grad_att = mm_t(grad_branch, full_out).astype(bf16)
    grad_att = grad_att.reshape(row_count, planes, share).transpose(1, 0, 2)
    grad_att = jnp.concatenate(exchange(grad_att))
    grad_out_w = t_mm(attended, grad_branch).astype(bf16)
    grad_out_w = grad_out_w.reshape(planes, columns, strip, width).transpose(1, 0, 2, 3)
    mixed_part = combine(tie(expert_out, grad_att, grad_out_w))
    mixed = lax.psum_scatter(mixed_part, "ctx", scatter_dimension=0, tiled=True)
    output = (middle + mixed.astype(f32)).astype(bf16)
    grad_out_w = lax.all_to_all(
        tie(grad_out_w, mixed_part), "fsdp", 0, 0, tiled=True
    )
    grad_att = tie(grad_att, mixed_part)
    grad_query, grad_key, grad_value = attend_back(seq_ids, query, key, values, grad_att)
    grad_query, grad_key, dots, grad_gains = turn_back(
        raw, scales, gains, cosine, sine, grad_query, grad_key
    )
    dots = plane_sum(dots.T).T * (scales * scales) / width
    grad_qkv = jnp.concatenate(
        [
            scales[:, :1] * grad_query - raw[:, :share] * (scales[:, :1] * dots[:, :1]),
            scales[:, 1:] * grad_key - raw[:, share : 2 * share] * (scales[:, 1:] * dots[:, 1:]),
            grad_value,
        ],
        axis=1,
    ).astype(bf16)
    grad_qkv = tie(grad_qkv, mixed, grad_out_w)
    grad_out_w = jnp.sum(grad_out_w.astype(f32), axis=0).astype(bf16)
    grad_part = mm_t(grad_qkv, packed[:, : 3 * share])
    grad_h_one = lax.psum_scatter(
        grad_part.astype(bf16), "ctx", scatter_dimension=0, tiled=True
    ).astype(f32)
    grad_attn_gain = jnp.sum(grad_part * (hidden_wide * scale_one), axis=0)
    rows_of = jnp.arange(planes)[:, None] == plane
    gains = [jnp.where(rows_of, g[None], 0.0).reshape(width) for g in grad_gains]
    gains = [g[:, None] for g in [grad_attn_gain, grad_ffn_gain] + gains]
    small = jnp.concatenate([grad_router] + gains, axis=1).reshape(planes * columns, -1)
    small = lax.all_to_all(small, both, 0, 0, tiled=True)
    grad_qkv = tie(grad_qkv, small)
    small = jnp.sum(small, axis=0).reshape(strip, -1)
    grad_out_w = sum(x.astype(f32) for x in exchange(grad_out_w))
    sums = t_mm(h_one, grad_qkv).astype(bf16)
    sums = sums.reshape(planes, columns, strip, -1).transpose(1, 0, 2, 3)
    sums = lax.all_to_all(sums, "fsdp", 0, 0, tiled=True)
    sums = jnp.sum(sums.astype(f32), axis=0).astype(bf16)
    sums = lax.all_to_all(sums, "ctx", 0, 0, tiled=True)
    grad_qkv_w = sums.reshape(planes, strip, 3, share).transpose(2, 1, 0, 3)
    grad_qkv_w = grad_qkv_w.reshape(3, strip, width).astype(f32)

    x_hat = hidden[0].astype(f32)
    scale_mine = lax.rsqrt(jnp.mean(x_hat * x_hat, axis=-1, keepdims=True) + epsilon)
    x_hat = x_hat * scale_mine
    grad_hat = grad_h_one * gain_attn
    grad_input = grad_middle + scale_mine * (
        grad_hat - x_hat * jnp.mean(grad_hat * x_hat, axis=-1, keepdims=True)
    )

    return (
        output[None],
        grad_input[None],
        grad_qkv_w[0],
        grad_qkv_w[1],
        grad_qkv_w[2],
        grad_out_w,
        small[:, :experts],
        small[:, experts],
        small[:, experts + 1],
        small[:, experts + 2],
        small[:, experts + 3],
        gate_grad,
        up_grad,
        down_grad,
    )


def solution(mesh):
    placed = (
        P("fsdp", "ctx", None),
        P("fsdp", None),
        P("fsdp", None),
        P("fsdp", "ctx", None),
        P("fsdp", "ctx", None),
        P(("ctx", "fsdp"), None),
        P(("ctx", "fsdp"), None),
        P(("ctx", "fsdp"), None),
        P(("ctx", "fsdp"), None),
        P(("ctx", "fsdp"), None),
        P(("ctx", "fsdp")),
        P(("ctx", "fsdp")),
        P(("ctx", "fsdp")),
        P(("ctx", "fsdp")),
        P("fsdp", "ctx", None),
        P("fsdp", "ctx", None),
        P("fsdp", "ctx", None),
    )

    def shards(*operands):
        experts_here = operands[14].shape[0]
        heads = operands[0].shape[2] // HEAD_DIM
        planes = mesh.shape["ctx"]
        whole_experts = experts_here == planes and heads % planes == 0 and planes in (2, 4)
        return (plane_shards if whole_experts else general_shards)(*operands)

    return jax.shard_map(
        shards,
        mesh=mesh,
        in_specs=placed,
        out_specs=(
            P("fsdp", "ctx", None),
            P("fsdp", "ctx", None),
            P(("ctx", "fsdp"), None),
            P(("ctx", "fsdp"), None),
            P(("ctx", "fsdp"), None),
            P(("ctx", "fsdp"), None),
            P(("ctx", "fsdp"), None),
            P(("ctx", "fsdp")),
            P(("ctx", "fsdp")),
            P(("ctx", "fsdp")),
            P(("ctx", "fsdp")),
            P("fsdp", "ctx", None),
            P("fsdp", "ctx", None),
            P("fsdp", "ctx", None),
        ),
        check_vma=False,
    )
```

```python
from functools import partial
import math

import jax
import jax.numpy as jnp
from jax import lax
from jax.experimental import pallas as pl
from jax.experimental.pallas import tpu as pltpu
from jax.sharding import PartitionSpec as P

HEAD_DIM = 128


epsilon = 1e-06
rope_base = 10000.0
masked_value = -1e30


def rms_scaled(values, gain):
    return values * lax.rsqrt(jnp.mean(values * values, axis=-1, keepdims=True) + epsilon) * gain


def rotate(values, places):
    row_count = values.shape[0]
    head_count = values.shape[1] // HEAD_DIM
    half_width = HEAD_DIM // 2
    frequency = rope_base ** (-2.0 * jnp.arange(half_width).astype(jnp.float32) / HEAD_DIM)
    angles = places.astype(jnp.float32)[:, None] * frequency[None, :]
    cosine = jnp.cos(angles)[:, None, :]
    sine_part = jnp.sin(angles)[:, None, :]
    split_heads = values.reshape(row_count, head_count, HEAD_DIM)
    first_half = split_heads[:, :, :half_width]
    second_half = split_heads[:, :, half_width:]
    turned = jnp.concatenate(
        [
            first_half * cosine - second_half * sine_part,
            second_half * cosine + first_half * sine_part,
        ],
        axis=-1,
    )
    return turned.reshape(row_count, head_count * HEAD_DIM)


def qk_post(values, gain, places):
    return rotate(rms_scaled(values, gain), places)


def route_weights(logits, chosen):
    router_probs = jax.nn.softmax(logits, axis=-1)
    return jnp.sum(jnp.where(chosen, router_probs[:, None, :], 0.0), axis=-1)


def seq_layout(order_row, seq_lengths):
    seq_ends = jnp.cumsum(seq_lengths)
    seq_ids = jnp.sum((order_row[:, None] >= seq_ends[None, :]).astype(jnp.int32), axis=1)
    starts = seq_ends - seq_lengths
    chosen = seq_ids[:, None] == jnp.arange(seq_lengths.shape[0], dtype=jnp.int32)[None, :]
    seq_start = jnp.sum(jnp.where(chosen, starts[None, :], 0), axis=1)
    return (seq_ids, order_row - seq_start)


def general_shards(
    hidden,
    token_order,
    lengths,
    routes,
    grad_output,
    w_query,
    w_key,
    w_value,
    w_out,
    w_router,
    attn_gain,
    ffn_gain,
    query_gain,
    key_gain,
    w_gate,
    w_up,
    w_down,
):
    hidden_in = hidden[0].astype(jnp.float32)
    row_count = hidden_in.shape[0]
    model_width = hidden_in.shape[1]
    head_count = model_width // HEAD_DIM
    score_scale = 1.0 / math.sqrt(HEAD_DIM)
    seq_all, place_all = seq_layout(token_order[0], lengths[0])
    first_row = lax.axis_index("ctx") * row_count
    seq_mine = lax.dynamic_slice_in_dim(seq_all, first_row, row_count)
    place_mine = lax.dynamic_slice_in_dim(place_all, first_row, row_count)
    same_seq = seq_mine[:, None] == seq_all[None, :]
    gathered = (
        lax.all_gather(w_query, ("ctx", "fsdp"), axis=0, tiled=True),
        lax.all_gather(w_key, ("ctx", "fsdp"), axis=0, tiled=True),
        lax.all_gather(w_value, ("ctx", "fsdp"), axis=0, tiled=True),
        lax.all_gather(w_out, ("ctx", "fsdp"), axis=0, tiled=True),
        lax.all_gather(w_router, ("ctx", "fsdp"), axis=0, tiled=True),
        lax.all_gather(attn_gain, ("ctx", "fsdp"), axis=0, tiled=True),
        lax.all_gather(ffn_gain, ("ctx", "fsdp"), axis=0, tiled=True),
        lax.all_gather(query_gain, ("ctx", "fsdp"), axis=0, tiled=True),
        lax.all_gather(key_gain, ("ctx", "fsdp"), axis=0, tiled=True),
    )
    (
        full_query,
        full_key,
        full_value,
        full_out,
        full_router,
        gain_attn,
        gain_ffn,
        gain_query,
        gain_key,
    ) = gathered
    gain_attn = gain_attn.astype(jnp.float32)
    gain_ffn = gain_ffn.astype(jnp.float32)
    gain_query = gain_query.astype(jnp.float32)
    gain_key = gain_key.astype(jnp.float32)
    h_one, norm_one_back = jax.vjp(rms_scaled, hidden_in, gain_attn)
    h_one_low = h_one.astype(jnp.bfloat16)
    query_raw = jnp.dot(h_one_low, full_query, preferred_element_type=jnp.float32)
    key_raw = jnp.dot(h_one_low, full_key, preferred_element_type=jnp.float32)
    values_low = jnp.dot(h_one_low, full_value, preferred_element_type=jnp.float32).astype(
        jnp.bfloat16
    )
    query_rot, query_back = jax.vjp(partial(qk_post, places=place_mine), query_raw, gain_query)
    key_rot, key_back = jax.vjp(partial(qk_post, places=place_mine), key_raw, gain_key)
    query_low = query_rot.astype(jnp.bfloat16)
    key_low = key_rot.astype(jnp.bfloat16)
    key_all, value_all = (
        lax.all_gather(key_low, "ctx", axis=0, tiled=True),
        lax.all_gather(values_low, "ctx", axis=0, tiled=True),
    )
    query_heads = query_low.reshape(row_count, head_count, HEAD_DIM)
    key_heads = key_all.reshape(-1, head_count, HEAD_DIM)
    value_heads = value_all.reshape(-1, head_count, HEAD_DIM)

    def scores_of():
        raw_scores = (
            jnp.einsum("thd,khd->htk", query_heads, key_heads, preferred_element_type=jnp.float32)
            * score_scale
        )
        return jnp.where(same_seq[None, :, :], raw_scores, masked_value)

    scores = scores_of()
    row_top = jnp.max(scores, axis=-1, keepdims=True)
    log_total = row_top + jnp.log(jnp.sum(jnp.exp(scores - row_top), axis=-1, keepdims=True))
    probs_low = jnp.exp(scores - log_total).astype(jnp.bfloat16)
    attended = jnp.einsum(
        "htk,khd->thd", probs_low, value_heads, preferred_element_type=jnp.float32
    )
    attended_low = attended.reshape(row_count, model_width).astype(jnp.bfloat16)
    middle = hidden_in + jnp.dot(attended_low, full_out, preferred_element_type=jnp.float32)
    h_two, norm_two_back = jax.vjp(rms_scaled, middle, gain_ffn)
    h_two_low = h_two.astype(jnp.bfloat16)
    logits = jnp.dot(h_two_low, full_router, preferred_element_type=jnp.float32)
    expert_count = full_router.shape[1]
    route_rows = routes[0]
    top_k = route_rows.shape[1]
    chosen = route_rows[:, :, None] == jnp.arange(expert_count, dtype=jnp.int32)[None, None, :]
    picked, route_back = jax.vjp(partial(route_weights, chosen=chosen), logits)
    pair_count = row_count * top_k
    capacity = 5 * row_count * top_k // (4 * expert_count)
    slot_count = expert_count * capacity
    group_size = lax.axis_size("fsdp")
    local_experts = w_gate.shape[0]
    pair_expert = route_rows.reshape(pair_count)
    one_hot = (pair_expert[:, None] == jnp.arange(expert_count, dtype=jnp.int32)[None, :]).astype(
        jnp.int32
    )
    slot_rank = jnp.sum(one_hot * (jnp.cumsum(one_hot, axis=0) - 1), axis=1)
    slot_ids = pair_expert * capacity + slot_rank
    source = (
        jnp.full((slot_count,), pair_count, jnp.int32)
        .at[slot_ids]
        .set(jnp.arange(pair_count, dtype=jnp.int32))
    )
    filled = source < pair_count
    source_pair = jnp.minimum(source, pair_count - 1)
    send_rows = jnp.where(
        filled[:, None], h_two_low[source_pair // top_k], jnp.zeros((), jnp.bfloat16)
    )
    send_rows = send_rows.reshape(group_size, local_experts, capacity, model_width)
    gate_full, up_full, down_full = (
        lax.all_gather(w_gate, "ctx", axis=1, tiled=True),
        lax.all_gather(w_up, "ctx", axis=1, tiled=True),
        lax.all_gather(w_down, "ctx", axis=1, tiled=True),
    )
    arrived_rows = lax.all_to_all(send_rows, "fsdp", split_axis=0, concat_axis=0, tiled=True)
    gate_part = jnp.einsum(
        "secd,edf->secf", arrived_rows, gate_full, preferred_element_type=jnp.float32
    )
    up_part = jnp.einsum(
        "secd,edf->secf", arrived_rows, up_full, preferred_element_type=jnp.float32
    )
    act_part = (jax.nn.silu(gate_part) * up_part).astype(jnp.bfloat16)
    result = jnp.einsum(
        "secf,efd->secd", act_part, down_full, preferred_element_type=jnp.float32
    ).astype(jnp.bfloat16)
    returned = lax.all_to_all(result, "fsdp", split_axis=0, concat_axis=0, tiled=True).reshape(
        slot_count, model_width
    )
    pair_out = returned[slot_ids].reshape(row_count, top_k, model_width)
    output = (middle + jnp.sum(picked[:, :, None] * pair_out, axis=1)).astype(jnp.bfloat16)
    grad_top = grad_output[0].astype(jnp.float32)
    grad_picked = jnp.sum(grad_top[:, None, :] * pair_out, axis=-1)
    grad_pair = (
        (picked[:, :, None] * grad_top[:, None, :])
        .astype(jnp.bfloat16)
        .reshape(pair_count, model_width)
    )
    grad_send = jnp.where(filled[:, None], grad_pair[source_pair], jnp.zeros((), jnp.bfloat16))
    grad_send = grad_send.reshape(group_size, local_experts, capacity, model_width)
    grad_arrived = lax.all_to_all(grad_send, "fsdp", split_axis=0, concat_axis=0, tiled=True)
    sigma = jax.nn.sigmoid(gate_part)
    act_low = (gate_part * sigma * up_part).astype(jnp.bfloat16)
    grad_act = jnp.einsum(
        "secd,efd->secf", grad_arrived, down_full, preferred_element_type=jnp.float32
    )
    grad_gate = (grad_act * up_part * sigma * (1.0 + gate_part * (1.0 - sigma))).astype(
        jnp.bfloat16
    )
    grad_up = (grad_act * gate_part * sigma).astype(jnp.bfloat16)
    grad_back = jnp.einsum(
        "secf,edf->secd", grad_gate, gate_full, preferred_element_type=jnp.float32
    )
    grad_back = (
        grad_back
        + jnp.einsum("secf,edf->secd", grad_up, up_full, preferred_element_type=jnp.float32)
    ).astype(jnp.bfloat16)
    grad_return = lax.all_to_all(
        grad_back, "fsdp", split_axis=0, concat_axis=0, tiled=True
    ).reshape(slot_count, model_width)
    grad_h_two = jnp.sum(
        grad_return[slot_ids].reshape(row_count, top_k, model_width).astype(jnp.float32), axis=1
    )
    (grad_logits,) = route_back(grad_picked)
    grad_logits_low = grad_logits.astype(jnp.bfloat16)
    grad_h_two = grad_h_two + jnp.einsum(
        "te,de->td", grad_logits_low, full_router, preferred_element_type=jnp.float32
    )
    grad_router = jnp.einsum(
        "td,te->de", h_two_low, grad_logits_low, preferred_element_type=jnp.float32
    )
    grad_middle, grad_ffn_gain = norm_two_back(grad_h_two)
    grad_middle = grad_middle + grad_top
    grad_branch = grad_middle.astype(jnp.bfloat16)
    grad_out_w = jnp.einsum(
        "td,te->de", attended_low, grad_branch, preferred_element_type=jnp.float32
    )
    grad_att = jnp.einsum(
        "te,de->td", grad_branch, full_out, preferred_element_type=jnp.float32
    ).astype(jnp.bfloat16)
    grad_att = grad_att.reshape(row_count, head_count, HEAD_DIM)
    scores = scores_of()
    probs_full = jnp.exp(scores - log_total)
    probs_again = probs_full.astype(jnp.bfloat16)
    grad_probs = jnp.einsum(
        "thd,khd->htk", grad_att, value_heads, preferred_element_type=jnp.float32
    )
    spread = jnp.sum(probs_full * grad_probs, axis=-1, keepdims=True)
    grad_scores = (probs_full * (grad_probs - spread)).astype(jnp.bfloat16)
    grad_query = (
        jnp.einsum(
            "htk,khd->thd", grad_scores, key_heads, preferred_element_type=jnp.float32
        ).reshape(row_count, model_width)
        * score_scale
    )
    grad_key_part = (
        jnp.einsum(
            "htk,thd->khd", grad_scores, query_heads, preferred_element_type=jnp.float32
        ).reshape(-1, model_width)
        * score_scale
    )
    grad_value_part = jnp.einsum(
        "htk,thd->khd", probs_again, grad_att, preferred_element_type=jnp.float32
    ).reshape(-1, model_width)
    grad_key, grad_value = (
        lax.psum_scatter(
            grad_key_part.astype(jnp.bfloat16), "ctx", scatter_dimension=0, tiled=True
        ).astype(jnp.float32),
        lax.psum_scatter(
            grad_value_part.astype(jnp.bfloat16), "ctx", scatter_dimension=0, tiled=True
        ).astype(jnp.float32),
    )
    grad_q_raw, grad_q_gain = query_back(grad_query)
    grad_k_raw, grad_k_gain = key_back(grad_key)
    grad_q_low = grad_q_raw.astype(jnp.bfloat16)
    grad_k_low = grad_k_raw.astype(jnp.bfloat16)
    grad_v_low = grad_value.astype(jnp.bfloat16)
    grad_query_w = jnp.einsum(
        "td,te->de", h_one_low, grad_q_low, preferred_element_type=jnp.float32
    )
    grad_key_w = jnp.einsum("td,te->de", h_one_low, grad_k_low, preferred_element_type=jnp.float32)
    grad_value_w = jnp.einsum(
        "td,te->de", h_one_low, grad_v_low, preferred_element_type=jnp.float32
    )
    grad_h_one = jnp.einsum("te,de->td", grad_q_low, full_query, preferred_element_type=jnp.float32)
    grad_h_one = grad_h_one + jnp.einsum(
        "te,de->td", grad_k_low, full_key, preferred_element_type=jnp.float32
    )
    grad_h_one = grad_h_one + jnp.einsum(
        "te,de->td", grad_v_low, full_value, preferred_element_type=jnp.float32
    )
    grad_input_norm, grad_attn_gain = norm_one_back(grad_h_one)
    grad_input = grad_middle + grad_input_norm
    totals = (
        lax.psum_scatter(grad_query_w, ("ctx", "fsdp"), scatter_dimension=0, tiled=True),
        lax.psum_scatter(grad_key_w, ("ctx", "fsdp"), scatter_dimension=0, tiled=True),
        lax.psum_scatter(grad_value_w, ("ctx", "fsdp"), scatter_dimension=0, tiled=True),
        lax.psum_scatter(grad_out_w, ("ctx", "fsdp"), scatter_dimension=0, tiled=True),
        lax.psum_scatter(grad_router, ("ctx", "fsdp"), scatter_dimension=0, tiled=True),
        lax.psum_scatter(grad_attn_gain, ("ctx", "fsdp"), scatter_dimension=0, tiled=True),
        lax.psum_scatter(grad_ffn_gain, ("ctx", "fsdp"), scatter_dimension=0, tiled=True),
        lax.psum_scatter(grad_q_gain, ("ctx", "fsdp"), scatter_dimension=0, tiled=True),
        lax.psum_scatter(grad_k_gain, ("ctx", "fsdp"), scatter_dimension=0, tiled=True),
    )
    grad_down_w = jnp.einsum(
        "secf,secd->efd", act_low, grad_arrived, preferred_element_type=jnp.float32
    )
    grad_gate_w = jnp.einsum(
        "secd,secf->edf", arrived_rows, grad_gate, preferred_element_type=jnp.float32
    )
    grad_up_w = jnp.einsum(
        "secd,secf->edf", arrived_rows, grad_up, preferred_element_type=jnp.float32
    )
    gate_grad, up_grad, down_grad = (
        lax.psum_scatter(
            grad_gate_w.astype(jnp.bfloat16), "ctx", scatter_dimension=1, tiled=True
        ).astype(jnp.float32),
        lax.psum_scatter(
            grad_up_w.astype(jnp.bfloat16), "ctx", scatter_dimension=1, tiled=True
        ).astype(jnp.float32),
        lax.psum_scatter(
            grad_down_w.astype(jnp.bfloat16), "ctx", scatter_dimension=1, tiled=True
        ).astype(jnp.float32),
    )
    return (
        output[None],
        grad_input[None],
        totals[0],
        totals[1],
        totals[2],
        totals[3],
        totals[4],
        totals[5],
        totals[6],
        totals[7],
        totals[8],
        gate_grad,
        up_grad,
        down_grad,
    )


def masked_probs(query, key, seq_rows, seq_cols, scale):
    scores = (
        lax.dot_general(query, key, (((1,), (1,)), ((), ())), preferred_element_type=jnp.float32)
        * scale
    )
    scores = jnp.where(seq_rows == seq_cols, scores, masked_value)
    top = jnp.max(scores, axis=-1, keepdims=True)
    weights = jnp.exp(scores - top)
    return weights / jnp.sum(weights, axis=-1, keepdims=True)


def attend_kernel(scale, seq_rows, seq_cols, query, key, value, out):
    probs = masked_probs(query[...], key[...], seq_rows[...], seq_cols[...], scale)
    out[...] = jnp.dot(
        probs.astype(jnp.bfloat16), value[...], preferred_element_type=jnp.float32
    ).astype(out.dtype)


def attend_back_kernel(
    scale, seq_rows, seq_cols, query, key, value, grad, grad_query, grad_key, grad_value
):
    @pl.when(pl.program_id(1) == 0)
    def _():
        grad_key[...] = jnp.zeros_like(grad_key)
        grad_value[...] = jnp.zeros_like(grad_value)

    probs = masked_probs(query[...], key[...], seq_rows[...], seq_cols[...], scale)
    grad_probs = lax.dot_general(
        grad[...], value[...], (((1,), (1,)), ((), ())), preferred_element_type=jnp.float32
    )
    spread = jnp.sum(probs * grad_probs, axis=-1, keepdims=True)
    grad_scores = (probs * (grad_probs - spread)).astype(jnp.bfloat16)
    grad_query[...] = (
        jnp.dot(grad_scores, key[...], preferred_element_type=jnp.float32) * scale
    )
    grad_key[...] += (
        lax.dot_general(
            grad_scores,
            query[...],
            (((0,), (0,)), ((), ())),
            preferred_element_type=jnp.float32,
        )
        * scale
    )
    grad_value[...] += lax.dot_general(
        probs.astype(jnp.bfloat16),
        grad[...],
        (((0,), (0,)), ((), ())),
        preferred_element_type=jnp.float32,
    )


def attention_specs(rows, block):
    per_block = pl.BlockSpec((block, HEAD_DIM), lambda h, i: (i, h))
    per_head = pl.BlockSpec((rows, HEAD_DIM), lambda h, i: (0, h))
    seqs = [
        pl.BlockSpec((block, 1), lambda h, i: (i, 0)),
        pl.BlockSpec((1, rows), lambda h, i: (0, 0)),
    ]
    return per_block, per_head, seqs


def attend(seq_ids, query, key, value):
    rows, width = query.shape
    block = math.gcd(rows, 256)
    per_block, per_head, seqs = attention_specs(rows, block)
    pairs = rows * rows * width
    return pl.pallas_call(
        partial(attend_kernel, 1.0 / math.sqrt(HEAD_DIM)),
        grid=(width // HEAD_DIM, rows // block),
        in_specs=seqs + [per_block, per_head, per_head],
        out_specs=per_block,
        out_shape=jax.ShapeDtypeStruct((rows, width), jnp.bfloat16),
        cost_estimate=pl.CostEstimate(
            flops=4 * pairs, bytes_accessed=8 * rows * width, transcendentals=pairs // HEAD_DIM
        ),
        compiler_params=pltpu.CompilerParams(vmem_limit_bytes=48 << 20),
        name="attend",
    )(seq_ids[:, None], seq_ids[None, :], query, key, value)


def attend_back(seq_ids, query, key, value, grad):
    rows, width = query.shape
    block = math.gcd(rows, 256)
    per_block, per_head, seqs = attention_specs(rows, block)
    pairs = rows * rows * width
    return pl.pallas_call(
        partial(attend_back_kernel, 1.0 / math.sqrt(HEAD_DIM)),
        grid=(width // HEAD_DIM, rows // block),
        in_specs=seqs + [per_block, per_head, per_head, per_block],
        out_specs=(per_block, per_head, per_head),
        out_shape=(jax.ShapeDtypeStruct((rows, width), jnp.float32),) * 3,
        cost_estimate=pl.CostEstimate(
            flops=10 * pairs, bytes_accessed=20 * rows * width, transcendentals=pairs // HEAD_DIM
        ),
        compiler_params=pltpu.CompilerParams(vmem_limit_bytes=48 << 20),
        name="attend_back",
    )(seq_ids[:, None], seq_ids[None, :], query, key, value, grad)


def dispatch_kernel(position, rows, out):
    columns, _, capacity, width = out.shape
    count = rows.shape[1]
    slots = lax.broadcasted_iota(jnp.int32, (columns, capacity, count), 1)
    select = jnp.where(slots == position[:, 0], 1.0, 0.0)
    select = select.reshape(columns * capacity, count).astype(jnp.bfloat16)
    step = math.gcd(width, 512)
    for at in range(0, width, step):
        part = jnp.dot(select, rows[0, :, at : at + step], preferred_element_type=jnp.float32)
        part = part.reshape(columns, capacity, step).astype(out.dtype)
        out[:, 0, :, at : at + step] = part


def dispatch(position, capacity, rows):
    columns, planes, count = position.shape
    width = rows.shape[1]
    return pl.pallas_call(
        dispatch_kernel,
        grid=(planes,),
        in_specs=[
            pl.BlockSpec((columns, 1, 1, count), lambda b: (0, b, 0, 0)),
            pl.BlockSpec((1, count, width), lambda b: (b, 0, 0)),
        ],
        out_specs=pl.BlockSpec((columns, 1, capacity, width), lambda b: (0, b, 0, 0)),
        out_shape=jax.ShapeDtypeStruct((columns, planes, capacity, width), jnp.bfloat16),
        cost_estimate=pl.CostEstimate(
            flops=2 * position.size * capacity * width,
            bytes_accessed=2 * columns * planes * capacity * width,
            transcendentals=0,
        ),
        compiler_params=pltpu.CompilerParams(vmem_limit_bytes=40 << 20),
        name="dispatch",
    )(position[:, :, None], rows.reshape(planes, count, width))


def heads_of(width):
    return [slice(at, at + HEAD_DIM) for at in range(0, width, HEAD_DIM)]


def turn_kernel(raw, scales, gains, cosine, sine, query, key, value):
    width = query.shape[1]
    for which, out in ((0, query), (1, key)):
        scale = scales[:, which : which + 1]
        for head in heads_of(width):
            part = raw[:, which * width + head.start : which * width + head.stop]
            part = part * scale * gains[which : which + 1, head]
            swapped = pltpu.roll(part, HEAD_DIM // 2, 1)
            out[:, head] = (part * cosine[...] + swapped * sine[...]).astype(out.dtype)
    value[...] = raw[:, 2 * width : 3 * width].astype(value.dtype)


def turn_back_kernel(
    raw, scales, gains, cosine, sine, grad_query, grad_key, out_query, out_key, dots, grad_gains
):
    @pl.when(pl.program_id(0) == 0)
    def _():
        grad_gains[...] = jnp.zeros_like(grad_gains)

    width = grad_query.shape[1]
    for which, grad, out in ((0, grad_query, out_query), (1, grad_key, out_key)):
        scale = scales[:, which : which + 1]
        total = jnp.zeros_like(scale)
        for head in heads_of(width):
            part = grad[:, head]
            part = part * cosine[...] - pltpu.roll(part, HEAD_DIM // 2, 1) * sine[...]
            hat = raw[:, which * width + head.start : which * width + head.stop] * scale
            grad_gains[which : which + 1, head] += jnp.sum(part * hat, axis=0, keepdims=True)
            part = part * gains[which : which + 1, head]
            total += jnp.sum(part * hat, axis=1, keepdims=True)
            out[:, head] = part
        dots[:, which : which + 1] = total


def turn_specs(raw, gains):
    block = math.gcd(raw.shape[0], 256)
    return block, [
        pl.BlockSpec((block, raw.shape[1]), lambda i: (i, 0)),
        pl.BlockSpec((block, 2), lambda i: (i, 0)),
        pl.BlockSpec(gains.shape, lambda i: (0, 0)),
        pl.BlockSpec((block, HEAD_DIM), lambda i: (i, 0)),
        pl.BlockSpec((block, HEAD_DIM), lambda i: (i, 0)),
    ]


def turn(raw, scales, gains, cosine, sine):
    rows, width = raw.shape[0], gains.shape[1]
    block, specs = turn_specs(raw, gains)
    return pl.pallas_call(
        turn_kernel,
        grid=(rows // block,),
        in_specs=specs,
        out_specs=(pl.BlockSpec((block, width), lambda i: (i, 0)),) * 3,
        out_shape=(jax.ShapeDtypeStruct((rows, width), jnp.bfloat16),) * 3,
        cost_estimate=pl.CostEstimate(
            flops=16 * rows * width, bytes_accessed=18 * rows * width, transcendentals=0
        ),
        compiler_params=pltpu.CompilerParams(vmem_limit_bytes=40 << 20),
        name="turn",
    )(raw, scales, gains, cosine, sine)


def turn_back(raw, scales, gains, cosine, sine, grad_query, grad_key):
    rows, width = grad_query.shape
    block, specs = turn_specs(raw, gains)
    wide = pl.BlockSpec((block, width), lambda i: (i, 0))
    f32 = jnp.float32
    return pl.pallas_call(
        turn_back_kernel,
        grid=(rows // block,),
        in_specs=specs + [wide, wide],
        out_specs=(
            wide,
            wide,
            pl.BlockSpec((block, 2), lambda i: (i, 0)),
            pl.BlockSpec((2, width), lambda i: (0, 0)),
        ),
        out_shape=(
            jax.ShapeDtypeStruct((rows, width), f32),
            jax.ShapeDtypeStruct((rows, width), f32),
            jax.ShapeDtypeStruct((rows, 2), f32),
            jax.ShapeDtypeStruct((2, width), f32),
        ),
        cost_estimate=pl.CostEstimate(
            flops=24 * rows * width, bytes_accessed=28 * rows * width, transcendentals=0
        ),
        compiler_params=pltpu.CompilerParams(vmem_limit_bytes=40 << 20),
        name="turn_back",
    )(raw, scales, gains, cosine, sine, grad_query, grad_key)


def expert_in_kernel(
    rows, gate, up, router, own, gate_out, up_out, act_out, picked_out
):
    logits = jnp.dot(rows[...], router[...], preferred_element_type=jnp.float32)
    weights = jnp.exp(logits - jnp.max(logits, axis=1, keepdims=True))
    picked = jnp.sum(weights * own[...], axis=1, keepdims=True)
    picked = picked / jnp.sum(weights, axis=1, keepdims=True)
    gate_pre = jnp.dot(rows[...], gate[...], preferred_element_type=jnp.float32)
    up_pre = jnp.dot(rows[...], up[...], preferred_element_type=jnp.float32)
    act = (gate_pre * jax.nn.sigmoid(gate_pre) * up_pre).astype(jnp.bfloat16)
    gate_out[...] = gate_pre
    up_out[...] = up_pre
    act_out[...] = (act.astype(jnp.float32) * picked).astype(jnp.bfloat16)
    picked_out[...] = picked


def expert_back_kernel(
    grad, gate_in, up_in, picked, gate, up, down, grad_gate, grad_up, grad_picked, grad_rows
):
    grad_raw = lax.dot_general(
        grad[...], down[...], (((1,), (1,)), ((), ())), preferred_element_type=jnp.float32
    )
    gate_pre, up_pre = gate_in[...], up_in[...]
    sigma = jax.nn.sigmoid(gate_pre)
    silu = gate_pre * sigma
    act = (silu * up_pre).astype(jnp.bfloat16).astype(jnp.float32)
    grad_picked[...] = jnp.sum(grad_raw * act, axis=1, keepdims=True)
    grad_act = grad_raw * picked[...]
    low_gate = (grad_act * up_pre * (sigma + silu * (1.0 - sigma))).astype(jnp.bfloat16)
    low_up = (grad_act * silu).astype(jnp.bfloat16)
    grad_gate[...] = low_gate
    grad_up[...] = low_up
    back = lax.dot_general(
        low_gate, gate[...], (((1,), (1,)), ((), ())), preferred_element_type=jnp.float32
    )
    back = back + lax.dot_general(
        low_up, up[...], (((1,), (1,)), ((), ())), preferred_element_type=jnp.float32
    )
    grad_rows[...] = back.astype(jnp.bfloat16)


def whole(shape):
    return pl.BlockSpec(shape, lambda i: (0, 0), pipeline_mode=pl.Buffered(1))


def row_blocks(block, width):
    return pl.BlockSpec((block, width), lambda i: (i, 0))


def expert_in(rows, gate, up, router, own, block):
    count, width = rows.shape
    hidden = gate.shape[1]
    narrow = row_blocks(block, hidden)
    f32 = jnp.float32
    return pl.pallas_call(
        expert_in_kernel,
        grid=(count // block,),
        in_specs=[
            row_blocks(block, width),
            whole(gate.shape),
            whole(up.shape),
            whole(router.shape),
            whole(own.shape),
        ],
        out_specs=(narrow, narrow, narrow, row_blocks(block, 1)),
        out_shape=(
            jax.ShapeDtypeStruct((count, hidden), f32),
            jax.ShapeDtypeStruct((count, hidden), f32),
            jax.ShapeDtypeStruct((count, hidden), jnp.bfloat16),
            jax.ShapeDtypeStruct((count, 1), f32),
        ),
        cost_estimate=pl.CostEstimate(
            flops=4 * count * width * hidden,
            bytes_accessed=2 * count * width + (10 * count + 4 * width) * hidden,
            transcendentals=count * hidden,
        ),
        compiler_params=pltpu.CompilerParams(vmem_limit_bytes=56 << 20),
        name="expert_in",
    )(rows, gate, up, router, own)


def expert_back(grad, gate_pre, up_pre, picked, gate, up, down, block):
    count, width = grad.shape
    hidden = down.shape[0]
    wide, narrow, one = [row_blocks(block, size) for size in (width, hidden, 1)]
    low = jax.ShapeDtypeStruct((count, hidden), jnp.bfloat16)
    return pl.pallas_call(
        expert_back_kernel,
        grid=(count // block,),
        in_specs=[wide, narrow, narrow, one, whole(gate.shape), whole(up.shape), whole(down.shape)],
        out_specs=(narrow, narrow, one, wide),
        out_shape=(
            low,
            low,
            jax.ShapeDtypeStruct((count, 1), jnp.float32),
            jax.ShapeDtypeStruct((count, width), jnp.bfloat16),
        ),
        cost_estimate=pl.CostEstimate(
            flops=6 * count * width * hidden,
            bytes_accessed=4 * count * width + (12 * count + 6 * width) * hidden,
            transcendentals=count * hidden,
        ),
        compiler_params=pltpu.CompilerParams(vmem_limit_bytes=58 << 20),
        name="expert_back",
    )(grad, gate_pre, up_pre, picked, gate, up, down)


def tie(array, *others):
    anywhere = pl.BlockSpec(memory_space=pl.ANY)
    return pl.pallas_call(
        lambda *refs: None,
        in_specs=[anywhere] * (1 + len(others)),
        out_specs=anywhere,
        out_shape=jax.ShapeDtypeStruct(array.shape, array.dtype),
        input_output_aliases={0: 0},
        name="tie",
    )(array, *others)


def mm(left, right):
    return jnp.dot(left, right, preferred_element_type=jnp.float32)


def mm_t(left, right):
    return lax.dot_general(
        left, right, (((1,), (1,)), ((), ())), preferred_element_type=jnp.float32
    )


def t_mm(left, right):
    return lax.dot_general(
        left, right, (((0,), (0,)), ((), ())), preferred_element_type=jnp.float32
    )


def plane_shards(
    hidden,
    token_order,
    lengths,
    routes,
    grad_output,
    w_query,
    w_key,
    w_value,
    w_out,
    w_router,
    attn_gain,
    ffn_gain,
    query_gain,
    key_gain,
    w_gate,
    w_up,
    w_down,
):
    f32, bf16 = jnp.float32, jnp.bfloat16
    both = ("ctx", "fsdp")
    planes = lax.axis_size("ctx")
    columns = lax.axis_size("fsdp")
    plane = lax.axis_index("ctx")
    row_count, width = hidden.shape[1:]
    group_rows = row_count * planes
    share = width // planes
    strip = w_query.shape[0]
    first_row = plane * row_count

    experts = w_router.shape[1]
    qkv = jnp.stack([w_query, w_key, w_value], axis=1).reshape(strip, 3, planes, share)
    qkv = qkv.transpose(2, 0, 1, 3).reshape(planes, strip, 3 * share)
    small = [w_router] + [g[:, None] for g in (attn_gain, ffn_gain, query_gain, key_gain)]
    small = jnp.concatenate(small + [routes.astype(bf16).reshape(strip, -1)], axis=1)
    spare = -small.shape[1] % 128
    small = jnp.pad(small, ((0, 0), (0, spare)))
    small = jnp.broadcast_to(small[None], (planes,) + small.shape)
    own_out = jnp.broadcast_to(w_out[None], (planes,) + w_out.shape)
    packed = jnp.concatenate([qkv, small, own_out], axis=2)
    packed = lax.all_to_all(packed, "ctx", 0, 0, tiled=True)
    hidden_all = lax.all_gather(tie(hidden[0], packed), "ctx", axis=0, tiled=True)
    packed, out_rows = packed[:, :, :-width], packed[:, :, -width:]
    routes_at = 3 * share + experts + 4
    routes_all = packed[:, :, routes_at : packed.shape[2] - spare].astype(jnp.int32)
    routes_all = routes_all.reshape(group_rows, -1)
    packed = jnp.broadcast_to(packed[None], (columns,) + packed.shape)
    packed = lax.all_to_all(packed, "fsdp", 0, 0, tiled=True)
    packed = packed.transpose(1, 0, 2, 3).reshape(width, -1)
    full_router = packed[:, 3 * share : 3 * share + experts]
    gain_attn, gain_ffn, gain_query, gain_key = [
        packed[:, 3 * share + experts + i].astype(f32) for i in range(4)
    ]
    def swap(part, step):
        return lax.ppermute(part, "ctx", [(i, i ^ step) for i in range(planes)])

    def by_plane(came):
        came = jnp.stack(came)
        return [came[plane ^ i] for i in range(planes)]

    def exchange(parts, first=None, last=None):
        came = [parts[plane]]
        for step in range(1, planes):
            part = parts[plane ^ step]
            part = swap(part if first is None else tie(part, first), step)
            came.append(part if last is None else tie(part, last))
        return by_plane(came)

    def exchange_after(parts, earlier):
        came = [
            swap(part if before is None else tie(part, before), step)
            for step, before in enumerate(earlier, 1)
            for part in [parts[plane ^ step]]
        ]
        return came, jnp.stack(by_plane([parts[plane]] + came)).astype(f32)

    def plane_sum(part):
        return part + sum(swap(part, step) for step in range(1, planes))

    out_rows = jnp.broadcast_to(out_rows[None], (columns,) + out_rows.shape)
    grad_all = lax.all_gather(
        tie(grad_output[0], hidden_all, packed, out_rows), "ctx", axis=0, tiled=True
    )
    full_out = lax.all_to_all(out_rows, "fsdp", 0, 0, tiled=True)

    seq_ids, places = seq_layout(token_order[0], lengths[0])
    experts_here = w_gate.shape[0]
    column_expert = experts_here * jnp.arange(columns, dtype=jnp.int32) + plane
    named = jnp.any(routes_all[:, :, None] == column_expert[None, None, :], axis=1)
    named = named.reshape(planes, row_count, columns)
    capacity = 5 * row_count * routes.shape[2] // (4 * experts)
    rank = jnp.cumsum(named.astype(jnp.int32), axis=1) - 1
    position = jnp.where(named, rank, -1).transpose(2, 0, 1)
    slots = jnp.arange(capacity, dtype=jnp.int32)
    holds = position[:, :, None, :] == slots[None, None, :, None]
    select = holds.astype(bf16)

    def combine(rows):
        rows = rows.reshape(columns, planes, capacity, width)
        sums = jnp.einsum("fbsr,fbsd->brd", select, rows, preferred_element_type=f32)
        return sums.reshape(group_rows, width).astype(bf16)


    frequency = rope_base ** (
        -2.0 * jnp.arange(HEAD_DIM // 2).astype(f32) / HEAD_DIM
    )
    angles = places.astype(f32)[:, None] * frequency[None, :]
    cosine, sine = jnp.cos(angles), jnp.sin(angles)
    cosine = jnp.concatenate([cosine, cosine], axis=1)
    sine = jnp.concatenate([-sine, sine], axis=1)
    hidden_wide = hidden_all.astype(f32)
    scale_one = lax.rsqrt(jnp.mean(hidden_wide * hidden_wide, axis=-1, keepdims=True) + epsilon)
    h_one = (hidden_wide * scale_one * gain_attn).astype(bf16)
    raw = mm(h_one, packed)
    squares = jnp.stack(
        [jnp.sum(raw[:, :share] ** 2, axis=1), jnp.sum(raw[:, share : 2 * share] ** 2, axis=1)]
    )
    squares = plane_sum(squares)
    scales = lax.rsqrt(squares / width + epsilon).T
    gains = lax.dynamic_slice_in_dim(
        jnp.stack([gain_query, gain_key]), plane * share, share, axis=1
    )
    query, key, values = turn(raw, scales, gains, cosine, sine)
    attended = attend(seq_ids, query, key, values)
    full_out = tie(full_out, attended).transpose(1, 0, 2, 3).reshape(width, width)
    grad_send = dispatch(position, capacity, tie(grad_all, attended, full_out))
    attended = attended.reshape(planes, row_count, share)
    attended = jnp.concatenate(exchange(attended, grad_all), axis=1)
    grad_in = lax.all_to_all(grad_send, "fsdp", 0, 0, tiled=True).reshape(-1, width)
    middle = hidden[0].astype(f32) + mm(attended, full_out)
    scale_two = lax.rsqrt(jnp.mean(middle * middle, axis=-1, keepdims=True) + epsilon)
    middle_hat = middle * scale_two
    h_two = (middle_hat * gain_ffn).astype(bf16)

    h_two_all = lax.all_gather(tie(h_two, grad_send), "ctx", axis=0, tiled=True)
    came = [swap(tie(w_gate[plane ^ step], h_two_all), step) for step in range(1, planes)]
    gate = jnp.concatenate(by_plane([w_gate[plane]] + came))
    h_all = tie(h_two_all, grad_in, came[0])
    up = jnp.concatenate(exchange(w_up, h_two_all))
    probs = jax.nn.softmax(mm(h_two, full_router), axis=-1)
    rows_in = lax.all_to_all(dispatch(position, capacity, h_all), "fsdp", 0, 0, tiled=True)
    rows_in = rows_in.reshape(-1, width)
    own = experts_here * lax.axis_index("fsdp") + plane
    own = (jnp.arange(experts)[None, :] == own).astype(f32)
    slot_block = planes * capacity
    gate_pre, up_pre, act_picked, picked = expert_in(
        rows_in, gate, up, full_router, own, slot_block
    )
    down = jnp.concatenate(exchange(w_down, h_two_all, act_picked))
    grad_down_w = t_mm(act_picked, grad_in).astype(bf16)
    grad_gate, grad_up, grad_picked, grad_rows = expert_back(
        grad_in, tie(gate_pre, grad_down_w), up_pre, picked, gate, up, down, slot_block
    )

    def blocks(matrix):
        return matrix.reshape(planes, matrix.shape[0] // planes, matrix.shape[1])

    came, down_grad = exchange_after(blocks(grad_down_w), [None] * (planes - 1))
    grad_rows = tie(grad_rows, *came)
    grad_rows = lax.all_to_all(
        grad_rows.reshape(columns, planes * capacity, width), "fsdp", 0, 0, tiled=True
    )
    grad_gate_w = t_mm(rows_in, grad_gate).astype(bf16)
    grad_up_w = t_mm(rows_in, grad_up).astype(bf16)
    came, up_grad = exchange_after(blocks(grad_up_w), came)
    came, gate_grad = exchange_after(blocks(grad_gate_w), came)
    expert_out = mm(act_picked, down).astype(bf16)
    grad_picked = lax.all_to_all(
        tie(grad_picked, grad_rows).reshape(columns, planes, capacity), "fsdp", 0, 0, tiled=True
    )
    grad_rows = tie(grad_rows, *came, expert_out, grad_picked)
    expert_out = lax.all_to_all(
        expert_out.reshape(columns, planes * capacity, width), "fsdp", 0, 0, tiled=True
    )
    grad_h_two = lax.psum_scatter(
        combine(grad_rows), "ctx", scatter_dimension=0, tiled=True
    ).astype(f32)

    u_plane = jnp.sum(jnp.where(holds, grad_picked[..., None], 0.0), axis=2)
    u_mine = exchange(u_plane.transpose(1, 0, 2))
    u_mine = jnp.stack(u_mine, axis=1).reshape(experts, row_count).T
    grad_logits = probs * (u_mine - jnp.sum(probs * u_mine, axis=-1, keepdims=True))
    grad_logits = grad_logits.astype(bf16)
    grad_h_two = grad_h_two + mm_t(grad_logits, full_router)
    grad_router = t_mm(h_two, grad_logits)

    grad_top = grad_output[0].astype(f32)
    grad_ffn_gain = jnp.sum(grad_h_two * middle_hat, axis=0)
    grad_hat = grad_h_two * gain_ffn
    grad_middle = grad_top + scale_two * (
        grad_hat - middle_hat * jnp.mean(grad_hat * middle_hat, axis=-1, keepdims=True)
    )
    grad_branch = grad_middle.astype(bf16)
    def grad_heads(where):
        rows = lax.dynamic_slice_in_dim(full_out, where * share, share)
        return mm_t(grad_branch, rows).astype(bf16)

    came = [swap(grad_heads(plane ^ step), step) for step in range(1, planes)]
    grad_att = jnp.concatenate(by_plane([grad_heads(plane)] + came))
    grad_out_w = t_mm(attended, grad_branch).astype(bf16)
    grad_out_w = grad_out_w.reshape(planes, columns, strip, width).transpose(1, 0, 2, 3)
    mixed_part = combine(tie(expert_out, grad_att, grad_out_w))
    mixed = lax.psum_scatter(mixed_part, "ctx", scatter_dimension=0, tiled=True)
    output = (middle + mixed.astype(f32)).astype(bf16)
    grad_out_w = lax.all_to_all(
        tie(grad_out_w, mixed_part), "fsdp", 0, 0, tiled=True
    )
    grad_att = tie(grad_att, mixed_part)
    grad_query, grad_key, grad_value = attend_back(seq_ids, query, key, values, grad_att)
    grad_query, grad_key, dots, grad_gains = turn_back(
        raw, scales, gains, cosine, sine, grad_query, grad_key
    )
    dots = plane_sum(dots.T).T * (scales * scales) / width
    grad_qkv = jnp.concatenate(
        [
            scales[:, :1] * grad_query - raw[:, :share] * (scales[:, :1] * dots[:, :1]),
            scales[:, 1:] * grad_key - raw[:, share : 2 * share] * (scales[:, 1:] * dots[:, 1:]),
            grad_value,
        ],
        axis=1,
    ).astype(bf16)
    grad_part = mm_t(grad_qkv, packed[:, : 3 * share])
    grad_h_one = lax.psum_scatter(
        tie(grad_part.astype(bf16), mixed, grad_out_w), "ctx", scatter_dimension=0, tiled=True
    ).astype(f32)
    grad_attn_gain = jnp.sum(grad_part * (hidden_wide * scale_one), axis=0)
    rows_of = jnp.arange(planes)[:, None] == plane
    gains = [jnp.where(rows_of, g[None], 0.0).reshape(width) for g in grad_gains]
    gains = [g[:, None] for g in [grad_attn_gain, grad_ffn_gain] + gains]
    small = jnp.concatenate([grad_router] + gains, axis=1).reshape(planes * columns, -1)
    small = lax.all_to_all(small, both, 0, 0, tiled=True)
    sums = t_mm(h_one, grad_qkv).astype(bf16)
    sums = sums.reshape(planes, columns, strip, -1).transpose(1, 0, 2, 3)
    sums = lax.all_to_all(tie(sums, small), "fsdp", 0, 0, tiled=True)
    grad_out_w = jnp.sum(grad_out_w.astype(f32), axis=0).astype(bf16)
    small = jnp.sum(small, axis=0).reshape(strip, -1)
    came = [swap(grad_out_w[plane ^ step], step) for step in range(1, planes)]
    grad_out_w = sum(x.astype(f32) for x in [grad_out_w[plane]] + came)
    sums = jnp.sum(sums.astype(f32), axis=0).astype(bf16)
    sums = lax.all_to_all(tie(sums, *came), "ctx", 0, 0, tiled=True)
    grad_qkv_w = sums.reshape(planes, strip, 3, share).transpose(2, 1, 0, 3)
    grad_qkv_w = grad_qkv_w.reshape(3, strip, width).astype(f32)

    x_hat = hidden[0].astype(f32)
    scale_mine = lax.rsqrt(jnp.mean(x_hat * x_hat, axis=-1, keepdims=True) + epsilon)
    x_hat = x_hat * scale_mine
    grad_hat = grad_h_one * gain_attn
    grad_input = grad_middle + scale_mine * (
        grad_hat - x_hat * jnp.mean(grad_hat * x_hat, axis=-1, keepdims=True)
    )

    return (
        output[None],
        grad_input[None],
        grad_qkv_w[0],
        grad_qkv_w[1],
        grad_qkv_w[2],
        grad_out_w,
        small[:, :experts],
        small[:, experts],
        small[:, experts + 1],
        small[:, experts + 2],
        small[:, experts + 3],
        gate_grad,
        up_grad,
        down_grad,
    )


def solution(mesh):
    placed = (
        P("fsdp", "ctx", None),
        P("fsdp", None),
        P("fsdp", None),
        P("fsdp", "ctx", None),
        P("fsdp", "ctx", None),
        P(("ctx", "fsdp"), None),
        P(("ctx", "fsdp"), None),
        P(("ctx", "fsdp"), None),
        P(("ctx", "fsdp"), None),
        P(("ctx", "fsdp"), None),
        P(("ctx", "fsdp")),
        P(("ctx", "fsdp")),
        P(("ctx", "fsdp")),
        P(("ctx", "fsdp")),
        P("fsdp", "ctx", None),
        P("fsdp", "ctx", None),
        P("fsdp", "ctx", None),
    )

    def shards(*operands):
        experts_here = operands[14].shape[0]
        heads = operands[0].shape[2] // HEAD_DIM
        planes = mesh.shape["ctx"]
        whole_experts = experts_here == planes and heads % planes == 0 and planes in (2, 4)
        return (plane_shards if whole_experts else general_shards)(*operands)

    return jax.shard_map(
        shards,
        mesh=mesh,
        in_specs=placed,
        out_specs=(
            P("fsdp", "ctx", None),
            P("fsdp", "ctx", None),
            P(("ctx", "fsdp"), None),
            P(("ctx", "fsdp"), None),
            P(("ctx", "fsdp"), None),
            P(("ctx", "fsdp"), None),
            P(("ctx", "fsdp"), None),
            P(("ctx", "fsdp")),
            P(("ctx", "fsdp")),
            P(("ctx", "fsdp")),
            P(("ctx", "fsdp")),
            P("fsdp", "ctx", None),
            P("fsdp", "ctx", None),
            P("fsdp", "ctx", None),
        ),
        check_vma=False,
    )
```

```python
from functools import partial
import math

import jax
import jax.numpy as jnp
from jax import lax
from jax.experimental import pallas as pl
from jax.experimental.pallas import tpu as pltpu
from jax.sharding import PartitionSpec as P

HEAD_DIM = 128


epsilon = 1e-06
rope_base = 10000.0
masked_value = -1e30


def rms_scaled(values, gain):
    return values * lax.rsqrt(jnp.mean(values * values, axis=-1, keepdims=True) + epsilon) * gain


def rotate(values, places):
    row_count = values.shape[0]
    head_count = values.shape[1] // HEAD_DIM
    half_width = HEAD_DIM // 2
    frequency = rope_base ** (-2.0 * jnp.arange(half_width).astype(jnp.float32) / HEAD_DIM)
    angles = places.astype(jnp.float32)[:, None] * frequency[None, :]
    cosine = jnp.cos(angles)[:, None, :]
    sine_part = jnp.sin(angles)[:, None, :]
    split_heads = values.reshape(row_count, head_count, HEAD_DIM)
    first_half = split_heads[:, :, :half_width]
    second_half = split_heads[:, :, half_width:]
    turned = jnp.concatenate(
        [
            first_half * cosine - second_half * sine_part,
            second_half * cosine + first_half * sine_part,
        ],
        axis=-1,
    )
    return turned.reshape(row_count, head_count * HEAD_DIM)


def qk_post(values, gain, places):
    return rotate(rms_scaled(values, gain), places)


def route_weights(logits, chosen):
    router_probs = jax.nn.softmax(logits, axis=-1)
    return jnp.sum(jnp.where(chosen, router_probs[:, None, :], 0.0), axis=-1)


def seq_layout(order_row, seq_lengths):
    seq_ends = jnp.cumsum(seq_lengths)
    seq_ids = jnp.sum((order_row[:, None] >= seq_ends[None, :]).astype(jnp.int32), axis=1)
    starts = seq_ends - seq_lengths
    chosen = seq_ids[:, None] == jnp.arange(seq_lengths.shape[0], dtype=jnp.int32)[None, :]
    seq_start = jnp.sum(jnp.where(chosen, starts[None, :], 0), axis=1)
    return (seq_ids, order_row - seq_start)


def general_shards(
    hidden,
    token_order,
    lengths,
    routes,
    grad_output,
    w_query,
    w_key,
    w_value,
    w_out,
    w_router,
    attn_gain,
    ffn_gain,
    query_gain,
    key_gain,
    w_gate,
    w_up,
    w_down,
):
    hidden_in = hidden[0].astype(jnp.float32)
    row_count = hidden_in.shape[0]
    model_width = hidden_in.shape[1]
    head_count = model_width // HEAD_DIM
    score_scale = 1.0 / math.sqrt(HEAD_DIM)
    seq_all, place_all = seq_layout(token_order[0], lengths[0])
    first_row = lax.axis_index("ctx") * row_count
    seq_mine = lax.dynamic_slice_in_dim(seq_all, first_row, row_count)
    place_mine = lax.dynamic_slice_in_dim(place_all, first_row, row_count)
    same_seq = seq_mine[:, None] == seq_all[None, :]
    gathered = (
        lax.all_gather(w_query, ("ctx", "fsdp"), axis=0, tiled=True),
        lax.all_gather(w_key, ("ctx", "fsdp"), axis=0, tiled=True),
        lax.all_gather(w_value, ("ctx", "fsdp"), axis=0, tiled=True),
        lax.all_gather(w_out, ("ctx", "fsdp"), axis=0, tiled=True),
        lax.all_gather(w_router, ("ctx", "fsdp"), axis=0, tiled=True),
        lax.all_gather(attn_gain, ("ctx", "fsdp"), axis=0, tiled=True),
        lax.all_gather(ffn_gain, ("ctx", "fsdp"), axis=0, tiled=True),
        lax.all_gather(query_gain, ("ctx", "fsdp"), axis=0, tiled=True),
        lax.all_gather(key_gain, ("ctx", "fsdp"), axis=0, tiled=True),
    )
    (
        full_query,
        full_key,
        full_value,
        full_out,
        full_router,
        gain_attn,
        gain_ffn,
        gain_query,
        gain_key,
    ) = gathered
    gain_attn = gain_attn.astype(jnp.float32)
    gain_ffn = gain_ffn.astype(jnp.float32)
    gain_query = gain_query.astype(jnp.float32)
    gain_key = gain_key.astype(jnp.float32)
    h_one, norm_one_back = jax.vjp(rms_scaled, hidden_in, gain_attn)
    h_one_low = h_one.astype(jnp.bfloat16)
    query_raw = jnp.dot(h_one_low, full_query, preferred_element_type=jnp.float32)
    key_raw = jnp.dot(h_one_low, full_key, preferred_element_type=jnp.float32)
    values_low = jnp.dot(h_one_low, full_value, preferred_element_type=jnp.float32).astype(
        jnp.bfloat16
    )
    query_rot, query_back = jax.vjp(partial(qk_post, places=place_mine), query_raw, gain_query)
    key_rot, key_back = jax.vjp(partial(qk_post, places=place_mine), key_raw, gain_key)
    query_low = query_rot.astype(jnp.bfloat16)
    key_low = key_rot.astype(jnp.bfloat16)
    key_all, value_all = (
        lax.all_gather(key_low, "ctx", axis=0, tiled=True),
        lax.all_gather(values_low, "ctx", axis=0, tiled=True),
    )
    query_heads = query_low.reshape(row_count, head_count, HEAD_DIM)
    key_heads = key_all.reshape(-1, head_count, HEAD_DIM)
    value_heads = value_all.reshape(-1, head_count, HEAD_DIM)

    def scores_of():
        raw_scores = (
            jnp.einsum("thd,khd->htk", query_heads, key_heads, preferred_element_type=jnp.float32)
            * score_scale
        )
        return jnp.where(same_seq[None, :, :], raw_scores, masked_value)

    scores = scores_of()
    row_top = jnp.max(scores, axis=-1, keepdims=True)
    log_total = row_top + jnp.log(jnp.sum(jnp.exp(scores - row_top), axis=-1, keepdims=True))
    probs_low = jnp.exp(scores - log_total).astype(jnp.bfloat16)
    attended = jnp.einsum(
        "htk,khd->thd", probs_low, value_heads, preferred_element_type=jnp.float32
    )
    attended_low = attended.reshape(row_count, model_width).astype(jnp.bfloat16)
    middle = hidden_in + jnp.dot(attended_low, full_out, preferred_element_type=jnp.float32)
    h_two, norm_two_back = jax.vjp(rms_scaled, middle, gain_ffn)
    h_two_low = h_two.astype(jnp.bfloat16)
    logits = jnp.dot(h_two_low, full_router, preferred_element_type=jnp.float32)
    expert_count = full_router.shape[1]
    route_rows = routes[0]
    top_k = route_rows.shape[1]
    chosen = route_rows[:, :, None] == jnp.arange(expert_count, dtype=jnp.int32)[None, None, :]
    picked, route_back = jax.vjp(partial(route_weights, chosen=chosen), logits)
    pair_count = row_count * top_k
    capacity = 5 * row_count * top_k // (4 * expert_count)
    slot_count = expert_count * capacity
    group_size = lax.axis_size("fsdp")
    local_experts = w_gate.shape[0]
    pair_expert = route_rows.reshape(pair_count)
    one_hot = (pair_expert[:, None] == jnp.arange(expert_count, dtype=jnp.int32)[None, :]).astype(
        jnp.int32
    )
    slot_rank = jnp.sum(one_hot * (jnp.cumsum(one_hot, axis=0) - 1), axis=1)
    slot_ids = pair_expert * capacity + slot_rank
    source = (
        jnp.full((slot_count,), pair_count, jnp.int32)
        .at[slot_ids]
        .set(jnp.arange(pair_count, dtype=jnp.int32))
    )
    filled = source < pair_count
    source_pair = jnp.minimum(source, pair_count - 1)
    send_rows = jnp.where(
        filled[:, None], h_two_low[source_pair // top_k], jnp.zeros((), jnp.bfloat16)
    )
    send_rows = send_rows.reshape(group_size, local_experts, capacity, model_width)
    gate_full, up_full, down_full = (
        lax.all_gather(w_gate, "ctx", axis=1, tiled=True),
        lax.all_gather(w_up, "ctx", axis=1, tiled=True),
        lax.all_gather(w_down, "ctx", axis=1, tiled=True),
    )
    arrived_rows = lax.all_to_all(send_rows, "fsdp", split_axis=0, concat_axis=0, tiled=True)
    gate_part = jnp.einsum(
        "secd,edf->secf", arrived_rows, gate_full, preferred_element_type=jnp.float32
    )
    up_part = jnp.einsum(
        "secd,edf->secf", arrived_rows, up_full, preferred_element_type=jnp.float32
    )
    act_part = (jax.nn.silu(gate_part) * up_part).astype(jnp.bfloat16)
    result = jnp.einsum(
        "secf,efd->secd", act_part, down_full, preferred_element_type=jnp.float32
    ).astype(jnp.bfloat16)
    returned = lax.all_to_all(result, "fsdp", split_axis=0, concat_axis=0, tiled=True).reshape(
        slot_count, model_width
    )
    pair_out = returned[slot_ids].reshape(row_count, top_k, model_width)
    output = (middle + jnp.sum(picked[:, :, None] * pair_out, axis=1)).astype(jnp.bfloat16)
    grad_top = grad_output[0].astype(jnp.float32)
    grad_picked = jnp.sum(grad_top[:, None, :] * pair_out, axis=-1)
    grad_pair = (
        (picked[:, :, None] * grad_top[:, None, :])
        .astype(jnp.bfloat16)
        .reshape(pair_count, model_width)
    )
    grad_send = jnp.where(filled[:, None], grad_pair[source_pair], jnp.zeros((), jnp.bfloat16))
    grad_send = grad_send.reshape(group_size, local_experts, capacity, model_width)
    grad_arrived = lax.all_to_all(grad_send, "fsdp", split_axis=0, concat_axis=0, tiled=True)
    sigma = jax.nn.sigmoid(gate_part)
    act_low = (gate_part * sigma * up_part).astype(jnp.bfloat16)
    grad_act = jnp.einsum(
        "secd,efd->secf", grad_arrived, down_full, preferred_element_type=jnp.float32
    )
    grad_gate = (grad_act * up_part * sigma * (1.0 + gate_part * (1.0 - sigma))).astype(
        jnp.bfloat16
    )
    grad_up = (grad_act * gate_part * sigma).astype(jnp.bfloat16)
    grad_back = jnp.einsum(
        "secf,edf->secd", grad_gate, gate_full, preferred_element_type=jnp.float32
    )
    grad_back = (
        grad_back
        + jnp.einsum("secf,edf->secd", grad_up, up_full, preferred_element_type=jnp.float32)
    ).astype(jnp.bfloat16)
    grad_return = lax.all_to_all(
        grad_back, "fsdp", split_axis=0, concat_axis=0, tiled=True
    ).reshape(slot_count, model_width)
    grad_h_two = jnp.sum(
        grad_return[slot_ids].reshape(row_count, top_k, model_width).astype(jnp.float32), axis=1
    )
    (grad_logits,) = route_back(grad_picked)
    grad_logits_low = grad_logits.astype(jnp.bfloat16)
    grad_h_two = grad_h_two + jnp.einsum(
        "te,de->td", grad_logits_low, full_router, preferred_element_type=jnp.float32
    )
    grad_router = jnp.einsum(
        "td,te->de", h_two_low, grad_logits_low, preferred_element_type=jnp.float32
    )
    grad_middle, grad_ffn_gain = norm_two_back(grad_h_two)
    grad_middle = grad_middle + grad_top
    grad_branch = grad_middle.astype(jnp.bfloat16)
    grad_out_w = jnp.einsum(
        "td,te->de", attended_low, grad_branch, preferred_element_type=jnp.float32
    )
    grad_att = jnp.einsum(
        "te,de->td", grad_branch, full_out, preferred_element_type=jnp.float32
    ).astype(jnp.bfloat16)
    grad_att = grad_att.reshape(row_count, head_count, HEAD_DIM)
    scores = scores_of()
    probs_full = jnp.exp(scores - log_total)
    probs_again = probs_full.astype(jnp.bfloat16)
    grad_probs = jnp.einsum(
        "thd,khd->htk", grad_att, value_heads, preferred_element_type=jnp.float32
    )
    spread = jnp.sum(probs_full * grad_probs, axis=-1, keepdims=True)
    grad_scores = (probs_full * (grad_probs - spread)).astype(jnp.bfloat16)
    grad_query = (
        jnp.einsum(
            "htk,khd->thd", grad_scores, key_heads, preferred_element_type=jnp.float32
        ).reshape(row_count, model_width)
        * score_scale
    )
    grad_key_part = (
        jnp.einsum(
            "htk,thd->khd", grad_scores, query_heads, preferred_element_type=jnp.float32
        ).reshape(-1, model_width)
        * score_scale
    )
    grad_value_part = jnp.einsum(
        "htk,thd->khd", probs_again, grad_att, preferred_element_type=jnp.float32
    ).reshape(-1, model_width)
    grad_key, grad_value = (
        lax.psum_scatter(
            grad_key_part.astype(jnp.bfloat16), "ctx", scatter_dimension=0, tiled=True
        ).astype(jnp.float32),
        lax.psum_scatter(
            grad_value_part.astype(jnp.bfloat16), "ctx", scatter_dimension=0, tiled=True
        ).astype(jnp.float32),
    )
    grad_q_raw, grad_q_gain = query_back(grad_query)
    grad_k_raw, grad_k_gain = key_back(grad_key)
    grad_q_low = grad_q_raw.astype(jnp.bfloat16)
    grad_k_low = grad_k_raw.astype(jnp.bfloat16)
    grad_v_low = grad_value.astype(jnp.bfloat16)
    grad_query_w = jnp.einsum(
        "td,te->de", h_one_low, grad_q_low, preferred_element_type=jnp.float32
    )
    grad_key_w = jnp.einsum("td,te->de", h_one_low, grad_k_low, preferred_element_type=jnp.float32)
    grad_value_w = jnp.einsum(
        "td,te->de", h_one_low, grad_v_low, preferred_element_type=jnp.float32
    )
    grad_h_one = jnp.einsum("te,de->td", grad_q_low, full_query, preferred_element_type=jnp.float32)
    grad_h_one = grad_h_one + jnp.einsum(
        "te,de->td", grad_k_low, full_key, preferred_element_type=jnp.float32
    )
    grad_h_one = grad_h_one + jnp.einsum(
        "te,de->td", grad_v_low, full_value, preferred_element_type=jnp.float32
    )
    grad_input_norm, grad_attn_gain = norm_one_back(grad_h_one)
    grad_input = grad_middle + grad_input_norm
    totals = (
        lax.psum_scatter(grad_query_w, ("ctx", "fsdp"), scatter_dimension=0, tiled=True),
        lax.psum_scatter(grad_key_w, ("ctx", "fsdp"), scatter_dimension=0, tiled=True),
        lax.psum_scatter(grad_value_w, ("ctx", "fsdp"), scatter_dimension=0, tiled=True),
        lax.psum_scatter(grad_out_w, ("ctx", "fsdp"), scatter_dimension=0, tiled=True),
        lax.psum_scatter(grad_router, ("ctx", "fsdp"), scatter_dimension=0, tiled=True),
        lax.psum_scatter(grad_attn_gain, ("ctx", "fsdp"), scatter_dimension=0, tiled=True),
        lax.psum_scatter(grad_ffn_gain, ("ctx", "fsdp"), scatter_dimension=0, tiled=True),
        lax.psum_scatter(grad_q_gain, ("ctx", "fsdp"), scatter_dimension=0, tiled=True),
        lax.psum_scatter(grad_k_gain, ("ctx", "fsdp"), scatter_dimension=0, tiled=True),
    )
    grad_down_w = jnp.einsum(
        "secf,secd->efd", act_low, grad_arrived, preferred_element_type=jnp.float32
    )
    grad_gate_w = jnp.einsum(
        "secd,secf->edf", arrived_rows, grad_gate, preferred_element_type=jnp.float32
    )
    grad_up_w = jnp.einsum(
        "secd,secf->edf", arrived_rows, grad_up, preferred_element_type=jnp.float32
    )
    gate_grad, up_grad, down_grad = (
        lax.psum_scatter(
            grad_gate_w.astype(jnp.bfloat16), "ctx", scatter_dimension=1, tiled=True
        ).astype(jnp.float32),
        lax.psum_scatter(
            grad_up_w.astype(jnp.bfloat16), "ctx", scatter_dimension=1, tiled=True
        ).astype(jnp.float32),
        lax.psum_scatter(
            grad_down_w.astype(jnp.bfloat16), "ctx", scatter_dimension=1, tiled=True
        ).astype(jnp.float32),
    )
    return (
        output[None],
        grad_input[None],
        totals[0],
        totals[1],
        totals[2],
        totals[3],
        totals[4],
        totals[5],
        totals[6],
        totals[7],
        totals[8],
        gate_grad,
        up_grad,
        down_grad,
    )


def masked_probs(query, key, seq_rows, seq_cols, scale):
    scores = (
        lax.dot_general(query, key, (((1,), (1,)), ((), ())), preferred_element_type=jnp.float32)
        * scale
    )
    scores = jnp.where(seq_rows == seq_cols, scores, masked_value)
    top = jnp.max(scores, axis=-1, keepdims=True)
    weights = jnp.exp(scores - top)
    return weights / jnp.sum(weights, axis=-1, keepdims=True)


def attend_kernel(scale, seq_rows, seq_cols, query, key, value, out):
    probs = masked_probs(query[...], key[...], seq_rows[...], seq_cols[...], scale)
    out[...] = jnp.dot(
        probs.astype(jnp.bfloat16), value[...], preferred_element_type=jnp.float32
    ).astype(out.dtype)


def attend_back_kernel(
    scale, seq_rows, seq_cols, query, key, value, grad, grad_query, grad_key, grad_value
):
    @pl.when(pl.program_id(1) == 0)
    def _():
        grad_key[...] = jnp.zeros_like(grad_key)
        grad_value[...] = jnp.zeros_like(grad_value)

    probs = masked_probs(query[...], key[...], seq_rows[...], seq_cols[...], scale)
    grad_probs = lax.dot_general(
        grad[...], value[...], (((1,), (1,)), ((), ())), preferred_element_type=jnp.float32
    )
    spread = jnp.sum(probs * grad_probs, axis=-1, keepdims=True)
    grad_scores = (probs * (grad_probs - spread)).astype(jnp.bfloat16)
    grad_query[...] = (
        jnp.dot(grad_scores, key[...], preferred_element_type=jnp.float32) * scale
    )
    grad_key[...] += (
        lax.dot_general(
            grad_scores,
            query[...],
            (((0,), (0,)), ((), ())),
            preferred_element_type=jnp.float32,
        )
        * scale
    )
    grad_value[...] += lax.dot_general(
        probs.astype(jnp.bfloat16),
        grad[...],
        (((0,), (0,)), ((), ())),
        preferred_element_type=jnp.float32,
    )


def attention_specs(rows, block):
    per_block = pl.BlockSpec((block, HEAD_DIM), lambda h, i: (i, h))
    per_head = pl.BlockSpec((rows, HEAD_DIM), lambda h, i: (0, h))
    seqs = [
        pl.BlockSpec((block, 1), lambda h, i: (i, 0)),
        pl.BlockSpec((1, rows), lambda h, i: (0, 0)),
    ]
    return per_block, per_head, seqs


def attend(seq_ids, query, key, value):
    rows, width = query.shape
    block = math.gcd(rows, 256)
    per_block, per_head, seqs = attention_specs(rows, block)
    pairs = rows * rows * width
    return pl.pallas_call(
        partial(attend_kernel, 1.0 / math.sqrt(HEAD_DIM)),
        grid=(width // HEAD_DIM, rows // block),
        in_specs=seqs + [per_block, per_head, per_head],
        out_specs=per_block,
        out_shape=jax.ShapeDtypeStruct((rows, width), jnp.bfloat16),
        cost_estimate=pl.CostEstimate(
            flops=4 * pairs, bytes_accessed=8 * rows * width, transcendentals=pairs // HEAD_DIM
        ),
        compiler_params=pltpu.CompilerParams(vmem_limit_bytes=48 << 20),
        name="attend",
    )(seq_ids[:, None], seq_ids[None, :], query, key, value)


def attend_back(seq_ids, query, key, value, grad):
    rows, width = query.shape
    block = math.gcd(rows, 256)
    per_block, per_head, seqs = attention_specs(rows, block)
    pairs = rows * rows * width
    return pl.pallas_call(
        partial(attend_back_kernel, 1.0 / math.sqrt(HEAD_DIM)),
        grid=(width // HEAD_DIM, rows // block),
        in_specs=seqs + [per_block, per_head, per_head, per_block],
        out_specs=(per_block, per_head, per_head),
        out_shape=(jax.ShapeDtypeStruct((rows, width), jnp.float32),) * 3,
        cost_estimate=pl.CostEstimate(
            flops=10 * pairs, bytes_accessed=20 * rows * width, transcendentals=pairs // HEAD_DIM
        ),
        compiler_params=pltpu.CompilerParams(vmem_limit_bytes=48 << 20),
        name="attend_back",
    )(seq_ids[:, None], seq_ids[None, :], query, key, value, grad)


def dispatch_kernel(position, rows, out):
    columns, _, capacity, width = out.shape
    count = rows.shape[1]
    slots = lax.broadcasted_iota(jnp.int32, (columns, capacity, count), 1)
    select = jnp.where(slots == position[:, 0], 1.0, 0.0)
    select = select.reshape(columns * capacity, count).astype(jnp.bfloat16)
    step = math.gcd(width, 512)
    for at in range(0, width, step):
        part = jnp.dot(select, rows[0, :, at : at + step], preferred_element_type=jnp.float32)
        part = part.reshape(columns, capacity, step).astype(out.dtype)
        out[:, 0, :, at : at + step] = part


def dispatch(position, capacity, rows):
    columns, planes, count = position.shape
    width = rows.shape[1]
    return pl.pallas_call(
        dispatch_kernel,
        grid=(planes,),
        in_specs=[
            pl.BlockSpec((columns, 1, 1, count), lambda b: (0, b, 0, 0)),
            pl.BlockSpec((1, count, width), lambda b: (b, 0, 0)),
        ],
        out_specs=pl.BlockSpec((columns, 1, capacity, width), lambda b: (0, b, 0, 0)),
        out_shape=jax.ShapeDtypeStruct((columns, planes, capacity, width), jnp.bfloat16),
        cost_estimate=pl.CostEstimate(
            flops=2 * position.size * capacity * width,
            bytes_accessed=2 * columns * planes * capacity * width,
            transcendentals=0,
        ),
        compiler_params=pltpu.CompilerParams(vmem_limit_bytes=40 << 20),
        name="dispatch",
    )(position[:, :, None], rows.reshape(planes, count, width))


def heads_of(width):
    return [slice(at, at + HEAD_DIM) for at in range(0, width, HEAD_DIM)]


def turn_kernel(raw, scales, gains, cosine, sine, query, key, value):
    width = query.shape[1]
    for which, out in ((0, query), (1, key)):
        scale = scales[:, which : which + 1]
        for head in heads_of(width):
            part = raw[:, which * width + head.start : which * width + head.stop]
            part = part * scale * gains[which : which + 1, head]
            swapped = pltpu.roll(part, HEAD_DIM // 2, 1)
            out[:, head] = (part * cosine[...] + swapped * sine[...]).astype(out.dtype)
    value[...] = raw[:, 2 * width : 3 * width].astype(value.dtype)


def turn_back_kernel(
    raw, scales, gains, cosine, sine, grad_query, grad_key, out_query, out_key, dots, grad_gains
):
    @pl.when(pl.program_id(0) == 0)
    def _():
        grad_gains[...] = jnp.zeros_like(grad_gains)

    width = grad_query.shape[1]
    for which, grad, out in ((0, grad_query, out_query), (1, grad_key, out_key)):
        scale = scales[:, which : which + 1]
        total = jnp.zeros_like(scale)
        for head in heads_of(width):
            part = grad[:, head]
            part = part * cosine[...] - pltpu.roll(part, HEAD_DIM // 2, 1) * sine[...]
            hat = raw[:, which * width + head.start : which * width + head.stop] * scale
            grad_gains[which : which + 1, head] += jnp.sum(part * hat, axis=0, keepdims=True)
            part = part * gains[which : which + 1, head]
            total += jnp.sum(part * hat, axis=1, keepdims=True)
            out[:, head] = part
        dots[:, which : which + 1] = total


def turn_specs(raw, gains):
    block = math.gcd(raw.shape[0], 256)
    return block, [
        pl.BlockSpec((block, raw.shape[1]), lambda i: (i, 0)),
        pl.BlockSpec((block, 2), lambda i: (i, 0)),
        pl.BlockSpec(gains.shape, lambda i: (0, 0)),
        pl.BlockSpec((block, HEAD_DIM), lambda i: (i, 0)),
        pl.BlockSpec((block, HEAD_DIM), lambda i: (i, 0)),
    ]


def turn(raw, scales, gains, cosine, sine):
    rows, width = raw.shape[0], gains.shape[1]
    block, specs = turn_specs(raw, gains)
    return pl.pallas_call(
        turn_kernel,
        grid=(rows // block,),
        in_specs=specs,
        out_specs=(pl.BlockSpec((block, width), lambda i: (i, 0)),) * 3,
        out_shape=(jax.ShapeDtypeStruct((rows, width), jnp.bfloat16),) * 3,
        cost_estimate=pl.CostEstimate(
            flops=16 * rows * width, bytes_accessed=18 * rows * width, transcendentals=0
        ),
        compiler_params=pltpu.CompilerParams(vmem_limit_bytes=40 << 20),
        name="turn",
    )(raw, scales, gains, cosine, sine)


def turn_back(raw, scales, gains, cosine, sine, grad_query, grad_key):
    rows, width = grad_query.shape
    block, specs = turn_specs(raw, gains)
    wide = pl.BlockSpec((block, width), lambda i: (i, 0))
    f32 = jnp.float32
    return pl.pallas_call(
        turn_back_kernel,
        grid=(rows // block,),
        in_specs=specs + [wide, wide],
        out_specs=(
            wide,
            wide,
            pl.BlockSpec((block, 2), lambda i: (i, 0)),
            pl.BlockSpec((2, width), lambda i: (0, 0)),
        ),
        out_shape=(
            jax.ShapeDtypeStruct((rows, width), f32),
            jax.ShapeDtypeStruct((rows, width), f32),
            jax.ShapeDtypeStruct((rows, 2), f32),
            jax.ShapeDtypeStruct((2, width), f32),
        ),
        cost_estimate=pl.CostEstimate(
            flops=24 * rows * width, bytes_accessed=28 * rows * width, transcendentals=0
        ),
        compiler_params=pltpu.CompilerParams(vmem_limit_bytes=40 << 20),
        name="turn_back",
    )(raw, scales, gains, cosine, sine, grad_query, grad_key)


def expert_in_kernel(
    rows, gate, up, router, own, gate_out, up_out, act_out, picked_out
):
    logits = jnp.dot(rows[...], router[...], preferred_element_type=jnp.float32)
    weights = jnp.exp(logits - jnp.max(logits, axis=1, keepdims=True))
    picked = jnp.sum(weights * own[...], axis=1, keepdims=True)
    picked = picked / jnp.sum(weights, axis=1, keepdims=True)
    gate_pre = jnp.dot(rows[...], gate[...], preferred_element_type=jnp.float32)
    up_pre = jnp.dot(rows[...], up[...], preferred_element_type=jnp.float32)
    act = (gate_pre * jax.nn.sigmoid(gate_pre) * up_pre).astype(jnp.bfloat16)
    gate_out[...] = gate_pre
    up_out[...] = up_pre
    act_out[...] = (act.astype(jnp.float32) * picked).astype(jnp.bfloat16)
    picked_out[...] = picked


def expert_back_kernel(
    grad, gate_in, up_in, picked, gate, up, down, grad_gate, grad_up, grad_picked, grad_rows
):
    grad_raw = lax.dot_general(
        grad[...], down[...], (((1,), (1,)), ((), ())), preferred_element_type=jnp.float32
    )
    gate_pre, up_pre = gate_in[...], up_in[...]
    sigma = jax.nn.sigmoid(gate_pre)
    silu = gate_pre * sigma
    act = (silu * up_pre).astype(jnp.bfloat16).astype(jnp.float32)
    grad_picked[...] = jnp.sum(grad_raw * act, axis=1, keepdims=True)
    grad_act = grad_raw * picked[...]
    low_gate = (grad_act * up_pre * (sigma + silu * (1.0 - sigma))).astype(jnp.bfloat16)
    low_up = (grad_act * silu).astype(jnp.bfloat16)
    grad_gate[...] = low_gate
    grad_up[...] = low_up
    back = lax.dot_general(
        low_gate, gate[...], (((1,), (1,)), ((), ())), preferred_element_type=jnp.float32
    )
    back = back + lax.dot_general(
        low_up, up[...], (((1,), (1,)), ((), ())), preferred_element_type=jnp.float32
    )
    grad_rows[...] = back.astype(jnp.bfloat16)


def whole(shape):
    return pl.BlockSpec(shape, lambda i: (0, 0), pipeline_mode=pl.Buffered(1))


def row_blocks(block, width):
    return pl.BlockSpec((block, width), lambda i: (i, 0))


def expert_in(rows, gate, up, router, own, block):
    count, width = rows.shape
    hidden = gate.shape[1]
    narrow = row_blocks(block, hidden)
    f32 = jnp.float32
    return pl.pallas_call(
        expert_in_kernel,
        grid=(count // block,),
        in_specs=[
            row_blocks(block, width),
            whole(gate.shape),
            whole(up.shape),
            whole(router.shape),
            whole(own.shape),
        ],
        out_specs=(narrow, narrow, narrow, row_blocks(block, 1)),
        out_shape=(
            jax.ShapeDtypeStruct((count, hidden), f32),
            jax.ShapeDtypeStruct((count, hidden), f32),
            jax.ShapeDtypeStruct((count, hidden), jnp.bfloat16),
            jax.ShapeDtypeStruct((count, 1), f32),
        ),
        cost_estimate=pl.CostEstimate(
            flops=4 * count * width * hidden,
            bytes_accessed=2 * count * width + (10 * count + 4 * width) * hidden,
            transcendentals=count * hidden,
        ),
        compiler_params=pltpu.CompilerParams(vmem_limit_bytes=56 << 20),
        name="expert_in",
    )(rows, gate, up, router, own)


def expert_back(grad, gate_pre, up_pre, picked, gate, up, down, block):
    count, width = grad.shape
    hidden = down.shape[0]
    wide, narrow, one = [row_blocks(block, size) for size in (width, hidden, 1)]
    low = jax.ShapeDtypeStruct((count, hidden), jnp.bfloat16)
    return pl.pallas_call(
        expert_back_kernel,
        grid=(count // block,),
        in_specs=[wide, narrow, narrow, one, whole(gate.shape), whole(up.shape), whole(down.shape)],
        out_specs=(narrow, narrow, one, wide),
        out_shape=(
            low,
            low,
            jax.ShapeDtypeStruct((count, 1), jnp.float32),
            jax.ShapeDtypeStruct((count, width), jnp.bfloat16),
        ),
        cost_estimate=pl.CostEstimate(
            flops=6 * count * width * hidden,
            bytes_accessed=4 * count * width + (12 * count + 6 * width) * hidden,
            transcendentals=count * hidden,
        ),
        compiler_params=pltpu.CompilerParams(vmem_limit_bytes=58 << 20),
        name="expert_back",
    )(grad, gate_pre, up_pre, picked, gate, up, down)


def tie(array, *others):
    anywhere = pl.BlockSpec(memory_space=pl.ANY)
    return pl.pallas_call(
        lambda *refs: None,
        in_specs=[anywhere] * (1 + len(others)),
        out_specs=anywhere,
        out_shape=jax.ShapeDtypeStruct(array.shape, array.dtype),
        input_output_aliases={0: 0},
        name="tie",
    )(array, *others)


def mm(left, right):
    return jnp.dot(left, right, preferred_element_type=jnp.float32)


def mm_t(left, right):
    return lax.dot_general(
        left, right, (((1,), (1,)), ((), ())), preferred_element_type=jnp.float32
    )


def t_mm(left, right):
    return lax.dot_general(
        left, right, (((0,), (0,)), ((), ())), preferred_element_type=jnp.float32
    )


def plane_shards(
    hidden,
    token_order,
    lengths,
    routes,
    grad_output,
    w_query,
    w_key,
    w_value,
    w_out,
    w_router,
    attn_gain,
    ffn_gain,
    query_gain,
    key_gain,
    w_gate,
    w_up,
    w_down,
):
    f32, bf16 = jnp.float32, jnp.bfloat16
    both = ("ctx", "fsdp")
    planes = lax.axis_size("ctx")
    columns = lax.axis_size("fsdp")
    plane = lax.axis_index("ctx")
    row_count, width = hidden.shape[1:]
    group_rows = row_count * planes
    share = width // planes
    strip = w_query.shape[0]
    first_row = plane * row_count

    experts = w_router.shape[1]
    qkv = jnp.stack([w_query, w_key, w_value], axis=1).reshape(strip, 3, planes, share)
    qkv = qkv.transpose(2, 0, 1, 3).reshape(planes, strip, 3 * share)
    small = [w_router] + [g[:, None] for g in (attn_gain, ffn_gain, query_gain, key_gain)]
    small = jnp.concatenate(small + [routes.astype(bf16).reshape(strip, -1)], axis=1)
    spare = -small.shape[1] % 128
    small = jnp.pad(small, ((0, 0), (0, spare)))
    small = jnp.broadcast_to(small[None], (planes,) + small.shape)
    own_out = jnp.broadcast_to(w_out[None], (planes,) + w_out.shape)
    packed = jnp.concatenate([qkv, small, own_out], axis=2)
    packed = lax.all_to_all(packed, "ctx", 0, 0, tiled=True)
    hidden_all = lax.all_gather(hidden[0], "ctx", axis=0, tiled=True)
    packed, out_rows = packed[:, :, :-width], packed[:, :, -width:]
    routes_at = 3 * share + experts + 4
    routes_all = packed[:, :, routes_at : packed.shape[2] - spare].astype(jnp.int32)
    routes_all = routes_all.reshape(group_rows, -1)
    packed = jnp.broadcast_to(packed[None], (columns,) + packed.shape)
    packed = lax.all_to_all(packed, "fsdp", 0, 0, tiled=True)
    packed = packed.transpose(1, 0, 2, 3).reshape(width, -1)
    full_router = packed[:, 3 * share : 3 * share + experts]
    gain_attn, gain_ffn, gain_query, gain_key = [
        packed[:, 3 * share + experts + i].astype(f32) for i in range(4)
    ]
    def swap(part, step):
        return lax.ppermute(part, "ctx", [(i, i ^ step) for i in range(planes)])

    def by_plane(came):
        came = jnp.stack(came)
        return [came[plane ^ i] for i in range(planes)]

    def exchange(parts, first=None, last=None):
        came = [parts[plane]]
        for step in range(1, planes):
            part = parts[plane ^ step]
            part = swap(part if first is None else tie(part, first), step)
            came.append(part if last is None else tie(part, last))
        return by_plane(came)

    def exchange_after(parts, earlier):
        came = [
            swap(part if before is None else tie(part, before), step)
            for step, before in enumerate(earlier, 1)
            for part in [parts[plane ^ step]]
        ]
        return came, jnp.stack(by_plane([parts[plane]] + came)).astype(f32)

    def plane_sum(part):
        return part + sum(swap(part, step) for step in range(1, planes))

    out_rows = jnp.broadcast_to(out_rows[None], (columns,) + out_rows.shape)
    grad_all = lax.all_gather(
        tie(grad_output[0], hidden_all), "ctx", axis=0, tiled=True
    )
    full_out = lax.all_to_all(out_rows, "fsdp", 0, 0, tiled=True)

    seq_ids, places = seq_layout(token_order[0], lengths[0])
    experts_here = w_gate.shape[0]
    column_expert = experts_here * jnp.arange(columns, dtype=jnp.int32) + plane
    named = jnp.any(routes_all[:, :, None] == column_expert[None, None, :], axis=1)
    named = named.reshape(planes, row_count, columns)
    capacity = 5 * row_count * routes.shape[2] // (4 * experts)
    rank = jnp.cumsum(named.astype(jnp.int32), axis=1) - 1
    position = jnp.where(named, rank, -1).transpose(2, 0, 1)
    slots = jnp.arange(capacity, dtype=jnp.int32)
    holds = position[:, :, None, :] == slots[None, None, :, None]
    select = holds.astype(bf16)

    def combine(rows):
        rows = rows.reshape(columns, planes, capacity, width)
        sums = jnp.einsum("fbsr,fbsd->brd", select, rows, preferred_element_type=f32)
        return sums.reshape(group_rows, width).astype(bf16)


    frequency = rope_base ** (
        -2.0 * jnp.arange(HEAD_DIM // 2).astype(f32) / HEAD_DIM
    )
    angles = places.astype(f32)[:, None] * frequency[None, :]
    cosine, sine = jnp.cos(angles), jnp.sin(angles)
    cosine = jnp.concatenate([cosine, cosine], axis=1)
    sine = jnp.concatenate([-sine, sine], axis=1)
    hidden_wide = hidden_all.astype(f32)
    scale_one = lax.rsqrt(jnp.mean(hidden_wide * hidden_wide, axis=-1, keepdims=True) + epsilon)
    h_one = (hidden_wide * scale_one * gain_attn).astype(bf16)
    raw = mm(h_one, packed)
    squares = jnp.stack(
        [jnp.sum(raw[:, :share] ** 2, axis=1), jnp.sum(raw[:, share : 2 * share] ** 2, axis=1)]
    )
    squares = plane_sum(squares)
    scales = lax.rsqrt(squares / width + epsilon).T
    gains = lax.dynamic_slice_in_dim(
        jnp.stack([gain_query, gain_key]), plane * share, share, axis=1
    )
    query, key, values = turn(raw, scales, gains, cosine, sine)
    attended = attend(seq_ids, query, key, values)
    full_out = tie(full_out, attended).transpose(1, 0, 2, 3).reshape(width, width)
    grad_send = dispatch(position, capacity, tie(grad_all, attended, full_out))
    attended = attended.reshape(planes, row_count, share)
    attended = jnp.concatenate(exchange(attended, grad_all), axis=1)
    grad_in = lax.all_to_all(grad_send, "fsdp", 0, 0, tiled=True).reshape(-1, width)
    middle = hidden[0].astype(f32) + mm(attended, full_out)
    scale_two = lax.rsqrt(jnp.mean(middle * middle, axis=-1, keepdims=True) + epsilon)
    middle_hat = middle * scale_two
    h_two = (middle_hat * gain_ffn).astype(bf16)

    h_two_all = lax.all_gather(tie(h_two, grad_send), "ctx", axis=0, tiled=True)
    h_all = tie(h_two_all, grad_in)
    gate = jnp.concatenate(exchange(w_gate, h_two_all))
    came_up = [swap(tie(w_up[plane ^ step], h_two_all), step) for step in range(1, planes)]
    up = jnp.concatenate(by_plane([w_up[plane]] + came_up))
    probs = jax.nn.softmax(mm(h_two, full_router), axis=-1)
    rows_in = lax.all_to_all(dispatch(position, capacity, h_all), "fsdp", 0, 0, tiled=True)
    came = [
        swap(tie(w_down[plane ^ step], before), step) for step, before in enumerate(came_up, 1)
    ]
    rows_in = tie(rows_in, *came[:-1]).reshape(-1, width)
    own = experts_here * lax.axis_index("fsdp") + plane
    own = (jnp.arange(experts)[None, :] == own).astype(f32)
    slot_block = planes * capacity
    gate_pre, up_pre, act_picked, picked = expert_in(
        rows_in, gate, up, full_router, own, slot_block
    )
    came = [tie(part, act_picked) for part in came]
    down = jnp.concatenate(by_plane([w_down[plane]] + came))
    grad_down_w = t_mm(act_picked, grad_in).astype(bf16)
    grad_gate, grad_up, grad_picked, grad_rows = expert_back(
        grad_in, tie(gate_pre, grad_down_w), up_pre, picked, gate, up, down, slot_block
    )

    def blocks(matrix):
        return matrix.reshape(planes, matrix.shape[0] // planes, matrix.shape[1])

    came, down_grad = exchange_after(blocks(grad_down_w), [None] * (planes - 1))
    grad_rows = tie(grad_rows, *came)
    grad_rows = lax.all_to_all(
        grad_rows.reshape(columns, planes * capacity, width), "fsdp", 0, 0, tiled=True
    )
    grad_gate_w = t_mm(rows_in, grad_gate).astype(bf16)
    grad_up_w = t_mm(rows_in, grad_up).astype(bf16)
    came_up, up_grad = exchange_after(blocks(grad_up_w), came)
    came, gate_grad = exchange_after(blocks(grad_gate_w), came)
    expert_out = mm(act_picked, down).astype(bf16)
    grad_picked = lax.all_to_all(
        tie(grad_picked, grad_rows).reshape(columns, planes, capacity), "fsdp", 0, 0, tiled=True
    )
    grad_rows = tie(grad_rows, *came, *came_up, expert_out, grad_picked)
    expert_out = lax.all_to_all(
        expert_out.reshape(columns, planes * capacity, width), "fsdp", 0, 0, tiled=True
    )
    grad_h_two = lax.psum_scatter(
        combine(grad_rows), "ctx", scatter_dimension=0, tiled=True
    ).astype(f32)

    u_plane = jnp.sum(jnp.where(holds, grad_picked[..., None], 0.0), axis=2)
    u_mine = exchange(u_plane.transpose(1, 0, 2))
    u_mine = jnp.stack(u_mine, axis=1).reshape(experts, row_count).T
    grad_logits = probs * (u_mine - jnp.sum(probs * u_mine, axis=-1, keepdims=True))
    grad_logits = grad_logits.astype(bf16)
    grad_h_two = grad_h_two + mm_t(grad_logits, full_router)
    grad_router = t_mm(h_two, grad_logits)

    grad_top = grad_output[0].astype(f32)
    grad_ffn_gain = jnp.sum(grad_h_two * middle_hat, axis=0)
    grad_hat = grad_h_two * gain_ffn
    grad_middle = grad_top + scale_two * (
        grad_hat - middle_hat * jnp.mean(grad_hat * middle_hat, axis=-1, keepdims=True)
    )
    grad_branch = grad_middle.astype(bf16)
    def grad_heads(where):
        rows = lax.dynamic_slice_in_dim(full_out, where * share, share)
        return mm_t(grad_branch, rows).astype(bf16)

    came = [swap(grad_heads(plane ^ step), step) for step in range(1, planes)]
    grad_att = jnp.concatenate(by_plane([grad_heads(plane)] + came))
    grad_out_w = t_mm(attended, grad_branch).astype(bf16)
    grad_out_w = grad_out_w.reshape(planes, columns, strip, width).transpose(1, 0, 2, 3)
    mixed_part = combine(tie(expert_out, grad_att, grad_out_w))
    mixed = lax.psum_scatter(mixed_part, "ctx", scatter_dimension=0, tiled=True)
    output = (middle + mixed.astype(f32)).astype(bf16)
    grad_out_w = lax.all_to_all(
        tie(grad_out_w, mixed_part), "fsdp", 0, 0, tiled=True
    )
    grad_att = tie(grad_att, mixed_part)
    grad_query, grad_key, grad_value = attend_back(seq_ids, query, key, values, grad_att)
    grad_query, grad_key, dots, grad_gains = turn_back(
        raw, scales, gains, cosine, sine, grad_query, grad_key
    )
    dots = plane_sum(dots.T).T * (scales * scales) / width
    grad_qkv = jnp.concatenate(
        [
            scales[:, :1] * grad_query - raw[:, :share] * (scales[:, :1] * dots[:, :1]),
            scales[:, 1:] * grad_key - raw[:, share : 2 * share] * (scales[:, 1:] * dots[:, 1:]),
            grad_value,
        ],
        axis=1,
    ).astype(bf16)
    grad_part = mm_t(grad_qkv, packed[:, : 3 * share])
    grad_h_one = lax.psum_scatter(
        tie(grad_part.astype(bf16), mixed, grad_out_w), "ctx", scatter_dimension=0, tiled=True
    ).astype(f32)
    grad_attn_gain = jnp.sum(grad_part * (hidden_wide * scale_one), axis=0)
    rows_of = jnp.arange(planes)[:, None] == plane
    gains = [jnp.where(rows_of, g[None], 0.0).reshape(width) for g in grad_gains]
    gains = [g[:, None] for g in [grad_attn_gain, grad_ffn_gain] + gains]
    small = jnp.concatenate([grad_router] + gains, axis=1).reshape(planes * columns, -1)
    small = lax.all_to_all(small, both, 0, 0, tiled=True)
    sums = t_mm(h_one, grad_qkv).astype(bf16)
    sums = sums.reshape(planes, columns, strip, -1).transpose(1, 0, 2, 3)
    sums = lax.all_to_all(tie(sums, small), "fsdp", 0, 0, tiled=True)
    grad_out_w = jnp.sum(grad_out_w.astype(f32), axis=0).astype(bf16)
    small = jnp.sum(small, axis=0).reshape(strip, -1)
    sums = tie(jnp.sum(sums.astype(f32), axis=0).astype(bf16), grad_out_w)
    grad_out_w = sum(x.astype(f32) for x in exchange(grad_out_w, sums))
    sums = lax.all_to_all(sums, "ctx", 0, 0, tiled=True)
    grad_qkv_w = sums.reshape(planes, strip, 3, share).transpose(2, 1, 0, 3)
    grad_qkv_w = grad_qkv_w.reshape(3, strip, width).astype(f32)

    x_hat = hidden[0].astype(f32)
    scale_mine = lax.rsqrt(jnp.mean(x_hat * x_hat, axis=-1, keepdims=True) + epsilon)
    x_hat = x_hat * scale_mine
    grad_hat = grad_h_one * gain_attn
    grad_input = grad_middle + scale_mine * (
        grad_hat - x_hat * jnp.mean(grad_hat * x_hat, axis=-1, keepdims=True)
    )

    return (
        output[None],
        grad_input[None],
        grad_qkv_w[0],
        grad_qkv_w[1],
        grad_qkv_w[2],
        grad_out_w,
        small[:, :experts],
        small[:, experts],
        small[:, experts + 1],
        small[:, experts + 2],
        small[:, experts + 3],
        gate_grad,
        up_grad,
        down_grad,
    )


def solution(mesh):
    placed = (
        P("fsdp", "ctx", None),
        P("fsdp", None),
        P("fsdp", None),
        P("fsdp", "ctx", None),
        P("fsdp", "ctx", None),
        P(("ctx", "fsdp"), None),
        P(("ctx", "fsdp"), None),
        P(("ctx", "fsdp"), None),
        P(("ctx", "fsdp"), None),
        P(("ctx", "fsdp"), None),
        P(("ctx", "fsdp")),
        P(("ctx", "fsdp")),
        P(("ctx", "fsdp")),
        P(("ctx", "fsdp")),
        P("fsdp", "ctx", None),
        P("fsdp", "ctx", None),
        P("fsdp", "ctx", None),
    )

    def shards(*operands):
        experts_here = operands[14].shape[0]
        heads = operands[0].shape[2] // HEAD_DIM
        planes = mesh.shape["ctx"]
        whole_experts = experts_here == planes and heads % planes == 0 and planes in (2, 4)
        return (plane_shards if whole_experts else general_shards)(*operands)

    return jax.shard_map(
        shards,
        mesh=mesh,
        in_specs=placed,
        out_specs=(
            P("fsdp", "ctx", None),
            P("fsdp", "ctx", None),
            P(("ctx", "fsdp"), None),
            P(("ctx", "fsdp"), None),
            P(("ctx", "fsdp"), None),
            P(("ctx", "fsdp"), None),
            P(("ctx", "fsdp"), None),
            P(("ctx", "fsdp")),
            P(("ctx", "fsdp")),
            P(("ctx", "fsdp")),
            P(("ctx", "fsdp")),
            P("fsdp", "ctx", None),
            P("fsdp", "ctx", None),
            P("fsdp", "ctx", None),
        ),
        check_vma=False,
    )
```

```python
from functools import partial
import math

import jax
import jax.numpy as jnp
from jax import lax
from jax.experimental import pallas as pl
from jax.experimental.pallas import tpu as pltpu
from jax.sharding import PartitionSpec as P

HEAD_DIM = 128


epsilon = 1e-06
rope_base = 10000.0
masked_value = -1e30


def rms_scaled(values, gain):
    return values * lax.rsqrt(jnp.mean(values * values, axis=-1, keepdims=True) + epsilon) * gain


def rotate(values, places):
    row_count = values.shape[0]
    head_count = values.shape[1] // HEAD_DIM
    half_width = HEAD_DIM // 2
    frequency = rope_base ** (-2.0 * jnp.arange(half_width).astype(jnp.float32) / HEAD_DIM)
    angles = places.astype(jnp.float32)[:, None] * frequency[None, :]
    cosine = jnp.cos(angles)[:, None, :]
    sine_part = jnp.sin(angles)[:, None, :]
    split_heads = values.reshape(row_count, head_count, HEAD_DIM)
    first_half = split_heads[:, :, :half_width]
    second_half = split_heads[:, :, half_width:]
    turned = jnp.concatenate(
        [
            first_half * cosine - second_half * sine_part,
            second_half * cosine + first_half * sine_part,
        ],
        axis=-1,
    )
    return turned.reshape(row_count, head_count * HEAD_DIM)


def qk_post(values, gain, places):
    return rotate(rms_scaled(values, gain), places)


def route_weights(logits, chosen):
    router_probs = jax.nn.softmax(logits, axis=-1)
    return jnp.sum(jnp.where(chosen, router_probs[:, None, :], 0.0), axis=-1)


def seq_layout(order_row, seq_lengths):
    seq_ends = jnp.cumsum(seq_lengths)
    seq_ids = jnp.sum((order_row[:, None] >= seq_ends[None, :]).astype(jnp.int32), axis=1)
    starts = seq_ends - seq_lengths
    chosen = seq_ids[:, None] == jnp.arange(seq_lengths.shape[0], dtype=jnp.int32)[None, :]
    seq_start = jnp.sum(jnp.where(chosen, starts[None, :], 0), axis=1)
    return (seq_ids, order_row - seq_start)


def general_shards(
    hidden,
    token_order,
    lengths,
    routes,
    grad_output,
    w_query,
    w_key,
    w_value,
    w_out,
    w_router,
    attn_gain,
    ffn_gain,
    query_gain,
    key_gain,
    w_gate,
    w_up,
    w_down,
):
    hidden_in = hidden[0].astype(jnp.float32)
    row_count = hidden_in.shape[0]
    model_width = hidden_in.shape[1]
    head_count = model_width // HEAD_DIM
    score_scale = 1.0 / math.sqrt(HEAD_DIM)
    seq_all, place_all = seq_layout(token_order[0], lengths[0])
    first_row = lax.axis_index("ctx") * row_count
    seq_mine = lax.dynamic_slice_in_dim(seq_all, first_row, row_count)
    place_mine = lax.dynamic_slice_in_dim(place_all, first_row, row_count)
    same_seq = seq_mine[:, None] == seq_all[None, :]
    gathered = (
        lax.all_gather(w_query, ("ctx", "fsdp"), axis=0, tiled=True),
        lax.all_gather(w_key, ("ctx", "fsdp"), axis=0, tiled=True),
        lax.all_gather(w_value, ("ctx", "fsdp"), axis=0, tiled=True),
        lax.all_gather(w_out, ("ctx", "fsdp"), axis=0, tiled=True),
        lax.all_gather(w_router, ("ctx", "fsdp"), axis=0, tiled=True),
        lax.all_gather(attn_gain, ("ctx", "fsdp"), axis=0, tiled=True),
        lax.all_gather(ffn_gain, ("ctx", "fsdp"), axis=0, tiled=True),
        lax.all_gather(query_gain, ("ctx", "fsdp"), axis=0, tiled=True),
        lax.all_gather(key_gain, ("ctx", "fsdp"), axis=0, tiled=True),
    )
    (
        full_query,
        full_key,
        full_value,
        full_out,
        full_router,
        gain_attn,
        gain_ffn,
        gain_query,
        gain_key,
    ) = gathered
    gain_attn = gain_attn.astype(jnp.float32)
    gain_ffn = gain_ffn.astype(jnp.float32)
    gain_query = gain_query.astype(jnp.float32)
    gain_key = gain_key.astype(jnp.float32)
    h_one, norm_one_back = jax.vjp(rms_scaled, hidden_in, gain_attn)
    h_one_low = h_one.astype(jnp.bfloat16)
    query_raw = jnp.dot(h_one_low, full_query, preferred_element_type=jnp.float32)
    key_raw = jnp.dot(h_one_low, full_key, preferred_element_type=jnp.float32)
    values_low = jnp.dot(h_one_low, full_value, preferred_element_type=jnp.float32).astype(
        jnp.bfloat16
    )
    query_rot, query_back = jax.vjp(partial(qk_post, places=place_mine), query_raw, gain_query)
    key_rot, key_back = jax.vjp(partial(qk_post, places=place_mine), key_raw, gain_key)
    query_low = query_rot.astype(jnp.bfloat16)
    key_low = key_rot.astype(jnp.bfloat16)
    key_all, value_all = (
        lax.all_gather(key_low, "ctx", axis=0, tiled=True),
        lax.all_gather(values_low, "ctx", axis=0, tiled=True),
    )
    query_heads = query_low.reshape(row_count, head_count, HEAD_DIM)
    key_heads = key_all.reshape(-1, head_count, HEAD_DIM)
    value_heads = value_all.reshape(-1, head_count, HEAD_DIM)

    def scores_of():
        raw_scores = (
            jnp.einsum("thd,khd->htk", query_heads, key_heads, preferred_element_type=jnp.float32)
            * score_scale
        )
        return jnp.where(same_seq[None, :, :], raw_scores, masked_value)

    scores = scores_of()
    row_top = jnp.max(scores, axis=-1, keepdims=True)
    log_total = row_top + jnp.log(jnp.sum(jnp.exp(scores - row_top), axis=-1, keepdims=True))
    probs_low = jnp.exp(scores - log_total).astype(jnp.bfloat16)
    attended = jnp.einsum(
        "htk,khd->thd", probs_low, value_heads, preferred_element_type=jnp.float32
    )
    attended_low = attended.reshape(row_count, model_width).astype(jnp.bfloat16)
    middle = hidden_in + jnp.dot(attended_low, full_out, preferred_element_type=jnp.float32)
    h_two, norm_two_back = jax.vjp(rms_scaled, middle, gain_ffn)
    h_two_low = h_two.astype(jnp.bfloat16)
    logits = jnp.dot(h_two_low, full_router, preferred_element_type=jnp.float32)
    expert_count = full_router.shape[1]
    route_rows = routes[0]
    top_k = route_rows.shape[1]
    chosen = route_rows[:, :, None] == jnp.arange(expert_count, dtype=jnp.int32)[None, None, :]
    picked, route_back = jax.vjp(partial(route_weights, chosen=chosen), logits)
    pair_count = row_count * top_k
    capacity = 5 * row_count * top_k // (4 * expert_count)
    slot_count = expert_count * capacity
    group_size = lax.axis_size("fsdp")
    local_experts = w_gate.shape[0]
    pair_expert = route_rows.reshape(pair_count)
    one_hot = (pair_expert[:, None] == jnp.arange(expert_count, dtype=jnp.int32)[None, :]).astype(
        jnp.int32
    )
    slot_rank = jnp.sum(one_hot * (jnp.cumsum(one_hot, axis=0) - 1), axis=1)
    slot_ids = pair_expert * capacity + slot_rank
    source = (
        jnp.full((slot_count,), pair_count, jnp.int32)
        .at[slot_ids]
        .set(jnp.arange(pair_count, dtype=jnp.int32))
    )
    filled = source < pair_count
    source_pair = jnp.minimum(source, pair_count - 1)
    send_rows = jnp.where(
        filled[:, None], h_two_low[source_pair // top_k], jnp.zeros((), jnp.bfloat16)
    )
    send_rows = send_rows.reshape(group_size, local_experts, capacity, model_width)
    gate_full, up_full, down_full = (
        lax.all_gather(w_gate, "ctx", axis=1, tiled=True),
        lax.all_gather(w_up, "ctx", axis=1, tiled=True),
        lax.all_gather(w_down, "ctx", axis=1, tiled=True),
    )
    arrived_rows = lax.all_to_all(send_rows, "fsdp", split_axis=0, concat_axis=0, tiled=True)
    gate_part = jnp.einsum(
        "secd,edf->secf", arrived_rows, gate_full, preferred_element_type=jnp.float32
    )
    up_part = jnp.einsum(
        "secd,edf->secf", arrived_rows, up_full, preferred_element_type=jnp.float32
    )
    act_part = (jax.nn.silu(gate_part) * up_part).astype(jnp.bfloat16)
    result = jnp.einsum(
        "secf,efd->secd", act_part, down_full, preferred_element_type=jnp.float32
    ).astype(jnp.bfloat16)
    returned = lax.all_to_all(result, "fsdp", split_axis=0, concat_axis=0, tiled=True).reshape(
        slot_count, model_width
    )
    pair_out = returned[slot_ids].reshape(row_count, top_k, model_width)
    output = (middle + jnp.sum(picked[:, :, None] * pair_out, axis=1)).astype(jnp.bfloat16)
    grad_top = grad_output[0].astype(jnp.float32)
    grad_picked = jnp.sum(grad_top[:, None, :] * pair_out, axis=-1)
    grad_pair = (
        (picked[:, :, None] * grad_top[:, None, :])
        .astype(jnp.bfloat16)
        .reshape(pair_count, model_width)
    )
    grad_send = jnp.where(filled[:, None], grad_pair[source_pair], jnp.zeros((), jnp.bfloat16))
    grad_send = grad_send.reshape(group_size, local_experts, capacity, model_width)
    grad_arrived = lax.all_to_all(grad_send, "fsdp", split_axis=0, concat_axis=0, tiled=True)
    sigma = jax.nn.sigmoid(gate_part)
    act_low = (gate_part * sigma * up_part).astype(jnp.bfloat16)
    grad_act = jnp.einsum(
        "secd,efd->secf", grad_arrived, down_full, preferred_element_type=jnp.float32
    )
    grad_gate = (grad_act * up_part * sigma * (1.0 + gate_part * (1.0 - sigma))).astype(
        jnp.bfloat16
    )
    grad_up = (grad_act * gate_part * sigma).astype(jnp.bfloat16)
    grad_back = jnp.einsum(
        "secf,edf->secd", grad_gate, gate_full, preferred_element_type=jnp.float32
    )
    grad_back = (
        grad_back
        + jnp.einsum("secf,edf->secd", grad_up, up_full, preferred_element_type=jnp.float32)
    ).astype(jnp.bfloat16)
    grad_return = lax.all_to_all(
        grad_back, "fsdp", split_axis=0, concat_axis=0, tiled=True
    ).reshape(slot_count, model_width)
    grad_h_two = jnp.sum(
        grad_return[slot_ids].reshape(row_count, top_k, model_width).astype(jnp.float32), axis=1
    )
    (grad_logits,) = route_back(grad_picked)
    grad_logits_low = grad_logits.astype(jnp.bfloat16)
    grad_h_two = grad_h_two + jnp.einsum(
        "te,de->td", grad_logits_low, full_router, preferred_element_type=jnp.float32
    )
    grad_router = jnp.einsum(
        "td,te->de", h_two_low, grad_logits_low, preferred_element_type=jnp.float32
    )
    grad_middle, grad_ffn_gain = norm_two_back(grad_h_two)
    grad_middle = grad_middle + grad_top
    grad_branch = grad_middle.astype(jnp.bfloat16)
    grad_out_w = jnp.einsum(
        "td,te->de", attended_low, grad_branch, preferred_element_type=jnp.float32
    )
    grad_att = jnp.einsum(
        "te,de->td", grad_branch, full_out, preferred_element_type=jnp.float32
    ).astype(jnp.bfloat16)
    grad_att = grad_att.reshape(row_count, head_count, HEAD_DIM)
    scores = scores_of()
    probs_full = jnp.exp(scores - log_total)
    probs_again = probs_full.astype(jnp.bfloat16)
    grad_probs = jnp.einsum(
        "thd,khd->htk", grad_att, value_heads, preferred_element_type=jnp.float32
    )
    spread = jnp.sum(probs_full * grad_probs, axis=-1, keepdims=True)
    grad_scores = (probs_full * (grad_probs - spread)).astype(jnp.bfloat16)
    grad_query = (
        jnp.einsum(
            "htk,khd->thd", grad_scores, key_heads, preferred_element_type=jnp.float32
        ).reshape(row_count, model_width)
        * score_scale
    )
    grad_key_part = (
        jnp.einsum(
            "htk,thd->khd", grad_scores, query_heads, preferred_element_type=jnp.float32
        ).reshape(-1, model_width)
        * score_scale
    )
    grad_value_part = jnp.einsum(
        "htk,thd->khd", probs_again, grad_att, preferred_element_type=jnp.float32
    ).reshape(-1, model_width)
    grad_key, grad_value = (
        lax.psum_scatter(
            grad_key_part.astype(jnp.bfloat16), "ctx", scatter_dimension=0, tiled=True
        ).astype(jnp.float32),
        lax.psum_scatter(
            grad_value_part.astype(jnp.bfloat16), "ctx", scatter_dimension=0, tiled=True
        ).astype(jnp.float32),
    )
    grad_q_raw, grad_q_gain = query_back(grad_query)
    grad_k_raw, grad_k_gain = key_back(grad_key)
    grad_q_low = grad_q_raw.astype(jnp.bfloat16)
    grad_k_low = grad_k_raw.astype(jnp.bfloat16)
    grad_v_low = grad_value.astype(jnp.bfloat16)
    grad_query_w = jnp.einsum(
        "td,te->de", h_one_low, grad_q_low, preferred_element_type=jnp.float32
    )
    grad_key_w = jnp.einsum("td,te->de", h_one_low, grad_k_low, preferred_element_type=jnp.float32)
    grad_value_w = jnp.einsum(
        "td,te->de", h_one_low, grad_v_low, preferred_element_type=jnp.float32
    )
    grad_h_one = jnp.einsum("te,de->td", grad_q_low, full_query, preferred_element_type=jnp.float32)
    grad_h_one = grad_h_one + jnp.einsum(
        "te,de->td", grad_k_low, full_key, preferred_element_type=jnp.float32
    )
    grad_h_one = grad_h_one + jnp.einsum(
        "te,de->td", grad_v_low, full_value, preferred_element_type=jnp.float32
    )
    grad_input_norm, grad_attn_gain = norm_one_back(grad_h_one)
    grad_input = grad_middle + grad_input_norm
    totals = (
        lax.psum_scatter(grad_query_w, ("ctx", "fsdp"), scatter_dimension=0, tiled=True),
        lax.psum_scatter(grad_key_w, ("ctx", "fsdp"), scatter_dimension=0, tiled=True),
        lax.psum_scatter(grad_value_w, ("ctx", "fsdp"), scatter_dimension=0, tiled=True),
        lax.psum_scatter(grad_out_w, ("ctx", "fsdp"), scatter_dimension=0, tiled=True),
        lax.psum_scatter(grad_router, ("ctx", "fsdp"), scatter_dimension=0, tiled=True),
        lax.psum_scatter(grad_attn_gain, ("ctx", "fsdp"), scatter_dimension=0, tiled=True),
        lax.psum_scatter(grad_ffn_gain, ("ctx", "fsdp"), scatter_dimension=0, tiled=True),
        lax.psum_scatter(grad_q_gain, ("ctx", "fsdp"), scatter_dimension=0, tiled=True),
        lax.psum_scatter(grad_k_gain, ("ctx", "fsdp"), scatter_dimension=0, tiled=True),
    )
    grad_down_w = jnp.einsum(
        "secf,secd->efd", act_low, grad_arrived, preferred_element_type=jnp.float32
    )
    grad_gate_w = jnp.einsum(
        "secd,secf->edf", arrived_rows, grad_gate, preferred_element_type=jnp.float32
    )
    grad_up_w = jnp.einsum(
        "secd,secf->edf", arrived_rows, grad_up, preferred_element_type=jnp.float32
    )
    gate_grad, up_grad, down_grad = (
        lax.psum_scatter(
            grad_gate_w.astype(jnp.bfloat16), "ctx", scatter_dimension=1, tiled=True
        ).astype(jnp.float32),
        lax.psum_scatter(
            grad_up_w.astype(jnp.bfloat16), "ctx", scatter_dimension=1, tiled=True
        ).astype(jnp.float32),
        lax.psum_scatter(
            grad_down_w.astype(jnp.bfloat16), "ctx", scatter_dimension=1, tiled=True
        ).astype(jnp.float32),
    )
    return (
        output[None],
        grad_input[None],
        totals[0],
        totals[1],
        totals[2],
        totals[3],
        totals[4],
        totals[5],
        totals[6],
        totals[7],
        totals[8],
        gate_grad,
        up_grad,
        down_grad,
    )


def masked_probs(query, key, seq_rows, seq_cols, scale):
    scores = (
        lax.dot_general(query, key, (((1,), (1,)), ((), ())), preferred_element_type=jnp.float32)
        * scale
    )
    scores = jnp.where(seq_rows == seq_cols, scores, masked_value)
    top = jnp.max(scores, axis=-1, keepdims=True)
    weights = jnp.exp(scores - top)
    return weights / jnp.sum(weights, axis=-1, keepdims=True)


def attend_kernel(scale, seq_rows, seq_cols, query, key, value, out):
    probs = masked_probs(query[...], key[...], seq_rows[...], seq_cols[...], scale)
    out[...] = jnp.dot(
        probs.astype(jnp.bfloat16), value[...], preferred_element_type=jnp.float32
    ).astype(out.dtype)


def attend_back_kernel(
    scale, seq_rows, seq_cols, query, key, value, grad, grad_query, grad_key, grad_value
):
    @pl.when(pl.program_id(1) == 0)
    def _():
        grad_key[...] = jnp.zeros_like(grad_key)
        grad_value[...] = jnp.zeros_like(grad_value)

    probs = masked_probs(query[...], key[...], seq_rows[...], seq_cols[...], scale)
    grad_probs = lax.dot_general(
        grad[...], value[...], (((1,), (1,)), ((), ())), preferred_element_type=jnp.float32
    )
    spread = jnp.sum(probs * grad_probs, axis=-1, keepdims=True)
    grad_scores = (probs * (grad_probs - spread)).astype(jnp.bfloat16)
    grad_query[...] = (
        jnp.dot(grad_scores, key[...], preferred_element_type=jnp.float32) * scale
    )
    grad_key[...] += (
        lax.dot_general(
            grad_scores,
            query[...],
            (((0,), (0,)), ((), ())),
            preferred_element_type=jnp.float32,
        )
        * scale
    )
    grad_value[...] += lax.dot_general(
        probs.astype(jnp.bfloat16),
        grad[...],
        (((0,), (0,)), ((), ())),
        preferred_element_type=jnp.float32,
    )


def attention_specs(rows, block):
    per_block = pl.BlockSpec((block, HEAD_DIM), lambda h, i: (i, h))
    per_head = pl.BlockSpec((rows, HEAD_DIM), lambda h, i: (0, h))
    seqs = [
        pl.BlockSpec((block, 1), lambda h, i: (i, 0)),
        pl.BlockSpec((1, rows), lambda h, i: (0, 0)),
    ]
    return per_block, per_head, seqs


def attend(seq_ids, query, key, value):
    rows, width = query.shape
    block = math.gcd(rows, 256)
    per_block, per_head, seqs = attention_specs(rows, block)
    pairs = rows * rows * width
    return pl.pallas_call(
        partial(attend_kernel, 1.0 / math.sqrt(HEAD_DIM)),
        grid=(width // HEAD_DIM, rows // block),
        in_specs=seqs + [per_block, per_head, per_head],
        out_specs=per_block,
        out_shape=jax.ShapeDtypeStruct((rows, width), jnp.bfloat16),
        cost_estimate=pl.CostEstimate(
            flops=4 * pairs, bytes_accessed=8 * rows * width, transcendentals=pairs // HEAD_DIM
        ),
        compiler_params=pltpu.CompilerParams(vmem_limit_bytes=48 << 20),
        name="attend",
    )(seq_ids[:, None], seq_ids[None, :], query, key, value)


def attend_back(seq_ids, query, key, value, grad):
    rows, width = query.shape
    block = math.gcd(rows, 256)
    per_block, per_head, seqs = attention_specs(rows, block)
    pairs = rows * rows * width
    return pl.pallas_call(
        partial(attend_back_kernel, 1.0 / math.sqrt(HEAD_DIM)),
        grid=(width // HEAD_DIM, rows // block),
        in_specs=seqs + [per_block, per_head, per_head, per_block],
        out_specs=(per_block, per_head, per_head),
        out_shape=(jax.ShapeDtypeStruct((rows, width), jnp.float32),) * 3,
        cost_estimate=pl.CostEstimate(
            flops=10 * pairs, bytes_accessed=20 * rows * width, transcendentals=pairs // HEAD_DIM
        ),
        compiler_params=pltpu.CompilerParams(vmem_limit_bytes=48 << 20),
        name="attend_back",
    )(seq_ids[:, None], seq_ids[None, :], query, key, value, grad)


def dispatch_kernel(position, rows, out):
    columns, _, capacity, width = out.shape
    count = rows.shape[1]
    slots = lax.broadcasted_iota(jnp.int32, (columns, capacity, count), 1)
    select = jnp.where(slots == position[:, 0], 1.0, 0.0)
    select = select.reshape(columns * capacity, count).astype(jnp.bfloat16)
    step = math.gcd(width, 512)
    for at in range(0, width, step):
        part = jnp.dot(select, rows[0, :, at : at + step], preferred_element_type=jnp.float32)
        part = part.reshape(columns, capacity, step).astype(out.dtype)
        out[:, 0, :, at : at + step] = part


def dispatch(position, capacity, rows):
    columns, planes, count = position.shape
    width = rows.shape[1]
    return pl.pallas_call(
        dispatch_kernel,
        grid=(planes,),
        in_specs=[
            pl.BlockSpec((columns, 1, 1, count), lambda b: (0, b, 0, 0)),
            pl.BlockSpec((1, count, width), lambda b: (b, 0, 0)),
        ],
        out_specs=pl.BlockSpec((columns, 1, capacity, width), lambda b: (0, b, 0, 0)),
        out_shape=jax.ShapeDtypeStruct((columns, planes, capacity, width), jnp.bfloat16),
        cost_estimate=pl.CostEstimate(
            flops=2 * position.size * capacity * width,
            bytes_accessed=2 * columns * planes * capacity * width,
            transcendentals=0,
        ),
        compiler_params=pltpu.CompilerParams(vmem_limit_bytes=40 << 20),
        name="dispatch",
    )(position[:, :, None], rows.reshape(planes, count, width))


def heads_of(width):
    return [slice(at, at + HEAD_DIM) for at in range(0, width, HEAD_DIM)]


def turn_kernel(raw, scales, gains, cosine, sine, query, key, value):
    width = query.shape[1]
    for which, out in ((0, query), (1, key)):
        scale = scales[:, which : which + 1]
        for head in heads_of(width):
            part = raw[:, which * width + head.start : which * width + head.stop]
            part = part * scale * gains[which : which + 1, head]
            swapped = pltpu.roll(part, HEAD_DIM // 2, 1)
            out[:, head] = (part * cosine[...] + swapped * sine[...]).astype(out.dtype)
    value[...] = raw[:, 2 * width : 3 * width].astype(value.dtype)


def turn_back_kernel(
    raw, scales, gains, cosine, sine, grad_query, grad_key, out_query, out_key, dots, grad_gains
):
    @pl.when(pl.program_id(0) == 0)
    def _():
        grad_gains[...] = jnp.zeros_like(grad_gains)

    width = grad_query.shape[1]
    for which, grad, out in ((0, grad_query, out_query), (1, grad_key, out_key)):
        scale = scales[:, which : which + 1]
        total = jnp.zeros_like(scale)
        for head in heads_of(width):
            part = grad[:, head]
            part = part * cosine[...] - pltpu.roll(part, HEAD_DIM // 2, 1) * sine[...]
            hat = raw[:, which * width + head.start : which * width + head.stop] * scale
            grad_gains[which : which + 1, head] += jnp.sum(part * hat, axis=0, keepdims=True)
            part = part * gains[which : which + 1, head]
            total += jnp.sum(part * hat, axis=1, keepdims=True)
            out[:, head] = part
        dots[:, which : which + 1] = total


def turn_specs(raw, gains):
    block = math.gcd(raw.shape[0], 256)
    return block, [
        pl.BlockSpec((block, raw.shape[1]), lambda i: (i, 0)),
        pl.BlockSpec((block, 2), lambda i: (i, 0)),
        pl.BlockSpec(gains.shape, lambda i: (0, 0)),
        pl.BlockSpec((block, HEAD_DIM), lambda i: (i, 0)),
        pl.BlockSpec((block, HEAD_DIM), lambda i: (i, 0)),
    ]


def turn(raw, scales, gains, cosine, sine):
    rows, width = raw.shape[0], gains.shape[1]
    block, specs = turn_specs(raw, gains)
    return pl.pallas_call(
        turn_kernel,
        grid=(rows // block,),
        in_specs=specs,
        out_specs=(pl.BlockSpec((block, width), lambda i: (i, 0)),) * 3,
        out_shape=(jax.ShapeDtypeStruct((rows, width), jnp.bfloat16),) * 3,
        cost_estimate=pl.CostEstimate(
            flops=16 * rows * width, bytes_accessed=18 * rows * width, transcendentals=0
        ),
        compiler_params=pltpu.CompilerParams(vmem_limit_bytes=40 << 20),
        name="turn",
    )(raw, scales, gains, cosine, sine)


def turn_back(raw, scales, gains, cosine, sine, grad_query, grad_key):
    rows, width = grad_query.shape
    block, specs = turn_specs(raw, gains)
    wide = pl.BlockSpec((block, width), lambda i: (i, 0))
    f32 = jnp.float32
    return pl.pallas_call(
        turn_back_kernel,
        grid=(rows // block,),
        in_specs=specs + [wide, wide],
        out_specs=(
            wide,
            wide,
            pl.BlockSpec((block, 2), lambda i: (i, 0)),
            pl.BlockSpec((2, width), lambda i: (0, 0)),
        ),
        out_shape=(
            jax.ShapeDtypeStruct((rows, width), f32),
            jax.ShapeDtypeStruct((rows, width), f32),
            jax.ShapeDtypeStruct((rows, 2), f32),
            jax.ShapeDtypeStruct((2, width), f32),
        ),
        cost_estimate=pl.CostEstimate(
            flops=24 * rows * width, bytes_accessed=28 * rows * width, transcendentals=0
        ),
        compiler_params=pltpu.CompilerParams(vmem_limit_bytes=40 << 20),
        name="turn_back",
    )(raw, scales, gains, cosine, sine, grad_query, grad_key)


def expert_in_kernel(
    rows, gate, up, router, own, gate_out, up_out, act_out, picked_out
):
    logits = jnp.dot(rows[...], router[...], preferred_element_type=jnp.float32)
    weights = jnp.exp(logits - jnp.max(logits, axis=1, keepdims=True))
    picked = jnp.sum(weights * own[...], axis=1, keepdims=True)
    picked = picked / jnp.sum(weights, axis=1, keepdims=True)
    gate_pre = jnp.dot(rows[...], gate[...], preferred_element_type=jnp.float32)
    up_pre = jnp.dot(rows[...], up[...], preferred_element_type=jnp.float32)
    act = (gate_pre * jax.nn.sigmoid(gate_pre) * up_pre).astype(jnp.bfloat16)
    gate_out[...] = gate_pre
    up_out[...] = up_pre
    act_out[...] = (act.astype(jnp.float32) * picked).astype(jnp.bfloat16)
    picked_out[...] = picked


def expert_back_kernel(
    grad, gate_in, up_in, picked, gate, up, down, grad_gate, grad_up, grad_picked, grad_rows
):
    grad_raw = lax.dot_general(
        grad[...], down[...], (((1,), (1,)), ((), ())), preferred_element_type=jnp.float32
    )
    gate_pre, up_pre = gate_in[...], up_in[...]
    sigma = jax.nn.sigmoid(gate_pre)
    silu = gate_pre * sigma
    act = (silu * up_pre).astype(jnp.bfloat16).astype(jnp.float32)
    grad_picked[...] = jnp.sum(grad_raw * act, axis=1, keepdims=True)
    grad_act = grad_raw * picked[...]
    low_gate = (grad_act * up_pre * (sigma + silu * (1.0 - sigma))).astype(jnp.bfloat16)
    low_up = (grad_act * silu).astype(jnp.bfloat16)
    grad_gate[...] = low_gate
    grad_up[...] = low_up
    back = lax.dot_general(
        low_gate, gate[...], (((1,), (1,)), ((), ())), preferred_element_type=jnp.float32
    )
    back = back + lax.dot_general(
        low_up, up[...], (((1,), (1,)), ((), ())), preferred_element_type=jnp.float32
    )
    grad_rows[...] = back.astype(jnp.bfloat16)


def whole(shape):
    return pl.BlockSpec(shape, lambda i: (0, 0), pipeline_mode=pl.Buffered(1))


def row_blocks(block, width):
    return pl.BlockSpec((block, width), lambda i: (i, 0))


def expert_in(rows, gate, up, router, own, block):
    count, width = rows.shape
    hidden = gate.shape[1]
    narrow = row_blocks(block, hidden)
    f32 = jnp.float32
    return pl.pallas_call(
        expert_in_kernel,
        grid=(count // block,),
        in_specs=[
            row_blocks(block, width),
            whole(gate.shape),
            whole(up.shape),
            whole(router.shape),
            whole(own.shape),
        ],
        out_specs=(narrow, narrow, narrow, row_blocks(block, 1)),
        out_shape=(
            jax.ShapeDtypeStruct((count, hidden), f32),
            jax.ShapeDtypeStruct((count, hidden), f32),
            jax.ShapeDtypeStruct((count, hidden), jnp.bfloat16),
            jax.ShapeDtypeStruct((count, 1), f32),
        ),
        cost_estimate=pl.CostEstimate(
            flops=4 * count * width * hidden,
            bytes_accessed=2 * count * width + (10 * count + 4 * width) * hidden,
            transcendentals=count * hidden,
        ),
        compiler_params=pltpu.CompilerParams(vmem_limit_bytes=56 << 20),
        name="expert_in",
    )(rows, gate, up, router, own)


def expert_back(grad, gate_pre, up_pre, picked, gate, up, down, block):
    count, width = grad.shape
    hidden = down.shape[0]
    wide, narrow, one = [row_blocks(block, size) for size in (width, hidden, 1)]
    low = jax.ShapeDtypeStruct((count, hidden), jnp.bfloat16)
    return pl.pallas_call(
        expert_back_kernel,
        grid=(count // block,),
        in_specs=[wide, narrow, narrow, one, whole(gate.shape), whole(up.shape), whole(down.shape)],
        out_specs=(narrow, narrow, one, wide),
        out_shape=(
            low,
            low,
            jax.ShapeDtypeStruct((count, 1), jnp.float32),
            jax.ShapeDtypeStruct((count, width), jnp.bfloat16),
        ),
        cost_estimate=pl.CostEstimate(
            flops=6 * count * width * hidden,
            bytes_accessed=4 * count * width + (12 * count + 6 * width) * hidden,
            transcendentals=count * hidden,
        ),
        compiler_params=pltpu.CompilerParams(vmem_limit_bytes=58 << 20),
        name="expert_back",
    )(grad, gate_pre, up_pre, picked, gate, up, down)


def tie(array, *others):
    anywhere = pl.BlockSpec(memory_space=pl.ANY)
    return pl.pallas_call(
        lambda *refs: None,
        in_specs=[anywhere] * (1 + len(others)),
        out_specs=anywhere,
        out_shape=jax.ShapeDtypeStruct(array.shape, array.dtype),
        input_output_aliases={0: 0},
        name="tie",
    )(array, *others)


def mm(left, right):
    return jnp.dot(left, right, preferred_element_type=jnp.float32)


def mm_t(left, right):
    return lax.dot_general(
        left, right, (((1,), (1,)), ((), ())), preferred_element_type=jnp.float32
    )


def t_mm(left, right):
    return lax.dot_general(
        left, right, (((0,), (0,)), ((), ())), preferred_element_type=jnp.float32
    )


def plane_shards(
    hidden,
    token_order,
    lengths,
    routes,
    grad_output,
    w_query,
    w_key,
    w_value,
    w_out,
    w_router,
    attn_gain,
    ffn_gain,
    query_gain,
    key_gain,
    w_gate,
    w_up,
    w_down,
):
    f32, bf16 = jnp.float32, jnp.bfloat16
    both = ("ctx", "fsdp")
    planes = lax.axis_size("ctx")
    columns = lax.axis_size("fsdp")
    plane = lax.axis_index("ctx")
    row_count, width = hidden.shape[1:]
    group_rows = row_count * planes
    share = width // planes
    strip = w_query.shape[0]
    first_row = plane * row_count

    experts = w_router.shape[1]
    qkv = jnp.stack([w_query, w_key, w_value], axis=1).reshape(strip, 3, planes, share)
    qkv = qkv.transpose(2, 0, 1, 3).reshape(planes, strip, 3 * share)
    small = [w_router] + [g[:, None] for g in (attn_gain, ffn_gain, query_gain, key_gain)]
    small = jnp.concatenate(small + [routes.astype(bf16).reshape(strip, -1)], axis=1)
    spare = -small.shape[1] % 128
    small = jnp.pad(small, ((0, 0), (0, spare)))
    small = jnp.broadcast_to(small[None], (planes,) + small.shape)
    own_out = jnp.broadcast_to(w_out[None], (planes,) + w_out.shape)
    packed = jnp.concatenate([qkv, small, own_out], axis=2)
    packed = lax.all_to_all(packed, "ctx", 0, 0, tiled=True)
    hidden_all = lax.all_gather(tie(hidden[0], packed), "ctx", axis=0, tiled=True)
    packed, out_rows = packed[:, :, :-width], packed[:, :, -width:]
    routes_at = 3 * share + experts + 4
    routes_all = packed[:, :, routes_at : packed.shape[2] - spare].astype(jnp.int32)
    routes_all = routes_all.reshape(group_rows, -1)
    packed = jnp.broadcast_to(packed[None], (columns,) + packed.shape)
    packed = lax.all_to_all(packed, "fsdp", 0, 0, tiled=True)
    packed = packed.transpose(1, 0, 2, 3).reshape(width, -1)
    full_router = packed[:, 3 * share : 3 * share + experts]
    gain_attn, gain_ffn, gain_query, gain_key = [
        packed[:, 3 * share + experts + i].astype(f32) for i in range(4)
    ]
    def swap(part, step):
        return lax.ppermute(part, "ctx", [(i, i ^ step) for i in range(planes)])

    def by_plane(came):
        came = jnp.stack(came)
        return [came[plane ^ i] for i in range(planes)]

    def exchange(parts, first=None, last=None):
        came = [parts[plane]]
        for step in range(1, planes):
            part = parts[plane ^ step]
            part = swap(part if first is None else tie(part, first), step)
            came.append(part if last is None else tie(part, last))
        return by_plane(came)

    def exchange_after(parts, earlier):
        came = [
            swap(part if before is None else tie(part, before), step)
            for step, before in enumerate(earlier, 1)
            for part in [parts[plane ^ step]]
        ]
        return came, jnp.stack(by_plane([parts[plane]] + came)).astype(f32)

    def plane_sum(part):
        return part + sum(swap(part, step) for step in range(1, planes))

    out_rows = jnp.broadcast_to(out_rows[None], (columns,) + out_rows.shape)
    grad_all = lax.all_gather(
        tie(grad_output[0], hidden_all, packed, out_rows), "ctx", axis=0, tiled=True
    )
    full_out = lax.all_to_all(out_rows, "fsdp", 0, 0, tiled=True)

    seq_ids, places = seq_layout(token_order[0], lengths[0])
    experts_here = w_gate.shape[0]
    column_expert = experts_here * jnp.arange(columns, dtype=jnp.int32) + plane
    named = jnp.any(routes_all[:, :, None] == column_expert[None, None, :], axis=1)
    named = named.reshape(planes, row_count, columns)
    capacity = 5 * row_count * routes.shape[2] // (4 * experts)
    rank = jnp.cumsum(named.astype(jnp.int32), axis=1) - 1
    position = jnp.where(named, rank, -1).transpose(2, 0, 1)
    slots = jnp.arange(capacity, dtype=jnp.int32)
    holds = position[:, :, None, :] == slots[None, None, :, None]
    select = holds.astype(bf16)

    def combine(rows):
        rows = rows.reshape(columns, planes, capacity, width)
        sums = jnp.einsum("fbsr,fbsd->brd", select, rows, preferred_element_type=f32)
        return sums.reshape(group_rows, width).astype(bf16)


    frequency = rope_base ** (
        -2.0 * jnp.arange(HEAD_DIM // 2).astype(f32) / HEAD_DIM
    )
    angles = places.astype(f32)[:, None] * frequency[None, :]
    cosine, sine = jnp.cos(angles), jnp.sin(angles)
    cosine = jnp.concatenate([cosine, cosine], axis=1)
    sine = jnp.concatenate([-sine, sine], axis=1)
    hidden_wide = hidden_all.astype(f32)
    scale_one = lax.rsqrt(jnp.mean(hidden_wide * hidden_wide, axis=-1, keepdims=True) + epsilon)
    h_one = (hidden_wide * scale_one * gain_attn).astype(bf16)
    raw = mm(h_one, packed)
    squares = jnp.stack(
        [jnp.sum(raw[:, :share] ** 2, axis=1), jnp.sum(raw[:, share : 2 * share] ** 2, axis=1)]
    )
    squares = plane_sum(squares)
    scales = lax.rsqrt(squares / width + epsilon).T
    gains = lax.dynamic_slice_in_dim(
        jnp.stack([gain_query, gain_key]), plane * share, share, axis=1
    )
    query, key, values = turn(raw, scales, gains, cosine, sine)
    attended = attend(seq_ids, query, key, values)
    full_out = tie(full_out, attended).transpose(1, 0, 2, 3).reshape(width, width)
    grad_send = dispatch(position, capacity, tie(grad_all, attended, full_out))
    attended = attended.reshape(planes, row_count, share)
    attended = jnp.concatenate(exchange(attended, grad_all), axis=1)
    grad_in = lax.all_to_all(grad_send, "fsdp", 0, 0, tiled=True).reshape(-1, width)
    middle = hidden[0].astype(f32) + mm(attended, full_out)
    scale_two = lax.rsqrt(jnp.mean(middle * middle, axis=-1, keepdims=True) + epsilon)
    middle_hat = middle * scale_two
    h_two = (middle_hat * gain_ffn).astype(bf16)

    h_two_all = lax.all_gather(tie(h_two, grad_send), "ctx", axis=0, tiled=True)
    h_all = tie(h_two_all, grad_in)
    steps = range(1, planes)
    came_gate = [swap(tie(w_gate[plane ^ step], h_two_all), step) for step in steps]
    gate = jnp.concatenate(by_plane([w_gate[plane]] + came_gate))
    came_up = [
        swap(tie(w_up[plane ^ step], before), step) for step, before in zip(steps, came_gate)
    ]
    up = jnp.concatenate(by_plane([w_up[plane]] + came_up))
    came_down = [swap(tie(w_down[plane ^ step], *came_up), step) for step in steps]
    probs = jax.nn.softmax(mm(h_two, full_router), axis=-1)
    rows_in = lax.all_to_all(dispatch(position, capacity, h_all), "fsdp", 0, 0, tiled=True)
    rows_in = rows_in.reshape(-1, width)
    own = experts_here * lax.axis_index("fsdp") + plane
    own = (jnp.arange(experts)[None, :] == own).astype(f32)
    slot_block = planes * capacity
    gate_pre, up_pre, act_picked, picked = expert_in(
        rows_in, gate, up, full_router, own, slot_block
    )
    came_down = [tie(part, act_picked) for part in came_down]
    down = jnp.concatenate(by_plane([w_down[plane]] + came_down))
    grad_down_w = t_mm(act_picked, grad_in).astype(bf16)
    grad_gate, grad_up, grad_picked, grad_rows = expert_back(
        grad_in, tie(gate_pre, grad_down_w), up_pre, picked, gate, up, down, slot_block
    )

    def blocks(matrix):
        return matrix.reshape(planes, matrix.shape[0] // planes, matrix.shape[1])

    came, down_grad = exchange_after(blocks(grad_down_w), [None] * (planes - 1))
    grad_rows = tie(grad_rows, *came)
    grad_rows = lax.all_to_all(
        grad_rows.reshape(columns, planes * capacity, width), "fsdp", 0, 0, tiled=True
    )
    grad_gate_w = t_mm(rows_in, grad_gate).astype(bf16)
    grad_up_w = t_mm(rows_in, grad_up).astype(bf16)
    came, up_grad = exchange_after(blocks(grad_up_w), came)
    came, gate_grad = exchange_after(blocks(grad_gate_w), came)
    expert_out = mm(act_picked, down).astype(bf16)
    grad_picked = lax.all_to_all(
        tie(grad_picked, grad_rows).reshape(columns, planes, capacity), "fsdp", 0, 0, tiled=True
    )
    grad_rows = tie(grad_rows, *came, expert_out, grad_picked)
    expert_out = lax.all_to_all(
        expert_out.reshape(columns, planes * capacity, width), "fsdp", 0, 0, tiled=True
    )
    grad_h_two = lax.psum_scatter(
        combine(grad_rows), "ctx", scatter_dimension=0, tiled=True
    ).astype(f32)

    u_plane = jnp.sum(jnp.where(holds, grad_picked[..., None], 0.0), axis=2)
    u_mine = exchange(u_plane.transpose(1, 0, 2))
    u_mine = jnp.stack(u_mine, axis=1).reshape(experts, row_count).T
    grad_logits = probs * (u_mine - jnp.sum(probs * u_mine, axis=-1, keepdims=True))
    grad_logits = grad_logits.astype(bf16)
    grad_h_two = grad_h_two + mm_t(grad_logits, full_router)
    grad_router = t_mm(h_two, grad_logits)

    grad_top = grad_output[0].astype(f32)
    grad_ffn_gain = jnp.sum(grad_h_two * middle_hat, axis=0)
    grad_hat = grad_h_two * gain_ffn
    grad_middle = grad_top + scale_two * (
        grad_hat - middle_hat * jnp.mean(grad_hat * middle_hat, axis=-1, keepdims=True)
    )
    grad_branch = grad_middle.astype(bf16)
    def grad_heads(where):
        rows = lax.dynamic_slice_in_dim(full_out, where * share, share)
        return mm_t(grad_branch, rows).astype(bf16)

    came = [swap(grad_heads(plane ^ step), step) for step in range(1, planes)]
    grad_att = jnp.concatenate(by_plane([grad_heads(plane)] + came))
    grad_out_w = t_mm(attended, grad_branch).astype(bf16)
    grad_out_w = grad_out_w.reshape(planes, columns, strip, width).transpose(1, 0, 2, 3)
    mixed_part = combine(tie(expert_out, grad_att, grad_out_w))
    mixed = lax.psum_scatter(mixed_part, "ctx", scatter_dimension=0, tiled=True)
    output = (middle + mixed.astype(f32)).astype(bf16)
    grad_out_w = lax.all_to_all(
        tie(grad_out_w, mixed_part), "fsdp", 0, 0, tiled=True
    )
    grad_att = tie(grad_att, mixed_part)
    grad_query, grad_key, grad_value = attend_back(seq_ids, query, key, values, grad_att)
    grad_query, grad_key, dots, grad_gains = turn_back(
        raw, scales, gains, cosine, sine, grad_query, grad_key
    )
    dots = plane_sum(dots.T).T * (scales * scales) / width
    grad_qkv = jnp.concatenate(
        [
            scales[:, :1] * grad_query - raw[:, :share] * (scales[:, :1] * dots[:, :1]),
            scales[:, 1:] * grad_key - raw[:, share : 2 * share] * (scales[:, 1:] * dots[:, 1:]),
            grad_value,
        ],
        axis=1,
    ).astype(bf16)
    grad_part = mm_t(grad_qkv, packed[:, : 3 * share])
    sums = t_mm(h_one, grad_qkv).astype(bf16)
    sums = sums.reshape(planes, columns, strip, -1).transpose(1, 0, 2, 3)
    grad_h_one = lax.psum_scatter(
        tie(grad_part.astype(bf16), mixed, grad_out_w, sums), "ctx", scatter_dimension=0, tiled=True
    ).astype(f32)
    grad_attn_gain = jnp.sum(grad_part * (hidden_wide * scale_one), axis=0)
    rows_of = jnp.arange(planes)[:, None] == plane
    gains = [jnp.where(rows_of, g[None], 0.0).reshape(width) for g in grad_gains]
    gains = [g[:, None] for g in [grad_attn_gain, grad_ffn_gain] + gains]
    small = jnp.concatenate([grad_router] + gains, axis=1).reshape(planes * columns, -1)
    sums = lax.all_to_all(sums, "fsdp", 0, 0, tiled=True)
    small = lax.all_to_all(tie(small, sums), both, 0, 0, tiled=True)
    small = jnp.sum(small, axis=0).reshape(strip, -1)
    grad_out_w = jnp.sum(grad_out_w.astype(f32), axis=0).astype(bf16)
    sums = tie(jnp.sum(sums.astype(f32), axis=0).astype(bf16), grad_out_w, small)
    grad_out_w = sum(x.astype(f32) for x in exchange(grad_out_w, sums))
    sums = lax.all_to_all(sums, "ctx", 0, 0, tiled=True)
    grad_qkv_w = sums.reshape(planes, strip, 3, share).transpose(2, 1, 0, 3)
    grad_qkv_w = grad_qkv_w.reshape(3, strip, width).astype(f32)

    x_hat = hidden[0].astype(f32)
    scale_mine = lax.rsqrt(jnp.mean(x_hat * x_hat, axis=-1, keepdims=True) + epsilon)
    x_hat = x_hat * scale_mine
    grad_hat = grad_h_one * gain_attn
    grad_input = grad_middle + scale_mine * (
        grad_hat - x_hat * jnp.mean(grad_hat * x_hat, axis=-1, keepdims=True)
    )

    return (
        output[None],
        grad_input[None],
        grad_qkv_w[0],
        grad_qkv_w[1],
        grad_qkv_w[2],
        grad_out_w,
        small[:, :experts],
        small[:, experts],
        small[:, experts + 1],
        small[:, experts + 2],
        small[:, experts + 3],
        gate_grad,
        up_grad,
        down_grad,
    )


def solution(mesh):
    placed = (
        P("fsdp", "ctx", None),
        P("fsdp", None),
        P("fsdp", None),
        P("fsdp", "ctx", None),
        P("fsdp", "ctx", None),
        P(("ctx", "fsdp"), None),
        P(("ctx", "fsdp"), None),
        P(("ctx", "fsdp"), None),
        P(("ctx", "fsdp"), None),
        P(("ctx", "fsdp"), None),
        P(("ctx", "fsdp")),
        P(("ctx", "fsdp")),
        P(("ctx", "fsdp")),
        P(("ctx", "fsdp")),
        P("fsdp", "ctx", None),
        P("fsdp", "ctx", None),
        P("fsdp", "ctx", None),
    )

    def shards(*operands):
        experts_here = operands[14].shape[0]
        heads = operands[0].shape[2] // HEAD_DIM
        planes = mesh.shape["ctx"]
        whole_experts = experts_here == planes and heads % planes == 0 and planes in (2, 4)
        return (plane_shards if whole_experts else general_shards)(*operands)

    return jax.shard_map(
        shards,
        mesh=mesh,
        in_specs=placed,
        out_specs=(
            P("fsdp", "ctx", None),
            P("fsdp", "ctx", None),
            P(("ctx", "fsdp"), None),
            P(("ctx", "fsdp"), None),
            P(("ctx", "fsdp"), None),
            P(("ctx", "fsdp"), None),
            P(("ctx", "fsdp"), None),
            P(("ctx", "fsdp")),
            P(("ctx", "fsdp")),
            P(("ctx", "fsdp")),
            P(("ctx", "fsdp")),
            P("fsdp", "ctx", None),
            P("fsdp", "ctx", None),
            P("fsdp", "ctx", None),
        ),
        check_vma=False,
    )
```

```python
from functools import partial
import math

import jax
import jax.numpy as jnp
from jax import lax
from jax.experimental import pallas as pl
from jax.experimental.pallas import tpu as pltpu
from jax.sharding import PartitionSpec as P

HEAD_DIM = 128


epsilon = 1e-06
rope_base = 10000.0
masked_value = -1e30


def rms_scaled(values, gain):
    return values * lax.rsqrt(jnp.mean(values * values, axis=-1, keepdims=True) + epsilon) * gain


def rotate(values, places):
    row_count = values.shape[0]
    head_count = values.shape[1] // HEAD_DIM
    half_width = HEAD_DIM // 2
    frequency = rope_base ** (-2.0 * jnp.arange(half_width).astype(jnp.float32) / HEAD_DIM)
    angles = places.astype(jnp.float32)[:, None] * frequency[None, :]
    cosine = jnp.cos(angles)[:, None, :]
    sine_part = jnp.sin(angles)[:, None, :]
    split_heads = values.reshape(row_count, head_count, HEAD_DIM)
    first_half = split_heads[:, :, :half_width]
    second_half = split_heads[:, :, half_width:]
    turned = jnp.concatenate(
        [
            first_half * cosine - second_half * sine_part,
            second_half * cosine + first_half * sine_part,
        ],
        axis=-1,
    )
    return turned.reshape(row_count, head_count * HEAD_DIM)


def qk_post(values, gain, places):
    return rotate(rms_scaled(values, gain), places)


def route_weights(logits, chosen):
    router_probs = jax.nn.softmax(logits, axis=-1)
    return jnp.sum(jnp.where(chosen, router_probs[:, None, :], 0.0), axis=-1)


def seq_layout(order_row, seq_lengths):
    seq_ends = jnp.cumsum(seq_lengths)
    seq_ids = jnp.sum((order_row[:, None] >= seq_ends[None, :]).astype(jnp.int32), axis=1)
    starts = seq_ends - seq_lengths
    chosen = seq_ids[:, None] == jnp.arange(seq_lengths.shape[0], dtype=jnp.int32)[None, :]
    seq_start = jnp.sum(jnp.where(chosen, starts[None, :], 0), axis=1)
    return (seq_ids, order_row - seq_start)


def general_shards(
    hidden,
    token_order,
    lengths,
    routes,
    grad_output,
    w_query,
    w_key,
    w_value,
    w_out,
    w_router,
    attn_gain,
    ffn_gain,
    query_gain,
    key_gain,
    w_gate,
    w_up,
    w_down,
):
    hidden_in = hidden[0].astype(jnp.float32)
    row_count = hidden_in.shape[0]
    model_width = hidden_in.shape[1]
    head_count = model_width // HEAD_DIM
    score_scale = 1.0 / math.sqrt(HEAD_DIM)
    seq_all, place_all = seq_layout(token_order[0], lengths[0])
    first_row = lax.axis_index("ctx") * row_count
    seq_mine = lax.dynamic_slice_in_dim(seq_all, first_row, row_count)
    place_mine = lax.dynamic_slice_in_dim(place_all, first_row, row_count)
    same_seq = seq_mine[:, None] == seq_all[None, :]
    gathered = (
        lax.all_gather(w_query, ("ctx", "fsdp"), axis=0, tiled=True),
        lax.all_gather(w_key, ("ctx", "fsdp"), axis=0, tiled=True),
        lax.all_gather(w_value, ("ctx", "fsdp"), axis=0, tiled=True),
        lax.all_gather(w_out, ("ctx", "fsdp"), axis=0, tiled=True),
        lax.all_gather(w_router, ("ctx", "fsdp"), axis=0, tiled=True),
        lax.all_gather(attn_gain, ("ctx", "fsdp"), axis=0, tiled=True),
        lax.all_gather(ffn_gain, ("ctx", "fsdp"), axis=0, tiled=True),
        lax.all_gather(query_gain, ("ctx", "fsdp"), axis=0, tiled=True),
        lax.all_gather(key_gain, ("ctx", "fsdp"), axis=0, tiled=True),
    )
    (
        full_query,
        full_key,
        full_value,
        full_out,
        full_router,
        gain_attn,
        gain_ffn,
        gain_query,
        gain_key,
    ) = gathered
    gain_attn = gain_attn.astype(jnp.float32)
    gain_ffn = gain_ffn.astype(jnp.float32)
    gain_query = gain_query.astype(jnp.float32)
    gain_key = gain_key.astype(jnp.float32)
    h_one, norm_one_back = jax.vjp(rms_scaled, hidden_in, gain_attn)
    h_one_low = h_one.astype(jnp.bfloat16)
    query_raw = jnp.dot(h_one_low, full_query, preferred_element_type=jnp.float32)
    key_raw = jnp.dot(h_one_low, full_key, preferred_element_type=jnp.float32)
    values_low = jnp.dot(h_one_low, full_value, preferred_element_type=jnp.float32).astype(
        jnp.bfloat16
    )
    query_rot, query_back = jax.vjp(partial(qk_post, places=place_mine), query_raw, gain_query)
    key_rot, key_back = jax.vjp(partial(qk_post, places=place_mine), key_raw, gain_key)
    query_low = query_rot.astype(jnp.bfloat16)
    key_low = key_rot.astype(jnp.bfloat16)
    key_all, value_all = (
        lax.all_gather(key_low, "ctx", axis=0, tiled=True),
        lax.all_gather(values_low, "ctx", axis=0, tiled=True),
    )
    query_heads = query_low.reshape(row_count, head_count, HEAD_DIM)
    key_heads = key_all.reshape(-1, head_count, HEAD_DIM)
    value_heads = value_all.reshape(-1, head_count, HEAD_DIM)

    def scores_of():
        raw_scores = (
            jnp.einsum("thd,khd->htk", query_heads, key_heads, preferred_element_type=jnp.float32)
            * score_scale
        )
        return jnp.where(same_seq[None, :, :], raw_scores, masked_value)

    scores = scores_of()
    row_top = jnp.max(scores, axis=-1, keepdims=True)
    log_total = row_top + jnp.log(jnp.sum(jnp.exp(scores - row_top), axis=-1, keepdims=True))
    probs_low = jnp.exp(scores - log_total).astype(jnp.bfloat16)
    attended = jnp.einsum(
        "htk,khd->thd", probs_low, value_heads, preferred_element_type=jnp.float32
    )
    attended_low = attended.reshape(row_count, model_width).astype(jnp.bfloat16)
    middle = hidden_in + jnp.dot(attended_low, full_out, preferred_element_type=jnp.float32)
    h_two, norm_two_back = jax.vjp(rms_scaled, middle, gain_ffn)
    h_two_low = h_two.astype(jnp.bfloat16)
    logits = jnp.dot(h_two_low, full_router, preferred_element_type=jnp.float32)
    expert_count = full_router.shape[1]
    route_rows = routes[0]
    top_k = route_rows.shape[1]
    chosen = route_rows[:, :, None] == jnp.arange(expert_count, dtype=jnp.int32)[None, None, :]
    picked, route_back = jax.vjp(partial(route_weights, chosen=chosen), logits)
    pair_count = row_count * top_k
    capacity = 5 * row_count * top_k // (4 * expert_count)
    slot_count = expert_count * capacity
    group_size = lax.axis_size("fsdp")
    local_experts = w_gate.shape[0]
    pair_expert = route_rows.reshape(pair_count)
    one_hot = (pair_expert[:, None] == jnp.arange(expert_count, dtype=jnp.int32)[None, :]).astype(
        jnp.int32
    )
    slot_rank = jnp.sum(one_hot * (jnp.cumsum(one_hot, axis=0) - 1), axis=1)
    slot_ids = pair_expert * capacity + slot_rank
    source = (
        jnp.full((slot_count,), pair_count, jnp.int32)
        .at[slot_ids]
        .set(jnp.arange(pair_count, dtype=jnp.int32))
    )
    filled = source < pair_count
    source_pair = jnp.minimum(source, pair_count - 1)
    send_rows = jnp.where(
        filled[:, None], h_two_low[source_pair // top_k], jnp.zeros((), jnp.bfloat16)
    )
    send_rows = send_rows.reshape(group_size, local_experts, capacity, model_width)
    gate_full, up_full, down_full = (
        lax.all_gather(w_gate, "ctx", axis=1, tiled=True),
        lax.all_gather(w_up, "ctx", axis=1, tiled=True),
        lax.all_gather(w_down, "ctx", axis=1, tiled=True),
    )
    arrived_rows = lax.all_to_all(send_rows, "fsdp", split_axis=0, concat_axis=0, tiled=True)
    gate_part = jnp.einsum(
        "secd,edf->secf", arrived_rows, gate_full, preferred_element_type=jnp.float32
    )
    up_part = jnp.einsum(
        "secd,edf->secf", arrived_rows, up_full, preferred_element_type=jnp.float32
    )
    act_part = (jax.nn.silu(gate_part) * up_part).astype(jnp.bfloat16)
    result = jnp.einsum(
        "secf,efd->secd", act_part, down_full, preferred_element_type=jnp.float32
    ).astype(jnp.bfloat16)
    returned = lax.all_to_all(result, "fsdp", split_axis=0, concat_axis=0, tiled=True).reshape(
        slot_count, model_width
    )
    pair_out = returned[slot_ids].reshape(row_count, top_k, model_width)
    output = (middle + jnp.sum(picked[:, :, None] * pair_out, axis=1)).astype(jnp.bfloat16)
    grad_top = grad_output[0].astype(jnp.float32)
    grad_picked = jnp.sum(grad_top[:, None, :] * pair_out, axis=-1)
    grad_pair = (
        (picked[:, :, None] * grad_top[:, None, :])
        .astype(jnp.bfloat16)
        .reshape(pair_count, model_width)
    )
    grad_send = jnp.where(filled[:, None], grad_pair[source_pair], jnp.zeros((), jnp.bfloat16))
    grad_send = grad_send.reshape(group_size, local_experts, capacity, model_width)
    grad_arrived = lax.all_to_all(grad_send, "fsdp", split_axis=0, concat_axis=0, tiled=True)
    sigma = jax.nn.sigmoid(gate_part)
    act_low = (gate_part * sigma * up_part).astype(jnp.bfloat16)
    grad_act = jnp.einsum(
        "secd,efd->secf", grad_arrived, down_full, preferred_element_type=jnp.float32
    )
    grad_gate = (grad_act * up_part * sigma * (1.0 + gate_part * (1.0 - sigma))).astype(
        jnp.bfloat16
    )
    grad_up = (grad_act * gate_part * sigma).astype(jnp.bfloat16)
    grad_back = jnp.einsum(
        "secf,edf->secd", grad_gate, gate_full, preferred_element_type=jnp.float32
    )
    grad_back = (
        grad_back
        + jnp.einsum("secf,edf->secd", grad_up, up_full, preferred_element_type=jnp.float32)
    ).astype(jnp.bfloat16)
    grad_return = lax.all_to_all(
        grad_back, "fsdp", split_axis=0, concat_axis=0, tiled=True
    ).reshape(slot_count, model_width)
    grad_h_two = jnp.sum(
        grad_return[slot_ids].reshape(row_count, top_k, model_width).astype(jnp.float32), axis=1
    )
    (grad_logits,) = route_back(grad_picked)
    grad_logits_low = grad_logits.astype(jnp.bfloat16)
    grad_h_two = grad_h_two + jnp.einsum(
        "te,de->td", grad_logits_low, full_router, preferred_element_type=jnp.float32
    )
    grad_router = jnp.einsum(
        "td,te->de", h_two_low, grad_logits_low, preferred_element_type=jnp.float32
    )
    grad_middle, grad_ffn_gain = norm_two_back(grad_h_two)
    grad_middle = grad_middle + grad_top
    grad_branch = grad_middle.astype(jnp.bfloat16)
    grad_out_w = jnp.einsum(
        "td,te->de", attended_low, grad_branch, preferred_element_type=jnp.float32
    )
    grad_att = jnp.einsum(
        "te,de->td", grad_branch, full_out, preferred_element_type=jnp.float32
    ).astype(jnp.bfloat16)
    grad_att = grad_att.reshape(row_count, head_count, HEAD_DIM)
    scores = scores_of()
    probs_full = jnp.exp(scores - log_total)
    probs_again = probs_full.astype(jnp.bfloat16)
    grad_probs = jnp.einsum(
        "thd,khd->htk", grad_att, value_heads, preferred_element_type=jnp.float32
    )
    spread = jnp.sum(probs_full * grad_probs, axis=-1, keepdims=True)
    grad_scores = (probs_full * (grad_probs - spread)).astype(jnp.bfloat16)
    grad_query = (
        jnp.einsum(
            "htk,khd->thd", grad_scores, key_heads, preferred_element_type=jnp.float32
        ).reshape(row_count, model_width)
        * score_scale
    )
    grad_key_part = (
        jnp.einsum(
            "htk,thd->khd", grad_scores, query_heads, preferred_element_type=jnp.float32
        ).reshape(-1, model_width)
        * score_scale
    )
    grad_value_part = jnp.einsum(
        "htk,thd->khd", probs_again, grad_att, preferred_element_type=jnp.float32
    ).reshape(-1, model_width)
    grad_key, grad_value = (
        lax.psum_scatter(
            grad_key_part.astype(jnp.bfloat16), "ctx", scatter_dimension=0, tiled=True
        ).astype(jnp.float32),
        lax.psum_scatter(
            grad_value_part.astype(jnp.bfloat16), "ctx", scatter_dimension=0, tiled=True
        ).astype(jnp.float32),
    )
    grad_q_raw, grad_q_gain = query_back(grad_query)
    grad_k_raw, grad_k_gain = key_back(grad_key)
    grad_q_low = grad_q_raw.astype(jnp.bfloat16)
    grad_k_low = grad_k_raw.astype(jnp.bfloat16)
    grad_v_low = grad_value.astype(jnp.bfloat16)
    grad_query_w = jnp.einsum(
        "td,te->de", h_one_low, grad_q_low, preferred_element_type=jnp.float32
    )
    grad_key_w = jnp.einsum("td,te->de", h_one_low, grad_k_low, preferred_element_type=jnp.float32)
    grad_value_w = jnp.einsum(
        "td,te->de", h_one_low, grad_v_low, preferred_element_type=jnp.float32
    )
    grad_h_one = jnp.einsum("te,de->td", grad_q_low, full_query, preferred_element_type=jnp.float32)
    grad_h_one = grad_h_one + jnp.einsum(
        "te,de->td", grad_k_low, full_key, preferred_element_type=jnp.float32
    )
    grad_h_one = grad_h_one + jnp.einsum(
        "te,de->td", grad_v_low, full_value, preferred_element_type=jnp.float32
    )
    grad_input_norm, grad_attn_gain = norm_one_back(grad_h_one)
    grad_input = grad_middle + grad_input_norm
    totals = (
        lax.psum_scatter(grad_query_w, ("ctx", "fsdp"), scatter_dimension=0, tiled=True),
        lax.psum_scatter(grad_key_w, ("ctx", "fsdp"), scatter_dimension=0, tiled=True),
        lax.psum_scatter(grad_value_w, ("ctx", "fsdp"), scatter_dimension=0, tiled=True),
        lax.psum_scatter(grad_out_w, ("ctx", "fsdp"), scatter_dimension=0, tiled=True),
        lax.psum_scatter(grad_router, ("ctx", "fsdp"), scatter_dimension=0, tiled=True),
        lax.psum_scatter(grad_attn_gain, ("ctx", "fsdp"), scatter_dimension=0, tiled=True),
        lax.psum_scatter(grad_ffn_gain, ("ctx", "fsdp"), scatter_dimension=0, tiled=True),
        lax.psum_scatter(grad_q_gain, ("ctx", "fsdp"), scatter_dimension=0, tiled=True),
        lax.psum_scatter(grad_k_gain, ("ctx", "fsdp"), scatter_dimension=0, tiled=True),
    )
    grad_down_w = jnp.einsum(
        "secf,secd->efd", act_low, grad_arrived, preferred_element_type=jnp.float32
    )
    grad_gate_w = jnp.einsum(
        "secd,secf->edf", arrived_rows, grad_gate, preferred_element_type=jnp.float32
    )
    grad_up_w = jnp.einsum(
        "secd,secf->edf", arrived_rows, grad_up, preferred_element_type=jnp.float32
    )
    gate_grad, up_grad, down_grad = (
        lax.psum_scatter(
            grad_gate_w.astype(jnp.bfloat16), "ctx", scatter_dimension=1, tiled=True
        ).astype(jnp.float32),
        lax.psum_scatter(
            grad_up_w.astype(jnp.bfloat16), "ctx", scatter_dimension=1, tiled=True
        ).astype(jnp.float32),
        lax.psum_scatter(
            grad_down_w.astype(jnp.bfloat16), "ctx", scatter_dimension=1, tiled=True
        ).astype(jnp.float32),
    )
    return (
        output[None],
        grad_input[None],
        totals[0],
        totals[1],
        totals[2],
        totals[3],
        totals[4],
        totals[5],
        totals[6],
        totals[7],
        totals[8],
        gate_grad,
        up_grad,
        down_grad,
    )


def masked_probs(query, key, seq_rows, seq_cols, scale):
    scores = (
        lax.dot_general(query, key, (((1,), (1,)), ((), ())), preferred_element_type=jnp.float32)
        * scale
    )
    scores = jnp.where(seq_rows == seq_cols, scores, masked_value)
    top = jnp.max(scores, axis=-1, keepdims=True)
    weights = jnp.exp(scores - top)
    return weights / jnp.sum(weights, axis=-1, keepdims=True)


def attend_kernel(scale, seq_rows, seq_cols, query, key, value, out):
    probs = masked_probs(query[...], key[...], seq_rows[...], seq_cols[...], scale)
    out[...] = jnp.dot(
        probs.astype(jnp.bfloat16), value[...], preferred_element_type=jnp.float32
    ).astype(out.dtype)


def attend_back_kernel(
    scale, seq_rows, seq_cols, query, key, value, grad, grad_query, grad_key, grad_value
):
    @pl.when(pl.program_id(1) == 0)
    def _():
        grad_key[...] = jnp.zeros_like(grad_key)
        grad_value[...] = jnp.zeros_like(grad_value)

    probs = masked_probs(query[...], key[...], seq_rows[...], seq_cols[...], scale)
    grad_probs = lax.dot_general(
        grad[...], value[...], (((1,), (1,)), ((), ())), preferred_element_type=jnp.float32
    )
    spread = jnp.sum(probs * grad_probs, axis=-1, keepdims=True)
    grad_scores = (probs * (grad_probs - spread)).astype(jnp.bfloat16)
    grad_query[...] = (
        jnp.dot(grad_scores, key[...], preferred_element_type=jnp.float32) * scale
    )
    grad_key[...] += (
        lax.dot_general(
            grad_scores,
            query[...],
            (((0,), (0,)), ((), ())),
            preferred_element_type=jnp.float32,
        )
        * scale
    )
    grad_value[...] += lax.dot_general(
        probs.astype(jnp.bfloat16),
        grad[...],
        (((0,), (0,)), ((), ())),
        preferred_element_type=jnp.float32,
    )


def attention_specs(rows, block):
    per_block = pl.BlockSpec((block, HEAD_DIM), lambda h, i: (i, h))
    per_head = pl.BlockSpec((rows, HEAD_DIM), lambda h, i: (0, h))
    seqs = [
        pl.BlockSpec((block, 1), lambda h, i: (i, 0)),
        pl.BlockSpec((1, rows), lambda h, i: (0, 0)),
    ]
    return per_block, per_head, seqs


def attend(seq_ids, query, key, value):
    rows, width = query.shape
    block = math.gcd(rows, 256)
    per_block, per_head, seqs = attention_specs(rows, block)
    pairs = rows * rows * width
    return pl.pallas_call(
        partial(attend_kernel, 1.0 / math.sqrt(HEAD_DIM)),
        grid=(width // HEAD_DIM, rows // block),
        in_specs=seqs + [per_block, per_head, per_head],
        out_specs=per_block,
        out_shape=jax.ShapeDtypeStruct((rows, width), jnp.bfloat16),
        cost_estimate=pl.CostEstimate(
            flops=4 * pairs, bytes_accessed=8 * rows * width, transcendentals=pairs // HEAD_DIM
        ),
        compiler_params=pltpu.CompilerParams(vmem_limit_bytes=48 << 20),
        name="attend",
    )(seq_ids[:, None], seq_ids[None, :], query, key, value)


def attend_back(seq_ids, query, key, value, grad):
    rows, width = query.shape
    block = math.gcd(rows, 256)
    per_block, per_head, seqs = attention_specs(rows, block)
    pairs = rows * rows * width
    return pl.pallas_call(
        partial(attend_back_kernel, 1.0 / math.sqrt(HEAD_DIM)),
        grid=(width // HEAD_DIM, rows // block),
        in_specs=seqs + [per_block, per_head, per_head, per_block],
        out_specs=(per_block, per_head, per_head),
        out_shape=(jax.ShapeDtypeStruct((rows, width), jnp.float32),) * 3,
        cost_estimate=pl.CostEstimate(
            flops=10 * pairs, bytes_accessed=20 * rows * width, transcendentals=pairs // HEAD_DIM
        ),
        compiler_params=pltpu.CompilerParams(vmem_limit_bytes=48 << 20),
        name="attend_back",
    )(seq_ids[:, None], seq_ids[None, :], query, key, value, grad)


def dispatch_kernel(position, rows, out):
    columns, _, capacity, width = out.shape
    count = rows.shape[1]
    slots = lax.broadcasted_iota(jnp.int32, (columns, capacity, count), 1)
    select = jnp.where(slots == position[:, 0], 1.0, 0.0)
    select = select.reshape(columns * capacity, count).astype(jnp.bfloat16)
    step = math.gcd(width, 512)
    for at in range(0, width, step):
        part = jnp.dot(select, rows[0, :, at : at + step], preferred_element_type=jnp.float32)
        part = part.reshape(columns, capacity, step).astype(out.dtype)
        out[:, 0, :, at : at + step] = part


def dispatch(position, capacity, rows):
    columns, planes, count = position.shape
    width = rows.shape[1]
    return pl.pallas_call(
        dispatch_kernel,
        grid=(planes,),
        in_specs=[
            pl.BlockSpec((columns, 1, 1, count), lambda b: (0, b, 0, 0)),
            pl.BlockSpec((1, count, width), lambda b: (b, 0, 0)),
        ],
        out_specs=pl.BlockSpec((columns, 1, capacity, width), lambda b: (0, b, 0, 0)),
        out_shape=jax.ShapeDtypeStruct((columns, planes, capacity, width), jnp.bfloat16),
        cost_estimate=pl.CostEstimate(
            flops=2 * position.size * capacity * width,
            bytes_accessed=2 * columns * planes * capacity * width,
            transcendentals=0,
        ),
        compiler_params=pltpu.CompilerParams(vmem_limit_bytes=40 << 20),
        name="dispatch",
    )(position[:, :, None], rows.reshape(planes, count, width))


def heads_of(width):
    return [slice(at, at + HEAD_DIM) for at in range(0, width, HEAD_DIM)]


def turn_kernel(raw, scales, gains, cosine, sine, query, key, value):
    width = query.shape[1]
    for which, out in ((0, query), (1, key)):
        scale = scales[:, which : which + 1]
        for head in heads_of(width):
            part = raw[:, which * width + head.start : which * width + head.stop]
            part = part * scale * gains[which : which + 1, head]
            swapped = pltpu.roll(part, HEAD_DIM // 2, 1)
            out[:, head] = (part * cosine[...] + swapped * sine[...]).astype(out.dtype)
    value[...] = raw[:, 2 * width : 3 * width].astype(value.dtype)


def turn_back_kernel(
    raw, scales, gains, cosine, sine, grad_query, grad_key, out_query, out_key, dots, grad_gains
):
    @pl.when(pl.program_id(0) == 0)
    def _():
        grad_gains[...] = jnp.zeros_like(grad_gains)

    width = grad_query.shape[1]
    for which, grad, out in ((0, grad_query, out_query), (1, grad_key, out_key)):
        scale = scales[:, which : which + 1]
        total = jnp.zeros_like(scale)
        for head in heads_of(width):
            part = grad[:, head]
            part = part * cosine[...] - pltpu.roll(part, HEAD_DIM // 2, 1) * sine[...]
            hat = raw[:, which * width + head.start : which * width + head.stop] * scale
            grad_gains[which : which + 1, head] += jnp.sum(part * hat, axis=0, keepdims=True)
            part = part * gains[which : which + 1, head]
            total += jnp.sum(part * hat, axis=1, keepdims=True)
            out[:, head] = part
        dots[:, which : which + 1] = total


def turn_specs(raw, gains):
    block = math.gcd(raw.shape[0], 256)
    return block, [
        pl.BlockSpec((block, raw.shape[1]), lambda i: (i, 0)),
        pl.BlockSpec((block, 2), lambda i: (i, 0)),
        pl.BlockSpec(gains.shape, lambda i: (0, 0)),
        pl.BlockSpec((block, HEAD_DIM), lambda i: (i, 0)),
        pl.BlockSpec((block, HEAD_DIM), lambda i: (i, 0)),
    ]


def turn(raw, scales, gains, cosine, sine):
    rows, width = raw.shape[0], gains.shape[1]
    block, specs = turn_specs(raw, gains)
    return pl.pallas_call(
        turn_kernel,
        grid=(rows // block,),
        in_specs=specs,
        out_specs=(pl.BlockSpec((block, width), lambda i: (i, 0)),) * 3,
        out_shape=(jax.ShapeDtypeStruct((rows, width), jnp.bfloat16),) * 3,
        cost_estimate=pl.CostEstimate(
            flops=16 * rows * width, bytes_accessed=18 * rows * width, transcendentals=0
        ),
        compiler_params=pltpu.CompilerParams(vmem_limit_bytes=40 << 20),
        name="turn",
    )(raw, scales, gains, cosine, sine)


def turn_back(raw, scales, gains, cosine, sine, grad_query, grad_key):
    rows, width = grad_query.shape
    block, specs = turn_specs(raw, gains)
    wide = pl.BlockSpec((block, width), lambda i: (i, 0))
    f32 = jnp.float32
    return pl.pallas_call(
        turn_back_kernel,
        grid=(rows // block,),
        in_specs=specs + [wide, wide],
        out_specs=(
            wide,
            wide,
            pl.BlockSpec((block, 2), lambda i: (i, 0)),
            pl.BlockSpec((2, width), lambda i: (0, 0)),
        ),
        out_shape=(
            jax.ShapeDtypeStruct((rows, width), f32),
            jax.ShapeDtypeStruct((rows, width), f32),
            jax.ShapeDtypeStruct((rows, 2), f32),
            jax.ShapeDtypeStruct((2, width), f32),
        ),
        cost_estimate=pl.CostEstimate(
            flops=24 * rows * width, bytes_accessed=28 * rows * width, transcendentals=0
        ),
        compiler_params=pltpu.CompilerParams(vmem_limit_bytes=40 << 20),
        name="turn_back",
    )(raw, scales, gains, cosine, sine, grad_query, grad_key)


def expert_in_kernel(
    rows, gate, up, router, own, gate_out, up_out, act_out, picked_out
):
    logits = jnp.dot(rows[...], router[...], preferred_element_type=jnp.float32)
    weights = jnp.exp(logits - jnp.max(logits, axis=1, keepdims=True))
    picked = jnp.sum(weights * own[...], axis=1, keepdims=True)
    picked = picked / jnp.sum(weights, axis=1, keepdims=True)
    gate_pre = jnp.dot(rows[...], gate[...], preferred_element_type=jnp.float32)
    up_pre = jnp.dot(rows[...], up[...], preferred_element_type=jnp.float32)
    act = (gate_pre * jax.nn.sigmoid(gate_pre) * up_pre).astype(jnp.bfloat16)
    gate_out[...] = gate_pre
    up_out[...] = up_pre
    act_out[...] = (act.astype(jnp.float32) * picked).astype(jnp.bfloat16)
    picked_out[...] = picked


def expert_back_kernel(
    grad, gate_in, up_in, picked, gate, up, down, grad_gate, grad_up, grad_picked, grad_rows
):
    grad_raw = lax.dot_general(
        grad[...], down[...], (((1,), (1,)), ((), ())), preferred_element_type=jnp.float32
    )
    gate_pre, up_pre = gate_in[...], up_in[...]
    sigma = jax.nn.sigmoid(gate_pre)
    silu = gate_pre * sigma
    act = (silu * up_pre).astype(jnp.bfloat16).astype(jnp.float32)
    grad_picked[...] = jnp.sum(grad_raw * act, axis=1, keepdims=True)
    grad_act = grad_raw * picked[...]
    low_gate = (grad_act * up_pre * (sigma + silu * (1.0 - sigma))).astype(jnp.bfloat16)
    low_up = (grad_act * silu).astype(jnp.bfloat16)
    grad_gate[...] = low_gate
    grad_up[...] = low_up
    back = lax.dot_general(
        low_gate, gate[...], (((1,), (1,)), ((), ())), preferred_element_type=jnp.float32
    )
    back = back + lax.dot_general(
        low_up, up[...], (((1,), (1,)), ((), ())), preferred_element_type=jnp.float32
    )
    grad_rows[...] = back.astype(jnp.bfloat16)


def whole(shape):
    return pl.BlockSpec(shape, lambda i: (0, 0), pipeline_mode=pl.Buffered(1))


def row_blocks(block, width):
    return pl.BlockSpec((block, width), lambda i: (i, 0))


def expert_in(rows, gate, up, router, own, block):
    count, width = rows.shape
    hidden = gate.shape[1]
    narrow = row_blocks(block, hidden)
    f32 = jnp.float32
    return pl.pallas_call(
        expert_in_kernel,
        grid=(count // block,),
        in_specs=[
            row_blocks(block, width),
            whole(gate.shape),
            whole(up.shape),
            whole(router.shape),
            whole(own.shape),
        ],
        out_specs=(narrow, narrow, narrow, row_blocks(block, 1)),
        out_shape=(
            jax.ShapeDtypeStruct((count, hidden), f32),
            jax.ShapeDtypeStruct((count, hidden), f32),
            jax.ShapeDtypeStruct((count, hidden), jnp.bfloat16),
            jax.ShapeDtypeStruct((count, 1), f32),
        ),
        cost_estimate=pl.CostEstimate(
            flops=4 * count * width * hidden,
            bytes_accessed=2 * count * width + (10 * count + 4 * width) * hidden,
            transcendentals=count * hidden,
        ),
        compiler_params=pltpu.CompilerParams(vmem_limit_bytes=56 << 20),
        name="expert_in",
    )(rows, gate, up, router, own)


def expert_back(grad, gate_pre, up_pre, picked, gate, up, down, block):
    count, width = grad.shape
    hidden = down.shape[0]
    wide, narrow, one = [row_blocks(block, size) for size in (width, hidden, 1)]
    low = jax.ShapeDtypeStruct((count, hidden), jnp.bfloat16)
    return pl.pallas_call(
        expert_back_kernel,
        grid=(count // block,),
        in_specs=[wide, narrow, narrow, one, whole(gate.shape), whole(up.shape), whole(down.shape)],
        out_specs=(narrow, narrow, one, wide),
        out_shape=(
            low,
            low,
            jax.ShapeDtypeStruct((count, 1), jnp.float32),
            jax.ShapeDtypeStruct((count, width), jnp.bfloat16),
        ),
        cost_estimate=pl.CostEstimate(
            flops=6 * count * width * hidden,
            bytes_accessed=4 * count * width + (12 * count + 6 * width) * hidden,
            transcendentals=count * hidden,
        ),
        compiler_params=pltpu.CompilerParams(vmem_limit_bytes=58 << 20),
        name="expert_back",
    )(grad, gate_pre, up_pre, picked, gate, up, down)


def tie(array, *others):
    anywhere = pl.BlockSpec(memory_space=pl.ANY)
    return pl.pallas_call(
        lambda *refs: None,
        in_specs=[anywhere] * (1 + len(others)),
        out_specs=anywhere,
        out_shape=jax.ShapeDtypeStruct(array.shape, array.dtype),
        input_output_aliases={0: 0},
        name="tie",
    )(array, *others)


def mm(left, right):
    return jnp.dot(left, right, preferred_element_type=jnp.float32)


def mm_t(left, right):
    return lax.dot_general(
        left, right, (((1,), (1,)), ((), ())), preferred_element_type=jnp.float32
    )


def t_mm(left, right):
    return lax.dot_general(
        left, right, (((0,), (0,)), ((), ())), preferred_element_type=jnp.float32
    )


def plane_shards(
    hidden,
    token_order,
    lengths,
    routes,
    grad_output,
    w_query,
    w_key,
    w_value,
    w_out,
    w_router,
    attn_gain,
    ffn_gain,
    query_gain,
    key_gain,
    w_gate,
    w_up,
    w_down,
):
    f32, bf16 = jnp.float32, jnp.bfloat16
    both = ("ctx", "fsdp")
    planes = lax.axis_size("ctx")
    columns = lax.axis_size("fsdp")
    plane = lax.axis_index("ctx")
    row_count, width = hidden.shape[1:]
    group_rows = row_count * planes
    share = width // planes
    strip = w_query.shape[0]
    first_row = plane * row_count

    experts = w_router.shape[1]
    qkv = jnp.stack([w_query, w_key, w_value], axis=1).reshape(strip, 3, planes, share)
    qkv = qkv.transpose(2, 0, 1, 3).reshape(planes, strip, 3 * share)
    small = [w_router] + [g[:, None] for g in (attn_gain, ffn_gain, query_gain, key_gain)]
    small = jnp.concatenate(small + [routes.astype(bf16).reshape(strip, -1)], axis=1)
    spare = -small.shape[1] % 128
    small = jnp.pad(small, ((0, 0), (0, spare)))
    small = jnp.broadcast_to(small[None], (planes,) + small.shape)
    own_out = jnp.broadcast_to(w_out[None], (planes,) + w_out.shape)
    packed = jnp.concatenate([qkv, small, own_out], axis=2)
    packed = lax.all_to_all(packed, "ctx", 0, 0, tiled=True)
    hidden_all = lax.all_gather(tie(hidden[0], packed), "ctx", axis=0, tiled=True)
    packed, out_rows = packed[:, :, :-width], packed[:, :, -width:]
    routes_at = 3 * share + experts + 4
    routes_all = packed[:, :, routes_at : packed.shape[2] - spare].astype(jnp.int32)
    routes_all = routes_all.reshape(group_rows, -1)
    packed = jnp.broadcast_to(packed[None], (columns,) + packed.shape)
    packed = lax.all_to_all(packed, "fsdp", 0, 0, tiled=True)
    packed = packed.transpose(1, 0, 2, 3).reshape(width, -1)
    full_router = packed[:, 3 * share : 3 * share + experts]
    gain_attn, gain_ffn, gain_query, gain_key = [
        packed[:, 3 * share + experts + i].astype(f32) for i in range(4)
    ]
    def swap(part, step):
        return lax.ppermute(part, "ctx", [(i, i ^ step) for i in range(planes)])

    def by_plane(came):
        came = jnp.stack(came)
        return [came[plane ^ i] for i in range(planes)]

    def exchange(parts, first=None, last=None):
        came = [parts[plane]]
        for step in range(1, planes):
            part = parts[plane ^ step]
            part = swap(part if first is None else tie(part, first), step)
            came.append(part if last is None else tie(part, last))
        return by_plane(came)

    def exchange_after(parts, earlier):
        came = [
            swap(part if before is None else tie(part, before), step)
            for step, before in enumerate(earlier, 1)
            for part in [parts[plane ^ step]]
        ]
        return came, jnp.stack(by_plane([parts[plane]] + came)).astype(f32)

    def plane_sum(part):
        return part + sum(swap(part, step) for step in range(1, planes))

    out_rows = jnp.broadcast_to(out_rows[None], (columns,) + out_rows.shape)
    grad_all = lax.all_gather(
        tie(grad_output[0], hidden_all, packed, out_rows), "ctx", axis=0, tiled=True
    )
    full_out = lax.all_to_all(out_rows, "fsdp", 0, 0, tiled=True)

    seq_ids, places = seq_layout(token_order[0], lengths[0])
    experts_here = w_gate.shape[0]
    column_expert = experts_here * jnp.arange(columns, dtype=jnp.int32) + plane
    named = jnp.any(routes_all[:, :, None] == column_expert[None, None, :], axis=1)
    named = named.reshape(planes, row_count, columns)
    capacity = 5 * row_count * routes.shape[2] // (4 * experts)
    rank = jnp.cumsum(named.astype(jnp.int32), axis=1) - 1
    position = jnp.where(named, rank, -1).transpose(2, 0, 1)
    slots = jnp.arange(capacity, dtype=jnp.int32)
    holds = position[:, :, None, :] == slots[None, None, :, None]
    select = holds.astype(bf16)

    def combine(rows):
        rows = rows.reshape(columns, planes, capacity, width)
        sums = jnp.einsum("fbsr,fbsd->brd", select, rows, preferred_element_type=f32)
        return sums.reshape(group_rows, width).astype(bf16)


    frequency = rope_base ** (
        -2.0 * jnp.arange(HEAD_DIM // 2).astype(f32) / HEAD_DIM
    )
    angles = places.astype(f32)[:, None] * frequency[None, :]
    cosine, sine = jnp.cos(angles), jnp.sin(angles)
    cosine = jnp.concatenate([cosine, cosine], axis=1)
    sine = jnp.concatenate([-sine, sine], axis=1)
    hidden_wide = hidden_all.astype(f32)
    scale_one = lax.rsqrt(jnp.mean(hidden_wide * hidden_wide, axis=-1, keepdims=True) + epsilon)
    h_one = (hidden_wide * scale_one * gain_attn).astype(bf16)
    raw = mm(h_one, packed)
    squares = jnp.stack(
        [jnp.sum(raw[:, :share] ** 2, axis=1), jnp.sum(raw[:, share : 2 * share] ** 2, axis=1)]
    )
    squares = plane_sum(squares)
    scales = lax.rsqrt(squares / width + epsilon).T
    gains = lax.dynamic_slice_in_dim(
        jnp.stack([gain_query, gain_key]), plane * share, share, axis=1
    )
    query, key, values = turn(raw, scales, gains, cosine, sine)
    attended = attend(seq_ids, query, key, values)
    full_out = tie(full_out, attended).transpose(1, 0, 2, 3).reshape(width, width)
    grad_send = dispatch(position, capacity, tie(grad_all, attended, full_out))
    attended = attended.reshape(planes, row_count, share)
    attended = jnp.concatenate(exchange(attended, grad_all), axis=1)
    grad_in = lax.all_to_all(grad_send, "fsdp", 0, 0, tiled=True).reshape(-1, width)
    middle = hidden[0].astype(f32) + mm(attended, full_out)
    scale_two = lax.rsqrt(jnp.mean(middle * middle, axis=-1, keepdims=True) + epsilon)
    middle_hat = middle * scale_two
    h_two = (middle_hat * gain_ffn).astype(bf16)

    h_two_all = lax.all_gather(tie(h_two, grad_send), "ctx", axis=0, tiled=True)
    steps = range(1, planes)
    came_gate = [swap(tie(w_gate[plane ^ step], h_two_all), step) for step in steps]
    h_all = tie(h_two_all, grad_in, came_gate[planes // 2 - 1])
    gate = jnp.concatenate(by_plane([w_gate[plane]] + came_gate))
    came_up = [
        swap(tie(w_up[plane ^ step], before), step) for step, before in zip(steps, came_gate)
    ]
    up = jnp.concatenate(by_plane([w_up[plane]] + came_up))
    came_down = [swap(tie(w_down[plane ^ step], *came_up), step) for step in steps]
    probs = jax.nn.softmax(mm(h_two, full_router), axis=-1)
    rows_in = lax.all_to_all(dispatch(position, capacity, h_all), "fsdp", 0, 0, tiled=True)
    rows_in = rows_in.reshape(-1, width)
    own = experts_here * lax.axis_index("fsdp") + plane
    own = (jnp.arange(experts)[None, :] == own).astype(f32)
    slot_block = planes * capacity
    gate_pre, up_pre, act_picked, picked = expert_in(
        rows_in, gate, up, full_router, own, slot_block
    )
    came_down = [tie(part, act_picked) for part in came_down]
    down = jnp.concatenate(by_plane([w_down[plane]] + came_down))
    grad_down_w = t_mm(act_picked, grad_in).astype(bf16)
    grad_gate, grad_up, grad_picked, grad_rows = expert_back(
        grad_in, tie(gate_pre, grad_down_w), up_pre, picked, gate, up, down, slot_block
    )

    def blocks(matrix):
        return matrix.reshape(planes, matrix.shape[0] // planes, matrix.shape[1])

    came, down_grad = exchange_after(blocks(grad_down_w), [None] * (planes - 1))
    grad_rows = tie(grad_rows, *came)
    grad_rows = lax.all_to_all(
        grad_rows.reshape(columns, planes * capacity, width), "fsdp", 0, 0, tiled=True
    )
    grad_gate_w = t_mm(rows_in, grad_gate).astype(bf16)
    grad_up_w = t_mm(rows_in, grad_up).astype(bf16)
    came, up_grad = exchange_after(blocks(grad_up_w), came)
    came, gate_grad = exchange_after(blocks(grad_gate_w), came)
    expert_out = mm(act_picked, down).astype(bf16)
    grad_picked = lax.all_to_all(
        tie(grad_picked, grad_rows).reshape(columns, planes, capacity), "fsdp", 0, 0, tiled=True
    )
    grad_rows = tie(grad_rows, *came, expert_out, grad_picked)
    expert_out = lax.all_to_all(
        expert_out.reshape(columns, planes * capacity, width), "fsdp", 0, 0, tiled=True
    )
    grad_h_two = lax.psum_scatter(
        combine(grad_rows), "ctx", scatter_dimension=0, tiled=True
    ).astype(f32)

    u_plane = jnp.sum(jnp.where(holds, grad_picked[..., None], 0.0), axis=2)
    u_mine = exchange(u_plane.transpose(1, 0, 2))
    u_mine = jnp.stack(u_mine, axis=1).reshape(experts, row_count).T
    grad_logits = probs * (u_mine - jnp.sum(probs * u_mine, axis=-1, keepdims=True))
    grad_logits = grad_logits.astype(bf16)
    grad_h_two = grad_h_two + mm_t(grad_logits, full_router)
    grad_router = t_mm(h_two, grad_logits)

    grad_top = grad_output[0].astype(f32)
    grad_ffn_gain = jnp.sum(grad_h_two * middle_hat, axis=0)
    grad_hat = grad_h_two * gain_ffn
    grad_middle = grad_top + scale_two * (
        grad_hat - middle_hat * jnp.mean(grad_hat * middle_hat, axis=-1, keepdims=True)
    )
    grad_branch = grad_middle.astype(bf16)
    def grad_heads(where):
        rows = lax.dynamic_slice_in_dim(full_out, where * share, share)
        return mm_t(grad_branch, rows).astype(bf16)

    came = [swap(grad_heads(plane ^ step), step) for step in range(1, planes)]
    grad_att = jnp.concatenate(by_plane([grad_heads(plane)] + came))
    grad_out_w = t_mm(attended, grad_branch).astype(bf16)
    grad_out_w = grad_out_w.reshape(planes, columns, strip, width).transpose(1, 0, 2, 3)
    mixed_part = combine(tie(expert_out, grad_att, grad_out_w))
    mixed = lax.psum_scatter(mixed_part, "ctx", scatter_dimension=0, tiled=True)
    output = (middle + mixed.astype(f32)).astype(bf16)
    grad_out_w = lax.all_to_all(
        tie(grad_out_w, mixed_part), "fsdp", 0, 0, tiled=True
    )
    grad_att = tie(grad_att, mixed_part)
    grad_query, grad_key, grad_value = attend_back(seq_ids, query, key, values, grad_att)
    grad_query, grad_key, dots, grad_gains = turn_back(
        raw, scales, gains, cosine, sine, grad_query, grad_key
    )
    dots = plane_sum(dots.T).T * (scales * scales) / width
    grad_qkv = jnp.concatenate(
        [
            scales[:, :1] * grad_query - raw[:, :share] * (scales[:, :1] * dots[:, :1]),
            scales[:, 1:] * grad_key - raw[:, share : 2 * share] * (scales[:, 1:] * dots[:, 1:]),
            grad_value,
        ],
        axis=1,
    ).astype(bf16)
    grad_part = mm_t(grad_qkv, packed[:, : 3 * share])
    grad_out_w = jnp.sum(grad_out_w.astype(f32), axis=0).astype(bf16)
    came_out = [swap(grad_out_w[plane ^ step], step) for step in steps]
    grad_out_w = sum(x.astype(f32) for x in [grad_out_w[plane]] + came_out)
    sums = t_mm(h_one, grad_qkv).astype(bf16)
    sums = sums.reshape(planes, columns, strip, -1).transpose(1, 0, 2, 3)
    grad_h_one = lax.psum_scatter(
        tie(grad_part.astype(bf16), mixed, sums, *came_out), "ctx", scatter_dimension=0, tiled=True
    ).astype(f32)
    grad_attn_gain = jnp.sum(grad_part * (hidden_wide * scale_one), axis=0)
    rows_of = jnp.arange(planes)[:, None] == plane
    gains = [jnp.where(rows_of, g[None], 0.0).reshape(width) for g in grad_gains]
    gains = [g[:, None] for g in [grad_attn_gain, grad_ffn_gain] + gains]
    small = jnp.concatenate([grad_router] + gains, axis=1).reshape(planes, columns, -1)
    small = sum([small[plane]] + [swap(small[plane ^ step], step) for step in steps])
    sums = lax.all_to_all(sums, "fsdp", 0, 0, tiled=True)
    small = lax.all_to_all(tie(small, sums), "fsdp", 0, 0, tiled=True)
    small = jnp.sum(small, axis=0).reshape(strip, -1)
    sums = jnp.sum(sums.astype(f32), axis=0).astype(bf16)
    sums = lax.all_to_all(tie(sums, small), "ctx", 0, 0, tiled=True)
    grad_qkv_w = sums.reshape(planes, strip, 3, share).transpose(2, 1, 0, 3)
    grad_qkv_w = grad_qkv_w.reshape(3, strip, width).astype(f32)

    x_hat = hidden[0].astype(f32)
    scale_mine = lax.rsqrt(jnp.mean(x_hat * x_hat, axis=-1, keepdims=True) + epsilon)
    x_hat = x_hat * scale_mine
    grad_hat = grad_h_one * gain_attn
    grad_input = grad_middle + scale_mine * (
        grad_hat - x_hat * jnp.mean(grad_hat * x_hat, axis=-1, keepdims=True)
    )

    return (
        output[None],
        grad_input[None],
        grad_qkv_w[0],
        grad_qkv_w[1],
        grad_qkv_w[2],
        grad_out_w,
        small[:, :experts],
        small[:, experts],
        small[:, experts + 1],
        small[:, experts + 2],
        small[:, experts + 3],
        gate_grad,
        up_grad,
        down_grad,
    )


def solution(mesh):
    placed = (
        P("fsdp", "ctx", None),
        P("fsdp", None),
        P("fsdp", None),
        P("fsdp", "ctx", None),
        P("fsdp", "ctx", None),
        P(("ctx", "fsdp"), None),
        P(("ctx", "fsdp"), None),
        P(("ctx", "fsdp"), None),
        P(("ctx", "fsdp"), None),
        P(("ctx", "fsdp"), None),
        P(("ctx", "fsdp")),
        P(("ctx", "fsdp")),
        P(("ctx", "fsdp")),
        P(("ctx", "fsdp")),
        P("fsdp", "ctx", None),
        P("fsdp", "ctx", None),
        P("fsdp", "ctx", None),
    )

    def shards(*operands):
        experts_here = operands[14].shape[0]
        heads = operands[0].shape[2] // HEAD_DIM
        planes = mesh.shape["ctx"]
        whole_experts = experts_here == planes and heads % planes == 0 and planes in (2, 4)
        return (plane_shards if whole_experts else general_shards)(*operands)

    return jax.shard_map(
        shards,
        mesh=mesh,
        in_specs=placed,
        out_specs=(
            P("fsdp", "ctx", None),
            P("fsdp", "ctx", None),
            P(("ctx", "fsdp"), None),
            P(("ctx", "fsdp"), None),
            P(("ctx", "fsdp"), None),
            P(("ctx", "fsdp"), None),
            P(("ctx", "fsdp"), None),
            P(("ctx", "fsdp")),
            P(("ctx", "fsdp")),
            P(("ctx", "fsdp")),
            P(("ctx", "fsdp")),
            P("fsdp", "ctx", None),
            P("fsdp", "ctx", None),
            P("fsdp", "ctx", None),
        ),
        check_vma=False,
    )
```

```python
from functools import partial
import math

import jax
import jax.numpy as jnp
from jax import lax
from jax.experimental import pallas as pl
from jax.experimental.pallas import tpu as pltpu
from jax.sharding import PartitionSpec as P

HEAD_DIM = 128


epsilon = 1e-06
rope_base = 10000.0
masked_value = -1e30


def rms_scaled(values, gain):
    return values * lax.rsqrt(jnp.mean(values * values, axis=-1, keepdims=True) + epsilon) * gain


def rotate(values, places):
    row_count = values.shape[0]
    head_count = values.shape[1] // HEAD_DIM
    half_width = HEAD_DIM // 2
    frequency = rope_base ** (-2.0 * jnp.arange(half_width).astype(jnp.float32) / HEAD_DIM)
    angles = places.astype(jnp.float32)[:, None] * frequency[None, :]
    cosine = jnp.cos(angles)[:, None, :]
    sine_part = jnp.sin(angles)[:, None, :]
    split_heads = values.reshape(row_count, head_count, HEAD_DIM)
    first_half = split_heads[:, :, :half_width]
    second_half = split_heads[:, :, half_width:]
    turned = jnp.concatenate(
        [
            first_half * cosine - second_half * sine_part,
            second_half * cosine + first_half * sine_part,
        ],
        axis=-1,
    )
    return turned.reshape(row_count, head_count * HEAD_DIM)


def qk_post(values, gain, places):
    return rotate(rms_scaled(values, gain), places)


def route_weights(logits, chosen):
    router_probs = jax.nn.softmax(logits, axis=-1)
    return jnp.sum(jnp.where(chosen, router_probs[:, None, :], 0.0), axis=-1)


def seq_layout(order_row, seq_lengths):
    seq_ends = jnp.cumsum(seq_lengths)
    seq_ids = jnp.sum((order_row[:, None] >= seq_ends[None, :]).astype(jnp.int32), axis=1)
    starts = seq_ends - seq_lengths
    chosen = seq_ids[:, None] == jnp.arange(seq_lengths.shape[0], dtype=jnp.int32)[None, :]
    seq_start = jnp.sum(jnp.where(chosen, starts[None, :], 0), axis=1)
    return (seq_ids, order_row - seq_start)


def general_shards(
    hidden,
    token_order,
    lengths,
    routes,
    grad_output,
    w_query,
    w_key,
    w_value,
    w_out,
    w_router,
    attn_gain,
    ffn_gain,
    query_gain,
    key_gain,
    w_gate,
    w_up,
    w_down,
):
    hidden_in = hidden[0].astype(jnp.float32)
    row_count = hidden_in.shape[0]
    model_width = hidden_in.shape[1]
    head_count = model_width // HEAD_DIM
    score_scale = 1.0 / math.sqrt(HEAD_DIM)
    seq_all, place_all = seq_layout(token_order[0], lengths[0])
    first_row = lax.axis_index("ctx") * row_count
    seq_mine = lax.dynamic_slice_in_dim(seq_all, first_row, row_count)
    place_mine = lax.dynamic_slice_in_dim(place_all, first_row, row_count)
    same_seq = seq_mine[:, None] == seq_all[None, :]
    gathered = (
        lax.all_gather(w_query, ("ctx", "fsdp"), axis=0, tiled=True),
        lax.all_gather(w_key, ("ctx", "fsdp"), axis=0, tiled=True),
        lax.all_gather(w_value, ("ctx", "fsdp"), axis=0, tiled=True),
        lax.all_gather(w_out, ("ctx", "fsdp"), axis=0, tiled=True),
        lax.all_gather(w_router, ("ctx", "fsdp"), axis=0, tiled=True),
        lax.all_gather(attn_gain, ("ctx", "fsdp"), axis=0, tiled=True),
        lax.all_gather(ffn_gain, ("ctx", "fsdp"), axis=0, tiled=True),
        lax.all_gather(query_gain, ("ctx", "fsdp"), axis=0, tiled=True),
        lax.all_gather(key_gain, ("ctx", "fsdp"), axis=0, tiled=True),
    )
    (
        full_query,
        full_key,
        full_value,
        full_out,
        full_router,
        gain_attn,
        gain_ffn,
        gain_query,
        gain_key,
    ) = gathered
    gain_attn = gain_attn.astype(jnp.float32)
    gain_ffn = gain_ffn.astype(jnp.float32)
    gain_query = gain_query.astype(jnp.float32)
    gain_key = gain_key.astype(jnp.float32)
    h_one, norm_one_back = jax.vjp(rms_scaled, hidden_in, gain_attn)
    h_one_low = h_one.astype(jnp.bfloat16)
    query_raw = jnp.dot(h_one_low, full_query, preferred_element_type=jnp.float32)
    key_raw = jnp.dot(h_one_low, full_key, preferred_element_type=jnp.float32)
    values_low = jnp.dot(h_one_low, full_value, preferred_element_type=jnp.float32).astype(
        jnp.bfloat16
    )
    query_rot, query_back = jax.vjp(partial(qk_post, places=place_mine), query_raw, gain_query)
    key_rot, key_back = jax.vjp(partial(qk_post, places=place_mine), key_raw, gain_key)
    query_low = query_rot.astype(jnp.bfloat16)
    key_low = key_rot.astype(jnp.bfloat16)
    key_all, value_all = (
        lax.all_gather(key_low, "ctx", axis=0, tiled=True),
        lax.all_gather(values_low, "ctx", axis=0, tiled=True),
    )
    query_heads = query_low.reshape(row_count, head_count, HEAD_DIM)
    key_heads = key_all.reshape(-1, head_count, HEAD_DIM)
    value_heads = value_all.reshape(-1, head_count, HEAD_DIM)

    def scores_of():
        raw_scores = (
            jnp.einsum("thd,khd->htk", query_heads, key_heads, preferred_element_type=jnp.float32)
            * score_scale
        )
        return jnp.where(same_seq[None, :, :], raw_scores, masked_value)

    scores = scores_of()
    row_top = jnp.max(scores, axis=-1, keepdims=True)
    log_total = row_top + jnp.log(jnp.sum(jnp.exp(scores - row_top), axis=-1, keepdims=True))
    probs_low = jnp.exp(scores - log_total).astype(jnp.bfloat16)
    attended = jnp.einsum(
        "htk,khd->thd", probs_low, value_heads, preferred_element_type=jnp.float32
    )
    attended_low = attended.reshape(row_count, model_width).astype(jnp.bfloat16)
    middle = hidden_in + jnp.dot(attended_low, full_out, preferred_element_type=jnp.float32)
    h_two, norm_two_back = jax.vjp(rms_scaled, middle, gain_ffn)
    h_two_low = h_two.astype(jnp.bfloat16)
    logits = jnp.dot(h_two_low, full_router, preferred_element_type=jnp.float32)
    expert_count = full_router.shape[1]
    route_rows = routes[0]
    top_k = route_rows.shape[1]
    chosen = route_rows[:, :, None] == jnp.arange(expert_count, dtype=jnp.int32)[None, None, :]
    picked, route_back = jax.vjp(partial(route_weights, chosen=chosen), logits)
    pair_count = row_count * top_k
    capacity = 5 * row_count * top_k // (4 * expert_count)
    slot_count = expert_count * capacity
    group_size = lax.axis_size("fsdp")
    local_experts = w_gate.shape[0]
    pair_expert = route_rows.reshape(pair_count)
    one_hot = (pair_expert[:, None] == jnp.arange(expert_count, dtype=jnp.int32)[None, :]).astype(
        jnp.int32
    )
    slot_rank = jnp.sum(one_hot * (jnp.cumsum(one_hot, axis=0) - 1), axis=1)
    slot_ids = pair_expert * capacity + slot_rank
    source = (
        jnp.full((slot_count,), pair_count, jnp.int32)
        .at[slot_ids]
        .set(jnp.arange(pair_count, dtype=jnp.int32))
    )
    filled = source < pair_count
    source_pair = jnp.minimum(source, pair_count - 1)
    send_rows = jnp.where(
        filled[:, None], h_two_low[source_pair // top_k], jnp.zeros((), jnp.bfloat16)
    )
    send_rows = send_rows.reshape(group_size, local_experts, capacity, model_width)
    gate_full, up_full, down_full = (
        lax.all_gather(w_gate, "ctx", axis=1, tiled=True),
        lax.all_gather(w_up, "ctx", axis=1, tiled=True),
        lax.all_gather(w_down, "ctx", axis=1, tiled=True),
    )
    arrived_rows = lax.all_to_all(send_rows, "fsdp", split_axis=0, concat_axis=0, tiled=True)
    gate_part = jnp.einsum(
        "secd,edf->secf", arrived_rows, gate_full, preferred_element_type=jnp.float32
    )
    up_part = jnp.einsum(
        "secd,edf->secf", arrived_rows, up_full, preferred_element_type=jnp.float32
    )
    act_part = (jax.nn.silu(gate_part) * up_part).astype(jnp.bfloat16)
    result = jnp.einsum(
        "secf,efd->secd", act_part, down_full, preferred_element_type=jnp.float32
    ).astype(jnp.bfloat16)
    returned = lax.all_to_all(result, "fsdp", split_axis=0, concat_axis=0, tiled=True).reshape(
        slot_count, model_width
    )
    pair_out = returned[slot_ids].reshape(row_count, top_k, model_width)
    output = (middle + jnp.sum(picked[:, :, None] * pair_out, axis=1)).astype(jnp.bfloat16)
    grad_top = grad_output[0].astype(jnp.float32)
    grad_picked = jnp.sum(grad_top[:, None, :] * pair_out, axis=-1)
    grad_pair = (
        (picked[:, :, None] * grad_top[:, None, :])
        .astype(jnp.bfloat16)
        .reshape(pair_count, model_width)
    )
    grad_send = jnp.where(filled[:, None], grad_pair[source_pair], jnp.zeros((), jnp.bfloat16))
    grad_send = grad_send.reshape(group_size, local_experts, capacity, model_width)
    grad_arrived = lax.all_to_all(grad_send, "fsdp", split_axis=0, concat_axis=0, tiled=True)
    sigma = jax.nn.sigmoid(gate_part)
    act_low = (gate_part * sigma * up_part).astype(jnp.bfloat16)
    grad_act = jnp.einsum(
        "secd,efd->secf", grad_arrived, down_full, preferred_element_type=jnp.float32
    )
    grad_gate = (grad_act * up_part * sigma * (1.0 + gate_part * (1.0 - sigma))).astype(
        jnp.bfloat16
    )
    grad_up = (grad_act * gate_part * sigma).astype(jnp.bfloat16)
    grad_back = jnp.einsum(
        "secf,edf->secd", grad_gate, gate_full, preferred_element_type=jnp.float32
    )
    grad_back = (
        grad_back
        + jnp.einsum("secf,edf->secd", grad_up, up_full, preferred_element_type=jnp.float32)
    ).astype(jnp.bfloat16)
    grad_return = lax.all_to_all(
        grad_back, "fsdp", split_axis=0, concat_axis=0, tiled=True
    ).reshape(slot_count, model_width)
    grad_h_two = jnp.sum(
        grad_return[slot_ids].reshape(row_count, top_k, model_width).astype(jnp.float32), axis=1
    )
    (grad_logits,) = route_back(grad_picked)
    grad_logits_low = grad_logits.astype(jnp.bfloat16)
    grad_h_two = grad_h_two + jnp.einsum(
        "te,de->td", grad_logits_low, full_router, preferred_element_type=jnp.float32
    )
    grad_router = jnp.einsum(
        "td,te->de", h_two_low, grad_logits_low, preferred_element_type=jnp.float32
    )
    grad_middle, grad_ffn_gain = norm_two_back(grad_h_two)
    grad_middle = grad_middle + grad_top
    grad_branch = grad_middle.astype(jnp.bfloat16)
    grad_out_w = jnp.einsum(
        "td,te->de", attended_low, grad_branch, preferred_element_type=jnp.float32
    )
    grad_att = jnp.einsum(
        "te,de->td", grad_branch, full_out, preferred_element_type=jnp.float32
    ).astype(jnp.bfloat16)
    grad_att = grad_att.reshape(row_count, head_count, HEAD_DIM)
    scores = scores_of()
    probs_full = jnp.exp(scores - log_total)
    probs_again = probs_full.astype(jnp.bfloat16)
    grad_probs = jnp.einsum(
        "thd,khd->htk", grad_att, value_heads, preferred_element_type=jnp.float32
    )
    spread = jnp.sum(probs_full * grad_probs, axis=-1, keepdims=True)
    grad_scores = (probs_full * (grad_probs - spread)).astype(jnp.bfloat16)
    grad_query = (
        jnp.einsum(
            "htk,khd->thd", grad_scores, key_heads, preferred_element_type=jnp.float32
        ).reshape(row_count, model_width)
        * score_scale
    )
    grad_key_part = (
        jnp.einsum(
            "htk,thd->khd", grad_scores, query_heads, preferred_element_type=jnp.float32
        ).reshape(-1, model_width)
        * score_scale
    )
    grad_value_part = jnp.einsum(
        "htk,thd->khd", probs_again, grad_att, preferred_element_type=jnp.float32
    ).reshape(-1, model_width)
    grad_key, grad_value = (
        lax.psum_scatter(
            grad_key_part.astype(jnp.bfloat16), "ctx", scatter_dimension=0, tiled=True
        ).astype(jnp.float32),
        lax.psum_scatter(
            grad_value_part.astype(jnp.bfloat16), "ctx", scatter_dimension=0, tiled=True
        ).astype(jnp.float32),
    )
    grad_q_raw, grad_q_gain = query_back(grad_query)
    grad_k_raw, grad_k_gain = key_back(grad_key)
    grad_q_low = grad_q_raw.astype(jnp.bfloat16)
    grad_k_low = grad_k_raw.astype(jnp.bfloat16)
    grad_v_low = grad_value.astype(jnp.bfloat16)
    grad_query_w = jnp.einsum(
        "td,te->de", h_one_low, grad_q_low, preferred_element_type=jnp.float32
    )
    grad_key_w = jnp.einsum("td,te->de", h_one_low, grad_k_low, preferred_element_type=jnp.float32)
    grad_value_w = jnp.einsum(
        "td,te->de", h_one_low, grad_v_low, preferred_element_type=jnp.float32
    )
    grad_h_one = jnp.einsum("te,de->td", grad_q_low, full_query, preferred_element_type=jnp.float32)
    grad_h_one = grad_h_one + jnp.einsum(
        "te,de->td", grad_k_low, full_key, preferred_element_type=jnp.float32
    )
    grad_h_one = grad_h_one + jnp.einsum(
        "te,de->td", grad_v_low, full_value, preferred_element_type=jnp.float32
    )
    grad_input_norm, grad_attn_gain = norm_one_back(grad_h_one)
    grad_input = grad_middle + grad_input_norm
    totals = (
        lax.psum_scatter(grad_query_w, ("ctx", "fsdp"), scatter_dimension=0, tiled=True),
        lax.psum_scatter(grad_key_w, ("ctx", "fsdp"), scatter_dimension=0, tiled=True),
        lax.psum_scatter(grad_value_w, ("ctx", "fsdp"), scatter_dimension=0, tiled=True),
        lax.psum_scatter(grad_out_w, ("ctx", "fsdp"), scatter_dimension=0, tiled=True),
        lax.psum_scatter(grad_router, ("ctx", "fsdp"), scatter_dimension=0, tiled=True),
        lax.psum_scatter(grad_attn_gain, ("ctx", "fsdp"), scatter_dimension=0, tiled=True),
        lax.psum_scatter(grad_ffn_gain, ("ctx", "fsdp"), scatter_dimension=0, tiled=True),
        lax.psum_scatter(grad_q_gain, ("ctx", "fsdp"), scatter_dimension=0, tiled=True),
        lax.psum_scatter(grad_k_gain, ("ctx", "fsdp"), scatter_dimension=0, tiled=True),
    )
    grad_down_w = jnp.einsum(
        "secf,secd->efd", act_low, grad_arrived, preferred_element_type=jnp.float32
    )
    grad_gate_w = jnp.einsum(
        "secd,secf->edf", arrived_rows, grad_gate, preferred_element_type=jnp.float32
    )
    grad_up_w = jnp.einsum(
        "secd,secf->edf", arrived_rows, grad_up, preferred_element_type=jnp.float32
    )
    gate_grad, up_grad, down_grad = (
        lax.psum_scatter(
            grad_gate_w.astype(jnp.bfloat16), "ctx", scatter_dimension=1, tiled=True
        ).astype(jnp.float32),
        lax.psum_scatter(
            grad_up_w.astype(jnp.bfloat16), "ctx", scatter_dimension=1, tiled=True
        ).astype(jnp.float32),
        lax.psum_scatter(
            grad_down_w.astype(jnp.bfloat16), "ctx", scatter_dimension=1, tiled=True
        ).astype(jnp.float32),
    )
    return (
        output[None],
        grad_input[None],
        totals[0],
        totals[1],
        totals[2],
        totals[3],
        totals[4],
        totals[5],
        totals[6],
        totals[7],
        totals[8],
        gate_grad,
        up_grad,
        down_grad,
    )


def masked_probs(query, key, seq_rows, seq_cols, scale):
    scores = (
        lax.dot_general(query, key, (((1,), (1,)), ((), ())), preferred_element_type=jnp.float32)
        * scale
    )
    scores = jnp.where(seq_rows == seq_cols, scores, masked_value)
    top = jnp.max(scores, axis=-1, keepdims=True)
    weights = jnp.exp(scores - top)
    return weights / jnp.sum(weights, axis=-1, keepdims=True)


def attend_kernel(scale, seq_rows, seq_cols, query, key, value, out):
    probs = masked_probs(query[...], key[...], seq_rows[...], seq_cols[...], scale)
    out[...] = jnp.dot(
        probs.astype(jnp.bfloat16), value[...], preferred_element_type=jnp.float32
    ).astype(out.dtype)


def attend_back_kernel(
    scale, seq_rows, seq_cols, query, key, value, grad, grad_query, grad_key, grad_value
):
    @pl.when(pl.program_id(1) == 0)
    def _():
        grad_key[...] = jnp.zeros_like(grad_key)
        grad_value[...] = jnp.zeros_like(grad_value)

    probs = masked_probs(query[...], key[...], seq_rows[...], seq_cols[...], scale)
    grad_probs = lax.dot_general(
        grad[...], value[...], (((1,), (1,)), ((), ())), preferred_element_type=jnp.float32
    )
    spread = jnp.sum(probs * grad_probs, axis=-1, keepdims=True)
    grad_scores = (probs * (grad_probs - spread)).astype(jnp.bfloat16)
    grad_query[...] = (
        jnp.dot(grad_scores, key[...], preferred_element_type=jnp.float32) * scale
    )
    grad_key[...] += (
        lax.dot_general(
            grad_scores,
            query[...],
            (((0,), (0,)), ((), ())),
            preferred_element_type=jnp.float32,
        )
        * scale
    )
    grad_value[...] += lax.dot_general(
        probs.astype(jnp.bfloat16),
        grad[...],
        (((0,), (0,)), ((), ())),
        preferred_element_type=jnp.float32,
    )


def attention_specs(rows, block):
    per_block = pl.BlockSpec((block, HEAD_DIM), lambda h, i: (i, h))
    per_head = pl.BlockSpec((rows, HEAD_DIM), lambda h, i: (0, h))
    seqs = [
        pl.BlockSpec((block, 1), lambda h, i: (i, 0)),
        pl.BlockSpec((1, rows), lambda h, i: (0, 0)),
    ]
    return per_block, per_head, seqs


def attend(seq_ids, query, key, value):
    rows, width = query.shape
    block = math.gcd(rows, 256)
    per_block, per_head, seqs = attention_specs(rows, block)
    pairs = rows * rows * width
    return pl.pallas_call(
        partial(attend_kernel, 1.0 / math.sqrt(HEAD_DIM)),
        grid=(width // HEAD_DIM, rows // block),
        in_specs=seqs + [per_block, per_head, per_head],
        out_specs=per_block,
        out_shape=jax.ShapeDtypeStruct((rows, width), jnp.bfloat16),
        cost_estimate=pl.CostEstimate(
            flops=4 * pairs, bytes_accessed=8 * rows * width, transcendentals=pairs // HEAD_DIM
        ),
        compiler_params=pltpu.CompilerParams(vmem_limit_bytes=48 << 20),
        name="attend",
    )(seq_ids[:, None], seq_ids[None, :], query, key, value)


def attend_back(seq_ids, query, key, value, grad):
    rows, width = query.shape
    block = math.gcd(rows, 256)
    per_block, per_head, seqs = attention_specs(rows, block)
    pairs = rows * rows * width
    return pl.pallas_call(
        partial(attend_back_kernel, 1.0 / math.sqrt(HEAD_DIM)),
        grid=(width // HEAD_DIM, rows // block),
        in_specs=seqs + [per_block, per_head, per_head, per_block],
        out_specs=(per_block, per_head, per_head),
        out_shape=(jax.ShapeDtypeStruct((rows, width), jnp.float32),) * 3,
        cost_estimate=pl.CostEstimate(
            flops=10 * pairs, bytes_accessed=20 * rows * width, transcendentals=pairs // HEAD_DIM
        ),
        compiler_params=pltpu.CompilerParams(vmem_limit_bytes=48 << 20),
        name="attend_back",
    )(seq_ids[:, None], seq_ids[None, :], query, key, value, grad)


def dispatch_kernel(position, rows, out):
    columns, _, capacity, width = out.shape
    count = rows.shape[1]
    slots = lax.broadcasted_iota(jnp.int32, (columns, capacity, count), 1)
    select = jnp.where(slots == position[:, 0], 1.0, 0.0)
    select = select.reshape(columns * capacity, count).astype(jnp.bfloat16)
    step = math.gcd(width, 512)
    for at in range(0, width, step):
        part = jnp.dot(select, rows[0, :, at : at + step], preferred_element_type=jnp.float32)
        part = part.reshape(columns, capacity, step).astype(out.dtype)
        out[:, 0, :, at : at + step] = part


def dispatch(position, capacity, rows):
    columns, planes, count = position.shape
    width = rows.shape[1]
    return pl.pallas_call(
        dispatch_kernel,
        grid=(planes,),
        in_specs=[
            pl.BlockSpec((columns, 1, 1, count), lambda b: (0, b, 0, 0)),
            pl.BlockSpec((1, count, width), lambda b: (b, 0, 0)),
        ],
        out_specs=pl.BlockSpec((columns, 1, capacity, width), lambda b: (0, b, 0, 0)),
        out_shape=jax.ShapeDtypeStruct((columns, planes, capacity, width), jnp.bfloat16),
        cost_estimate=pl.CostEstimate(
            flops=2 * position.size * capacity * width,
            bytes_accessed=2 * columns * planes * capacity * width,
            transcendentals=0,
        ),
        compiler_params=pltpu.CompilerParams(vmem_limit_bytes=40 << 20),
        name="dispatch",
    )(position[:, :, None], rows.reshape(planes, count, width))


def heads_of(width):
    return [slice(at, at + HEAD_DIM) for at in range(0, width, HEAD_DIM)]


def turn_kernel(raw, scales, gains, cosine, sine, query, key, value):
    width = query.shape[1]
    for which, out in ((0, query), (1, key)):
        scale = scales[:, which : which + 1]
        for head in heads_of(width):
            part = raw[:, which * width + head.start : which * width + head.stop]
            part = part * scale * gains[which : which + 1, head]
            swapped = pltpu.roll(part, HEAD_DIM // 2, 1)
            out[:, head] = (part * cosine[...] + swapped * sine[...]).astype(out.dtype)
    value[...] = raw[:, 2 * width : 3 * width].astype(value.dtype)


def turn_back_kernel(
    raw, scales, gains, cosine, sine, grad_query, grad_key, out_query, out_key, dots, grad_gains
):
    @pl.when(pl.program_id(0) == 0)
    def _():
        grad_gains[...] = jnp.zeros_like(grad_gains)

    width = grad_query.shape[1]
    for which, grad, out in ((0, grad_query, out_query), (1, grad_key, out_key)):
        scale = scales[:, which : which + 1]
        total = jnp.zeros_like(scale)
        for head in heads_of(width):
            part = grad[:, head]
            part = part * cosine[...] - pltpu.roll(part, HEAD_DIM // 2, 1) * sine[...]
            hat = raw[:, which * width + head.start : which * width + head.stop] * scale
            grad_gains[which : which + 1, head] += jnp.sum(part * hat, axis=0, keepdims=True)
            part = part * gains[which : which + 1, head]
            total += jnp.sum(part * hat, axis=1, keepdims=True)
            out[:, head] = part
        dots[:, which : which + 1] = total


def turn_specs(raw, gains):
    block = math.gcd(raw.shape[0], 256)
    return block, [
        pl.BlockSpec((block, raw.shape[1]), lambda i: (i, 0)),
        pl.BlockSpec((block, 2), lambda i: (i, 0)),
        pl.BlockSpec(gains.shape, lambda i: (0, 0)),
        pl.BlockSpec((block, HEAD_DIM), lambda i: (i, 0)),
        pl.BlockSpec((block, HEAD_DIM), lambda i: (i, 0)),
    ]


def turn(raw, scales, gains, cosine, sine):
    rows, width = raw.shape[0], gains.shape[1]
    block, specs = turn_specs(raw, gains)
    return pl.pallas_call(
        turn_kernel,
        grid=(rows // block,),
        in_specs=specs,
        out_specs=(pl.BlockSpec((block, width), lambda i: (i, 0)),) * 3,
        out_shape=(jax.ShapeDtypeStruct((rows, width), jnp.bfloat16),) * 3,
        cost_estimate=pl.CostEstimate(
            flops=16 * rows * width, bytes_accessed=18 * rows * width, transcendentals=0
        ),
        compiler_params=pltpu.CompilerParams(vmem_limit_bytes=40 << 20),
        name="turn",
    )(raw, scales, gains, cosine, sine)


def turn_back(raw, scales, gains, cosine, sine, grad_query, grad_key):
    rows, width = grad_query.shape
    block, specs = turn_specs(raw, gains)
    wide = pl.BlockSpec((block, width), lambda i: (i, 0))
    f32 = jnp.float32
    return pl.pallas_call(
        turn_back_kernel,
        grid=(rows // block,),
        in_specs=specs + [wide, wide],
        out_specs=(
            wide,
            wide,
            pl.BlockSpec((block, 2), lambda i: (i, 0)),
            pl.BlockSpec((2, width), lambda i: (0, 0)),
        ),
        out_shape=(
            jax.ShapeDtypeStruct((rows, width), f32),
            jax.ShapeDtypeStruct((rows, width), f32),
            jax.ShapeDtypeStruct((rows, 2), f32),
            jax.ShapeDtypeStruct((2, width), f32),
        ),
        cost_estimate=pl.CostEstimate(
            flops=24 * rows * width, bytes_accessed=28 * rows * width, transcendentals=0
        ),
        compiler_params=pltpu.CompilerParams(vmem_limit_bytes=40 << 20),
        name="turn_back",
    )(raw, scales, gains, cosine, sine, grad_query, grad_key)


def expert_in_kernel(
    rows, gate, up, router, own, gate_out, up_out, act_out, picked_out
):
    logits = jnp.dot(rows[...], router[...], preferred_element_type=jnp.float32)
    weights = jnp.exp(logits - jnp.max(logits, axis=1, keepdims=True))
    picked = jnp.sum(weights * own[...], axis=1, keepdims=True)
    picked = picked / jnp.sum(weights, axis=1, keepdims=True)
    gate_pre = jnp.dot(rows[...], gate[...], preferred_element_type=jnp.float32)
    up_pre = jnp.dot(rows[...], up[...], preferred_element_type=jnp.float32)
    act = (gate_pre * jax.nn.sigmoid(gate_pre) * up_pre).astype(jnp.bfloat16)
    gate_out[...] = gate_pre
    up_out[...] = up_pre
    act_out[...] = (act.astype(jnp.float32) * picked).astype(jnp.bfloat16)
    picked_out[...] = picked


def expert_back_kernel(
    grad, gate_in, up_in, picked, gate, up, down, grad_gate, grad_up, grad_picked, grad_rows
):
    grad_raw = lax.dot_general(
        grad[...], down[...], (((1,), (1,)), ((), ())), preferred_element_type=jnp.float32
    )
    gate_pre, up_pre = gate_in[...], up_in[...]
    sigma = jax.nn.sigmoid(gate_pre)
    silu = gate_pre * sigma
    act = (silu * up_pre).astype(jnp.bfloat16).astype(jnp.float32)
    grad_picked[...] = jnp.sum(grad_raw * act, axis=1, keepdims=True)
    grad_act = grad_raw * picked[...]
    low_gate = (grad_act * up_pre * (sigma + silu * (1.0 - sigma))).astype(jnp.bfloat16)
    low_up = (grad_act * silu).astype(jnp.bfloat16)
    grad_gate[...] = low_gate
    grad_up[...] = low_up
    back = lax.dot_general(
        low_gate, gate[...], (((1,), (1,)), ((), ())), preferred_element_type=jnp.float32
    )
    back = back + lax.dot_general(
        low_up, up[...], (((1,), (1,)), ((), ())), preferred_element_type=jnp.float32
    )
    grad_rows[...] = back.astype(jnp.bfloat16)


def whole(shape):
    return pl.BlockSpec(shape, lambda i: (0, 0), pipeline_mode=pl.Buffered(1))


def row_blocks(block, width):
    return pl.BlockSpec((block, width), lambda i: (i, 0))


def expert_in(rows, gate, up, router, own, block):
    count, width = rows.shape
    hidden = gate.shape[1]
    narrow = row_blocks(block, hidden)
    f32 = jnp.float32
    return pl.pallas_call(
        expert_in_kernel,
        grid=(count // block,),
        in_specs=[
            row_blocks(block, width),
            whole(gate.shape),
            whole(up.shape),
            whole(router.shape),
            whole(own.shape),
        ],
        out_specs=(narrow, narrow, narrow, row_blocks(block, 1)),
        out_shape=(
            jax.ShapeDtypeStruct((count, hidden), f32),
            jax.ShapeDtypeStruct((count, hidden), f32),
            jax.ShapeDtypeStruct((count, hidden), jnp.bfloat16),
            jax.ShapeDtypeStruct((count, 1), f32),
        ),
        cost_estimate=pl.CostEstimate(
            flops=4 * count * width * hidden,
            bytes_accessed=2 * count * width + (10 * count + 4 * width) * hidden,
            transcendentals=count * hidden,
        ),
        compiler_params=pltpu.CompilerParams(vmem_limit_bytes=56 << 20),
        name="expert_in",
    )(rows, gate, up, router, own)


def expert_back(grad, gate_pre, up_pre, picked, gate, up, down, block):
    count, width = grad.shape
    hidden = down.shape[0]
    wide, narrow, one = [row_blocks(block, size) for size in (width, hidden, 1)]
    low = jax.ShapeDtypeStruct((count, hidden), jnp.bfloat16)
    return pl.pallas_call(
        expert_back_kernel,
        grid=(count // block,),
        in_specs=[wide, narrow, narrow, one, whole(gate.shape), whole(up.shape), whole(down.shape)],
        out_specs=(narrow, narrow, one, wide),
        out_shape=(
            low,
            low,
            jax.ShapeDtypeStruct((count, 1), jnp.float32),
            jax.ShapeDtypeStruct((count, width), jnp.bfloat16),
        ),
        cost_estimate=pl.CostEstimate(
            flops=6 * count * width * hidden,
            bytes_accessed=4 * count * width + (12 * count + 6 * width) * hidden,
            transcendentals=count * hidden,
        ),
        compiler_params=pltpu.CompilerParams(vmem_limit_bytes=58 << 20),
        name="expert_back",
    )(grad, gate_pre, up_pre, picked, gate, up, down)


def tie(array, *others):
    anywhere = pl.BlockSpec(memory_space=pl.ANY)
    return pl.pallas_call(
        lambda *refs: None,
        in_specs=[anywhere] * (1 + len(others)),
        out_specs=anywhere,
        out_shape=jax.ShapeDtypeStruct(array.shape, array.dtype),
        input_output_aliases={0: 0},
        name="tie",
    )(array, *others)


def mm(left, right):
    return jnp.dot(left, right, preferred_element_type=jnp.float32)


def mm_t(left, right):
    return lax.dot_general(
        left, right, (((1,), (1,)), ((), ())), preferred_element_type=jnp.float32
    )


def t_mm(left, right):
    return lax.dot_general(
        left, right, (((0,), (0,)), ((), ())), preferred_element_type=jnp.float32
    )


def plane_shards(
    hidden,
    token_order,
    lengths,
    routes,
    grad_output,
    w_query,
    w_key,
    w_value,
    w_out,
    w_router,
    attn_gain,
    ffn_gain,
    query_gain,
    key_gain,
    w_gate,
    w_up,
    w_down,
):
    f32, bf16 = jnp.float32, jnp.bfloat16
    both = ("ctx", "fsdp")
    planes = lax.axis_size("ctx")
    columns = lax.axis_size("fsdp")
    plane = lax.axis_index("ctx")
    row_count, width = hidden.shape[1:]
    group_rows = row_count * planes
    share = width // planes
    strip = w_query.shape[0]
    first_row = plane * row_count

    experts = w_router.shape[1]
    qkv = jnp.stack([w_query, w_key, w_value], axis=1).reshape(strip, 3, planes, share)
    qkv = qkv.transpose(2, 0, 1, 3).reshape(planes, strip, 3 * share)
    small = [w_router] + [g[:, None] for g in (attn_gain, ffn_gain, query_gain, key_gain)]
    small = jnp.concatenate(small + [routes.astype(bf16).reshape(strip, -1)], axis=1)
    spare = -small.shape[1] % 128
    small = jnp.pad(small, ((0, 0), (0, spare)))
    small = jnp.broadcast_to(small[None], (planes,) + small.shape)
    own_out = jnp.broadcast_to(w_out[None], (planes,) + w_out.shape)
    packed = jnp.concatenate([qkv, small, own_out], axis=2)
    packed = lax.all_to_all(packed, "ctx", 0, 0, tiled=True)
    hidden_all = lax.all_gather(tie(hidden[0], packed), "ctx", axis=0, tiled=True)
    packed, out_rows = packed[:, :, :-width], packed[:, :, -width:]
    routes_at = 3 * share + experts + 4
    routes_all = packed[:, :, routes_at : packed.shape[2] - spare].astype(jnp.int32)
    routes_all = routes_all.reshape(group_rows, -1)
    packed = jnp.broadcast_to(packed[None], (columns,) + packed.shape)
    packed = lax.all_to_all(packed, "fsdp", 0, 0, tiled=True)
    packed = packed.transpose(1, 0, 2, 3).reshape(width, -1)
    full_router = packed[:, 3 * share : 3 * share + experts]
    gain_attn, gain_ffn, gain_query, gain_key = [
        packed[:, 3 * share + experts + i].astype(f32) for i in range(4)
    ]
    def swap(part, step):
        return lax.ppermute(part, "ctx", [(i, i ^ step) for i in range(planes)])

    def by_plane(came):
        came = jnp.stack(came)
        return [came[plane ^ i] for i in range(planes)]

    def exchange(parts, first=None, last=None):
        came = [parts[plane]]
        for step in range(1, planes):
            part = parts[plane ^ step]
            part = swap(part if first is None else tie(part, first), step)
            came.append(part if last is None else tie(part, last))
        return by_plane(came)

    def exchange_after(parts, earlier):
        came = [
            swap(tie(part, *before) if before else part, step)
            for step, before in enumerate(earlier, 1)
            for part in [parts[plane ^ step]]
        ]
        return came, jnp.stack(by_plane([parts[plane]] + came)).astype(f32)

    def plane_sum(part):
        return part + sum(swap(part, step) for step in range(1, planes))

    out_rows = jnp.broadcast_to(out_rows[None], (columns,) + out_rows.shape)
    grad_all = lax.all_gather(
        tie(grad_output[0], hidden_all, packed, out_rows), "ctx", axis=0, tiled=True
    )
    full_out = lax.all_to_all(out_rows, "fsdp", 0, 0, tiled=True)

    seq_ids, places = seq_layout(token_order[0], lengths[0])
    experts_here = w_gate.shape[0]
    column_expert = experts_here * jnp.arange(columns, dtype=jnp.int32) + plane
    named = jnp.any(routes_all[:, :, None] == column_expert[None, None, :], axis=1)
    named = named.reshape(planes, row_count, columns)
    capacity = 5 * row_count * routes.shape[2] // (4 * experts)
    rank = jnp.cumsum(named.astype(jnp.int32), axis=1) - 1
    position = jnp.where(named, rank, -1).transpose(2, 0, 1)
    slots = jnp.arange(capacity, dtype=jnp.int32)
    holds = position[:, :, None, :] == slots[None, None, :, None]
    select = holds.astype(bf16)

    def combine(rows):
        rows = rows.reshape(columns, planes, capacity, width)
        sums = jnp.einsum("fbsr,fbsd->brd", select, rows, preferred_element_type=f32)
        return sums.reshape(group_rows, width).astype(bf16)


    frequency = rope_base ** (
        -2.0 * jnp.arange(HEAD_DIM // 2).astype(f32) / HEAD_DIM
    )
    angles = places.astype(f32)[:, None] * frequency[None, :]
    cosine, sine = jnp.cos(angles), jnp.sin(angles)
    cosine = jnp.concatenate([cosine, cosine], axis=1)
    sine = jnp.concatenate([-sine, sine], axis=1)
    hidden_wide = hidden_all.astype(f32)
    scale_one = lax.rsqrt(jnp.mean(hidden_wide * hidden_wide, axis=-1, keepdims=True) + epsilon)
    h_one = (hidden_wide * scale_one * gain_attn).astype(bf16)
    raw = mm(h_one, packed)
    squares = jnp.stack(
        [jnp.sum(raw[:, :share] ** 2, axis=1), jnp.sum(raw[:, share : 2 * share] ** 2, axis=1)]
    )
    squares = plane_sum(squares)
    scales = lax.rsqrt(squares / width + epsilon).T
    gains = lax.dynamic_slice_in_dim(
        jnp.stack([gain_query, gain_key]), plane * share, share, axis=1
    )
    query, key, values = turn(raw, scales, gains, cosine, sine)
    attended = attend(seq_ids, query, key, values)
    full_out = tie(full_out, attended).transpose(1, 0, 2, 3).reshape(width, width)
    grad_send = dispatch(position, capacity, tie(grad_all, attended, full_out))
    attended = attended.reshape(planes, row_count, share)
    attended = jnp.concatenate(exchange(attended, grad_all), axis=1)
    grad_in = lax.all_to_all(grad_send, "fsdp", 0, 0, tiled=True).reshape(-1, width)
    middle = hidden[0].astype(f32) + mm(attended, full_out)
    scale_two = lax.rsqrt(jnp.mean(middle * middle, axis=-1, keepdims=True) + epsilon)
    middle_hat = middle * scale_two
    h_two = (middle_hat * gain_ffn).astype(bf16)

    h_two_all = lax.all_gather(tie(h_two, grad_send), "ctx", axis=0, tiled=True)
    steps = range(1, planes)
    came_gate = [swap(tie(w_gate[plane ^ step], h_two_all), step) for step in steps]
    h_all = tie(h_two_all, grad_in, came_gate[planes // 2 - 1])
    gate = jnp.concatenate(by_plane([w_gate[plane]] + came_gate))
    came_up = [
        swap(tie(w_up[plane ^ step], before), step) for step, before in zip(steps, came_gate)
    ]
    up = jnp.concatenate(by_plane([w_up[plane]] + came_up))
    came_down = [swap(tie(w_down[plane ^ step], *came_up), step) for step in steps]
    probs = jax.nn.softmax(mm(h_two, full_router), axis=-1)
    rows_in = lax.all_to_all(dispatch(position, capacity, h_all), "fsdp", 0, 0, tiled=True)
    rows_in = rows_in.reshape(-1, width)
    own = experts_here * lax.axis_index("fsdp") + plane
    own = (jnp.arange(experts)[None, :] == own).astype(f32)
    slot_block = planes * capacity
    gate_pre, up_pre, act_picked, picked = expert_in(
        rows_in, gate, up, full_router, own, slot_block
    )
    came_down = [tie(part, act_picked) for part in came_down]
    down = jnp.concatenate(by_plane([w_down[plane]] + came_down))
    grad_down_w = t_mm(act_picked, grad_in).astype(bf16)
    grad_gate, grad_up, grad_picked, grad_rows = expert_back(
        grad_in, tie(gate_pre, grad_down_w), up_pre, picked, gate, up, down, slot_block
    )

    def blocks(matrix):
        return matrix.reshape(planes, matrix.shape[0] // planes, matrix.shape[1])

    came, down_grad = exchange_after(blocks(grad_down_w), [()] * (planes - 1))
    grad_up_w = t_mm(rows_in, grad_up).astype(bf16)
    grad_rows = tie(grad_rows, *came, grad_up_w)
    grad_rows = lax.all_to_all(
        grad_rows.reshape(columns, planes * capacity, width), "fsdp", 0, 0, tiled=True
    )
    grad_gate_w = t_mm(rows_in, grad_gate).astype(bf16)
    came, up_grad = exchange_after(blocks(grad_up_w), [(part,) for part in came])
    came, gate_grad = exchange_after(blocks(grad_gate_w), [(part,) for part in came])
    expert_out = mm(act_picked, down).astype(bf16)
    grad_picked = lax.all_to_all(
        tie(grad_picked, grad_rows).reshape(columns, planes, capacity), "fsdp", 0, 0, tiled=True
    )
    grad_rows = tie(grad_rows, *came, expert_out, grad_picked)
    expert_out = lax.all_to_all(
        expert_out.reshape(columns, planes * capacity, width), "fsdp", 0, 0, tiled=True
    )
    grad_h_two = lax.psum_scatter(
        combine(grad_rows), "ctx", scatter_dimension=0, tiled=True
    ).astype(f32)

    u_plane = jnp.sum(jnp.where(holds, grad_picked[..., None], 0.0), axis=2)
    u_mine = exchange(u_plane.transpose(1, 0, 2))
    u_mine = jnp.stack(u_mine, axis=1).reshape(experts, row_count).T
    grad_logits = probs * (u_mine - jnp.sum(probs * u_mine, axis=-1, keepdims=True))
    grad_logits = grad_logits.astype(bf16)
    grad_h_two = grad_h_two + mm_t(grad_logits, full_router)
    grad_router = t_mm(h_two, grad_logits)

    grad_top = grad_output[0].astype(f32)
    grad_ffn_gain = jnp.sum(grad_h_two * middle_hat, axis=0)
    grad_hat = grad_h_two * gain_ffn
    grad_middle = grad_top + scale_two * (
        grad_hat - middle_hat * jnp.mean(grad_hat * middle_hat, axis=-1, keepdims=True)
    )
    grad_branch = grad_middle.astype(bf16)
    def grad_heads(where):
        rows = lax.dynamic_slice_in_dim(full_out, where * share, share)
        return mm_t(grad_branch, rows).astype(bf16)

    came = [swap(grad_heads(plane ^ step), step) for step in range(1, planes)]
    grad_att = jnp.concatenate(by_plane([grad_heads(plane)] + came))
    grad_out_w = t_mm(attended, grad_branch).astype(bf16)
    grad_out_w = grad_out_w.reshape(planes, columns, strip, width).transpose(1, 0, 2, 3)
    mixed_part = combine(tie(expert_out, grad_att, grad_out_w))
    mixed = lax.psum_scatter(mixed_part, "ctx", scatter_dimension=0, tiled=True)
    output = (middle + mixed.astype(f32)).astype(bf16)
    grad_out_w = lax.all_to_all(
        tie(grad_out_w, mixed_part), "fsdp", 0, 0, tiled=True
    )
    grad_att = tie(grad_att, mixed_part)
    grad_query, grad_key, grad_value = attend_back(seq_ids, query, key, values, grad_att)
    grad_query, grad_key, dots, grad_gains = turn_back(
        raw, scales, gains, cosine, sine, grad_query, grad_key
    )
    dots = plane_sum(dots.T).T * (scales * scales) / width
    grad_qkv = jnp.concatenate(
        [
            scales[:, :1] * grad_query - raw[:, :share] * (scales[:, :1] * dots[:, :1]),
            scales[:, 1:] * grad_key - raw[:, share : 2 * share] * (scales[:, 1:] * dots[:, 1:]),
            grad_value,
        ],
        axis=1,
    ).astype(bf16)
    grad_part = mm_t(grad_qkv, packed[:, : 3 * share])
    sums = t_mm(h_one, grad_qkv).astype(bf16)
    sums = sums.reshape(planes, columns, strip, -1).transpose(1, 0, 2, 3)
    grad_h_one = lax.psum_scatter(
        tie(grad_part.astype(bf16), mixed, grad_out_w), "ctx", scatter_dimension=0, tiled=True
    ).astype(f32)
    grad_attn_gain = jnp.sum(grad_part * (hidden_wide * scale_one), axis=0)
    rows_of = jnp.arange(planes)[:, None] == plane
    gains = [jnp.where(rows_of, g[None], 0.0).reshape(width) for g in grad_gains]
    gains = [g[:, None] for g in [grad_attn_gain, grad_ffn_gain] + gains]
    small = jnp.concatenate([grad_router] + gains, axis=1).reshape(planes, columns, -1)
    small = sum([small[plane]] + [swap(small[plane ^ step], step) for step in steps])
    sums = lax.all_to_all(sums, "fsdp", 0, 0, tiled=True)
    grad_out_w = jnp.sum(grad_out_w.astype(f32), axis=0).astype(bf16)
    came_out = [swap(grad_out_w[plane ^ step], step) for step in steps]
    grad_out_w = sum(x.astype(f32) for x in [grad_out_w[plane]] + came_out)
    small = lax.all_to_all(tie(small, sums, *came_out), "fsdp", 0, 0, tiled=True)
    small = jnp.sum(small, axis=0).reshape(strip, -1)
    sums = jnp.sum(sums.astype(f32), axis=0).astype(bf16)
    sums = lax.all_to_all(tie(sums, small), "ctx", 0, 0, tiled=True)
    grad_qkv_w = sums.reshape(planes, strip, 3, share).transpose(2, 1, 0, 3)
    grad_qkv_w = grad_qkv_w.reshape(3, strip, width).astype(f32)

    x_hat = hidden[0].astype(f32)
    scale_mine = lax.rsqrt(jnp.mean(x_hat * x_hat, axis=-1, keepdims=True) + epsilon)
    x_hat = x_hat * scale_mine
    grad_hat = grad_h_one * gain_attn
    grad_input = grad_middle + scale_mine * (
        grad_hat - x_hat * jnp.mean(grad_hat * x_hat, axis=-1, keepdims=True)
    )

    return (
        output[None],
        grad_input[None],
        grad_qkv_w[0],
        grad_qkv_w[1],
        grad_qkv_w[2],
        grad_out_w,
        small[:, :experts],
        small[:, experts],
        small[:, experts + 1],
        small[:, experts + 2],
        small[:, experts + 3],
        gate_grad,
        up_grad,
        down_grad,
    )


def solution(mesh):
    placed = (
        P("fsdp", "ctx", None),
        P("fsdp", None),
        P("fsdp", None),
        P("fsdp", "ctx", None),
        P("fsdp", "ctx", None),
        P(("ctx", "fsdp"), None),
        P(("ctx", "fsdp"), None),
        P(("ctx", "fsdp"), None),
        P(("ctx", "fsdp"), None),
        P(("ctx", "fsdp"), None),
        P(("ctx", "fsdp")),
        P(("ctx", "fsdp")),
        P(("ctx", "fsdp")),
        P(("ctx", "fsdp")),
        P("fsdp", "ctx", None),
        P("fsdp", "ctx", None),
        P("fsdp", "ctx", None),
    )

    def shards(*operands):
        experts_here = operands[14].shape[0]
        heads = operands[0].shape[2] // HEAD_DIM
        planes = mesh.shape["ctx"]
        whole_experts = experts_here == planes and heads % planes == 0 and planes in (2, 4)
        return (plane_shards if whole_experts else general_shards)(*operands)

    return jax.shard_map(
        shards,
        mesh=mesh,
        in_specs=placed,
        out_specs=(
            P("fsdp", "ctx", None),
            P("fsdp", "ctx", None),
            P(("ctx", "fsdp"), None),
            P(("ctx", "fsdp"), None),
            P(("ctx", "fsdp"), None),
            P(("ctx", "fsdp"), None),
            P(("ctx", "fsdp"), None),
            P(("ctx", "fsdp")),
            P(("ctx", "fsdp")),
            P(("ctx", "fsdp")),
            P(("ctx", "fsdp")),
            P("fsdp", "ctx", None),
            P("fsdp", "ctx", None),
            P("fsdp", "ctx", None),
        ),
        check_vma=False,
    )
```

```python
from functools import partial
import math

import jax
import jax.numpy as jnp
from jax import lax
from jax.experimental import pallas as pl
from jax.experimental.pallas import tpu as pltpu
from jax.sharding import PartitionSpec as P

HEAD_DIM = 128


epsilon = 1e-06
rope_base = 10000.0
masked_value = -1e30


def rms_scaled(values, gain):
    return values * lax.rsqrt(jnp.mean(values * values, axis=-1, keepdims=True) + epsilon) * gain


def rotate(values, places):
    row_count = values.shape[0]
    head_count = values.shape[1] // HEAD_DIM
    half_width = HEAD_DIM // 2
    frequency = rope_base ** (-2.0 * jnp.arange(half_width).astype(jnp.float32) / HEAD_DIM)
    angles = places.astype(jnp.float32)[:, None] * frequency[None, :]
    cosine = jnp.cos(angles)[:, None, :]
    sine_part = jnp.sin(angles)[:, None, :]
    split_heads = values.reshape(row_count, head_count, HEAD_DIM)
    first_half = split_heads[:, :, :half_width]
    second_half = split_heads[:, :, half_width:]
    turned = jnp.concatenate(
        [
            first_half * cosine - second_half * sine_part,
            second_half * cosine + first_half * sine_part,
        ],
        axis=-1,
    )
    return turned.reshape(row_count, head_count * HEAD_DIM)


def qk_post(values, gain, places):
    return rotate(rms_scaled(values, gain), places)


def route_weights(logits, chosen):
    router_probs = jax.nn.softmax(logits, axis=-1)
    return jnp.sum(jnp.where(chosen, router_probs[:, None, :], 0.0), axis=-1)


def seq_layout(order_row, seq_lengths):
    seq_ends = jnp.cumsum(seq_lengths)
    seq_ids = jnp.sum((order_row[:, None] >= seq_ends[None, :]).astype(jnp.int32), axis=1)
    starts = seq_ends - seq_lengths
    chosen = seq_ids[:, None] == jnp.arange(seq_lengths.shape[0], dtype=jnp.int32)[None, :]
    seq_start = jnp.sum(jnp.where(chosen, starts[None, :], 0), axis=1)
    return (seq_ids, order_row - seq_start)


def general_shards(
    hidden,
    token_order,
    lengths,
    routes,
    grad_output,
    w_query,
    w_key,
    w_value,
    w_out,
    w_router,
    attn_gain,
    ffn_gain,
    query_gain,
    key_gain,
    w_gate,
    w_up,
    w_down,
):
    hidden_in = hidden[0].astype(jnp.float32)
    row_count = hidden_in.shape[0]
    model_width = hidden_in.shape[1]
    head_count = model_width // HEAD_DIM
    score_scale = 1.0 / math.sqrt(HEAD_DIM)
    seq_all, place_all = seq_layout(token_order[0], lengths[0])
    first_row = lax.axis_index("ctx") * row_count
    seq_mine = lax.dynamic_slice_in_dim(seq_all, first_row, row_count)
    place_mine = lax.dynamic_slice_in_dim(place_all, first_row, row_count)
    same_seq = seq_mine[:, None] == seq_all[None, :]
    gathered = (
        lax.all_gather(w_query, ("ctx", "fsdp"), axis=0, tiled=True),
        lax.all_gather(w_key, ("ctx", "fsdp"), axis=0, tiled=True),
        lax.all_gather(w_value, ("ctx", "fsdp"), axis=0, tiled=True),
        lax.all_gather(w_out, ("ctx", "fsdp"), axis=0, tiled=True),
        lax.all_gather(w_router, ("ctx", "fsdp"), axis=0, tiled=True),
        lax.all_gather(attn_gain, ("ctx", "fsdp"), axis=0, tiled=True),
        lax.all_gather(ffn_gain, ("ctx", "fsdp"), axis=0, tiled=True),
        lax.all_gather(query_gain, ("ctx", "fsdp"), axis=0, tiled=True),
        lax.all_gather(key_gain, ("ctx", "fsdp"), axis=0, tiled=True),
    )
    (
        full_query,
        full_key,
        full_value,
        full_out,
        full_router,
        gain_attn,
        gain_ffn,
        gain_query,
        gain_key,
    ) = gathered
    gain_attn = gain_attn.astype(jnp.float32)
    gain_ffn = gain_ffn.astype(jnp.float32)
    gain_query = gain_query.astype(jnp.float32)
    gain_key = gain_key.astype(jnp.float32)
    h_one, norm_one_back = jax.vjp(rms_scaled, hidden_in, gain_attn)
    h_one_low = h_one.astype(jnp.bfloat16)
    query_raw = jnp.dot(h_one_low, full_query, preferred_element_type=jnp.float32)
    key_raw = jnp.dot(h_one_low, full_key, preferred_element_type=jnp.float32)
    values_low = jnp.dot(h_one_low, full_value, preferred_element_type=jnp.float32).astype(
        jnp.bfloat16
    )
    query_rot, query_back = jax.vjp(partial(qk_post, places=place_mine), query_raw, gain_query)
    key_rot, key_back = jax.vjp(partial(qk_post, places=place_mine), key_raw, gain_key)
    query_low = query_rot.astype(jnp.bfloat16)
    key_low = key_rot.astype(jnp.bfloat16)
    key_all, value_all = (
        lax.all_gather(key_low, "ctx", axis=0, tiled=True),
        lax.all_gather(values_low, "ctx", axis=0, tiled=True),
    )
    query_heads = query_low.reshape(row_count, head_count, HEAD_DIM)
    key_heads = key_all.reshape(-1, head_count, HEAD_DIM)
    value_heads = value_all.reshape(-1, head_count, HEAD_DIM)

    def scores_of():
        raw_scores = (
            jnp.einsum("thd,khd->htk", query_heads, key_heads, preferred_element_type=jnp.float32)
            * score_scale
        )
        return jnp.where(same_seq[None, :, :], raw_scores, masked_value)

    scores = scores_of()
    row_top = jnp.max(scores, axis=-1, keepdims=True)
    log_total = row_top + jnp.log(jnp.sum(jnp.exp(scores - row_top), axis=-1, keepdims=True))
    probs_low = jnp.exp(scores - log_total).astype(jnp.bfloat16)
    attended = jnp.einsum(
        "htk,khd->thd", probs_low, value_heads, preferred_element_type=jnp.float32
    )
    attended_low = attended.reshape(row_count, model_width).astype(jnp.bfloat16)
    middle = hidden_in + jnp.dot(attended_low, full_out, preferred_element_type=jnp.float32)
    h_two, norm_two_back = jax.vjp(rms_scaled, middle, gain_ffn)
    h_two_low = h_two.astype(jnp.bfloat16)
    logits = jnp.dot(h_two_low, full_router, preferred_element_type=jnp.float32)
    expert_count = full_router.shape[1]
    route_rows = routes[0]
    top_k = route_rows.shape[1]
    chosen = route_rows[:, :, None] == jnp.arange(expert_count, dtype=jnp.int32)[None, None, :]
    picked, route_back = jax.vjp(partial(route_weights, chosen=chosen), logits)
    pair_count = row_count * top_k
    capacity = 5 * row_count * top_k // (4 * expert_count)
    slot_count = expert_count * capacity
    group_size = lax.axis_size("fsdp")
    local_experts = w_gate.shape[0]
    pair_expert = route_rows.reshape(pair_count)
    one_hot = (pair_expert[:, None] == jnp.arange(expert_count, dtype=jnp.int32)[None, :]).astype(
        jnp.int32
    )
    slot_rank = jnp.sum(one_hot * (jnp.cumsum(one_hot, axis=0) - 1), axis=1)
    slot_ids = pair_expert * capacity + slot_rank
    source = (
        jnp.full((slot_count,), pair_count, jnp.int32)
        .at[slot_ids]
        .set(jnp.arange(pair_count, dtype=jnp.int32))
    )
    filled = source < pair_count
    source_pair = jnp.minimum(source, pair_count - 1)
    send_rows = jnp.where(
        filled[:, None], h_two_low[source_pair // top_k], jnp.zeros((), jnp.bfloat16)
    )
    send_rows = send_rows.reshape(group_size, local_experts, capacity, model_width)
    gate_full, up_full, down_full = (
        lax.all_gather(w_gate, "ctx", axis=1, tiled=True),
        lax.all_gather(w_up, "ctx", axis=1, tiled=True),
        lax.all_gather(w_down, "ctx", axis=1, tiled=True),
    )
    arrived_rows = lax.all_to_all(send_rows, "fsdp", split_axis=0, concat_axis=0, tiled=True)
    gate_part = jnp.einsum(
        "secd,edf->secf", arrived_rows, gate_full, preferred_element_type=jnp.float32
    )
    up_part = jnp.einsum(
        "secd,edf->secf", arrived_rows, up_full, preferred_element_type=jnp.float32
    )
    act_part = (jax.nn.silu(gate_part) * up_part).astype(jnp.bfloat16)
    result = jnp.einsum(
        "secf,efd->secd", act_part, down_full, preferred_element_type=jnp.float32
    ).astype(jnp.bfloat16)
    returned = lax.all_to_all(result, "fsdp", split_axis=0, concat_axis=0, tiled=True).reshape(
        slot_count, model_width
    )
    pair_out = returned[slot_ids].reshape(row_count, top_k, model_width)
    output = (middle + jnp.sum(picked[:, :, None] * pair_out, axis=1)).astype(jnp.bfloat16)
    grad_top = grad_output[0].astype(jnp.float32)
    grad_picked = jnp.sum(grad_top[:, None, :] * pair_out, axis=-1)
    grad_pair = (
        (picked[:, :, None] * grad_top[:, None, :])
        .astype(jnp.bfloat16)
        .reshape(pair_count, model_width)
    )
    grad_send = jnp.where(filled[:, None], grad_pair[source_pair], jnp.zeros((), jnp.bfloat16))
    grad_send = grad_send.reshape(group_size, local_experts, capacity, model_width)
    grad_arrived = lax.all_to_all(grad_send, "fsdp", split_axis=0, concat_axis=0, tiled=True)
    sigma = jax.nn.sigmoid(gate_part)
    act_low = (gate_part * sigma * up_part).astype(jnp.bfloat16)
    grad_act = jnp.einsum(
        "secd,efd->secf", grad_arrived, down_full, preferred_element_type=jnp.float32
    )
    grad_gate = (grad_act * up_part * sigma * (1.0 + gate_part * (1.0 - sigma))).astype(
        jnp.bfloat16
    )
    grad_up = (grad_act * gate_part * sigma).astype(jnp.bfloat16)
    grad_back = jnp.einsum(
        "secf,edf->secd", grad_gate, gate_full, preferred_element_type=jnp.float32
    )
    grad_back = (
        grad_back
        + jnp.einsum("secf,edf->secd", grad_up, up_full, preferred_element_type=jnp.float32)
    ).astype(jnp.bfloat16)
    grad_return = lax.all_to_all(
        grad_back, "fsdp", split_axis=0, concat_axis=0, tiled=True
    ).reshape(slot_count, model_width)
    grad_h_two = jnp.sum(
        grad_return[slot_ids].reshape(row_count, top_k, model_width).astype(jnp.float32), axis=1
    )
    (grad_logits,) = route_back(grad_picked)
    grad_logits_low = grad_logits.astype(jnp.bfloat16)
    grad_h_two = grad_h_two + jnp.einsum(
        "te,de->td", grad_logits_low, full_router, preferred_element_type=jnp.float32
    )
    grad_router = jnp.einsum(
        "td,te->de", h_two_low, grad_logits_low, preferred_element_type=jnp.float32
    )
    grad_middle, grad_ffn_gain = norm_two_back(grad_h_two)
    grad_middle = grad_middle + grad_top
    grad_branch = grad_middle.astype(jnp.bfloat16)
    grad_out_w = jnp.einsum(
        "td,te->de", attended_low, grad_branch, preferred_element_type=jnp.float32
    )
    grad_att = jnp.einsum(
        "te,de->td", grad_branch, full_out, preferred_element_type=jnp.float32
    ).astype(jnp.bfloat16)
    grad_att = grad_att.reshape(row_count, head_count, HEAD_DIM)
    scores = scores_of()
    probs_full = jnp.exp(scores - log_total)
    probs_again = probs_full.astype(jnp.bfloat16)
    grad_probs = jnp.einsum(
        "thd,khd->htk", grad_att, value_heads, preferred_element_type=jnp.float32
    )
    spread = jnp.sum(probs_full * grad_probs, axis=-1, keepdims=True)
    grad_scores = (probs_full * (grad_probs - spread)).astype(jnp.bfloat16)
    grad_query = (
        jnp.einsum(
            "htk,khd->thd", grad_scores, key_heads, preferred_element_type=jnp.float32
        ).reshape(row_count, model_width)
        * score_scale
    )
    grad_key_part = (
        jnp.einsum(
            "htk,thd->khd", grad_scores, query_heads, preferred_element_type=jnp.float32
        ).reshape(-1, model_width)
        * score_scale
    )
    grad_value_part = jnp.einsum(
        "htk,thd->khd", probs_again, grad_att, preferred_element_type=jnp.float32
    ).reshape(-1, model_width)
    grad_key, grad_value = (
        lax.psum_scatter(
            grad_key_part.astype(jnp.bfloat16), "ctx", scatter_dimension=0, tiled=True
        ).astype(jnp.float32),
        lax.psum_scatter(
            grad_value_part.astype(jnp.bfloat16), "ctx", scatter_dimension=0, tiled=True
        ).astype(jnp.float32),
    )
    grad_q_raw, grad_q_gain = query_back(grad_query)
    grad_k_raw, grad_k_gain = key_back(grad_key)
    grad_q_low = grad_q_raw.astype(jnp.bfloat16)
    grad_k_low = grad_k_raw.astype(jnp.bfloat16)
    grad_v_low = grad_value.astype(jnp.bfloat16)
    grad_query_w = jnp.einsum(
        "td,te->de", h_one_low, grad_q_low, preferred_element_type=jnp.float32
    )
    grad_key_w = jnp.einsum("td,te->de", h_one_low, grad_k_low, preferred_element_type=jnp.float32)
    grad_value_w = jnp.einsum(
        "td,te->de", h_one_low, grad_v_low, preferred_element_type=jnp.float32
    )
    grad_h_one = jnp.einsum("te,de->td", grad_q_low, full_query, preferred_element_type=jnp.float32)
    grad_h_one = grad_h_one + jnp.einsum(
        "te,de->td", grad_k_low, full_key, preferred_element_type=jnp.float32
    )
    grad_h_one = grad_h_one + jnp.einsum(
        "te,de->td", grad_v_low, full_value, preferred_element_type=jnp.float32
    )
    grad_input_norm, grad_attn_gain = norm_one_back(grad_h_one)
    grad_input = grad_middle + grad_input_norm
    totals = (
        lax.psum_scatter(grad_query_w, ("ctx", "fsdp"), scatter_dimension=0, tiled=True),
        lax.psum_scatter(grad_key_w, ("ctx", "fsdp"), scatter_dimension=0, tiled=True),
        lax.psum_scatter(grad_value_w, ("ctx", "fsdp"), scatter_dimension=0, tiled=True),
        lax.psum_scatter(grad_out_w, ("ctx", "fsdp"), scatter_dimension=0, tiled=True),
        lax.psum_scatter(grad_router, ("ctx", "fsdp"), scatter_dimension=0, tiled=True),
        lax.psum_scatter(grad_attn_gain, ("ctx", "fsdp"), scatter_dimension=0, tiled=True),
        lax.psum_scatter(grad_ffn_gain, ("ctx", "fsdp"), scatter_dimension=0, tiled=True),
        lax.psum_scatter(grad_q_gain, ("ctx", "fsdp"), scatter_dimension=0, tiled=True),
        lax.psum_scatter(grad_k_gain, ("ctx", "fsdp"), scatter_dimension=0, tiled=True),
    )
    grad_down_w = jnp.einsum(
        "secf,secd->efd", act_low, grad_arrived, preferred_element_type=jnp.float32
    )
    grad_gate_w = jnp.einsum(
        "secd,secf->edf", arrived_rows, grad_gate, preferred_element_type=jnp.float32
    )
    grad_up_w = jnp.einsum(
        "secd,secf->edf", arrived_rows, grad_up, preferred_element_type=jnp.float32
    )
    gate_grad, up_grad, down_grad = (
        lax.psum_scatter(
            grad_gate_w.astype(jnp.bfloat16), "ctx", scatter_dimension=1, tiled=True
        ).astype(jnp.float32),
        lax.psum_scatter(
            grad_up_w.astype(jnp.bfloat16), "ctx", scatter_dimension=1, tiled=True
        ).astype(jnp.float32),
        lax.psum_scatter(
            grad_down_w.astype(jnp.bfloat16), "ctx", scatter_dimension=1, tiled=True
        ).astype(jnp.float32),
    )
    return (
        output[None],
        grad_input[None],
        totals[0],
        totals[1],
        totals[2],
        totals[3],
        totals[4],
        totals[5],
        totals[6],
        totals[7],
        totals[8],
        gate_grad,
        up_grad,
        down_grad,
    )


def masked_probs(query, key, seq_rows, seq_cols, scale):
    scores = (
        lax.dot_general(query, key, (((1,), (1,)), ((), ())), preferred_element_type=jnp.float32)
        * scale
    )
    scores = jnp.where(seq_rows == seq_cols, scores, masked_value)
    top = jnp.max(scores, axis=-1, keepdims=True)
    weights = jnp.exp(scores - top)
    return weights / jnp.sum(weights, axis=-1, keepdims=True)


def attend_kernel(scale, seq_rows, seq_cols, query, key, value, out):
    probs = masked_probs(query[...], key[...], seq_rows[...], seq_cols[...], scale)
    out[...] = jnp.dot(
        probs.astype(jnp.bfloat16), value[...], preferred_element_type=jnp.float32
    ).astype(out.dtype)


def attend_back_kernel(
    scale, seq_rows, seq_cols, query, key, value, grad, grad_query, grad_key, grad_value
):
    @pl.when(pl.program_id(1) == 0)
    def _():
        grad_key[...] = jnp.zeros_like(grad_key)
        grad_value[...] = jnp.zeros_like(grad_value)

    probs = masked_probs(query[...], key[...], seq_rows[...], seq_cols[...], scale)
    grad_probs = lax.dot_general(
        grad[...], value[...], (((1,), (1,)), ((), ())), preferred_element_type=jnp.float32
    )
    spread = jnp.sum(probs * grad_probs, axis=-1, keepdims=True)
    grad_scores = (probs * (grad_probs - spread)).astype(jnp.bfloat16)
    grad_query[...] = (
        jnp.dot(grad_scores, key[...], preferred_element_type=jnp.float32) * scale
    )
    grad_key[...] += (
        lax.dot_general(
            grad_scores,
            query[...],
            (((0,), (0,)), ((), ())),
            preferred_element_type=jnp.float32,
        )
        * scale
    )
    grad_value[...] += lax.dot_general(
        probs.astype(jnp.bfloat16),
        grad[...],
        (((0,), (0,)), ((), ())),
        preferred_element_type=jnp.float32,
    )


def attention_specs(rows, block):
    per_block = pl.BlockSpec((block, HEAD_DIM), lambda h, i: (i, h))
    per_head = pl.BlockSpec((rows, HEAD_DIM), lambda h, i: (0, h))
    seqs = [
        pl.BlockSpec((block, 1), lambda h, i: (i, 0)),
        pl.BlockSpec((1, rows), lambda h, i: (0, 0)),
    ]
    return per_block, per_head, seqs


def attend(seq_ids, query, key, value):
    rows, width = query.shape
    block = math.gcd(rows, 256)
    per_block, per_head, seqs = attention_specs(rows, block)
    pairs = rows * rows * width
    return pl.pallas_call(
        partial(attend_kernel, 1.0 / math.sqrt(HEAD_DIM)),
        grid=(width // HEAD_DIM, rows // block),
        in_specs=seqs + [per_block, per_head, per_head],
        out_specs=per_block,
        out_shape=jax.ShapeDtypeStruct((rows, width), jnp.bfloat16),
        cost_estimate=pl.CostEstimate(
            flops=4 * pairs, bytes_accessed=8 * rows * width, transcendentals=pairs // HEAD_DIM
        ),
        compiler_params=pltpu.CompilerParams(vmem_limit_bytes=48 << 20),
        name="attend",
    )(seq_ids[:, None], seq_ids[None, :], query, key, value)


def attend_back(seq_ids, query, key, value, grad):
    rows, width = query.shape
    block = math.gcd(rows, 256)
    per_block, per_head, seqs = attention_specs(rows, block)
    pairs = rows * rows * width
    return pl.pallas_call(
        partial(attend_back_kernel, 1.0 / math.sqrt(HEAD_DIM)),
        grid=(width // HEAD_DIM, rows // block),
        in_specs=seqs + [per_block, per_head, per_head, per_block],
        out_specs=(per_block, per_head, per_head),
        out_shape=(jax.ShapeDtypeStruct((rows, width), jnp.float32),) * 3,
        cost_estimate=pl.CostEstimate(
            flops=10 * pairs, bytes_accessed=20 * rows * width, transcendentals=pairs // HEAD_DIM
        ),
        compiler_params=pltpu.CompilerParams(vmem_limit_bytes=48 << 20),
        name="attend_back",
    )(seq_ids[:, None], seq_ids[None, :], query, key, value, grad)


def dispatch_kernel(position, rows, out):
    columns, _, capacity, width = out.shape
    count = rows.shape[1]
    slots = lax.broadcasted_iota(jnp.int32, (columns, capacity, count), 1)
    select = jnp.where(slots == position[:, 0], 1.0, 0.0)
    select = select.reshape(columns * capacity, count).astype(jnp.bfloat16)
    step = math.gcd(width, 512)
    for at in range(0, width, step):
        part = jnp.dot(select, rows[0, :, at : at + step], preferred_element_type=jnp.float32)
        part = part.reshape(columns, capacity, step).astype(out.dtype)
        out[:, 0, :, at : at + step] = part


def dispatch(position, capacity, rows):
    columns, planes, count = position.shape
    width = rows.shape[1]
    return pl.pallas_call(
        dispatch_kernel,
        grid=(planes,),
        in_specs=[
            pl.BlockSpec((columns, 1, 1, count), lambda b: (0, b, 0, 0)),
            pl.BlockSpec((1, count, width), lambda b: (b, 0, 0)),
        ],
        out_specs=pl.BlockSpec((columns, 1, capacity, width), lambda b: (0, b, 0, 0)),
        out_shape=jax.ShapeDtypeStruct((columns, planes, capacity, width), jnp.bfloat16),
        cost_estimate=pl.CostEstimate(
            flops=2 * position.size * capacity * width,
            bytes_accessed=2 * columns * planes * capacity * width,
            transcendentals=0,
        ),
        compiler_params=pltpu.CompilerParams(vmem_limit_bytes=40 << 20),
        name="dispatch",
    )(position[:, :, None], rows.reshape(planes, count, width))


def heads_of(width):
    return [slice(at, at + HEAD_DIM) for at in range(0, width, HEAD_DIM)]


def turn_kernel(raw, scales, gains, cosine, sine, query, key, value):
    width = query.shape[1]
    for which, out in ((0, query), (1, key)):
        scale = scales[:, which : which + 1]
        for head in heads_of(width):
            part = raw[:, which * width + head.start : which * width + head.stop]
            part = part * scale * gains[which : which + 1, head]
            swapped = pltpu.roll(part, HEAD_DIM // 2, 1)
            out[:, head] = (part * cosine[...] + swapped * sine[...]).astype(out.dtype)
    value[...] = raw[:, 2 * width : 3 * width].astype(value.dtype)


def turn_back_kernel(
    raw, scales, gains, cosine, sine, grad_query, grad_key, out_query, out_key, dots, grad_gains
):
    @pl.when(pl.program_id(0) == 0)
    def _():
        grad_gains[...] = jnp.zeros_like(grad_gains)

    width = grad_query.shape[1]
    for which, grad, out in ((0, grad_query, out_query), (1, grad_key, out_key)):
        scale = scales[:, which : which + 1]
        total = jnp.zeros_like(scale)
        for head in heads_of(width):
            part = grad[:, head]
            part = part * cosine[...] - pltpu.roll(part, HEAD_DIM // 2, 1) * sine[...]
            hat = raw[:, which * width + head.start : which * width + head.stop] * scale
            grad_gains[which : which + 1, head] += jnp.sum(part * hat, axis=0, keepdims=True)
            part = part * gains[which : which + 1, head]
            total += jnp.sum(part * hat, axis=1, keepdims=True)
            out[:, head] = part
        dots[:, which : which + 1] = total


def turn_specs(raw, gains):
    block = math.gcd(raw.shape[0], 256)
    return block, [
        pl.BlockSpec((block, raw.shape[1]), lambda i: (i, 0)),
        pl.BlockSpec((block, 2), lambda i: (i, 0)),
        pl.BlockSpec(gains.shape, lambda i: (0, 0)),
        pl.BlockSpec((block, HEAD_DIM), lambda i: (i, 0)),
        pl.BlockSpec((block, HEAD_DIM), lambda i: (i, 0)),
    ]


def turn(raw, scales, gains, cosine, sine):
    rows, width = raw.shape[0], gains.shape[1]
    block, specs = turn_specs(raw, gains)
    return pl.pallas_call(
        turn_kernel,
        grid=(rows // block,),
        in_specs=specs,
        out_specs=(pl.BlockSpec((block, width), lambda i: (i, 0)),) * 3,
        out_shape=(jax.ShapeDtypeStruct((rows, width), jnp.bfloat16),) * 3,
        cost_estimate=pl.CostEstimate(
            flops=16 * rows * width, bytes_accessed=18 * rows * width, transcendentals=0
        ),
        compiler_params=pltpu.CompilerParams(vmem_limit_bytes=40 << 20),
        name="turn",
    )(raw, scales, gains, cosine, sine)


def turn_back(raw, scales, gains, cosine, sine, grad_query, grad_key):
    rows, width = grad_query.shape
    block, specs = turn_specs(raw, gains)
    wide = pl.BlockSpec((block, width), lambda i: (i, 0))
    f32 = jnp.float32
    return pl.pallas_call(
        turn_back_kernel,
        grid=(rows // block,),
        in_specs=specs + [wide, wide],
        out_specs=(
            wide,
            wide,
            pl.BlockSpec((block, 2), lambda i: (i, 0)),
            pl.BlockSpec((2, width), lambda i: (0, 0)),
        ),
        out_shape=(
            jax.ShapeDtypeStruct((rows, width), f32),
            jax.ShapeDtypeStruct((rows, width), f32),
            jax.ShapeDtypeStruct((rows, 2), f32),
            jax.ShapeDtypeStruct((2, width), f32),
        ),
        cost_estimate=pl.CostEstimate(
            flops=24 * rows * width, bytes_accessed=28 * rows * width, transcendentals=0
        ),
        compiler_params=pltpu.CompilerParams(vmem_limit_bytes=40 << 20),
        name="turn_back",
    )(raw, scales, gains, cosine, sine, grad_query, grad_key)


def expert_in_kernel(
    rows, gate, up, router, own, gate_out, up_out, act_out, picked_out
):
    logits = jnp.dot(rows[...], router[...], preferred_element_type=jnp.float32)
    weights = jnp.exp(logits - jnp.max(logits, axis=1, keepdims=True))
    picked = jnp.sum(weights * own[...], axis=1, keepdims=True)
    picked = picked / jnp.sum(weights, axis=1, keepdims=True)
    gate_pre = jnp.dot(rows[...], gate[...], preferred_element_type=jnp.float32)
    up_pre = jnp.dot(rows[...], up[...], preferred_element_type=jnp.float32)
    act = (gate_pre * jax.nn.sigmoid(gate_pre) * up_pre).astype(jnp.bfloat16)
    gate_out[...] = gate_pre
    up_out[...] = up_pre
    act_out[...] = (act.astype(jnp.float32) * picked).astype(jnp.bfloat16)
    picked_out[...] = picked


def expert_back_kernel(
    grad, gate_in, up_in, picked, gate, up, down, grad_gate, grad_up, grad_picked, grad_rows
):
    grad_raw = lax.dot_general(
        grad[...], down[...], (((1,), (1,)), ((), ())), preferred_element_type=jnp.float32
    )
    gate_pre, up_pre = gate_in[...], up_in[...]
    sigma = jax.nn.sigmoid(gate_pre)
    silu = gate_pre * sigma
    act = (silu * up_pre).astype(jnp.bfloat16).astype(jnp.float32)
    grad_picked[...] = jnp.sum(grad_raw * act, axis=1, keepdims=True)
    grad_act = grad_raw * picked[...]
    low_gate = (grad_act * up_pre * (sigma + silu * (1.0 - sigma))).astype(jnp.bfloat16)
    low_up = (grad_act * silu).astype(jnp.bfloat16)
    grad_gate[...] = low_gate
    grad_up[...] = low_up
    back = lax.dot_general(
        low_gate, gate[...], (((1,), (1,)), ((), ())), preferred_element_type=jnp.float32
    )
    back = back + lax.dot_general(
        low_up, up[...], (((1,), (1,)), ((), ())), preferred_element_type=jnp.float32
    )
    grad_rows[...] = back.astype(jnp.bfloat16)


def whole(shape):
    return pl.BlockSpec(shape, lambda i: (0, 0), pipeline_mode=pl.Buffered(1))


def row_blocks(block, width):
    return pl.BlockSpec((block, width), lambda i: (i, 0))


def expert_in(rows, gate, up, router, own, block):
    count, width = rows.shape
    hidden = gate.shape[1]
    narrow = row_blocks(block, hidden)
    f32 = jnp.float32
    return pl.pallas_call(
        expert_in_kernel,
        grid=(count // block,),
        in_specs=[
            row_blocks(block, width),
            whole(gate.shape),
            whole(up.shape),
            whole(router.shape),
            whole(own.shape),
        ],
        out_specs=(narrow, narrow, narrow, row_blocks(block, 1)),
        out_shape=(
            jax.ShapeDtypeStruct((count, hidden), f32),
            jax.ShapeDtypeStruct((count, hidden), f32),
            jax.ShapeDtypeStruct((count, hidden), jnp.bfloat16),
            jax.ShapeDtypeStruct((count, 1), f32),
        ),
        cost_estimate=pl.CostEstimate(
            flops=4 * count * width * hidden,
            bytes_accessed=2 * count * width + (10 * count + 4 * width) * hidden,
            transcendentals=count * hidden,
        ),
        compiler_params=pltpu.CompilerParams(vmem_limit_bytes=56 << 20),
        name="expert_in",
    )(rows, gate, up, router, own)


def expert_back(grad, gate_pre, up_pre, picked, gate, up, down, block):
    count, width = grad.shape
    hidden = down.shape[0]
    wide, narrow, one = [row_blocks(block, size) for size in (width, hidden, 1)]
    low = jax.ShapeDtypeStruct((count, hidden), jnp.bfloat16)
    return pl.pallas_call(
        expert_back_kernel,
        grid=(count // block,),
        in_specs=[wide, narrow, narrow, one, whole(gate.shape), whole(up.shape), whole(down.shape)],
        out_specs=(narrow, narrow, one, wide),
        out_shape=(
            low,
            low,
            jax.ShapeDtypeStruct((count, 1), jnp.float32),
            jax.ShapeDtypeStruct((count, width), jnp.bfloat16),
        ),
        cost_estimate=pl.CostEstimate(
            flops=6 * count * width * hidden,
            bytes_accessed=4 * count * width + (12 * count + 6 * width) * hidden,
            transcendentals=count * hidden,
        ),
        compiler_params=pltpu.CompilerParams(vmem_limit_bytes=58 << 20),
        name="expert_back",
    )(grad, gate_pre, up_pre, picked, gate, up, down)


def tie(array, *others):
    anywhere = pl.BlockSpec(memory_space=pl.ANY)
    return pl.pallas_call(
        lambda *refs: None,
        in_specs=[anywhere] * (1 + len(others)),
        out_specs=anywhere,
        out_shape=jax.ShapeDtypeStruct(array.shape, array.dtype),
        input_output_aliases={0: 0},
        name="tie",
    )(array, *others)


def mm(left, right):
    return jnp.dot(left, right, preferred_element_type=jnp.float32)


def mm_t(left, right):
    return lax.dot_general(
        left, right, (((1,), (1,)), ((), ())), preferred_element_type=jnp.float32
    )


def t_mm(left, right):
    return lax.dot_general(
        left, right, (((0,), (0,)), ((), ())), preferred_element_type=jnp.float32
    )


def plane_shards(
    hidden,
    token_order,
    lengths,
    routes,
    grad_output,
    w_query,
    w_key,
    w_value,
    w_out,
    w_router,
    attn_gain,
    ffn_gain,
    query_gain,
    key_gain,
    w_gate,
    w_up,
    w_down,
):
    f32, bf16 = jnp.float32, jnp.bfloat16
    both = ("ctx", "fsdp")
    planes = lax.axis_size("ctx")
    columns = lax.axis_size("fsdp")
    plane = lax.axis_index("ctx")
    row_count, width = hidden.shape[1:]
    group_rows = row_count * planes
    share = width // planes
    strip = w_query.shape[0]
    first_row = plane * row_count

    experts = w_router.shape[1]
    qkv = jnp.stack([w_query, w_key, w_value], axis=1).reshape(strip, 3, planes, share)
    qkv = qkv.transpose(2, 0, 1, 3).reshape(planes, strip, 3 * share)
    small = [w_router] + [g[:, None] for g in (attn_gain, ffn_gain, query_gain, key_gain)]
    small = jnp.concatenate(small + [routes.astype(bf16).reshape(strip, -1)], axis=1)
    spare = -small.shape[1] % 128
    small = jnp.pad(small, ((0, 0), (0, spare)))
    small = jnp.broadcast_to(small[None], (planes,) + small.shape)
    own_out = jnp.broadcast_to(w_out[None], (planes,) + w_out.shape)
    packed = jnp.concatenate([qkv, small, own_out], axis=2)
    packed = lax.all_to_all(packed, "ctx", 0, 0, tiled=True)
    hidden_all = lax.all_gather(tie(hidden[0], packed), "ctx", axis=0, tiled=True)
    packed, out_rows = packed[:, :, :-width], packed[:, :, -width:]
    routes_at = 3 * share + experts + 4
    routes_all = packed[:, :, routes_at : packed.shape[2] - spare].astype(jnp.int32)
    routes_all = routes_all.reshape(group_rows, -1)
    packed = jnp.broadcast_to(packed[None], (columns,) + packed.shape)
    packed = lax.all_to_all(packed, "fsdp", 0, 0, tiled=True)
    packed = packed.transpose(1, 0, 2, 3).reshape(width, -1)
    full_router = packed[:, 3 * share : 3 * share + experts]
    gain_attn, gain_ffn, gain_query, gain_key = [
        packed[:, 3 * share + experts + i].astype(f32) for i in range(4)
    ]
    def swap(part, step):
        return lax.ppermute(part, "ctx", [(i, i ^ step) for i in range(planes)])

    def by_plane(came):
        came = jnp.stack(came)
        return [came[plane ^ i] for i in range(planes)]

    def exchange(parts, first=None, last=None):
        came = [parts[plane]]
        for step in range(1, planes):
            part = parts[plane ^ step]
            part = swap(part if first is None else tie(part, first), step)
            came.append(part if last is None else tie(part, last))
        return by_plane(came)

    def exchange_after(parts, earlier):
        came = [
            swap(tie(part, *before) if before else part, step)
            for step, before in enumerate(earlier, 1)
            for part in [parts[plane ^ step]]
        ]
        return came, jnp.stack(by_plane([parts[plane]] + came)).astype(f32)

    def plane_sum(part):
        return part + sum(swap(part, step) for step in range(1, planes))

    out_rows = jnp.broadcast_to(out_rows[None], (columns,) + out_rows.shape)
    grad_all = lax.all_gather(
        tie(grad_output[0], hidden_all, packed, out_rows), "ctx", axis=0, tiled=True
    )
    full_out = lax.all_to_all(out_rows, "fsdp", 0, 0, tiled=True)

    seq_ids, places = seq_layout(token_order[0], lengths[0])
    experts_here = w_gate.shape[0]
    column_expert = experts_here * jnp.arange(columns, dtype=jnp.int32) + plane
    named = jnp.any(routes_all[:, :, None] == column_expert[None, None, :], axis=1)
    named = named.reshape(planes, row_count, columns)
    capacity = 5 * row_count * routes.shape[2] // (4 * experts)
    rank = jnp.cumsum(named.astype(jnp.int32), axis=1) - 1
    position = jnp.where(named, rank, -1).transpose(2, 0, 1)
    slots = jnp.arange(capacity, dtype=jnp.int32)
    holds = position[:, :, None, :] == slots[None, None, :, None]
    select = holds.astype(bf16)

    def combine(rows):
        rows = rows.reshape(columns, planes, capacity, width)
        sums = jnp.einsum("fbsr,fbsd->brd", select, rows, preferred_element_type=f32)
        return sums.reshape(group_rows, width).astype(bf16)


    frequency = rope_base ** (
        -2.0 * jnp.arange(HEAD_DIM // 2).astype(f32) / HEAD_DIM
    )
    angles = places.astype(f32)[:, None] * frequency[None, :]
    cosine, sine = jnp.cos(angles), jnp.sin(angles)
    cosine = jnp.concatenate([cosine, cosine], axis=1)
    sine = jnp.concatenate([-sine, sine], axis=1)
    hidden_wide = hidden_all.astype(f32)
    scale_one = lax.rsqrt(jnp.mean(hidden_wide * hidden_wide, axis=-1, keepdims=True) + epsilon)
    h_one = (hidden_wide * scale_one * gain_attn).astype(bf16)
    raw = mm(h_one, packed)
    squares = jnp.stack(
        [jnp.sum(raw[:, :share] ** 2, axis=1), jnp.sum(raw[:, share : 2 * share] ** 2, axis=1)]
    )
    squares = plane_sum(squares)
    scales = lax.rsqrt(squares / width + epsilon).T
    gains = lax.dynamic_slice_in_dim(
        jnp.stack([gain_query, gain_key]), plane * share, share, axis=1
    )
    query, key, values = turn(raw, scales, gains, cosine, sine)
    attended = attend(seq_ids, query, key, values)
    full_out = tie(full_out, attended).transpose(1, 0, 2, 3).reshape(width, width)
    grad_send = dispatch(position, capacity, tie(grad_all, attended, full_out))
    attended = attended.reshape(planes, row_count, share)
    attended = jnp.concatenate(exchange(attended, grad_all), axis=1)
    grad_in = lax.all_to_all(grad_send, "fsdp", 0, 0, tiled=True).reshape(-1, width)
    middle = hidden[0].astype(f32) + mm(attended, full_out)
    scale_two = lax.rsqrt(jnp.mean(middle * middle, axis=-1, keepdims=True) + epsilon)
    middle_hat = middle * scale_two
    h_two = (middle_hat * gain_ffn).astype(bf16)

    h_two_all = lax.all_gather(tie(h_two, grad_send), "ctx", axis=0, tiled=True)
    steps = range(1, planes)
    came_gate = [swap(tie(w_gate[plane ^ step], h_two_all), step) for step in steps]
    h_all = tie(h_two_all, grad_in, came_gate[planes // 2 - 1])
    gate = jnp.concatenate(by_plane([w_gate[plane]] + came_gate))
    came_up = [
        swap(tie(w_up[plane ^ step], before), step) for step, before in zip(steps, came_gate)
    ]
    up = jnp.concatenate(by_plane([w_up[plane]] + came_up))
    came_down = [swap(tie(w_down[plane ^ step], *came_up), step) for step in steps]
    probs = jax.nn.softmax(mm(h_two, full_router), axis=-1)
    rows_in = lax.all_to_all(dispatch(position, capacity, h_all), "fsdp", 0, 0, tiled=True)
    rows_in = rows_in.reshape(-1, width)
    own = experts_here * lax.axis_index("fsdp") + plane
    own = (jnp.arange(experts)[None, :] == own).astype(f32)
    slot_block = planes * capacity
    gate_pre, up_pre, act_picked, picked = expert_in(
        rows_in, gate, up, full_router, own, slot_block
    )
    came_down = [tie(part, act_picked) for part in came_down]
    down = jnp.concatenate(by_plane([w_down[plane]] + came_down))
    grad_down_w = t_mm(act_picked, grad_in).astype(bf16)
    grad_gate, grad_up, grad_picked, grad_rows = expert_back(
        grad_in, tie(gate_pre, grad_down_w), up_pre, picked, gate, up, down, slot_block
    )

    def blocks(matrix):
        return matrix.reshape(planes, matrix.shape[0] // planes, matrix.shape[1])

    came, down_grad = exchange_after(blocks(grad_down_w), [()] * (planes - 1))
    grad_up_w = t_mm(rows_in, grad_up).astype(bf16)
    grad_rows = tie(grad_rows, *came, grad_up_w)
    grad_rows = lax.all_to_all(
        grad_rows.reshape(columns, planes * capacity, width), "fsdp", 0, 0, tiled=True
    )
    grad_gate_w = t_mm(rows_in, grad_gate).astype(bf16)
    came, up_grad = exchange_after(blocks(grad_up_w), [(part,) for part in came])
    expert_out = mm(tie(act_picked, came[-1]), down).astype(bf16)
    earlier = [(came[0], expert_out)] + [(part,) for part in came[1:]]
    came, gate_grad = exchange_after(blocks(grad_gate_w), earlier)
    grad_picked = lax.all_to_all(
        tie(grad_picked, grad_rows).reshape(columns, planes, capacity), "fsdp", 0, 0, tiled=True
    )
    grad_rows = tie(grad_rows, *came, expert_out, grad_picked)
    expert_out = lax.all_to_all(
        expert_out.reshape(columns, planes * capacity, width), "fsdp", 0, 0, tiled=True
    )
    grad_h_two = lax.psum_scatter(
        combine(grad_rows), "ctx", scatter_dimension=0, tiled=True
    ).astype(f32)

    u_plane = jnp.sum(jnp.where(holds, grad_picked[..., None], 0.0), axis=2)
    u_mine = exchange(u_plane.transpose(1, 0, 2))
    u_mine = jnp.stack(u_mine, axis=1).reshape(experts, row_count).T
    grad_logits = probs * (u_mine - jnp.sum(probs * u_mine, axis=-1, keepdims=True))
    grad_logits = grad_logits.astype(bf16)
    grad_h_two = grad_h_two + mm_t(grad_logits, full_router)
    grad_router = t_mm(h_two, grad_logits)

    grad_top = grad_output[0].astype(f32)
    grad_ffn_gain = jnp.sum(grad_h_two * middle_hat, axis=0)
    grad_hat = grad_h_two * gain_ffn
    grad_middle = grad_top + scale_two * (
        grad_hat - middle_hat * jnp.mean(grad_hat * middle_hat, axis=-1, keepdims=True)
    )
    grad_branch = grad_middle.astype(bf16)
    def grad_heads(where):
        rows = lax.dynamic_slice_in_dim(full_out, where * share, share)
        return mm_t(grad_branch, rows).astype(bf16)

    came = [swap(grad_heads(plane ^ step), step) for step in range(1, planes)]
    grad_att = jnp.concatenate(by_plane([grad_heads(plane)] + came))
    grad_out_w = t_mm(attended, grad_branch).astype(bf16)
    grad_out_w = grad_out_w.reshape(planes, columns, strip, width).transpose(1, 0, 2, 3)
    mixed_part = combine(tie(expert_out, grad_att, grad_out_w))
    mixed = lax.psum_scatter(mixed_part, "ctx", scatter_dimension=0, tiled=True)
    output = (middle + mixed.astype(f32)).astype(bf16)
    grad_out_w = lax.all_to_all(
        tie(grad_out_w, mixed_part), "fsdp", 0, 0, tiled=True
    )
    grad_att = tie(grad_att, mixed_part)
    grad_query, grad_key, grad_value = attend_back(seq_ids, query, key, values, grad_att)
    grad_query, grad_key, dots, grad_gains = turn_back(
        raw, scales, gains, cosine, sine, grad_query, grad_key
    )
    dots = plane_sum(dots.T).T * (scales * scales) / width
    grad_qkv = jnp.concatenate(
        [
            scales[:, :1] * grad_query - raw[:, :share] * (scales[:, :1] * dots[:, :1]),
            scales[:, 1:] * grad_key - raw[:, share : 2 * share] * (scales[:, 1:] * dots[:, 1:]),
            grad_value,
        ],
        axis=1,
    ).astype(bf16)
    grad_part = mm_t(grad_qkv, packed[:, : 3 * share])
    sums = t_mm(h_one, grad_qkv).astype(bf16)
    sums = sums.reshape(planes, columns, strip, -1).transpose(1, 0, 2, 3)
    grad_h_one = lax.psum_scatter(
        tie(grad_part.astype(bf16), mixed, grad_out_w), "ctx", scatter_dimension=0, tiled=True
    ).astype(f32)
    grad_attn_gain = jnp.sum(grad_part * (hidden_wide * scale_one), axis=0)
    rows_of = jnp.arange(planes)[:, None] == plane
    gains = [jnp.where(rows_of, g[None], 0.0).reshape(width) for g in grad_gains]
    gains = [g[:, None] for g in [grad_attn_gain, grad_ffn_gain] + gains]
    small = jnp.concatenate([grad_router] + gains, axis=1).reshape(planes, columns, -1)
    small = sum([small[plane]] + [swap(small[plane ^ step], step) for step in steps])
    sums = lax.all_to_all(sums, "fsdp", 0, 0, tiled=True)
    grad_out_w = jnp.sum(grad_out_w.astype(f32), axis=0).astype(bf16)
    came_out = [swap(grad_out_w[plane ^ step], step) for step in steps]
    grad_out_w = sum(x.astype(f32) for x in [grad_out_w[plane]] + came_out)
    small = lax.all_to_all(tie(small, sums, *came_out), "fsdp", 0, 0, tiled=True)
    small = jnp.sum(small, axis=0).reshape(strip, -1)
    sums = jnp.sum(sums.astype(f32), axis=0).astype(bf16)
    sums = lax.all_to_all(tie(sums, small), "ctx", 0, 0, tiled=True)
    grad_qkv_w = sums.reshape(planes, strip, 3, share).transpose(2, 1, 0, 3)
    grad_qkv_w = grad_qkv_w.reshape(3, strip, width).astype(f32)

    x_hat = hidden[0].astype(f32)
    scale_mine = lax.rsqrt(jnp.mean(x_hat * x_hat, axis=-1, keepdims=True) + epsilon)
    x_hat = x_hat * scale_mine
    grad_hat = grad_h_one * gain_attn
    grad_input = grad_middle + scale_mine * (
        grad_hat - x_hat * jnp.mean(grad_hat * x_hat, axis=-1, keepdims=True)
    )

    return (
        output[None],
        grad_input[None],
        grad_qkv_w[0],
        grad_qkv_w[1],
        grad_qkv_w[2],
        grad_out_w,
        small[:, :experts],
        small[:, experts],
        small[:, experts + 1],
        small[:, experts + 2],
        small[:, experts + 3],
        gate_grad,
        up_grad,
        down_grad,
    )


def solution(mesh):
    placed = (
        P("fsdp", "ctx", None),
        P("fsdp", None),
        P("fsdp", None),
        P("fsdp", "ctx", None),
        P("fsdp", "ctx", None),
        P(("ctx", "fsdp"), None),
        P(("ctx", "fsdp"), None),
        P(("ctx", "fsdp"), None),
        P(("ctx", "fsdp"), None),
        P(("ctx", "fsdp"), None),
        P(("ctx", "fsdp")),
        P(("ctx", "fsdp")),
        P(("ctx", "fsdp")),
        P(("ctx", "fsdp")),
        P("fsdp", "ctx", None),
        P("fsdp", "ctx", None),
        P("fsdp", "ctx", None),
    )

    def shards(*operands):
        experts_here = operands[14].shape[0]
        heads = operands[0].shape[2] // HEAD_DIM
        planes = mesh.shape["ctx"]
        whole_experts = experts_here == planes and heads % planes == 0 and planes in (2, 4)
        return (plane_shards if whole_experts else general_shards)(*operands)

    return jax.shard_map(
        shards,
        mesh=mesh,
        in_specs=placed,
        out_specs=(
            P("fsdp", "ctx", None),
            P("fsdp", "ctx", None),
            P(("ctx", "fsdp"), None),
            P(("ctx", "fsdp"), None),
            P(("ctx", "fsdp"), None),
            P(("ctx", "fsdp"), None),
            P(("ctx", "fsdp"), None),
            P(("ctx", "fsdp")),
            P(("ctx", "fsdp")),
            P(("ctx", "fsdp")),
            P(("ctx", "fsdp")),
            P("fsdp", "ctx", None),
            P("fsdp", "ctx", None),
            P("fsdp", "ctx", None),
        ),
        check_vma=False,
    )
```

```python
from functools import partial
import math

import jax
import jax.numpy as jnp
from jax import lax
from jax.experimental import pallas as pl
from jax.experimental.pallas import tpu as pltpu
from jax.sharding import PartitionSpec as P

HEAD_DIM = 128


epsilon = 1e-06
rope_base = 10000.0
masked_value = -1e30


def rms_scaled(values, gain):
    return values * lax.rsqrt(jnp.mean(values * values, axis=-1, keepdims=True) + epsilon) * gain


def rotate(values, places):
    row_count = values.shape[0]
    head_count = values.shape[1] // HEAD_DIM
    half_width = HEAD_DIM // 2
    frequency = rope_base ** (-2.0 * jnp.arange(half_width).astype(jnp.float32) / HEAD_DIM)
    angles = places.astype(jnp.float32)[:, None] * frequency[None, :]
    cosine = jnp.cos(angles)[:, None, :]
    sine_part = jnp.sin(angles)[:, None, :]
    split_heads = values.reshape(row_count, head_count, HEAD_DIM)
    first_half = split_heads[:, :, :half_width]
    second_half = split_heads[:, :, half_width:]
    turned = jnp.concatenate(
        [
            first_half * cosine - second_half * sine_part,
            second_half * cosine + first_half * sine_part,
        ],
        axis=-1,
    )
    return turned.reshape(row_count, head_count * HEAD_DIM)


def qk_post(values, gain, places):
    return rotate(rms_scaled(values, gain), places)


def route_weights(logits, chosen):
    router_probs = jax.nn.softmax(logits, axis=-1)
    return jnp.sum(jnp.where(chosen, router_probs[:, None, :], 0.0), axis=-1)


def seq_layout(order_row, seq_lengths):
    seq_ends = jnp.cumsum(seq_lengths)
    seq_ids = jnp.sum((order_row[:, None] >= seq_ends[None, :]).astype(jnp.int32), axis=1)
    starts = seq_ends - seq_lengths
    chosen = seq_ids[:, None] == jnp.arange(seq_lengths.shape[0], dtype=jnp.int32)[None, :]
    seq_start = jnp.sum(jnp.where(chosen, starts[None, :], 0), axis=1)
    return (seq_ids, order_row - seq_start)


def general_shards(
    hidden,
    token_order,
    lengths,
    routes,
    grad_output,
    w_query,
    w_key,
    w_value,
    w_out,
    w_router,
    attn_gain,
    ffn_gain,
    query_gain,
    key_gain,
    w_gate,
    w_up,
    w_down,
):
    hidden_in = hidden[0].astype(jnp.float32)
    row_count = hidden_in.shape[0]
    model_width = hidden_in.shape[1]
    head_count = model_width // HEAD_DIM
    score_scale = 1.0 / math.sqrt(HEAD_DIM)
    seq_all, place_all = seq_layout(token_order[0], lengths[0])
    first_row = lax.axis_index("ctx") * row_count
    seq_mine = lax.dynamic_slice_in_dim(seq_all, first_row, row_count)
    place_mine = lax.dynamic_slice_in_dim(place_all, first_row, row_count)
    same_seq = seq_mine[:, None] == seq_all[None, :]
    gathered = (
        lax.all_gather(w_query, ("ctx", "fsdp"), axis=0, tiled=True),
        lax.all_gather(w_key, ("ctx", "fsdp"), axis=0, tiled=True),
        lax.all_gather(w_value, ("ctx", "fsdp"), axis=0, tiled=True),
        lax.all_gather(w_out, ("ctx", "fsdp"), axis=0, tiled=True),
        lax.all_gather(w_router, ("ctx", "fsdp"), axis=0, tiled=True),
        lax.all_gather(attn_gain, ("ctx", "fsdp"), axis=0, tiled=True),
        lax.all_gather(ffn_gain, ("ctx", "fsdp"), axis=0, tiled=True),
        lax.all_gather(query_gain, ("ctx", "fsdp"), axis=0, tiled=True),
        lax.all_gather(key_gain, ("ctx", "fsdp"), axis=0, tiled=True),
    )
    (
        full_query,
        full_key,
        full_value,
        full_out,
        full_router,
        gain_attn,
        gain_ffn,
        gain_query,
        gain_key,
    ) = gathered
    gain_attn = gain_attn.astype(jnp.float32)
    gain_ffn = gain_ffn.astype(jnp.float32)
    gain_query = gain_query.astype(jnp.float32)
    gain_key = gain_key.astype(jnp.float32)
    h_one, norm_one_back = jax.vjp(rms_scaled, hidden_in, gain_attn)
    h_one_low = h_one.astype(jnp.bfloat16)
    query_raw = jnp.dot(h_one_low, full_query, preferred_element_type=jnp.float32)
    key_raw = jnp.dot(h_one_low, full_key, preferred_element_type=jnp.float32)
    values_low = jnp.dot(h_one_low, full_value, preferred_element_type=jnp.float32).astype(
        jnp.bfloat16
    )
    query_rot, query_back = jax.vjp(partial(qk_post, places=place_mine), query_raw, gain_query)
    key_rot, key_back = jax.vjp(partial(qk_post, places=place_mine), key_raw, gain_key)
    query_low = query_rot.astype(jnp.bfloat16)
    key_low = key_rot.astype(jnp.bfloat16)
    key_all, value_all = (
        lax.all_gather(key_low, "ctx", axis=0, tiled=True),
        lax.all_gather(values_low, "ctx", axis=0, tiled=True),
    )
    query_heads = query_low.reshape(row_count, head_count, HEAD_DIM)
    key_heads = key_all.reshape(-1, head_count, HEAD_DIM)
    value_heads = value_all.reshape(-1, head_count, HEAD_DIM)

    def scores_of():
        raw_scores = (
            jnp.einsum("thd,khd->htk", query_heads, key_heads, preferred_element_type=jnp.float32)
            * score_scale
        )
        return jnp.where(same_seq[None, :, :], raw_scores, masked_value)

    scores = scores_of()
    row_top = jnp.max(scores, axis=-1, keepdims=True)
    log_total = row_top + jnp.log(jnp.sum(jnp.exp(scores - row_top), axis=-1, keepdims=True))
    probs_low = jnp.exp(scores - log_total).astype(jnp.bfloat16)
    attended = jnp.einsum(
        "htk,khd->thd", probs_low, value_heads, preferred_element_type=jnp.float32
    )
    attended_low = attended.reshape(row_count, model_width).astype(jnp.bfloat16)
    middle = hidden_in + jnp.dot(attended_low, full_out, preferred_element_type=jnp.float32)
    h_two, norm_two_back = jax.vjp(rms_scaled, middle, gain_ffn)
    h_two_low = h_two.astype(jnp.bfloat16)
    logits = jnp.dot(h_two_low, full_router, preferred_element_type=jnp.float32)
    expert_count = full_router.shape[1]
    route_rows = routes[0]
    top_k = route_rows.shape[1]
    chosen = route_rows[:, :, None] == jnp.arange(expert_count, dtype=jnp.int32)[None, None, :]
    picked, route_back = jax.vjp(partial(route_weights, chosen=chosen), logits)
    pair_count = row_count * top_k
    capacity = 5 * row_count * top_k // (4 * expert_count)
    slot_count = expert_count * capacity
    group_size = lax.axis_size("fsdp")
    local_experts = w_gate.shape[0]
    pair_expert = route_rows.reshape(pair_count)
    one_hot = (pair_expert[:, None] == jnp.arange(expert_count, dtype=jnp.int32)[None, :]).astype(
        jnp.int32
    )
    slot_rank = jnp.sum(one_hot * (jnp.cumsum(one_hot, axis=0) - 1), axis=1)
    slot_ids = pair_expert * capacity + slot_rank
    source = (
        jnp.full((slot_count,), pair_count, jnp.int32)
        .at[slot_ids]
        .set(jnp.arange(pair_count, dtype=jnp.int32))
    )
    filled = source < pair_count
    source_pair = jnp.minimum(source, pair_count - 1)
    send_rows = jnp.where(
        filled[:, None], h_two_low[source_pair // top_k], jnp.zeros((), jnp.bfloat16)
    )
    send_rows = send_rows.reshape(group_size, local_experts, capacity, model_width)
    gate_full, up_full, down_full = (
        lax.all_gather(w_gate, "ctx", axis=1, tiled=True),
        lax.all_gather(w_up, "ctx", axis=1, tiled=True),
        lax.all_gather(w_down, "ctx", axis=1, tiled=True),
    )
    arrived_rows = lax.all_to_all(send_rows, "fsdp", split_axis=0, concat_axis=0, tiled=True)
    gate_part = jnp.einsum(
        "secd,edf->secf", arrived_rows, gate_full, preferred_element_type=jnp.float32
    )
    up_part = jnp.einsum(
        "secd,edf->secf", arrived_rows, up_full, preferred_element_type=jnp.float32
    )
    act_part = (jax.nn.silu(gate_part) * up_part).astype(jnp.bfloat16)
    result = jnp.einsum(
        "secf,efd->secd", act_part, down_full, preferred_element_type=jnp.float32
    ).astype(jnp.bfloat16)
    returned = lax.all_to_all(result, "fsdp", split_axis=0, concat_axis=0, tiled=True).reshape(
        slot_count, model_width
    )
    pair_out = returned[slot_ids].reshape(row_count, top_k, model_width)
    output = (middle + jnp.sum(picked[:, :, None] * pair_out, axis=1)).astype(jnp.bfloat16)
    grad_top = grad_output[0].astype(jnp.float32)
    grad_picked = jnp.sum(grad_top[:, None, :] * pair_out, axis=-1)
    grad_pair = (
        (picked[:, :, None] * grad_top[:, None, :])
        .astype(jnp.bfloat16)
        .reshape(pair_count, model_width)
    )
    grad_send = jnp.where(filled[:, None], grad_pair[source_pair], jnp.zeros((), jnp.bfloat16))
    grad_send = grad_send.reshape(group_size, local_experts, capacity, model_width)
    grad_arrived = lax.all_to_all(grad_send, "fsdp", split_axis=0, concat_axis=0, tiled=True)
    sigma = jax.nn.sigmoid(gate_part)
    act_low = (gate_part * sigma * up_part).astype(jnp.bfloat16)
    grad_act = jnp.einsum(
        "secd,efd->secf", grad_arrived, down_full, preferred_element_type=jnp.float32
    )
    grad_gate = (grad_act * up_part * sigma * (1.0 + gate_part * (1.0 - sigma))).astype(
        jnp.bfloat16
    )
    grad_up = (grad_act * gate_part * sigma).astype(jnp.bfloat16)
    grad_back = jnp.einsum(
        "secf,edf->secd", grad_gate, gate_full, preferred_element_type=jnp.float32
    )
    grad_back = (
        grad_back
        + jnp.einsum("secf,edf->secd", grad_up, up_full, preferred_element_type=jnp.float32)
    ).astype(jnp.bfloat16)
    grad_return = lax.all_to_all(
        grad_back, "fsdp", split_axis=0, concat_axis=0, tiled=True
    ).reshape(slot_count, model_width)
    grad_h_two = jnp.sum(
        grad_return[slot_ids].reshape(row_count, top_k, model_width).astype(jnp.float32), axis=1
    )
    (grad_logits,) = route_back(grad_picked)
    grad_logits_low = grad_logits.astype(jnp.bfloat16)
    grad_h_two = grad_h_two + jnp.einsum(
        "te,de->td", grad_logits_low, full_router, preferred_element_type=jnp.float32
    )
    grad_router = jnp.einsum(
        "td,te->de", h_two_low, grad_logits_low, preferred_element_type=jnp.float32
    )
    grad_middle, grad_ffn_gain = norm_two_back(grad_h_two)
    grad_middle = grad_middle + grad_top
    grad_branch = grad_middle.astype(jnp.bfloat16)
    grad_out_w = jnp.einsum(
        "td,te->de", attended_low, grad_branch, preferred_element_type=jnp.float32
    )
    grad_att = jnp.einsum(
        "te,de->td", grad_branch, full_out, preferred_element_type=jnp.float32
    ).astype(jnp.bfloat16)
    grad_att = grad_att.reshape(row_count, head_count, HEAD_DIM)
    scores = scores_of()
    probs_full = jnp.exp(scores - log_total)
    probs_again = probs_full.astype(jnp.bfloat16)
    grad_probs = jnp.einsum(
        "thd,khd->htk", grad_att, value_heads, preferred_element_type=jnp.float32
    )
    spread = jnp.sum(probs_full * grad_probs, axis=-1, keepdims=True)
    grad_scores = (probs_full * (grad_probs - spread)).astype(jnp.bfloat16)
    grad_query = (
        jnp.einsum(
            "htk,khd->thd", grad_scores, key_heads, preferred_element_type=jnp.float32
        ).reshape(row_count, model_width)
        * score_scale
    )
    grad_key_part = (
        jnp.einsum(
            "htk,thd->khd", grad_scores, query_heads, preferred_element_type=jnp.float32
        ).reshape(-1, model_width)
        * score_scale
    )
    grad_value_part = jnp.einsum(
        "htk,thd->khd", probs_again, grad_att, preferred_element_type=jnp.float32
    ).reshape(-1, model_width)
    grad_key, grad_value = (
        lax.psum_scatter(
            grad_key_part.astype(jnp.bfloat16), "ctx", scatter_dimension=0, tiled=True
        ).astype(jnp.float32),
        lax.psum_scatter(
            grad_value_part.astype(jnp.bfloat16), "ctx", scatter_dimension=0, tiled=True
        ).astype(jnp.float32),
    )
    grad_q_raw, grad_q_gain = query_back(grad_query)
    grad_k_raw, grad_k_gain = key_back(grad_key)
    grad_q_low = grad_q_raw.astype(jnp.bfloat16)
    grad_k_low = grad_k_raw.astype(jnp.bfloat16)
    grad_v_low = grad_value.astype(jnp.bfloat16)
    grad_query_w = jnp.einsum(
        "td,te->de", h_one_low, grad_q_low, preferred_element_type=jnp.float32
    )
    grad_key_w = jnp.einsum("td,te->de", h_one_low, grad_k_low, preferred_element_type=jnp.float32)
    grad_value_w = jnp.einsum(
        "td,te->de", h_one_low, grad_v_low, preferred_element_type=jnp.float32
    )
    grad_h_one = jnp.einsum("te,de->td", grad_q_low, full_query, preferred_element_type=jnp.float32)
    grad_h_one = grad_h_one + jnp.einsum(
        "te,de->td", grad_k_low, full_key, preferred_element_type=jnp.float32
    )
    grad_h_one = grad_h_one + jnp.einsum(
        "te,de->td", grad_v_low, full_value, preferred_element_type=jnp.float32
    )
    grad_input_norm, grad_attn_gain = norm_one_back(grad_h_one)
    grad_input = grad_middle + grad_input_norm
    totals = (
        lax.psum_scatter(grad_query_w, ("ctx", "fsdp"), scatter_dimension=0, tiled=True),
        lax.psum_scatter(grad_key_w, ("ctx", "fsdp"), scatter_dimension=0, tiled=True),
        lax.psum_scatter(grad_value_w, ("ctx", "fsdp"), scatter_dimension=0, tiled=True),
        lax.psum_scatter(grad_out_w, ("ctx", "fsdp"), scatter_dimension=0, tiled=True),
        lax.psum_scatter(grad_router, ("ctx", "fsdp"), scatter_dimension=0, tiled=True),
        lax.psum_scatter(grad_attn_gain, ("ctx", "fsdp"), scatter_dimension=0, tiled=True),
        lax.psum_scatter(grad_ffn_gain, ("ctx", "fsdp"), scatter_dimension=0, tiled=True),
        lax.psum_scatter(grad_q_gain, ("ctx", "fsdp"), scatter_dimension=0, tiled=True),
        lax.psum_scatter(grad_k_gain, ("ctx", "fsdp"), scatter_dimension=0, tiled=True),
    )
    grad_down_w = jnp.einsum(
        "secf,secd->efd", act_low, grad_arrived, preferred_element_type=jnp.float32
    )
    grad_gate_w = jnp.einsum(
        "secd,secf->edf", arrived_rows, grad_gate, preferred_element_type=jnp.float32
    )
    grad_up_w = jnp.einsum(
        "secd,secf->edf", arrived_rows, grad_up, preferred_element_type=jnp.float32
    )
    gate_grad, up_grad, down_grad = (
        lax.psum_scatter(
            grad_gate_w.astype(jnp.bfloat16), "ctx", scatter_dimension=1, tiled=True
        ).astype(jnp.float32),
        lax.psum_scatter(
            grad_up_w.astype(jnp.bfloat16), "ctx", scatter_dimension=1, tiled=True
        ).astype(jnp.float32),
        lax.psum_scatter(
            grad_down_w.astype(jnp.bfloat16), "ctx", scatter_dimension=1, tiled=True
        ).astype(jnp.float32),
    )
    return (
        output[None],
        grad_input[None],
        totals[0],
        totals[1],
        totals[2],
        totals[3],
        totals[4],
        totals[5],
        totals[6],
        totals[7],
        totals[8],
        gate_grad,
        up_grad,
        down_grad,
    )


def masked_probs(query, key, seq_rows, seq_cols, scale):
    scores = (
        lax.dot_general(query, key, (((1,), (1,)), ((), ())), preferred_element_type=jnp.float32)
        * scale
    )
    scores = jnp.where(seq_rows == seq_cols, scores, masked_value)
    top = jnp.max(scores, axis=-1, keepdims=True)
    weights = jnp.exp(scores - top)
    return weights / jnp.sum(weights, axis=-1, keepdims=True)


def attend_kernel(scale, seq_rows, seq_cols, query, key, value, out):
    probs = masked_probs(query[...], key[...], seq_rows[...], seq_cols[...], scale)
    out[...] = jnp.dot(
        probs.astype(jnp.bfloat16), value[...], preferred_element_type=jnp.float32
    ).astype(out.dtype)


def attend_back_kernel(
    scale, seq_rows, seq_cols, query, key, value, grad, grad_query, grad_key, grad_value
):
    @pl.when(pl.program_id(1) == 0)
    def _():
        grad_key[...] = jnp.zeros_like(grad_key)
        grad_value[...] = jnp.zeros_like(grad_value)

    probs = masked_probs(query[...], key[...], seq_rows[...], seq_cols[...], scale)
    grad_probs = lax.dot_general(
        grad[...], value[...], (((1,), (1,)), ((), ())), preferred_element_type=jnp.float32
    )
    spread = jnp.sum(probs * grad_probs, axis=-1, keepdims=True)
    grad_scores = (probs * (grad_probs - spread)).astype(jnp.bfloat16)
    grad_query[...] = (
        jnp.dot(grad_scores, key[...], preferred_element_type=jnp.float32) * scale
    )
    grad_key[...] += (
        lax.dot_general(
            grad_scores,
            query[...],
            (((0,), (0,)), ((), ())),
            preferred_element_type=jnp.float32,
        )
        * scale
    )
    grad_value[...] += lax.dot_general(
        probs.astype(jnp.bfloat16),
        grad[...],
        (((0,), (0,)), ((), ())),
        preferred_element_type=jnp.float32,
    )


def attention_specs(rows, block):
    per_block = pl.BlockSpec((block, HEAD_DIM), lambda h, i: (i, h))
    per_head = pl.BlockSpec((rows, HEAD_DIM), lambda h, i: (0, h))
    seqs = [
        pl.BlockSpec((block, 1), lambda h, i: (i, 0)),
        pl.BlockSpec((1, rows), lambda h, i: (0, 0)),
    ]
    return per_block, per_head, seqs


def attend(seq_ids, query, key, value):
    rows, width = query.shape
    block = math.gcd(rows, 256)
    per_block, per_head, seqs = attention_specs(rows, block)
    pairs = rows * rows * width
    return pl.pallas_call(
        partial(attend_kernel, 1.0 / math.sqrt(HEAD_DIM)),
        grid=(width // HEAD_DIM, rows // block),
        in_specs=seqs + [per_block, per_head, per_head],
        out_specs=per_block,
        out_shape=jax.ShapeDtypeStruct((rows, width), jnp.bfloat16),
        cost_estimate=pl.CostEstimate(
            flops=4 * pairs, bytes_accessed=8 * rows * width, transcendentals=pairs // HEAD_DIM
        ),
        compiler_params=pltpu.CompilerParams(vmem_limit_bytes=48 << 20),
        name="attend",
    )(seq_ids[:, None], seq_ids[None, :], query, key, value)


def attend_back(seq_ids, query, key, value, grad):
    rows, width = query.shape
    block = math.gcd(rows, 256)
    per_block, per_head, seqs = attention_specs(rows, block)
    pairs = rows * rows * width
    return pl.pallas_call(
        partial(attend_back_kernel, 1.0 / math.sqrt(HEAD_DIM)),
        grid=(width // HEAD_DIM, rows // block),
        in_specs=seqs + [per_block, per_head, per_head, per_block],
        out_specs=(per_block, per_head, per_head),
        out_shape=(jax.ShapeDtypeStruct((rows, width), jnp.float32),) * 3,
        cost_estimate=pl.CostEstimate(
            flops=10 * pairs, bytes_accessed=20 * rows * width, transcendentals=pairs // HEAD_DIM
        ),
        compiler_params=pltpu.CompilerParams(vmem_limit_bytes=48 << 20),
        name="attend_back",
    )(seq_ids[:, None], seq_ids[None, :], query, key, value, grad)


def dispatch_kernel(position, rows, out):
    columns, _, capacity, width = out.shape
    count = rows.shape[1]
    slots = lax.broadcasted_iota(jnp.int32, (columns, capacity, count), 1)
    select = jnp.where(slots == position[:, 0], 1.0, 0.0)
    select = select.reshape(columns * capacity, count).astype(jnp.bfloat16)
    step = math.gcd(width, 512)
    for at in range(0, width, step):
        part = jnp.dot(select, rows[0, :, at : at + step], preferred_element_type=jnp.float32)
        part = part.reshape(columns, capacity, step).astype(out.dtype)
        out[:, 0, :, at : at + step] = part


def dispatch(position, capacity, rows):
    columns, planes, count = position.shape
    width = rows.shape[1]
    return pl.pallas_call(
        dispatch_kernel,
        grid=(planes,),
        in_specs=[
            pl.BlockSpec((columns, 1, 1, count), lambda b: (0, b, 0, 0)),
            pl.BlockSpec((1, count, width), lambda b: (b, 0, 0)),
        ],
        out_specs=pl.BlockSpec((columns, 1, capacity, width), lambda b: (0, b, 0, 0)),
        out_shape=jax.ShapeDtypeStruct((columns, planes, capacity, width), jnp.bfloat16),
        cost_estimate=pl.CostEstimate(
            flops=2 * position.size * capacity * width,
            bytes_accessed=2 * columns * planes * capacity * width,
            transcendentals=0,
        ),
        compiler_params=pltpu.CompilerParams(vmem_limit_bytes=40 << 20),
        name="dispatch",
    )(position[:, :, None], rows.reshape(planes, count, width))


def heads_of(width):
    return [slice(at, at + HEAD_DIM) for at in range(0, width, HEAD_DIM)]


def turn_kernel(raw, scales, gains, cosine, sine, query, key, value):
    width = query.shape[1]
    for which, out in ((0, query), (1, key)):
        scale = scales[:, which : which + 1]
        for head in heads_of(width):
            part = raw[:, which * width + head.start : which * width + head.stop]
            part = part * scale * gains[which : which + 1, head]
            swapped = pltpu.roll(part, HEAD_DIM // 2, 1)
            out[:, head] = (part * cosine[...] + swapped * sine[...]).astype(out.dtype)
    value[...] = raw[:, 2 * width : 3 * width].astype(value.dtype)


def turn_back_kernel(
    raw, scales, gains, cosine, sine, grad_query, grad_key, out_query, out_key, dots, grad_gains
):
    @pl.when(pl.program_id(0) == 0)
    def _():
        grad_gains[...] = jnp.zeros_like(grad_gains)

    width = grad_query.shape[1]
    for which, grad, out in ((0, grad_query, out_query), (1, grad_key, out_key)):
        scale = scales[:, which : which + 1]
        total = jnp.zeros_like(scale)
        for head in heads_of(width):
            part = grad[:, head]
            part = part * cosine[...] - pltpu.roll(part, HEAD_DIM // 2, 1) * sine[...]
            hat = raw[:, which * width + head.start : which * width + head.stop] * scale
            grad_gains[which : which + 1, head] += jnp.sum(part * hat, axis=0, keepdims=True)
            part = part * gains[which : which + 1, head]
            total += jnp.sum(part * hat, axis=1, keepdims=True)
            out[:, head] = part
        dots[:, which : which + 1] = total


def turn_specs(raw, gains):
    block = math.gcd(raw.shape[0], 256)
    return block, [
        pl.BlockSpec((block, raw.shape[1]), lambda i: (i, 0)),
        pl.BlockSpec((block, 2), lambda i: (i, 0)),
        pl.BlockSpec(gains.shape, lambda i: (0, 0)),
        pl.BlockSpec((block, HEAD_DIM), lambda i: (i, 0)),
        pl.BlockSpec((block, HEAD_DIM), lambda i: (i, 0)),
    ]


def turn(raw, scales, gains, cosine, sine):
    rows, width = raw.shape[0], gains.shape[1]
    block, specs = turn_specs(raw, gains)
    return pl.pallas_call(
        turn_kernel,
        grid=(rows // block,),
        in_specs=specs,
        out_specs=(pl.BlockSpec((block, width), lambda i: (i, 0)),) * 3,
        out_shape=(jax.ShapeDtypeStruct((rows, width), jnp.bfloat16),) * 3,
        cost_estimate=pl.CostEstimate(
            flops=16 * rows * width, bytes_accessed=18 * rows * width, transcendentals=0
        ),
        compiler_params=pltpu.CompilerParams(vmem_limit_bytes=40 << 20),
        name="turn",
    )(raw, scales, gains, cosine, sine)


def turn_back(raw, scales, gains, cosine, sine, grad_query, grad_key):
    rows, width = grad_query.shape
    block, specs = turn_specs(raw, gains)
    wide = pl.BlockSpec((block, width), lambda i: (i, 0))
    f32 = jnp.float32
    return pl.pallas_call(
        turn_back_kernel,
        grid=(rows // block,),
        in_specs=specs + [wide, wide],
        out_specs=(
            wide,
            wide,
            pl.BlockSpec((block, 2), lambda i: (i, 0)),
            pl.BlockSpec((2, width), lambda i: (0, 0)),
        ),
        out_shape=(
            jax.ShapeDtypeStruct((rows, width), f32),
            jax.ShapeDtypeStruct((rows, width), f32),
            jax.ShapeDtypeStruct((rows, 2), f32),
            jax.ShapeDtypeStruct((2, width), f32),
        ),
        cost_estimate=pl.CostEstimate(
            flops=24 * rows * width, bytes_accessed=28 * rows * width, transcendentals=0
        ),
        compiler_params=pltpu.CompilerParams(vmem_limit_bytes=40 << 20),
        name="turn_back",
    )(raw, scales, gains, cosine, sine, grad_query, grad_key)


def expert_in_kernel(
    rows, gate, up, router, own, gate_out, up_out, act_out, picked_out
):
    logits = jnp.dot(rows[...], router[...], preferred_element_type=jnp.float32)
    weights = jnp.exp(logits - jnp.max(logits, axis=1, keepdims=True))
    picked = jnp.sum(weights * own[...], axis=1, keepdims=True)
    picked = picked / jnp.sum(weights, axis=1, keepdims=True)
    gate_pre = jnp.dot(rows[...], gate[...], preferred_element_type=jnp.float32)
    up_pre = jnp.dot(rows[...], up[...], preferred_element_type=jnp.float32)
    act = (gate_pre * jax.nn.sigmoid(gate_pre) * up_pre).astype(jnp.bfloat16)
    gate_out[...] = gate_pre
    up_out[...] = up_pre
    act_out[...] = (act.astype(jnp.float32) * picked).astype(jnp.bfloat16)
    picked_out[...] = picked


def expert_back_kernel(
    grad, gate_in, up_in, picked, gate, up, down, grad_gate, grad_up, grad_picked, grad_rows
):
    grad_raw = lax.dot_general(
        grad[...], down[...], (((1,), (1,)), ((), ())), preferred_element_type=jnp.float32
    )
    gate_pre, up_pre = gate_in[...], up_in[...]
    sigma = jax.nn.sigmoid(gate_pre)
    silu = gate_pre * sigma
    act = (silu * up_pre).astype(jnp.bfloat16).astype(jnp.float32)
    grad_picked[...] = jnp.sum(grad_raw * act, axis=1, keepdims=True)
    grad_act = grad_raw * picked[...]
    low_gate = (grad_act * up_pre * (sigma + silu * (1.0 - sigma))).astype(jnp.bfloat16)
    low_up = (grad_act * silu).astype(jnp.bfloat16)
    grad_gate[...] = low_gate
    grad_up[...] = low_up
    back = lax.dot_general(
        low_gate, gate[...], (((1,), (1,)), ((), ())), preferred_element_type=jnp.float32
    )
    back = back + lax.dot_general(
        low_up, up[...], (((1,), (1,)), ((), ())), preferred_element_type=jnp.float32
    )
    grad_rows[...] = back.astype(jnp.bfloat16)


def whole(shape):
    return pl.BlockSpec(shape, lambda i: (0, 0), pipeline_mode=pl.Buffered(1))


def row_blocks(block, width):
    return pl.BlockSpec((block, width), lambda i: (i, 0))


def expert_in(rows, gate, up, router, own, block):
    count, width = rows.shape
    hidden = gate.shape[1]
    narrow = row_blocks(block, hidden)
    f32 = jnp.float32
    return pl.pallas_call(
        expert_in_kernel,
        grid=(count // block,),
        in_specs=[
            row_blocks(block, width),
            whole(gate.shape),
            whole(up.shape),
            whole(router.shape),
            whole(own.shape),
        ],
        out_specs=(narrow, narrow, narrow, row_blocks(block, 1)),
        out_shape=(
            jax.ShapeDtypeStruct((count, hidden), f32),
            jax.ShapeDtypeStruct((count, hidden), f32),
            jax.ShapeDtypeStruct((count, hidden), jnp.bfloat16),
            jax.ShapeDtypeStruct((count, 1), f32),
        ),
        cost_estimate=pl.CostEstimate(
            flops=4 * count * width * hidden,
            bytes_accessed=2 * count * width + (10 * count + 4 * width) * hidden,
            transcendentals=count * hidden,
        ),
        compiler_params=pltpu.CompilerParams(vmem_limit_bytes=56 << 20),
        name="expert_in",
    )(rows, gate, up, router, own)


def expert_back(grad, gate_pre, up_pre, picked, gate, up, down, block):
    count, width = grad.shape
    hidden = down.shape[0]
    wide, narrow, one = [row_blocks(block, size) for size in (width, hidden, 1)]
    low = jax.ShapeDtypeStruct((count, hidden), jnp.bfloat16)
    return pl.pallas_call(
        expert_back_kernel,
        grid=(count // block,),
        in_specs=[wide, narrow, narrow, one, whole(gate.shape), whole(up.shape), whole(down.shape)],
        out_specs=(narrow, narrow, one, wide),
        out_shape=(
            low,
            low,
            jax.ShapeDtypeStruct((count, 1), jnp.float32),
            jax.ShapeDtypeStruct((count, width), jnp.bfloat16),
        ),
        cost_estimate=pl.CostEstimate(
            flops=6 * count * width * hidden,
            bytes_accessed=4 * count * width + (12 * count + 6 * width) * hidden,
            transcendentals=count * hidden,
        ),
        compiler_params=pltpu.CompilerParams(vmem_limit_bytes=58 << 20),
        name="expert_back",
    )(grad, gate_pre, up_pre, picked, gate, up, down)


def tie(array, *others):
    anywhere = pl.BlockSpec(memory_space=pl.ANY)
    return pl.pallas_call(
        lambda *refs: None,
        in_specs=[anywhere] * (1 + len(others)),
        out_specs=anywhere,
        out_shape=jax.ShapeDtypeStruct(array.shape, array.dtype),
        input_output_aliases={0: 0},
        name="tie",
    )(array, *others)


def mm(left, right):
    return jnp.dot(left, right, preferred_element_type=jnp.float32)


def mm_t(left, right):
    return lax.dot_general(
        left, right, (((1,), (1,)), ((), ())), preferred_element_type=jnp.float32
    )


def t_mm(left, right):
    return lax.dot_general(
        left, right, (((0,), (0,)), ((), ())), preferred_element_type=jnp.float32
    )


def plane_shards(
    hidden,
    token_order,
    lengths,
    routes,
    grad_output,
    w_query,
    w_key,
    w_value,
    w_out,
    w_router,
    attn_gain,
    ffn_gain,
    query_gain,
    key_gain,
    w_gate,
    w_up,
    w_down,
):
    f32, bf16 = jnp.float32, jnp.bfloat16
    both = ("ctx", "fsdp")
    planes = lax.axis_size("ctx")
    columns = lax.axis_size("fsdp")
    plane = lax.axis_index("ctx")
    row_count, width = hidden.shape[1:]
    group_rows = row_count * planes
    share = width // planes
    strip = w_query.shape[0]
    first_row = plane * row_count

    experts = w_router.shape[1]
    qkv = jnp.stack([w_query, w_key, w_value], axis=1).reshape(strip, 3, planes, share)
    qkv = qkv.transpose(2, 0, 1, 3).reshape(planes, strip, 3 * share)
    small = [w_router] + [g[:, None] for g in (attn_gain, ffn_gain, query_gain, key_gain)]
    small = jnp.concatenate(small + [routes.astype(bf16).reshape(strip, -1)], axis=1)
    spare = -small.shape[1] % 128
    small = jnp.pad(small, ((0, 0), (0, spare)))
    small = jnp.broadcast_to(small[None], (planes,) + small.shape)
    own_out = jnp.broadcast_to(w_out[None], (planes,) + w_out.shape)
    packed = jnp.concatenate([qkv, small, own_out], axis=2)
    packed = lax.all_to_all(packed, "ctx", 0, 0, tiled=True)
    hidden_all = lax.all_gather(tie(hidden[0], packed), "ctx", axis=0, tiled=True)
    packed, out_rows = packed[:, :, :-width], packed[:, :, -width:]
    routes_at = 3 * share + experts + 4
    routes_all = packed[:, :, routes_at : packed.shape[2] - spare].astype(jnp.int32)
    routes_all = routes_all.reshape(group_rows, -1)
    packed = jnp.broadcast_to(packed[None], (columns,) + packed.shape)
    packed = lax.all_to_all(packed, "fsdp", 0, 0, tiled=True)
    packed = packed.transpose(1, 0, 2, 3).reshape(width, -1)
    full_router = packed[:, 3 * share : 3 * share + experts]
    gain_attn, gain_ffn, gain_query, gain_key = [
        packed[:, 3 * share + experts + i].astype(f32) for i in range(4)
    ]
    def swap(part, step):
        return lax.ppermute(part, "ctx", [(i, i ^ step) for i in range(planes)])

    def by_plane(came):
        came = jnp.stack(came)
        return [came[plane ^ i] for i in range(planes)]

    def exchange(parts, first=None, last=None):
        came = [parts[plane]]
        for step in range(1, planes):
            part = parts[plane ^ step]
            part = swap(part if first is None else tie(part, first), step)
            came.append(part if last is None else tie(part, last))
        return by_plane(came)

    def exchange_after(parts, earlier):
        came = [
            swap(tie(part, *before) if before else part, step)
            for step, before in enumerate(earlier, 1)
            for part in [parts[plane ^ step]]
        ]
        return came, jnp.stack(by_plane([parts[plane]] + came)).astype(f32)

    def plane_sum(part):
        return part + sum(swap(part, step) for step in range(1, planes))

    out_rows = jnp.broadcast_to(out_rows[None], (columns,) + out_rows.shape)
    grad_all = lax.all_gather(
        tie(grad_output[0], hidden_all, packed, out_rows), "ctx", axis=0, tiled=True
    )
    full_out = lax.all_to_all(out_rows, "fsdp", 0, 0, tiled=True)

    seq_ids, places = seq_layout(token_order[0], lengths[0])
    experts_here = w_gate.shape[0]
    column_expert = experts_here * jnp.arange(columns, dtype=jnp.int32) + plane
    named = jnp.any(routes_all[:, :, None] == column_expert[None, None, :], axis=1)
    named = named.reshape(planes, row_count, columns)
    capacity = 5 * row_count * routes.shape[2] // (4 * experts)
    rank = jnp.cumsum(named.astype(jnp.int32), axis=1) - 1
    position = jnp.where(named, rank, -1).transpose(2, 0, 1)
    slots = jnp.arange(capacity, dtype=jnp.int32)
    holds = position[:, :, None, :] == slots[None, None, :, None]
    select = holds.astype(bf16)

    def combine(rows):
        rows = rows.reshape(columns, planes, capacity, width)
        sums = jnp.einsum("fbsr,fbsd->brd", select, rows, preferred_element_type=f32)
        return sums.reshape(group_rows, width).astype(bf16)


    frequency = rope_base ** (
        -2.0 * jnp.arange(HEAD_DIM // 2).astype(f32) / HEAD_DIM
    )
    angles = places.astype(f32)[:, None] * frequency[None, :]
    cosine, sine = jnp.cos(angles), jnp.sin(angles)
    cosine = jnp.concatenate([cosine, cosine], axis=1)
    sine = jnp.concatenate([-sine, sine], axis=1)
    hidden_wide = hidden_all.astype(f32)
    scale_one = lax.rsqrt(jnp.mean(hidden_wide * hidden_wide, axis=-1, keepdims=True) + epsilon)
    h_one = (hidden_wide * scale_one * gain_attn).astype(bf16)
    raw = mm(h_one, packed)
    squares = jnp.stack(
        [jnp.sum(raw[:, :share] ** 2, axis=1), jnp.sum(raw[:, share : 2 * share] ** 2, axis=1)]
    )
    squares = plane_sum(squares)
    scales = lax.rsqrt(squares / width + epsilon).T
    gains = lax.dynamic_slice_in_dim(
        jnp.stack([gain_query, gain_key]), plane * share, share, axis=1
    )
    query, key, values = turn(raw, scales, gains, cosine, sine)
    attended = attend(seq_ids, query, key, values)
    full_out = tie(full_out, attended).transpose(1, 0, 2, 3).reshape(width, width)
    grad_send = dispatch(position, capacity, tie(grad_all, attended, full_out))
    attended = attended.reshape(planes, row_count, share)
    attended = jnp.concatenate(exchange(attended, grad_all), axis=1)
    grad_in = lax.all_to_all(grad_send, "fsdp", 0, 0, tiled=True).reshape(-1, width)
    middle = hidden[0].astype(f32) + mm(attended, full_out)
    scale_two = lax.rsqrt(jnp.mean(middle * middle, axis=-1, keepdims=True) + epsilon)
    middle_hat = middle * scale_two
    h_two = (middle_hat * gain_ffn).astype(bf16)

    h_two_all = lax.all_gather(tie(h_two, grad_send), "ctx", axis=0, tiled=True)
    steps = range(1, planes)
    came_gate = [swap(tie(w_gate[plane ^ step], h_two_all), step) for step in steps]
    h_all = tie(h_two_all, grad_in, came_gate[planes // 2 - 1])
    gate = jnp.concatenate(by_plane([w_gate[plane]] + came_gate))
    came_up = [
        swap(tie(w_up[plane ^ step], before), step) for step, before in zip(steps, came_gate)
    ]
    up = jnp.concatenate(by_plane([w_up[plane]] + came_up))
    came_down = [swap(tie(w_down[plane ^ step], *came_up), step) for step in steps]
    probs = jax.nn.softmax(mm(h_two, full_router), axis=-1)
    rows_in = lax.all_to_all(dispatch(position, capacity, h_all), "fsdp", 0, 0, tiled=True)
    rows_in = rows_in.reshape(-1, width)
    own = experts_here * lax.axis_index("fsdp") + plane
    own = (jnp.arange(experts)[None, :] == own).astype(f32)
    slot_block = planes * capacity
    gate_pre, up_pre, act_picked, picked = expert_in(
        rows_in, gate, up, full_router, own, slot_block
    )
    came_down = [tie(part, act_picked) for part in came_down]
    down = jnp.concatenate(by_plane([w_down[plane]] + came_down))
    grad_down_w = t_mm(act_picked, grad_in).astype(bf16)
    grad_gate, grad_up, grad_picked, grad_rows = expert_back(
        grad_in, tie(gate_pre, grad_down_w), up_pre, picked, gate, up, down, slot_block
    )

    def blocks(matrix):
        return matrix.reshape(planes, matrix.shape[0] // planes, matrix.shape[1])

    came, down_grad = exchange_after(blocks(grad_down_w), [()] * (planes - 1))
    grad_up_w = t_mm(rows_in, grad_up).astype(bf16)
    grad_rows = tie(grad_rows, *came, grad_up_w)
    grad_rows = lax.all_to_all(
        grad_rows.reshape(columns, planes * capacity, width), "fsdp", 0, 0, tiled=True
    )
    grad_gate_w = t_mm(rows_in, grad_gate).astype(bf16)
    came, up_grad = exchange_after(blocks(grad_up_w), [(part,) for part in came])
    expert_out = mm(tie(act_picked, came[-1]), down).astype(bf16)
    earlier = [(came[0], expert_out)] + [(part,) for part in came[1:]]
    came, gate_grad = exchange_after(blocks(grad_gate_w), earlier)
    grad_picked = lax.all_to_all(
        tie(grad_picked, grad_rows).reshape(columns, planes, capacity), "fsdp", 0, 0, tiled=True
    )
    grad_rows = tie(grad_rows, *came, expert_out, grad_picked)
    expert_out = lax.all_to_all(
        expert_out.reshape(columns, planes * capacity, width), "fsdp", 0, 0, tiled=True
    )
    grad_h_two = lax.psum_scatter(
        combine(grad_rows), "ctx", scatter_dimension=0, tiled=True
    ).astype(f32)

    u_plane = jnp.sum(jnp.where(holds, grad_picked[..., None], 0.0), axis=2)
    u_mine = exchange(u_plane.transpose(1, 0, 2))
    u_mine = jnp.stack(u_mine, axis=1).reshape(experts, row_count).T
    grad_logits = probs * (u_mine - jnp.sum(probs * u_mine, axis=-1, keepdims=True))
    grad_logits = grad_logits.astype(bf16)
    grad_h_two = grad_h_two + mm_t(grad_logits, full_router)
    grad_router = t_mm(h_two, grad_logits)

    grad_top = grad_output[0].astype(f32)
    grad_ffn_gain = jnp.sum(grad_h_two * middle_hat, axis=0)
    grad_hat = grad_h_two * gain_ffn
    grad_middle = grad_top + scale_two * (
        grad_hat - middle_hat * jnp.mean(grad_hat * middle_hat, axis=-1, keepdims=True)
    )
    grad_branch = grad_middle.astype(bf16)
    def grad_heads(where):
        rows = lax.dynamic_slice_in_dim(full_out, where * share, share)
        return mm_t(grad_branch, rows).astype(bf16)

    came = [swap(grad_heads(plane ^ step), step) for step in range(1, planes)]
    grad_att = jnp.concatenate(by_plane([grad_heads(plane)] + came))
    grad_out_w = t_mm(attended, grad_branch).astype(bf16)
    grad_out_w = grad_out_w.reshape(planes, columns, strip, width).transpose(1, 0, 2, 3)
    mixed_part = combine(tie(expert_out, grad_att, grad_out_w))
    mixed = lax.psum_scatter(mixed_part, "ctx", scatter_dimension=0, tiled=True)
    output = (middle + mixed.astype(f32)).astype(bf16)
    grad_out_w = lax.all_to_all(
        tie(grad_out_w, mixed_part), "fsdp", 0, 0, tiled=True
    )
    grad_att = tie(grad_att, mixed_part)
    grad_query, grad_key, grad_value = attend_back(seq_ids, query, key, values, grad_att)
    grad_query, grad_key, dots, grad_gains = turn_back(
        raw, scales, gains, cosine, sine, grad_query, grad_key
    )
    dots = plane_sum(dots.T).T * (scales * scales) / width
    grad_qkv = jnp.concatenate(
        [
            scales[:, :1] * grad_query - raw[:, :share] * (scales[:, :1] * dots[:, :1]),
            scales[:, 1:] * grad_key - raw[:, share : 2 * share] * (scales[:, 1:] * dots[:, 1:]),
            grad_value,
        ],
        axis=1,
    ).astype(bf16)
    grad_part = mm_t(grad_qkv, packed[:, : 3 * share])
    sums = t_mm(h_one, grad_qkv).astype(bf16)
    sums = sums.reshape(planes, columns, strip, -1).transpose(1, 0, 2, 3)
    grad_h_one = lax.psum_scatter(
        tie(grad_part.astype(bf16), mixed, grad_out_w), "ctx", scatter_dimension=0, tiled=True
    ).astype(f32)
    grad_attn_gain = jnp.sum(grad_part * (hidden_wide * scale_one), axis=0)
    rows_of = jnp.arange(planes)[:, None] == plane
    gains = [jnp.where(rows_of, g[None], 0.0).reshape(width) for g in grad_gains]
    gains = [g[:, None] for g in [grad_attn_gain, grad_ffn_gain] + gains]
    small = jnp.concatenate([grad_router] + gains, axis=1).reshape(planes, columns, -1)
    small = sum([small[plane]] + [swap(small[plane ^ step], step) for step in steps])
    sums = lax.all_to_all(sums, "fsdp", 0, 0, tiled=True)
    grad_out_w = jnp.sum(grad_out_w.astype(f32), axis=0).astype(bf16)
    small = lax.all_to_all(tie(small, sums, grad_out_w), "fsdp", 0, 0, tiled=True)
    small = jnp.sum(small, axis=0).reshape(strip, -1)
    sums = tie(jnp.sum(sums.astype(f32), axis=0).astype(bf16), small)
    grad_out_w = sum(x.astype(f32) for x in exchange(grad_out_w, sums))
    sums = lax.all_to_all(sums, "ctx", 0, 0, tiled=True)
    grad_qkv_w = sums.reshape(planes, strip, 3, share).transpose(2, 1, 0, 3)
    grad_qkv_w = grad_qkv_w.reshape(3, strip, width).astype(f32)

    x_hat = hidden[0].astype(f32)
    scale_mine = lax.rsqrt(jnp.mean(x_hat * x_hat, axis=-1, keepdims=True) + epsilon)
    x_hat = x_hat * scale_mine
    grad_hat = grad_h_one * gain_attn
    grad_input = grad_middle + scale_mine * (
        grad_hat - x_hat * jnp.mean(grad_hat * x_hat, axis=-1, keepdims=True)
    )

    return (
        output[None],
        grad_input[None],
        grad_qkv_w[0],
        grad_qkv_w[1],
        grad_qkv_w[2],
        grad_out_w,
        small[:, :experts],
        small[:, experts],
        small[:, experts + 1],
        small[:, experts + 2],
        small[:, experts + 3],
        gate_grad,
        up_grad,
        down_grad,
    )


def solution(mesh):
    placed = (
        P("fsdp", "ctx", None),
        P("fsdp", None),
        P("fsdp", None),
        P("fsdp", "ctx", None),
        P("fsdp", "ctx", None),
        P(("ctx", "fsdp"), None),
        P(("ctx", "fsdp"), None),
        P(("ctx", "fsdp"), None),
        P(("ctx", "fsdp"), None),
        P(("ctx", "fsdp"), None),
        P(("ctx", "fsdp")),
        P(("ctx", "fsdp")),
        P(("ctx", "fsdp")),
        P(("ctx", "fsdp")),
        P("fsdp", "ctx", None),
        P("fsdp", "ctx", None),
        P("fsdp", "ctx", None),
    )

    def shards(*operands):
        experts_here = operands[14].shape[0]
        heads = operands[0].shape[2] // HEAD_DIM
        planes = mesh.shape["ctx"]
        whole_experts = experts_here == planes and heads % planes == 0 and planes in (2, 4)
        return (plane_shards if whole_experts else general_shards)(*operands)

    return jax.shard_map(
        shards,
        mesh=mesh,
        in_specs=placed,
        out_specs=(
            P("fsdp", "ctx", None),
            P("fsdp", "ctx", None),
            P(("ctx", "fsdp"), None),
            P(("ctx", "fsdp"), None),
            P(("ctx", "fsdp"), None),
            P(("ctx", "fsdp"), None),
            P(("ctx", "fsdp"), None),
            P(("ctx", "fsdp")),
            P(("ctx", "fsdp")),
            P(("ctx", "fsdp")),
            P(("ctx", "fsdp")),
            P("fsdp", "ctx", None),
            P("fsdp", "ctx", None),
            P("fsdp", "ctx", None),
        ),
        check_vma=False,
    )
```

```python
from functools import partial
import math

import jax
import jax.numpy as jnp
from jax import lax
from jax.experimental import pallas as pl
from jax.experimental.pallas import tpu as pltpu
from jax.sharding import PartitionSpec as P

HEAD_DIM = 128


epsilon = 1e-06
rope_base = 10000.0
masked_value = -1e30


def rms_scaled(values, gain):
    return values * lax.rsqrt(jnp.mean(values * values, axis=-1, keepdims=True) + epsilon) * gain


def rotate(values, places):
    row_count = values.shape[0]
    head_count = values.shape[1] // HEAD_DIM
    half_width = HEAD_DIM // 2
    frequency = rope_base ** (-2.0 * jnp.arange(half_width).astype(jnp.float32) / HEAD_DIM)
    angles = places.astype(jnp.float32)[:, None] * frequency[None, :]
    cosine = jnp.cos(angles)[:, None, :]
    sine_part = jnp.sin(angles)[:, None, :]
    split_heads = values.reshape(row_count, head_count, HEAD_DIM)
    first_half = split_heads[:, :, :half_width]
    second_half = split_heads[:, :, half_width:]
    turned = jnp.concatenate(
        [
            first_half * cosine - second_half * sine_part,
            second_half * cosine + first_half * sine_part,
        ],
        axis=-1,
    )
    return turned.reshape(row_count, head_count * HEAD_DIM)


def qk_post(values, gain, places):
    return rotate(rms_scaled(values, gain), places)


def route_weights(logits, chosen):
    router_probs = jax.nn.softmax(logits, axis=-1)
    return jnp.sum(jnp.where(chosen, router_probs[:, None, :], 0.0), axis=-1)


def seq_layout(order_row, seq_lengths):
    seq_ends = jnp.cumsum(seq_lengths)
    seq_ids = jnp.sum((order_row[:, None] >= seq_ends[None, :]).astype(jnp.int32), axis=1)
    starts = seq_ends - seq_lengths
    chosen = seq_ids[:, None] == jnp.arange(seq_lengths.shape[0], dtype=jnp.int32)[None, :]
    seq_start = jnp.sum(jnp.where(chosen, starts[None, :], 0), axis=1)
    return (seq_ids, order_row - seq_start)


def general_shards(
    hidden,
    token_order,
    lengths,
    routes,
    grad_output,
    w_query,
    w_key,
    w_value,
    w_out,
    w_router,
    attn_gain,
    ffn_gain,
    query_gain,
    key_gain,
    w_gate,
    w_up,
    w_down,
):
    hidden_in = hidden[0].astype(jnp.float32)
    row_count = hidden_in.shape[0]
    model_width = hidden_in.shape[1]
    head_count = model_width // HEAD_DIM
    score_scale = 1.0 / math.sqrt(HEAD_DIM)
    seq_all, place_all = seq_layout(token_order[0], lengths[0])
    first_row = lax.axis_index("ctx") * row_count
    seq_mine = lax.dynamic_slice_in_dim(seq_all, first_row, row_count)
    place_mine = lax.dynamic_slice_in_dim(place_all, first_row, row_count)
    same_seq = seq_mine[:, None] == seq_all[None, :]
    gathered = (
        lax.all_gather(w_query, ("ctx", "fsdp"), axis=0, tiled=True),
        lax.all_gather(w_key, ("ctx", "fsdp"), axis=0, tiled=True),
        lax.all_gather(w_value, ("ctx", "fsdp"), axis=0, tiled=True),
        lax.all_gather(w_out, ("ctx", "fsdp"), axis=0, tiled=True),
        lax.all_gather(w_router, ("ctx", "fsdp"), axis=0, tiled=True),
        lax.all_gather(attn_gain, ("ctx", "fsdp"), axis=0, tiled=True),
        lax.all_gather(ffn_gain, ("ctx", "fsdp"), axis=0, tiled=True),
        lax.all_gather(query_gain, ("ctx", "fsdp"), axis=0, tiled=True),
        lax.all_gather(key_gain, ("ctx", "fsdp"), axis=0, tiled=True),
    )
    (
        full_query,
        full_key,
        full_value,
        full_out,
        full_router,
        gain_attn,
        gain_ffn,
        gain_query,
        gain_key,
    ) = gathered
    gain_attn = gain_attn.astype(jnp.float32)
    gain_ffn = gain_ffn.astype(jnp.float32)
    gain_query = gain_query.astype(jnp.float32)
    gain_key = gain_key.astype(jnp.float32)
    h_one, norm_one_back = jax.vjp(rms_scaled, hidden_in, gain_attn)
    h_one_low = h_one.astype(jnp.bfloat16)
    query_raw = jnp.dot(h_one_low, full_query, preferred_element_type=jnp.float32)
    key_raw = jnp.dot(h_one_low, full_key, preferred_element_type=jnp.float32)
    values_low = jnp.dot(h_one_low, full_value, preferred_element_type=jnp.float32).astype(
        jnp.bfloat16
    )
    query_rot, query_back = jax.vjp(partial(qk_post, places=place_mine), query_raw, gain_query)
    key_rot, key_back = jax.vjp(partial(qk_post, places=place_mine), key_raw, gain_key)
    query_low = query_rot.astype(jnp.bfloat16)
    key_low = key_rot.astype(jnp.bfloat16)
    key_all, value_all = (
        lax.all_gather(key_low, "ctx", axis=0, tiled=True),
        lax.all_gather(values_low, "ctx", axis=0, tiled=True),
    )
    query_heads = query_low.reshape(row_count, head_count, HEAD_DIM)
    key_heads = key_all.reshape(-1, head_count, HEAD_DIM)
    value_heads = value_all.reshape(-1, head_count, HEAD_DIM)

    def scores_of():
        raw_scores = (
            jnp.einsum("thd,khd->htk", query_heads, key_heads, preferred_element_type=jnp.float32)
            * score_scale
        )
        return jnp.where(same_seq[None, :, :], raw_scores, masked_value)

    scores = scores_of()
    row_top = jnp.max(scores, axis=-1, keepdims=True)
    log_total = row_top + jnp.log(jnp.sum(jnp.exp(scores - row_top), axis=-1, keepdims=True))
    probs_low = jnp.exp(scores - log_total).astype(jnp.bfloat16)
    attended = jnp.einsum(
        "htk,khd->thd", probs_low, value_heads, preferred_element_type=jnp.float32
    )
    attended_low = attended.reshape(row_count, model_width).astype(jnp.bfloat16)
    middle = hidden_in + jnp.dot(attended_low, full_out, preferred_element_type=jnp.float32)
    h_two, norm_two_back = jax.vjp(rms_scaled, middle, gain_ffn)
    h_two_low = h_two.astype(jnp.bfloat16)
    logits = jnp.dot(h_two_low, full_router, preferred_element_type=jnp.float32)
    expert_count = full_router.shape[1]
    route_rows = routes[0]
    top_k = route_rows.shape[1]
    chosen = route_rows[:, :, None] == jnp.arange(expert_count, dtype=jnp.int32)[None, None, :]
    picked, route_back = jax.vjp(partial(route_weights, chosen=chosen), logits)
    pair_count = row_count * top_k
    capacity = 5 * row_count * top_k // (4 * expert_count)
    slot_count = expert_count * capacity
    group_size = lax.axis_size("fsdp")
    local_experts = w_gate.shape[0]
    pair_expert = route_rows.reshape(pair_count)
    one_hot = (pair_expert[:, None] == jnp.arange(expert_count, dtype=jnp.int32)[None, :]).astype(
        jnp.int32
    )
    slot_rank = jnp.sum(one_hot * (jnp.cumsum(one_hot, axis=0) - 1), axis=1)
    slot_ids = pair_expert * capacity + slot_rank
    source = (
        jnp.full((slot_count,), pair_count, jnp.int32)
        .at[slot_ids]
        .set(jnp.arange(pair_count, dtype=jnp.int32))
    )
    filled = source < pair_count
    source_pair = jnp.minimum(source, pair_count - 1)
    send_rows = jnp.where(
        filled[:, None], h_two_low[source_pair // top_k], jnp.zeros((), jnp.bfloat16)
    )
    send_rows = send_rows.reshape(group_size, local_experts, capacity, model_width)
    gate_full, up_full, down_full = (
        lax.all_gather(w_gate, "ctx", axis=1, tiled=True),
        lax.all_gather(w_up, "ctx", axis=1, tiled=True),
        lax.all_gather(w_down, "ctx", axis=1, tiled=True),
    )
    arrived_rows = lax.all_to_all(send_rows, "fsdp", split_axis=0, concat_axis=0, tiled=True)
    gate_part = jnp.einsum(
        "secd,edf->secf", arrived_rows, gate_full, preferred_element_type=jnp.float32
    )
    up_part = jnp.einsum(
        "secd,edf->secf", arrived_rows, up_full, preferred_element_type=jnp.float32
    )
    act_part = (jax.nn.silu(gate_part) * up_part).astype(jnp.bfloat16)
    result = jnp.einsum(
        "secf,efd->secd", act_part, down_full, preferred_element_type=jnp.float32
    ).astype(jnp.bfloat16)
    returned = lax.all_to_all(result, "fsdp", split_axis=0, concat_axis=0, tiled=True).reshape(
        slot_count, model_width
    )
    pair_out = returned[slot_ids].reshape(row_count, top_k, model_width)
    output = (middle + jnp.sum(picked[:, :, None] * pair_out, axis=1)).astype(jnp.bfloat16)
    grad_top = grad_output[0].astype(jnp.float32)
    grad_picked = jnp.sum(grad_top[:, None, :] * pair_out, axis=-1)
    grad_pair = (
        (picked[:, :, None] * grad_top[:, None, :])
        .astype(jnp.bfloat16)
        .reshape(pair_count, model_width)
    )
    grad_send = jnp.where(filled[:, None], grad_pair[source_pair], jnp.zeros((), jnp.bfloat16))
    grad_send = grad_send.reshape(group_size, local_experts, capacity, model_width)
    grad_arrived = lax.all_to_all(grad_send, "fsdp", split_axis=0, concat_axis=0, tiled=True)
    sigma = jax.nn.sigmoid(gate_part)
    act_low = (gate_part * sigma * up_part).astype(jnp.bfloat16)
    grad_act = jnp.einsum(
        "secd,efd->secf", grad_arrived, down_full, preferred_element_type=jnp.float32
    )
    grad_gate = (grad_act * up_part * sigma * (1.0 + gate_part * (1.0 - sigma))).astype(
        jnp.bfloat16
    )
    grad_up = (grad_act * gate_part * sigma).astype(jnp.bfloat16)
    grad_back = jnp.einsum(
        "secf,edf->secd", grad_gate, gate_full, preferred_element_type=jnp.float32
    )
    grad_back = (
        grad_back
        + jnp.einsum("secf,edf->secd", grad_up, up_full, preferred_element_type=jnp.float32)
    ).astype(jnp.bfloat16)
    grad_return = lax.all_to_all(
        grad_back, "fsdp", split_axis=0, concat_axis=0, tiled=True
    ).reshape(slot_count, model_width)
    grad_h_two = jnp.sum(
        grad_return[slot_ids].reshape(row_count, top_k, model_width).astype(jnp.float32), axis=1
    )
    (grad_logits,) = route_back(grad_picked)
    grad_logits_low = grad_logits.astype(jnp.bfloat16)
    grad_h_two = grad_h_two + jnp.einsum(
        "te,de->td", grad_logits_low, full_router, preferred_element_type=jnp.float32
    )
    grad_router = jnp.einsum(
        "td,te->de", h_two_low, grad_logits_low, preferred_element_type=jnp.float32
    )
    grad_middle, grad_ffn_gain = norm_two_back(grad_h_two)
    grad_middle = grad_middle + grad_top
    grad_branch = grad_middle.astype(jnp.bfloat16)
    grad_out_w = jnp.einsum(
        "td,te->de", attended_low, grad_branch, preferred_element_type=jnp.float32
    )
    grad_att = jnp.einsum(
        "te,de->td", grad_branch, full_out, preferred_element_type=jnp.float32
    ).astype(jnp.bfloat16)
    grad_att = grad_att.reshape(row_count, head_count, HEAD_DIM)
    scores = scores_of()
    probs_full = jnp.exp(scores - log_total)
    probs_again = probs_full.astype(jnp.bfloat16)
    grad_probs = jnp.einsum(
        "thd,khd->htk", grad_att, value_heads, preferred_element_type=jnp.float32
    )
    spread = jnp.sum(probs_full * grad_probs, axis=-1, keepdims=True)
    grad_scores = (probs_full * (grad_probs - spread)).astype(jnp.bfloat16)
    grad_query = (
        jnp.einsum(
            "htk,khd->thd", grad_scores, key_heads, preferred_element_type=jnp.float32
        ).reshape(row_count, model_width)
        * score_scale
    )
    grad_key_part = (
        jnp.einsum(
            "htk,thd->khd", grad_scores, query_heads, preferred_element_type=jnp.float32
        ).reshape(-1, model_width)
        * score_scale
    )
    grad_value_part = jnp.einsum(
        "htk,thd->khd", probs_again, grad_att, preferred_element_type=jnp.float32
    ).reshape(-1, model_width)
    grad_key, grad_value = (
        lax.psum_scatter(
            grad_key_part.astype(jnp.bfloat16), "ctx", scatter_dimension=0, tiled=True
        ).astype(jnp.float32),
        lax.psum_scatter(
            grad_value_part.astype(jnp.bfloat16), "ctx", scatter_dimension=0, tiled=True
        ).astype(jnp.float32),
    )
    grad_q_raw, grad_q_gain = query_back(grad_query)
    grad_k_raw, grad_k_gain = key_back(grad_key)
    grad_q_low = grad_q_raw.astype(jnp.bfloat16)
    grad_k_low = grad_k_raw.astype(jnp.bfloat16)
    grad_v_low = grad_value.astype(jnp.bfloat16)
    grad_query_w = jnp.einsum(
        "td,te->de", h_one_low, grad_q_low, preferred_element_type=jnp.float32
    )
    grad_key_w = jnp.einsum("td,te->de", h_one_low, grad_k_low, preferred_element_type=jnp.float32)
    grad_value_w = jnp.einsum(
        "td,te->de", h_one_low, grad_v_low, preferred_element_type=jnp.float32
    )
    grad_h_one = jnp.einsum("te,de->td", grad_q_low, full_query, preferred_element_type=jnp.float32)
    grad_h_one = grad_h_one + jnp.einsum(
        "te,de->td", grad_k_low, full_key, preferred_element_type=jnp.float32
    )
    grad_h_one = grad_h_one + jnp.einsum(
        "te,de->td", grad_v_low, full_value, preferred_element_type=jnp.float32
    )
    grad_input_norm, grad_attn_gain = norm_one_back(grad_h_one)
    grad_input = grad_middle + grad_input_norm
    totals = (
        lax.psum_scatter(grad_query_w, ("ctx", "fsdp"), scatter_dimension=0, tiled=True),
        lax.psum_scatter(grad_key_w, ("ctx", "fsdp"), scatter_dimension=0, tiled=True),
        lax.psum_scatter(grad_value_w, ("ctx", "fsdp"), scatter_dimension=0, tiled=True),
        lax.psum_scatter(grad_out_w, ("ctx", "fsdp"), scatter_dimension=0, tiled=True),
        lax.psum_scatter(grad_router, ("ctx", "fsdp"), scatter_dimension=0, tiled=True),
        lax.psum_scatter(grad_attn_gain, ("ctx", "fsdp"), scatter_dimension=0, tiled=True),
        lax.psum_scatter(grad_ffn_gain, ("ctx", "fsdp"), scatter_dimension=0, tiled=True),
        lax.psum_scatter(grad_q_gain, ("ctx", "fsdp"), scatter_dimension=0, tiled=True),
        lax.psum_scatter(grad_k_gain, ("ctx", "fsdp"), scatter_dimension=0, tiled=True),
    )
    grad_down_w = jnp.einsum(
        "secf,secd->efd", act_low, grad_arrived, preferred_element_type=jnp.float32
    )
    grad_gate_w = jnp.einsum(
        "secd,secf->edf", arrived_rows, grad_gate, preferred_element_type=jnp.float32
    )
    grad_up_w = jnp.einsum(
        "secd,secf->edf", arrived_rows, grad_up, preferred_element_type=jnp.float32
    )
    gate_grad, up_grad, down_grad = (
        lax.psum_scatter(
            grad_gate_w.astype(jnp.bfloat16), "ctx", scatter_dimension=1, tiled=True
        ).astype(jnp.float32),
        lax.psum_scatter(
            grad_up_w.astype(jnp.bfloat16), "ctx", scatter_dimension=1, tiled=True
        ).astype(jnp.float32),
        lax.psum_scatter(
            grad_down_w.astype(jnp.bfloat16), "ctx", scatter_dimension=1, tiled=True
        ).astype(jnp.float32),
    )
    return (
        output[None],
        grad_input[None],
        totals[0],
        totals[1],
        totals[2],
        totals[3],
        totals[4],
        totals[5],
        totals[6],
        totals[7],
        totals[8],
        gate_grad,
        up_grad,
        down_grad,
    )


def masked_probs(query, key, seq_rows, seq_cols, scale):
    scores = (
        lax.dot_general(query, key, (((1,), (1,)), ((), ())), preferred_element_type=jnp.float32)
        * scale
    )
    scores = jnp.where(seq_rows == seq_cols, scores, masked_value)
    top = jnp.max(scores, axis=-1, keepdims=True)
    weights = jnp.exp(scores - top)
    return weights / jnp.sum(weights, axis=-1, keepdims=True)


def attend_kernel(scale, seq_rows, seq_cols, query, key, value, out):
    probs = masked_probs(query[...], key[...], seq_rows[...], seq_cols[...], scale)
    out[...] = jnp.dot(
        probs.astype(jnp.bfloat16), value[...], preferred_element_type=jnp.float32
    ).astype(out.dtype)


def attend_back_kernel(
    scale, seq_rows, seq_cols, query, key, value, grad, grad_query, grad_key, grad_value
):
    @pl.when(pl.program_id(1) == 0)
    def _():
        grad_key[...] = jnp.zeros_like(grad_key)
        grad_value[...] = jnp.zeros_like(grad_value)

    probs = masked_probs(query[...], key[...], seq_rows[...], seq_cols[...], scale)
    grad_probs = lax.dot_general(
        grad[...], value[...], (((1,), (1,)), ((), ())), preferred_element_type=jnp.float32
    )
    spread = jnp.sum(probs * grad_probs, axis=-1, keepdims=True)
    grad_scores = (probs * (grad_probs - spread)).astype(jnp.bfloat16)
    grad_query[...] = (
        jnp.dot(grad_scores, key[...], preferred_element_type=jnp.float32) * scale
    )
    grad_key[...] += (
        lax.dot_general(
            grad_scores,
            query[...],
            (((0,), (0,)), ((), ())),
            preferred_element_type=jnp.float32,
        )
        * scale
    )
    grad_value[...] += lax.dot_general(
        probs.astype(jnp.bfloat16),
        grad[...],
        (((0,), (0,)), ((), ())),
        preferred_element_type=jnp.float32,
    )


def attention_specs(rows, block):
    per_block = pl.BlockSpec((block, HEAD_DIM), lambda h, i: (i, h))
    per_head = pl.BlockSpec((rows, HEAD_DIM), lambda h, i: (0, h))
    seqs = [
        pl.BlockSpec((block, 1), lambda h, i: (i, 0)),
        pl.BlockSpec((1, rows), lambda h, i: (0, 0)),
    ]
    return per_block, per_head, seqs


def attend(seq_ids, query, key, value):
    rows, width = query.shape
    block = math.gcd(rows, 256)
    per_block, per_head, seqs = attention_specs(rows, block)
    pairs = rows * rows * width
    return pl.pallas_call(
        partial(attend_kernel, 1.0 / math.sqrt(HEAD_DIM)),
        grid=(width // HEAD_DIM, rows // block),
        in_specs=seqs + [per_block, per_head, per_head],
        out_specs=per_block,
        out_shape=jax.ShapeDtypeStruct((rows, width), jnp.bfloat16),
        cost_estimate=pl.CostEstimate(
            flops=4 * pairs, bytes_accessed=8 * rows * width, transcendentals=pairs // HEAD_DIM
        ),
        compiler_params=pltpu.CompilerParams(vmem_limit_bytes=48 << 20),
        name="attend",
    )(seq_ids[:, None], seq_ids[None, :], query, key, value)


def attend_back(seq_ids, query, key, value, grad):
    rows, width = query.shape
    block = math.gcd(rows, 256)
    per_block, per_head, seqs = attention_specs(rows, block)
    pairs = rows * rows * width
    return pl.pallas_call(
        partial(attend_back_kernel, 1.0 / math.sqrt(HEAD_DIM)),
        grid=(width // HEAD_DIM, rows // block),
        in_specs=seqs + [per_block, per_head, per_head, per_block],
        out_specs=(per_block, per_head, per_head),
        out_shape=(jax.ShapeDtypeStruct((rows, width), jnp.float32),) * 3,
        cost_estimate=pl.CostEstimate(
            flops=10 * pairs, bytes_accessed=20 * rows * width, transcendentals=pairs // HEAD_DIM
        ),
        compiler_params=pltpu.CompilerParams(vmem_limit_bytes=48 << 20),
        name="attend_back",
    )(seq_ids[:, None], seq_ids[None, :], query, key, value, grad)


def dispatch_kernel(position, rows, out):
    columns, _, capacity, width = out.shape
    count = rows.shape[1]
    slots = lax.broadcasted_iota(jnp.int32, (columns, capacity, count), 1)
    select = jnp.where(slots == position[:, 0], 1.0, 0.0)
    select = select.reshape(columns * capacity, count).astype(jnp.bfloat16)
    step = math.gcd(width, 512)
    for at in range(0, width, step):
        part = jnp.dot(select, rows[0, :, at : at + step], preferred_element_type=jnp.float32)
        part = part.reshape(columns, capacity, step).astype(out.dtype)
        out[:, 0, :, at : at + step] = part


def dispatch(position, capacity, rows):
    columns, planes, count = position.shape
    width = rows.shape[1]
    return pl.pallas_call(
        dispatch_kernel,
        grid=(planes,),
        in_specs=[
            pl.BlockSpec((columns, 1, 1, count), lambda b: (0, b, 0, 0)),
            pl.BlockSpec((1, count, width), lambda b: (b, 0, 0)),
        ],
        out_specs=pl.BlockSpec((columns, 1, capacity, width), lambda b: (0, b, 0, 0)),
        out_shape=jax.ShapeDtypeStruct((columns, planes, capacity, width), jnp.bfloat16),
        cost_estimate=pl.CostEstimate(
            flops=2 * position.size * capacity * width,
            bytes_accessed=2 * columns * planes * capacity * width,
            transcendentals=0,
        ),
        compiler_params=pltpu.CompilerParams(vmem_limit_bytes=40 << 20),
        name="dispatch",
    )(position[:, :, None], rows.reshape(planes, count, width))


def heads_of(width):
    return [slice(at, at + HEAD_DIM) for at in range(0, width, HEAD_DIM)]


def turn_kernel(raw, scales, gains, cosine, sine, query, key, value):
    width = query.shape[1]
    for which, out in ((0, query), (1, key)):
        scale = scales[:, which : which + 1]
        for head in heads_of(width):
            part = raw[:, which * width + head.start : which * width + head.stop]
            part = part * scale * gains[which : which + 1, head]
            swapped = pltpu.roll(part, HEAD_DIM // 2, 1)
            out[:, head] = (part * cosine[...] + swapped * sine[...]).astype(out.dtype)
    value[...] = raw[:, 2 * width : 3 * width].astype(value.dtype)


def turn_back_kernel(
    raw, scales, gains, cosine, sine, grad_query, grad_key, out_query, out_key, dots, grad_gains
):
    @pl.when(pl.program_id(0) == 0)
    def _():
        grad_gains[...] = jnp.zeros_like(grad_gains)

    width = grad_query.shape[1]
    for which, grad, out in ((0, grad_query, out_query), (1, grad_key, out_key)):
        scale = scales[:, which : which + 1]
        total = jnp.zeros_like(scale)
        for head in heads_of(width):
            part = grad[:, head]
            part = part * cosine[...] - pltpu.roll(part, HEAD_DIM // 2, 1) * sine[...]
            hat = raw[:, which * width + head.start : which * width + head.stop] * scale
            grad_gains[which : which + 1, head] += jnp.sum(part * hat, axis=0, keepdims=True)
            part = part * gains[which : which + 1, head]
            total += jnp.sum(part * hat, axis=1, keepdims=True)
            out[:, head] = part
        dots[:, which : which + 1] = total


def turn_specs(raw, gains):
    block = math.gcd(raw.shape[0], 256)
    return block, [
        pl.BlockSpec((block, raw.shape[1]), lambda i: (i, 0)),
        pl.BlockSpec((block, 2), lambda i: (i, 0)),
        pl.BlockSpec(gains.shape, lambda i: (0, 0)),
        pl.BlockSpec((block, HEAD_DIM), lambda i: (i, 0)),
        pl.BlockSpec((block, HEAD_DIM), lambda i: (i, 0)),
    ]


def turn(raw, scales, gains, cosine, sine):
    rows, width = raw.shape[0], gains.shape[1]
    block, specs = turn_specs(raw, gains)
    return pl.pallas_call(
        turn_kernel,
        grid=(rows // block,),
        in_specs=specs,
        out_specs=(pl.BlockSpec((block, width), lambda i: (i, 0)),) * 3,
        out_shape=(jax.ShapeDtypeStruct((rows, width), jnp.bfloat16),) * 3,
        cost_estimate=pl.CostEstimate(
            flops=16 * rows * width, bytes_accessed=18 * rows * width, transcendentals=0
        ),
        compiler_params=pltpu.CompilerParams(vmem_limit_bytes=40 << 20),
        name="turn",
    )(raw, scales, gains, cosine, sine)


def turn_back(raw, scales, gains, cosine, sine, grad_query, grad_key):
    rows, width = grad_query.shape
    block, specs = turn_specs(raw, gains)
    wide = pl.BlockSpec((block, width), lambda i: (i, 0))
    f32 = jnp.float32
    return pl.pallas_call(
        turn_back_kernel,
        grid=(rows // block,),
        in_specs=specs + [wide, wide],
        out_specs=(
            wide,
            wide,
            pl.BlockSpec((block, 2), lambda i: (i, 0)),
            pl.BlockSpec((2, width), lambda i: (0, 0)),
        ),
        out_shape=(
            jax.ShapeDtypeStruct((rows, width), f32),
            jax.ShapeDtypeStruct((rows, width), f32),
            jax.ShapeDtypeStruct((rows, 2), f32),
            jax.ShapeDtypeStruct((2, width), f32),
        ),
        cost_estimate=pl.CostEstimate(
            flops=24 * rows * width, bytes_accessed=28 * rows * width, transcendentals=0
        ),
        compiler_params=pltpu.CompilerParams(vmem_limit_bytes=40 << 20),
        name="turn_back",
    )(raw, scales, gains, cosine, sine, grad_query, grad_key)


def expert_in_kernel(
    rows, gate, up, router, own, gate_out, up_out, act_out, picked_out
):
    logits = jnp.dot(rows[...], router[...], preferred_element_type=jnp.float32)
    weights = jnp.exp(logits - jnp.max(logits, axis=1, keepdims=True))
    picked = jnp.sum(weights * own[...], axis=1, keepdims=True)
    picked = picked / jnp.sum(weights, axis=1, keepdims=True)
    gate_pre = jnp.dot(rows[...], gate[...], preferred_element_type=jnp.float32)
    up_pre = jnp.dot(rows[...], up[...], preferred_element_type=jnp.float32)
    act = (gate_pre * jax.nn.sigmoid(gate_pre) * up_pre).astype(jnp.bfloat16)
    gate_out[...] = gate_pre
    up_out[...] = up_pre
    act_out[...] = (act.astype(jnp.float32) * picked).astype(jnp.bfloat16)
    picked_out[...] = picked


def expert_back_kernel(
    grad, gate_in, up_in, picked, gate, up, down, grad_gate, grad_up, grad_picked, grad_rows
):
    grad_raw = lax.dot_general(
        grad[...], down[...], (((1,), (1,)), ((), ())), preferred_element_type=jnp.float32
    )
    gate_pre, up_pre = gate_in[...], up_in[...]
    sigma = jax.nn.sigmoid(gate_pre)
    silu = gate_pre * sigma
    act = (silu * up_pre).astype(jnp.bfloat16).astype(jnp.float32)
    grad_picked[...] = jnp.sum(grad_raw * act, axis=1, keepdims=True)
    grad_act = grad_raw * picked[...]
    low_gate = (grad_act * up_pre * (sigma + silu * (1.0 - sigma))).astype(jnp.bfloat16)
    low_up = (grad_act * silu).astype(jnp.bfloat16)
    grad_gate[...] = low_gate
    grad_up[...] = low_up
    back = lax.dot_general(
        low_gate, gate[...], (((1,), (1,)), ((), ())), preferred_element_type=jnp.float32
    )
    back = back + lax.dot_general(
        low_up, up[...], (((1,), (1,)), ((), ())), preferred_element_type=jnp.float32
    )
    grad_rows[...] = back.astype(jnp.bfloat16)


def whole(shape):
    return pl.BlockSpec(shape, lambda i: (0, 0), pipeline_mode=pl.Buffered(1))


def row_blocks(block, width):
    return pl.BlockSpec((block, width), lambda i: (i, 0))


def expert_in(rows, gate, up, router, own, block):
    count, width = rows.shape
    hidden = gate.shape[1]
    narrow = row_blocks(block, hidden)
    f32 = jnp.float32
    return pl.pallas_call(
        expert_in_kernel,
        grid=(count // block,),
        in_specs=[
            row_blocks(block, width),
            whole(gate.shape),
            whole(up.shape),
            whole(router.shape),
            whole(own.shape),
        ],
        out_specs=(narrow, narrow, narrow, row_blocks(block, 1)),
        out_shape=(
            jax.ShapeDtypeStruct((count, hidden), f32),
            jax.ShapeDtypeStruct((count, hidden), f32),
            jax.ShapeDtypeStruct((count, hidden), jnp.bfloat16),
            jax.ShapeDtypeStruct((count, 1), f32),
        ),
        cost_estimate=pl.CostEstimate(
            flops=4 * count * width * hidden,
            bytes_accessed=2 * count * width + (10 * count + 4 * width) * hidden,
            transcendentals=count * hidden,
        ),
        compiler_params=pltpu.CompilerParams(vmem_limit_bytes=56 << 20),
        name="expert_in",
    )(rows, gate, up, router, own)


def expert_back(grad, gate_pre, up_pre, picked, gate, up, down, block):
    count, width = grad.shape
    hidden = down.shape[0]
    wide, narrow, one = [row_blocks(block, size) for size in (width, hidden, 1)]
    low = jax.ShapeDtypeStruct((count, hidden), jnp.bfloat16)
    return pl.pallas_call(
        expert_back_kernel,
        grid=(count // block,),
        in_specs=[wide, narrow, narrow, one, whole(gate.shape), whole(up.shape), whole(down.shape)],
        out_specs=(narrow, narrow, one, wide),
        out_shape=(
            low,
            low,
            jax.ShapeDtypeStruct((count, 1), jnp.float32),
            jax.ShapeDtypeStruct((count, width), jnp.bfloat16),
        ),
        cost_estimate=pl.CostEstimate(
            flops=6 * count * width * hidden,
            bytes_accessed=4 * count * width + (12 * count + 6 * width) * hidden,
            transcendentals=count * hidden,
        ),
        compiler_params=pltpu.CompilerParams(vmem_limit_bytes=58 << 20),
        name="expert_back",
    )(grad, gate_pre, up_pre, picked, gate, up, down)


def tie(array, *others):
    anywhere = pl.BlockSpec(memory_space=pl.ANY)
    return pl.pallas_call(
        lambda *refs: None,
        in_specs=[anywhere] * (1 + len(others)),
        out_specs=anywhere,
        out_shape=jax.ShapeDtypeStruct(array.shape, array.dtype),
        input_output_aliases={0: 0},
        name="tie",
    )(array, *others)


def mm(left, right):
    return jnp.dot(left, right, preferred_element_type=jnp.float32)


def mm_t(left, right):
    return lax.dot_general(
        left, right, (((1,), (1,)), ((), ())), preferred_element_type=jnp.float32
    )


def t_mm(left, right):
    return lax.dot_general(
        left, right, (((0,), (0,)), ((), ())), preferred_element_type=jnp.float32
    )


def plane_shards(
    hidden,
    token_order,
    lengths,
    routes,
    grad_output,
    w_query,
    w_key,
    w_value,
    w_out,
    w_router,
    attn_gain,
    ffn_gain,
    query_gain,
    key_gain,
    w_gate,
    w_up,
    w_down,
):
    f32, bf16 = jnp.float32, jnp.bfloat16
    both = ("ctx", "fsdp")
    planes = lax.axis_size("ctx")
    columns = lax.axis_size("fsdp")
    plane = lax.axis_index("ctx")
    row_count, width = hidden.shape[1:]
    group_rows = row_count * planes
    share = width // planes
    strip = w_query.shape[0]
    first_row = plane * row_count

    experts = w_router.shape[1]
    qkv = jnp.stack([w_query, w_key, w_value], axis=1).reshape(strip, 3, planes, share)
    qkv = qkv.transpose(2, 0, 1, 3).reshape(planes, strip, 3 * share)
    small = [w_router] + [g[:, None] for g in (attn_gain, ffn_gain, query_gain, key_gain)]
    small = jnp.concatenate(small + [routes.astype(bf16).reshape(strip, -1)], axis=1)
    spare = -small.shape[1] % 128
    small = jnp.pad(small, ((0, 0), (0, spare)))
    small = jnp.broadcast_to(small[None], (planes,) + small.shape)
    own_out = jnp.broadcast_to(w_out[None], (planes,) + w_out.shape)
    packed = jnp.concatenate([qkv, small, own_out], axis=2)
    packed = lax.all_to_all(packed, "ctx", 0, 0, tiled=True)
    hidden_all = lax.all_gather(tie(hidden[0], packed), "ctx", axis=0, tiled=True)
    packed, out_rows = packed[:, :, :-width], packed[:, :, -width:]
    routes_at = 3 * share + experts + 4
    routes_all = packed[:, :, routes_at : packed.shape[2] - spare].astype(jnp.int32)
    routes_all = routes_all.reshape(group_rows, -1)
    packed = jnp.broadcast_to(packed[None], (columns,) + packed.shape)
    packed = lax.all_to_all(packed, "fsdp", 0, 0, tiled=True)
    packed = packed.transpose(1, 0, 2, 3).reshape(width, -1)
    full_router = packed[:, 3 * share : 3 * share + experts]
    gain_attn, gain_ffn, gain_query, gain_key = [
        packed[:, 3 * share + experts + i].astype(f32) for i in range(4)
    ]
    def swap(part, step):
        return lax.ppermute(part, "ctx", [(i, i ^ step) for i in range(planes)])

    def by_plane(came):
        came = jnp.stack(came)
        return [came[plane ^ i] for i in range(planes)]

    def exchange(parts, first=None, last=None):
        came = [parts[plane]]
        for step in range(1, planes):
            part = parts[plane ^ step]
            part = swap(part if first is None else tie(part, first), step)
            came.append(part if last is None else tie(part, last))
        return by_plane(came)

    def exchange_after(parts, earlier):
        came = [
            swap(tie(part, *before) if before else part, step)
            for step, before in enumerate(earlier, 1)
            for part in [parts[plane ^ step]]
        ]
        return came, jnp.stack(by_plane([parts[plane]] + came)).astype(f32)

    def plane_sum(part):
        return part + sum(swap(part, step) for step in range(1, planes))

    out_rows = jnp.broadcast_to(out_rows[None], (columns,) + out_rows.shape)
    grad_all = lax.all_gather(
        tie(grad_output[0], hidden_all, packed, out_rows), "ctx", axis=0, tiled=True
    )
    full_out = lax.all_to_all(out_rows, "fsdp", 0, 0, tiled=True)

    seq_ids, places = seq_layout(token_order[0], lengths[0])
    experts_here = w_gate.shape[0]
    column_expert = experts_here * jnp.arange(columns, dtype=jnp.int32) + plane
    named = jnp.any(routes_all[:, :, None] == column_expert[None, None, :], axis=1)
    named = named.reshape(planes, row_count, columns)
    capacity = 5 * row_count * routes.shape[2] // (4 * experts)
    rank = jnp.cumsum(named.astype(jnp.int32), axis=1) - 1
    position = jnp.where(named, rank, -1).transpose(2, 0, 1)
    slots = jnp.arange(capacity, dtype=jnp.int32)
    holds = position[:, :, None, :] == slots[None, None, :, None]
    select = holds.astype(bf16)

    def combine(rows):
        rows = rows.reshape(columns, planes, capacity, -1)
        sums = jnp.einsum("fbsr,fbsd->brd", select, rows, preferred_element_type=f32)
        return sums.reshape(group_rows, -1).astype(bf16)


    frequency = rope_base ** (
        -2.0 * jnp.arange(HEAD_DIM // 2).astype(f32) / HEAD_DIM
    )
    angles = places.astype(f32)[:, None] * frequency[None, :]
    cosine, sine = jnp.cos(angles), jnp.sin(angles)
    cosine = jnp.concatenate([cosine, cosine], axis=1)
    sine = jnp.concatenate([-sine, sine], axis=1)
    hidden_wide = hidden_all.astype(f32)
    scale_one = lax.rsqrt(jnp.mean(hidden_wide * hidden_wide, axis=-1, keepdims=True) + epsilon)
    h_one = (hidden_wide * scale_one * gain_attn).astype(bf16)
    raw = mm(h_one, packed)
    squares = jnp.stack(
        [jnp.sum(raw[:, :share] ** 2, axis=1), jnp.sum(raw[:, share : 2 * share] ** 2, axis=1)]
    )
    squares = plane_sum(squares)
    scales = lax.rsqrt(squares / width + epsilon).T
    gains = lax.dynamic_slice_in_dim(
        jnp.stack([gain_query, gain_key]), plane * share, share, axis=1
    )
    query, key, values = turn(raw, scales, gains, cosine, sine)
    attended = attend(seq_ids, query, key, values)
    full_out = tie(full_out, attended).transpose(1, 0, 2, 3).reshape(width, width)
    grad_send = dispatch(position, capacity, tie(grad_all, attended, full_out))
    attended = attended.reshape(planes, row_count, share)
    attended = jnp.concatenate(exchange(attended, grad_all), axis=1)
    grad_in = lax.all_to_all(grad_send, "fsdp", 0, 0, tiled=True).reshape(-1, width)
    middle = hidden[0].astype(f32) + mm(attended, full_out)
    scale_two = lax.rsqrt(jnp.mean(middle * middle, axis=-1, keepdims=True) + epsilon)
    middle_hat = middle * scale_two
    h_two = (middle_hat * gain_ffn).astype(bf16)

    h_two_all = lax.all_gather(tie(h_two, grad_send), "ctx", axis=0, tiled=True)
    steps = range(1, planes)
    came_gate = [swap(tie(w_gate[plane ^ step], h_two_all), step) for step in steps]
    h_all = tie(h_two_all, grad_in, came_gate[planes // 2 - 1])
    gate = jnp.concatenate(by_plane([w_gate[plane]] + came_gate))
    came_up = [
        swap(tie(w_up[plane ^ step], before), step) for step, before in zip(steps, came_gate)
    ]
    up = jnp.concatenate(by_plane([w_up[plane]] + came_up))
    came_down = [swap(tie(w_down[plane ^ step], *came_up), step) for step in steps]
    probs = jax.nn.softmax(mm(h_two, full_router), axis=-1)
    rows_in = lax.all_to_all(dispatch(position, capacity, h_all), "fsdp", 0, 0, tiled=True)
    rows_in = rows_in.reshape(-1, width)
    own = experts_here * lax.axis_index("fsdp") + plane
    own = (jnp.arange(experts)[None, :] == own).astype(f32)
    slot_block = planes * capacity
    gate_pre, up_pre, act_picked, picked = expert_in(
        rows_in, gate, up, full_router, own, slot_block
    )
    came_down = [tie(part, act_picked) for part in came_down]
    down = jnp.concatenate(by_plane([w_down[plane]] + came_down))
    grad_down_w = t_mm(act_picked, grad_in).astype(bf16)
    grad_gate, grad_up, grad_picked, grad_rows = expert_back(
        grad_in, tie(gate_pre, grad_down_w), up_pre, picked, gate, up, down, slot_block
    )

    def blocks(matrix):
        return matrix.reshape(planes, matrix.shape[0] // planes, matrix.shape[1])

    came, down_grad = exchange_after(blocks(grad_down_w), [()] * (planes - 1))
    grad_up_w = t_mm(rows_in, grad_up).astype(bf16)
    grad_rows = tie(grad_rows, *came, grad_up_w)
    grad_rows = lax.all_to_all(
        grad_rows.reshape(columns, planes * capacity, width), "fsdp", 0, 0, tiled=True
    )
    grad_gate_w = t_mm(rows_in, grad_gate).astype(bf16)
    came, up_grad = exchange_after(blocks(grad_up_w), [(part,) for part in came])
    late_act = tie(act_picked, came[-1])
    halves = [mm(late_act, half).astype(bf16) for half in jnp.split(down, 2, axis=1)]
    earlier = [(came[0], *halves)] + [(part,) for part in came[1:]]
    came, gate_grad = exchange_after(blocks(grad_gate_w), earlier)
    grad_picked = lax.all_to_all(
        tie(grad_picked, grad_rows).reshape(columns, planes, capacity), "fsdp", 0, 0, tiled=True
    )
    grad_rows = tie(grad_rows, *came, *halves, grad_picked)
    halves = [
        lax.all_to_all(half.reshape(columns, planes * capacity, -1), "fsdp", 0, 0, tiled=True)
        for half in halves
    ]
    grad_h_two = lax.psum_scatter(
        combine(grad_rows), "ctx", scatter_dimension=0, tiled=True
    ).astype(f32)

    u_plane = jnp.sum(jnp.where(holds, grad_picked[..., None], 0.0), axis=2)
    u_mine = exchange(u_plane.transpose(1, 0, 2))
    u_mine = jnp.stack(u_mine, axis=1).reshape(experts, row_count).T
    grad_logits = probs * (u_mine - jnp.sum(probs * u_mine, axis=-1, keepdims=True))
    grad_logits = grad_logits.astype(bf16)
    grad_h_two = grad_h_two + mm_t(grad_logits, full_router)
    grad_router = t_mm(h_two, grad_logits)

    grad_top = grad_output[0].astype(f32)
    grad_ffn_gain = jnp.sum(grad_h_two * middle_hat, axis=0)
    grad_hat = grad_h_two * gain_ffn
    grad_middle = grad_top + scale_two * (
        grad_hat - middle_hat * jnp.mean(grad_hat * middle_hat, axis=-1, keepdims=True)
    )
    grad_branch = grad_middle.astype(bf16)
    def grad_heads(where):
        rows = lax.dynamic_slice_in_dim(full_out, where * share, share)
        return mm_t(grad_branch, rows).astype(bf16)

    came = [swap(grad_heads(plane ^ step), step) for step in range(1, planes)]
    grad_att = jnp.concatenate(by_plane([grad_heads(plane)] + came))
    grad_out_w = t_mm(attended, grad_branch).astype(bf16)
    grad_out_w = grad_out_w.reshape(planes, columns, strip, width).transpose(1, 0, 2, 3)
    first_part = combine(halves[0])
    first_mixed = lax.psum_scatter(first_part, "ctx", scatter_dimension=0, tiled=True)
    grad_att = tie(grad_att, first_part, grad_out_w)
    grad_query, grad_key, grad_value = attend_back(seq_ids, query, key, values, grad_att)
    last_part = combine(tie(halves[1], grad_query))
    last_mixed = lax.psum_scatter(last_part, "ctx", scatter_dimension=0, tiled=True)
    mixed = jnp.concatenate([first_mixed, last_mixed], axis=1).astype(f32)
    output = (middle + mixed).astype(bf16)
    grad_out_w = lax.all_to_all(
        tie(grad_out_w, last_part), "fsdp", 0, 0, tiled=True
    )
    grad_query, grad_key, dots, grad_gains = turn_back(
        raw, scales, gains, cosine, sine, grad_query, grad_key
    )
    dots = plane_sum(dots.T).T * (scales * scales) / width
    grad_qkv = jnp.concatenate(
        [
            scales[:, :1] * grad_query - raw[:, :share] * (scales[:, :1] * dots[:, :1]),
            scales[:, 1:] * grad_key - raw[:, share : 2 * share] * (scales[:, 1:] * dots[:, 1:]),
            grad_value,
        ],
        axis=1,
    ).astype(bf16)
    grad_part = mm_t(grad_qkv, packed[:, : 3 * share])
    sums = t_mm(h_one, grad_qkv).astype(bf16)
    sums = sums.reshape(planes, columns, strip, -1).transpose(1, 0, 2, 3)
    grad_h_one = lax.psum_scatter(
        tie(grad_part.astype(bf16), first_mixed, last_mixed), "ctx", scatter_dimension=0, tiled=True
    ).astype(f32)
    grad_attn_gain = jnp.sum(grad_part * (hidden_wide * scale_one), axis=0)
    rows_of = jnp.arange(planes)[:, None] == plane
    gains = [jnp.where(rows_of, g[None], 0.0).reshape(width) for g in grad_gains]
    gains = [g[:, None] for g in [grad_attn_gain, grad_ffn_gain] + gains]
    small = jnp.concatenate([grad_router] + gains, axis=1).reshape(planes, columns, -1)
    small = sum([small[plane]] + [swap(small[plane ^ step], step) for step in steps])
    sums = lax.all_to_all(tie(sums, grad_out_w), "fsdp", 0, 0, tiled=True)
    grad_out_w = jnp.sum(grad_out_w.astype(f32), axis=0).astype(bf16)
    came_out = [swap(grad_out_w[plane ^ step], step) for step in steps]
    grad_out_w = sum(x.astype(f32) for x in [grad_out_w[plane]] + came_out)
    small = lax.all_to_all(tie(small, sums, *came_out), "fsdp", 0, 0, tiled=True)
    small = jnp.sum(small, axis=0).reshape(strip, -1)
    sums = jnp.sum(sums.astype(f32), axis=0).astype(bf16)
    sums = lax.all_to_all(tie(sums, small), "ctx", 0, 0, tiled=True)
    grad_qkv_w = sums.reshape(planes, strip, 3, share).transpose(2, 1, 0, 3)
    grad_qkv_w = grad_qkv_w.reshape(3, strip, width).astype(f32)

    x_hat = hidden[0].astype(f32)
    scale_mine = lax.rsqrt(jnp.mean(x_hat * x_hat, axis=-1, keepdims=True) + epsilon)
    x_hat = x_hat * scale_mine
    grad_hat = grad_h_one * gain_attn
    grad_input = grad_middle + scale_mine * (
        grad_hat - x_hat * jnp.mean(grad_hat * x_hat, axis=-1, keepdims=True)
    )

    return (
        output[None],
        grad_input[None],
        grad_qkv_w[0],
        grad_qkv_w[1],
        grad_qkv_w[2],
        grad_out_w,
        small[:, :experts],
        small[:, experts],
        small[:, experts + 1],
        small[:, experts + 2],
        small[:, experts + 3],
        gate_grad,
        up_grad,
        down_grad,
    )


def solution(mesh):
    placed = (
        P("fsdp", "ctx", None),
        P("fsdp", None),
        P("fsdp", None),
        P("fsdp", "ctx", None),
        P("fsdp", "ctx", None),
        P(("ctx", "fsdp"), None),
        P(("ctx", "fsdp"), None),
        P(("ctx", "fsdp"), None),
        P(("ctx", "fsdp"), None),
        P(("ctx", "fsdp"), None),
        P(("ctx", "fsdp")),
        P(("ctx", "fsdp")),
        P(("ctx", "fsdp")),
        P(("ctx", "fsdp")),
        P("fsdp", "ctx", None),
        P("fsdp", "ctx", None),
        P("fsdp", "ctx", None),
    )

    def shards(*operands):
        experts_here = operands[14].shape[0]
        heads = operands[0].shape[2] // HEAD_DIM
        planes = mesh.shape["ctx"]
        whole_experts = experts_here == planes and heads % planes == 0 and planes in (2, 4)
        return (plane_shards if whole_experts else general_shards)(*operands)

    return jax.shard_map(
        shards,
        mesh=mesh,
        in_specs=placed,
        out_specs=(
            P("fsdp", "ctx", None),
            P("fsdp", "ctx", None),
            P(("ctx", "fsdp"), None),
            P(("ctx", "fsdp"), None),
            P(("ctx", "fsdp"), None),
            P(("ctx", "fsdp"), None),
            P(("ctx", "fsdp"), None),
            P(("ctx", "fsdp")),
            P(("ctx", "fsdp")),
            P(("ctx", "fsdp")),
            P(("ctx", "fsdp")),
            P("fsdp", "ctx", None),
            P("fsdp", "ctx", None),
            P("fsdp", "ctx", None),
        ),
        check_vma=False,
    )
```
